32 devices in a mesh: dp: 16 (over z, y, core), mp: 2 (over x).
Axes of the slice: x: 2, y: 2, z: 4, core: 2. Of those that a mesh axis runs over, the one named last changes fastest.
Arguments:
- pieces: bfloat16 [16384, 8, 512], P(('dp', 'mp')), may hold values from -6 to 6
- counts: int32 [16384], P(('dp', 'mp')), may hold values from 1 to 8
- token_index: int32 [16384], P('dp'), may hold values from 0 to 16383
- hyper_input: bfloat16 [512, 1536], P(('dp', 'mp')), may hold values from -0.25 to 0.25
- hyper_output: bfloat16 [512, 512], P(('dp', 'mp')), may hold values from -0.5 to 0.5
- hyper_expand: bfloat16 [512, 2048], P(('dp', 'mp')), may hold values from -0.25 to 0.25
- hyper_reduce: bfloat16 [2048, 512], P(('dp', 'mp')), may hold values from -0.125 to 0.125
- hyper_norms: bfloat16 [512, 4], P(('dp', 'mp')), may hold values from -0.5 to 1.5, as said below
- embed_weight: bfloat16 [512, 2048], P(('dp', 'mp')), may hold values from -0.25 to 0.25
- attention_gain: float32 [2048], replicated, may hold values from 0.5 to 1.5
- dense_gain: float32 [2048], replicated, may hold values from 0.1 to 1.9
- frozen_query_weight: bfloat16 [2048, 2048], P(None, 'mp'), may hold values from -0.125 to 0.125
- frozen_key_weight: bfloat16 [2048, 256], P(None, 'mp'), may hold values from -0.125 to 0.125
- frozen_value_weight: bfloat16 [2048, 256], P(None, 'mp'), may hold values from -0.125 to 0.125
- frozen_output_weight: bfloat16 [2048, 2048], P('mp'), may hold values from -0.5 to 0.5
- gate_weight: bfloat16 [2048, 5632], P(None, 'mp'), may hold values from -0.125 to 0.125
- up_weight: bfloat16 [2048, 5632], P(None, 'mp'), may hold values from -0.125 to 0.125
- down_weight: bfloat16 [5632, 2048], P('mp'), may hold values from -0.078125 to 0.078125
- upstream: bfloat16 [16384, 2048], P('dp'), may hold values from -6 to 6
Outputs:
- model_out: bfloat16 [16384, 2048], P('dp', 'mp')
- pieces_gradient: bfloat16 [16384, 8, 512], P(('dp', 'mp'))
- hyper_input_gradient: float32 [512, 1536], P(('dp', 'mp'))
- hyper_output_gradient: float32 [512, 512], P(('dp', 'mp'))
- hyper_expand_gradient: float32 [512, 2048], P(('dp', 'mp'))
- hyper_reduce_gradient: float32 [2048, 512], P(('dp', 'mp'))
- hyper_norms_gradient: float32 [512, 4], P(('dp', 'mp'))
- embed_weight_gradient: float32 [512, 2048], P(('dp', 'mp'))
The draws below stay inside these ranges and needn't reach their ends.
Inputs may be any that keep to these rules, and one draw needn't show every extreme that they name: `counts`: the number of live slots of each entry; slots at or past it are padding. `hyper_norms`: columns 0 and 2 are the two norms' gains, columns 1 and 3 their shifts.
All inputs are finite; a program needn't handle non-finite values.
Results may differ from the reference program's by a relative error of at most 0.025.
Values may be sent and summed in bfloat16 or wider, within the bound.
No kernel may reach another device: no remote copies, remote signals or barrier semaphores. Data moves between devices by JAX's collectives and lax.ppermute only.
A program may use at most 448 MiB of HBM per device.

```python
import math
import jax
import jax.numpy as jnp
import numpy as np
from jax import lax

D = 2048
QH = 32
KVH = 4
HEAD_WIDTH = 64
FF = 5632
HID = 512
HHEADS = 8
HHD = 64
HFF = 2048
SLOTS = 8
VOCAB = 16384
SEQUENCE_LENGTH = 1024
TOKENS = 16384
N_DP = 16
N_MP = 2


def draw_hyper_norms(key, part):
    key = jax.random.fold_in(key, 7)
    gain_key, shift_key = jax.random.split(key)
    gains = 1.0 + 0.2 * jax.random.truncated_normal(gain_key, -2.5, 2.5, (HID, 2), jnp.float32)
    shifts = 0.25 * jax.random.truncated_normal(shift_key, -2.0, 2.0, (HID, 2), jnp.float32)
    stacked = jnp.stack([gains[:, 0], shifts[:, 0], gains[:, 1], shifts[:, 1]], axis=1)
    return stacked.astype(jnp.bfloat16)


def plant(values, own_key, smallest, top_value):
    shape = values.shape
    spot = [jax.random.randint(jax.random.fold_in(own_key, axis), (), 0, shape[axis]) for axis in range(len(shape))]
    values = values.at[tuple(spot)].set(smallest)
    longest = shape.index(max(shape))
    spot[longest] = (spot[longest] + 1) % shape[longest]
    return values.at[tuple(spot)].set(top_value)


def level_of(stream_key, shape, shards, low, top_value):
    def one(axis_at, shards_of):
        draws = jax.random.uniform(jax.random.fold_in(jax.random.fold_in(stream_key, 6), axis_at), (shards_of,), jnp.float32, low / len(shards), top_value / len(shards))
        return jnp.repeat(jnp.exp(draws), shape[axis_at] // shards_of).reshape((-1,) + (1,) * (len(shape) - axis_at - 1))

    level = one(*shards[0])
    for cut in shards[1:]:
        level = level * one(*cut)
    return level


def cumulative_ranks(number_of, skew):
    loads = [(1 << 20) // math.isqrt(standing ** skew) + 1 for standing in range(1, number_of + 1)]
    deviation = 1 + sum(loads) // (1 << 30)
    return np.cumsum(np.array([max(1, weight // deviation) for weight in loads]))


def ranked(stream_key, extent, number_of, skew):
    listing = cumulative_ranks(number_of, skew)
    pick = jax.random.randint(jax.random.fold_in(stream_key, 1), extent, 0, int(listing[number_of - 1]))
    rank = jnp.searchsorted(jnp.asarray(listing, jnp.int32), pick, side="right")
    return jax.random.permutation(jax.random.fold_in(stream_key, 2), number_of)[rank].astype(jnp.int32)


def centred(rng, dims, deviation, most, cuts=(), kind=jnp.bfloat16):
    factor_of = level_of(rng, dims, cuts, -0.22, 0.18) if cuts else 1.0
    drawn = jax.random.normal(rng, dims, jnp.float32) * deviation * factor_of
    return jnp.minimum(jnp.maximum(drawn, -most), most).astype(kind)


def setup_inputs(seed: int = 0) -> dict:
    streams_of = jax.random.split(jax.random.key(seed), 20)
    pieces = centred(streams_of[0], (VOCAB, SLOTS, HID), 1.0, 6.0, ((0, 32),))
    counts = plant(jax.random.randint(streams_of[1], (VOCAB,), 1, SLOTS + 1), jax.random.fold_in(streams_of[1], 1), 1, SLOTS).astype(jnp.int32)
    token_index = plant(ranked(streams_of[2], (TOKENS,), VOCAB, 2), jax.random.fold_in(streams_of[2], 3), 0, VOCAB - 1).astype(jnp.int32)
    hyper_input = centred(streams_of[3], (HID, 3 * HID), HID ** -0.5, 0.25, ((0, 32),))
    hyper_output = centred(streams_of[4], (HID, HID), (HID // 4) ** -0.5, 0.5, ((0, 32),))
    hyper_expand = centred(streams_of[5], (HID, HFF), HID ** -0.5, 0.25, ((0, 32),))
    hyper_reduce = centred(streams_of[6], (HFF, HID), HFF ** -0.5, 0.125, ((0, 32),))
    hyper_norms = draw_hyper_norms(jax.random.fold_in(streams_of[19], 71), 0)
    embed_weight = centred(streams_of[8], (HID, D), HID ** -0.5, 0.25, ((0, 32),))
    attention_gain = jnp.clip(1.0 + 0.1 * jax.random.normal(streams_of[9], (D,), jnp.float32), 0.5, 1.5)
    dense_gain = jnp.clip(1.0 + 0.18 * jax.random.normal(streams_of[10], (D,), jnp.float32), 0.1, 1.9)
    frozen_query_weight = centred(streams_of[11], (D, QH * HEAD_WIDTH), D ** -0.5, 0.125, ((1, 2),))
    frozen_key_weight = centred(streams_of[12], (D, KVH * HEAD_WIDTH), D ** -0.5, 0.125, ((1, 2),))
    frozen_value_weight = centred(streams_of[13], (D, KVH * HEAD_WIDTH), D ** -0.5, 0.125, ((1, 2),))
    frozen_output_weight = centred(streams_of[14], (QH * HEAD_WIDTH, D), (QH * HEAD_WIDTH // 16) ** -0.5, 0.5, ((0, 2),))
    gate_weight = centred(streams_of[15], (D, FF), D ** -0.5, 0.125, ((1, 2),))
    up_weight = centred(streams_of[16], (D, FF), D ** -0.5, 0.125, ((1, 2),))
    down_weight = centred(streams_of[17], (FF, D), FF ** -0.5, 0.078125, ((0, 2),))
    upstream = centred(streams_of[18], (TOKENS, D), 1.0, 6.0, ((0, 16),))
    return {"pieces": pieces, "counts": counts, "token_index": token_index, "hyper_input": hyper_input, "hyper_output": hyper_output, "hyper_expand": hyper_expand, "hyper_reduce": hyper_reduce, "hyper_norms": hyper_norms, "embed_weight": embed_weight, "attention_gain": attention_gain, "dense_gain": dense_gain, "frozen_query_weight": frozen_query_weight, "frozen_key_weight": frozen_key_weight, "frozen_value_weight": frozen_value_weight, "frozen_output_weight": frozen_output_weight, "gate_weight": gate_weight, "up_weight": up_weight, "down_weight": down_weight, "upstream": upstream}


@jax.custom_vjp
def reduced_precision(v):
    return lax.optimization_barrier(v.astype(jnp.bfloat16)).astype(jnp.float32)

@jax.custom_vjp
def reduced_backward(v):
    return v

def low_keep(v):
    return (reduced_precision(v), None)

def low_pass(kept, grad):
    return (grad,)

def back_keep(v):
    return (v, None)

def back_low(kept, grad):
    return (reduced_precision(grad),)
reduced_precision.defvjp(low_keep, low_pass)
reduced_backward.defvjp(back_keep, back_low)
EPS = 1e-05
NEGATIVE = -1000000000.0
PRECISE_MATMUL = lax.Precision.HIGHEST

def layer_norm(value, gain, shift):
    centered = value - lax.optimization_barrier(jnp.mean(value, axis=-1, keepdims=True))
    spread = lax.optimization_barrier(jnp.mean(centered * centered, axis=-1, keepdims=True))
    return centered * lax.rsqrt(spread + EPS) * gain + shift

def rms_norm(value, gain):
    return value * lax.rsqrt(lax.optimization_barrier(jnp.mean(value * value, axis=-1, keepdims=True)) + EPS) * gain

def rotate(value, cosine, sine):
    half = value.shape[-1] // 2
    first = value[..., :half]
    second = value[..., half:]
    return jnp.concatenate([first * cosine - second * sine, second * cosine + first * sine], axis=-1)

def rope_tables(length, head_size):
    positions = jnp.arange(length, dtype=jnp.float32)
    inverse = 10000.0 ** (-jnp.arange(0, head_size, 2, dtype=jnp.float32) / head_size)
    angles = positions[:, None] * inverse[None, :]
    return (jnp.cos(angles), jnp.sin(angles))

def hyper_rows(pieces_float, rows_count, in_weight, out_weight, expand_weight, reduce_weight, norm_values):
    entries = pieces_float.shape[0]
    first_normed = reduced_precision(layer_norm(pieces_float, norm_values[:, 0], norm_values[:, 1]))
    mixed = reduced_precision(reduced_backward(jnp.einsum('vsh,hc->vsc', first_normed, in_weight, precision=PRECISE_MATMUL)))
    query = mixed[:, 0, :HID].reshape(entries, HHEADS, HHD)
    keys = mixed[:, :, HID:2 * HID].reshape(entries, SLOTS, HHEADS, HHD)
    value_rows = mixed[:, :, 2 * HID:].reshape(entries, SLOTS, HHEADS, HHD)
    scores = reduced_backward(jnp.einsum('vhd,vshd->vhs', query, keys, precision=PRECISE_MATMUL) * HHD ** (-0.5))
    live = jnp.arange(SLOTS, dtype=jnp.int32)[None, :] < rows_count[:, None]
    scores = jnp.where(live[:, None, :], scores, NEGATIVE)
    probs = reduced_precision(jax.nn.softmax(scores, axis=-1))
    attended_rows = reduced_precision(reduced_backward(jnp.einsum('vhs,vshd->vhd', probs, value_rows, precision=PRECISE_MATMUL))).reshape(entries, HID)
    hidden_state = pieces_float[:, 0, :] + reduced_backward(jnp.dot(attended_rows, out_weight, precision=PRECISE_MATMUL))
    second = reduced_precision(layer_norm(hidden_state, norm_values[:, 2], norm_values[:, 3]))
    expanded = reduced_backward(jnp.dot(second, expand_weight, precision=PRECISE_MATMUL))
    active = reduced_precision(jax.nn.gelu(expanded, approximate=False))
    return reduced_precision(hidden_state + reduced_backward(jnp.dot(active, reduce_weight, precision=PRECISE_MATMUL)))

def lm_rows(embedded, frozen, cosine, sine):
    attention_gain, dense_gain, frozen_query_weight, frozen_key_weight, frozen_value_weight, frozen_output_weight, gate_weight, up_weight, down_weight = frozen
    group_count = embedded.shape[0]
    heads_query = QH // N_MP
    key_head_count = KVH // N_MP
    repeat = QH // KVH
    units = FF // N_MP
    scale = HEAD_WIDTH ** (-0.5)
    causal = jnp.arange(SEQUENCE_LENGTH)[:, None] >= jnp.arange(SEQUENCE_LENGTH)[None, :]
    normed = rms_norm(embedded, attention_gain)
    hidden_state = embedded
    for shard in range(N_MP):
        sharded_input = reduced_precision(reduced_backward(normed))
        query_columns = slice(shard * heads_query * HEAD_WIDTH, (shard + 1) * heads_query * HEAD_WIDTH)
        key_columns = slice(shard * key_head_count * HEAD_WIDTH, (shard + 1) * key_head_count * HEAD_WIDTH)
        query_before_rotary = reduced_backward(jnp.einsum('nuj,jt->nut', sharded_input, frozen_query_weight[:, query_columns], precision=PRECISE_MATMUL))
        queries = reduced_precision(rotate(query_before_rotary.reshape(group_count, SEQUENCE_LENGTH, key_head_count, repeat, HEAD_WIDTH), cosine[:, None, None, :], sine[:, None, None, :]))
        key_before_rotary = reduced_backward(jnp.einsum('nuj,jt->nut', sharded_input, frozen_key_weight[:, key_columns], precision=PRECISE_MATMUL))
        keys = reduced_precision(rotate(key_before_rotary.reshape(group_count, SEQUENCE_LENGTH, key_head_count, HEAD_WIDTH), cosine[:, None, :], sine[:, None, :]))
        value_rows = reduced_precision(reduced_backward(jnp.einsum('nuj,jt->nut', sharded_input, frozen_value_weight[:, key_columns], precision=PRECISE_MATMUL))).reshape(group_count, SEQUENCE_LENGTH, key_head_count, HEAD_WIDTH)
        scores = reduced_backward(jnp.einsum('gqkrd,gtkd->gkrqt', queries, keys, precision=PRECISE_MATMUL) * scale)
        probs = reduced_precision(jax.nn.softmax(jnp.where(causal, scores, NEGATIVE), axis=-1))
        attended_rows = reduced_precision(reduced_backward(jnp.einsum('gkrqt,gtkd->gqkrd', probs, value_rows, precision=PRECISE_MATMUL))).reshape(group_count, SEQUENCE_LENGTH, heads_query * HEAD_WIDTH)
        hidden_state = hidden_state + reduced_precision(reduced_backward(jnp.einsum('bos,sj->boj', attended_rows, frozen_output_weight[query_columns, :], precision=PRECISE_MATMUL)))
    normed_second = rms_norm(hidden_state, dense_gain)
    result = hidden_state
    for shard in range(N_MP):
        sharded_input = reduced_precision(reduced_backward(normed_second))
        unit_span = slice(shard * units, (shard + 1) * units)
        gate_pre = reduced_backward(jnp.einsum('gld,df->glf', sharded_input, gate_weight[:, unit_span], precision=PRECISE_MATMUL))
        up_pre = reduced_backward(jnp.einsum('gld,df->glf', sharded_input, up_weight[:, unit_span], precision=PRECISE_MATMUL))
        active = reduced_precision(jax.nn.silu(gate_pre) * up_pre)
        result = result + reduced_precision(reduced_backward(jnp.einsum('glf,fd->gld', active, down_weight[unit_span, :], precision=PRECISE_MATMUL)))
    return result

def reference(pieces, counts, token_index, hyper_input, hyper_output, hyper_expand, hyper_reduce, hyper_norms, embed_weight, attention_gain, dense_gain, frozen_query_weight, frozen_key_weight, frozen_value_weight, frozen_output_weight, gate_weight, up_weight, down_weight, upstream):
    frozen = tuple((weight.astype(jnp.float32) for weight in (attention_gain, dense_gain, frozen_query_weight, frozen_key_weight, frozen_value_weight, frozen_output_weight, gate_weight, up_weight, down_weight)))
    cosine, sine = rope_tables(SEQUENCE_LENGTH, HEAD_WIDTH)
    vocab_block = math.gcd(VOCAB, 2048)
    seq_group = math.gcd(N_DP, max(1, 2048 // SEQUENCE_LENGTH))

    def forward(pieces_float, in_weight, out_weight, expand_weight, reduce_weight, norm_values, embed_float):

        def vocab_rows(blocks):
            return hyper_rows(blocks[0], blocks[1], in_weight, out_weight, expand_weight, reduce_weight, norm_values)
        pooled = lax.map(jax.checkpoint(vocab_rows), (pieces_float.reshape(VOCAB // vocab_block, vocab_block, SLOTS, HID), counts.reshape(VOCAB // vocab_block, vocab_block)))
        pooled = pooled.reshape(VOCAB, HID)
        table = reduced_precision(jnp.dot(pooled, embed_float, precision=PRECISE_MATMUL))
        embedded = reduced_backward(jnp.take(table, token_index, axis=0))

        def seq_rows(block):
            return lm_rows(block, frozen, cosine, sine)
        outputs = lax.map(jax.checkpoint(seq_rows), embedded.reshape(N_DP // seq_group, seq_group, SEQUENCE_LENGTH, D))
        return outputs.reshape(N_DP * SEQUENCE_LENGTH, D)
    result, pull = jax.vjp(forward, pieces.astype(jnp.float32), hyper_input.astype(jnp.float32), hyper_output.astype(jnp.float32), hyper_expand.astype(jnp.float32), hyper_reduce.astype(jnp.float32), hyper_norms.astype(jnp.float32), embed_weight.astype(jnp.float32))
    grads = pull(upstream.astype(jnp.float32))
    return (result.astype(jnp.bfloat16), grads[0].astype(jnp.bfloat16), grads[1], grads[2], grads[3], grads[4], grads[5], grads[6])
```

```python
import jax
import jax.numpy as jnp
from jax import lax
from jax.sharding import PartitionSpec as P

HEAD_WIDTH = 64
HHD = 64
BLOCK_PARTS = 4
UNIT = 512


EPS = 1e-05
NEGATIVE = -1000000000.0


def matmul(left, right):
    return jnp.dot(left, right, preferred_element_type=jnp.float32)


def matmul_first(left, right):
    return lax.dot_general(
        left, right, (((0,), (0,)), ((), ())), preferred_element_type=jnp.float32
    )


def matmul_last(left, right):
    return lax.dot_general(
        left, right, (((1,), (1,)), ((), ())), preferred_element_type=jnp.float32
    )


def layer_norm(value, gain, shift):
    centered = value - jnp.mean(value, axis=-1, keepdims=True)
    spread = jnp.mean(centered * centered, axis=-1, keepdims=True)
    return centered * lax.rsqrt(spread + EPS) * gain + shift


def rms_norm(value, gain):
    return value * lax.rsqrt(jnp.mean(value * value, axis=-1, keepdims=True) + EPS) * gain


def rotate(value, cosine, sine):
    half = value.shape[-1] // 2
    first = value[..., :half]
    second = value[..., half:]
    return jnp.concatenate(
        [first * cosine - second * sine, second * cosine + first * sine], axis=-1
    )


def rope_tables(length, head_size):
    positions = jnp.arange(length, dtype=jnp.float32)
    inverse = 10000.0 ** (-jnp.arange(0, head_size, 2, dtype=jnp.float32) / head_size)
    angles = positions[:, None] * inverse[None, :]
    return (jnp.cos(angles), jnp.sin(angles))


def exact_gelu(value):
    return jax.nn.gelu(value, approximate=False)


def gated_units(gate_pre, up_pre):
    return jax.nn.silu(gate_pre) * up_pre


def rounded(value):
    return lax.optimization_barrier(value.astype(jnp.bfloat16)).astype(jnp.float32)


def hyper_forward(rows_in, rows_count, weights):
    in_weight, out_weight, expand_weight, reduce_weight, norm_table = (
        weights[0],
        weights[1],
        weights[2],
        weights[3],
        weights[4],
    )
    entries, slots, width = rows_in.shape
    heads = width // HHD
    scale = HHD ** (-0.5)
    norm_values = norm_table.astype(jnp.float32)
    pieces_float = rows_in.astype(jnp.float32)
    first_normed, first_pull = jax.vjp(
        layer_norm, pieces_float, norm_values[:, 0], norm_values[:, 1]
    )
    first_low = first_normed.astype(jnp.bfloat16)
    flat_low = first_low.reshape(entries * slots, width)
    pair = (
        matmul(flat_low, in_weight[:, width:])
        .astype(jnp.bfloat16)
        .reshape(entries, slots, 2, heads, HHD)
    )
    keys = pair[:, :, 0]
    value_rows = pair[:, :, 1]
    lead_low = first_low[:, 0, :]
    query = matmul(lead_low, in_weight[:, :width]).astype(jnp.bfloat16).reshape(entries, heads, HHD)
    scores = jnp.einsum("vhd,vshd->vhs", query, keys, preferred_element_type=jnp.float32) * scale
    live = lax.broadcasted_iota(jnp.int32, (entries, slots), 1) < rows_count[:, None]
    scores = jnp.where(live[:, None, :], scores, NEGATIVE)
    probs = jax.nn.softmax(scores, axis=-1)
    probs_low = probs.astype(jnp.bfloat16)
    attended_rows = (
        jnp.einsum("vhs,vshd->vhd", probs_low, value_rows, preferred_element_type=jnp.float32)
        .astype(jnp.bfloat16)
        .reshape(entries, width)
    )
    hidden_state = pieces_float[:, 0, :] + matmul(attended_rows, out_weight)
    second, second_pull = jax.vjp(layer_norm, hidden_state, norm_values[:, 2], norm_values[:, 3])
    second_low = second.astype(jnp.bfloat16)
    expanded = matmul(second_low, expand_weight)
    active, gelu_pull = jax.vjp(exact_gelu, expanded)
    active_low = active.astype(jnp.bfloat16)
    pooled = (hidden_state + matmul(active_low, reduce_weight)).astype(jnp.bfloat16)
    saved = (
        first_pull,
        flat_low,
        lead_low,
        keys,
        value_rows,
        query,
        probs,
        probs_low,
        attended_rows,
        second_pull,
        second_low,
        gelu_pull,
        active_low,
    )
    return (pooled, saved)


def hyper_backward(saved, grad_pooled, weights):
    in_weight, out_weight, expand_weight, reduce_weight = (
        weights[0],
        weights[1],
        weights[2],
        weights[3],
    )
    (
        first_pull,
        flat_low,
        lead_low,
        keys,
        value_rows,
        query,
        probs,
        probs_low,
        attended_rows,
        second_pull,
        second_low,
        gelu_pull,
        active_low,
    ) = saved
    entries, heads, head_size = query.shape
    width = heads * head_size
    slots = keys.shape[1]
    scale = head_size ** (-0.5)
    grad_low = grad_pooled.astype(jnp.bfloat16)
    reduce_grad = matmul_first(active_low, grad_low)
    (grad_expanded,) = gelu_pull(matmul_last(grad_low, reduce_weight))
    grad_expanded = grad_expanded.astype(jnp.bfloat16)
    expand_grad = matmul_first(second_low, grad_expanded)
    grad_hidden_norm, gain_two, shift_two = second_pull(matmul_last(grad_expanded, expand_weight))
    grad_hidden = grad_pooled + grad_hidden_norm
    hidden_low = grad_hidden.astype(jnp.bfloat16)
    output_grad = matmul_first(attended_rows, hidden_low)
    grad_attended = (
        matmul_last(hidden_low, out_weight).astype(jnp.bfloat16).reshape(entries, heads, head_size)
    )
    grad_probs = jnp.einsum(
        "vhd,vshd->vhs", grad_attended, value_rows, preferred_element_type=jnp.float32
    )
    grad_scores = (
        probs * (grad_probs - jnp.sum(probs * grad_probs, axis=-1, keepdims=True))
    ).astype(jnp.bfloat16)
    grad_query = (
        (jnp.einsum("vhs,vshd->vhd", grad_scores, keys, preferred_element_type=jnp.float32) * scale)
        .astype(jnp.bfloat16)
        .reshape(entries, width)
    )
    grad_keys = (
        jnp.einsum("vhs,vhd->vshd", grad_scores, query, preferred_element_type=jnp.float32) * scale
    )
    grad_values = jnp.einsum(
        "vhs,vhd->vshd", probs_low, grad_attended, preferred_element_type=jnp.float32
    )
    grad_pair = (
        jnp.stack([grad_keys, grad_values], axis=2)
        .astype(jnp.bfloat16)
        .reshape(entries * slots, 2 * width)
    )
    input_grad = jnp.concatenate(
        [matmul_first(lead_low, grad_query), matmul_first(flat_low, grad_pair)], axis=1
    )
    grad_first = matmul_last(grad_pair, in_weight[:, width:]).reshape(entries, slots, width)
    grad_first = grad_first.at[:, 0, :].add(matmul_last(grad_query, in_weight[:, :width]))
    grad_pieces, gain_one, shift_one = first_pull(grad_first)
    grad_pieces = grad_pieces.at[:, 0, :].add(grad_hidden)
    norm_grad = jnp.stack([gain_one, shift_one, gain_two, shift_two], axis=1)
    return (grad_pieces, (input_grad, output_grad, expand_grad, reduce_grad, norm_grad))


def causal_mask(length):
    return lax.broadcasted_iota(jnp.int32, (length, length), 0) >= lax.broadcasted_iota(
        jnp.int32, (length, length), 1
    )


def log2_of(number):
    return number.bit_length() - 1


def swap(value, mask, devices):
    return lax.ppermute(value, ("dp", "mp"), [(d, d ^ mask) for d in range(devices)])


def gather_blocks(block, me, devices, order):
    bits = log2_of(devices)
    held = block.reshape((1,) * bits + block.shape)
    for bit in order:
        axis = bits - 1 - bit
        arrived = swap(held, 1 << bit, devices)
        upper = ((me >> bit) & 1) == 1
        held = jnp.where(
            upper,
            jnp.concatenate([arrived, held], axis),
            jnp.concatenate([held, arrived], axis),
        )
    return held.reshape((devices,) + block.shape)


def scatter_blocks(blocks, me, devices, order):
    bits = log2_of(devices)
    held = blocks.reshape((2,) * bits + blocks.shape[1:])
    for bit in order:
        axis = bits - 1 - bit
        mine = (me >> bit) & 1
        leaving = lax.dynamic_slice_in_dim(held, 1 - mine, 1, axis).astype(jnp.bfloat16)
        staying = lax.dynamic_slice_in_dim(held, mine, 1, axis)
        held = staying + swap(leaving, 1 << bit, devices).astype(jnp.float32)
    return held.reshape(blocks.shape[1:])


def fold(value, devices):
    rows, width = value.shape
    parts = width // UNIT
    each = rows // devices
    return (
        value.reshape(devices, each, parts, UNIT).transpose(0, 2, 1, 3).reshape(devices, parts * each, UNIT)
    )


def unfold(blocks, parts):
    devices, total, unit = blocks.shape
    each = total // parts
    return blocks.reshape(devices, parts, each, unit).transpose(0, 2, 1, 3).reshape(devices * each, parts * unit)


def attention_forward(queries, keys, value_rows, base):
    rows, heads, head_size = queries.shape
    groups = keys.shape[0]
    repeat = heads // groups
    length = keys.shape[1]
    scale = head_size ** (-0.5)
    causal = base + lax.broadcasted_iota(jnp.int32, (rows, length), 0) >= lax.broadcasted_iota(
        jnp.int32, (rows, length), 1
    )
    outputs = []
    sums = []
    for group in range(groups):
        query_group = queries[:, group * repeat : (group + 1) * repeat, :]
        scores = (
            jnp.einsum("qrd,kd->rqk", query_group, keys[group], preferred_element_type=jnp.float32)
            * scale
        )
        scores = jnp.where(causal, scores, NEGATIVE)
        highest = jnp.max(scores, axis=-1, keepdims=True)
        exponent = jnp.exp(scores - highest)
        total = jnp.sum(exponent, axis=-1, keepdims=True)
        probs_low = (exponent / total).astype(jnp.bfloat16)
        outputs.append(
            jnp.einsum(
                "rqk,kd->qrd", probs_low, value_rows[group], preferred_element_type=jnp.float32
            )
        )
        sums.append(highest + jnp.log(total))
    return (jnp.concatenate(outputs, axis=1).astype(jnp.bfloat16), sums)


def attention_backward(queries, keys, value_rows, grad_out, sums, base):
    rows, heads, head_size = queries.shape
    groups = keys.shape[0]
    repeat = heads // groups
    length = keys.shape[1]
    scale = head_size ** (-0.5)
    causal = base + lax.broadcasted_iota(jnp.int32, (rows, length), 0) >= lax.broadcasted_iota(
        jnp.int32, (rows, length), 1
    )
    grad_queries = []
    grad_keys = []
    grad_values = []
    for group in range(groups):
        query_group = queries[:, group * repeat : (group + 1) * repeat, :]
        key_group = keys[group]
        value_group = value_rows[group]
        grad_group = grad_out[:, group * repeat : (group + 1) * repeat, :]
        scores = (
            jnp.einsum("qrd,kd->rqk", query_group, key_group, preferred_element_type=jnp.float32)
            * scale
        )
        probs = jnp.exp(jnp.where(causal, scores, NEGATIVE) - sums[group])
        grad_probs = jnp.einsum(
            "qrd,kd->rqk", grad_group, value_group, preferred_element_type=jnp.float32
        )
        grad_scores = (
            probs * (grad_probs - jnp.sum(probs * grad_probs, axis=-1, keepdims=True))
        ).astype(jnp.bfloat16)
        grad_queries.append(
            jnp.einsum("rqk,kd->qrd", grad_scores, key_group, preferred_element_type=jnp.float32)
            * scale
        )
        grad_keys.append(
            jnp.einsum("rqk,qrd->kd", grad_scores, query_group, preferred_element_type=jnp.float32)
            * scale
        )
        grad_values.append(
            jnp.einsum(
                "rqk,qrd->kd",
                probs.astype(jnp.bfloat16),
                grad_group,
                preferred_element_type=jnp.float32,
            )
        )
    return (
        jnp.concatenate(grad_queries, axis=1),
        jnp.stack(grad_keys, axis=0),
        jnp.stack(grad_values, axis=0),
    )


def route(token_index, me, devices, local_vocab, capacity, mp_count):
    groups = devices // mp_count
    every = lax.all_gather(token_index, "dp", axis=0, tiled=True)
    step = token_index.shape[0] // BLOCK_PARTS
    cut = every.reshape(groups, BLOCK_PARTS, step)
    asked = jnp.stack(
        [
            jnp.concatenate([cut[:, 0], cut[:, 3]], axis=1),
            jnp.concatenate([cut[:, 1], cut[:, 2]], axis=1),
        ],
        axis=1,
    ).reshape(devices, 2 * step)
    count = 2 * step
    places = jnp.arange(count, dtype=jnp.int32)
    same = asked[:, :, None] == asked[:, None, :]
    earlier = places[:, None] > places[None, :]
    repeated = jnp.any(same & earlier[None], axis=2)
    first = jnp.logical_not(repeated)
    owner = asked // local_vocab
    before = (
        (owner[:, :, None] == owner[:, None, :])
        & (asked[:, None, :] < asked[:, :, None])
        & first[:, None, :]
    )
    rank = jnp.sum(before.astype(jnp.int32), axis=2)
    rounds = jnp.max(rank) // capacity + 1
    own_rank = lax.dynamic_index_in_dim(rank, me, 0, False)
    own_owner = lax.dynamic_index_in_dim(owner, me, 0, False)
    entries = me * local_vocab + jnp.arange(local_vocab, dtype=jnp.int32)
    present = jnp.any(asked[:, :, None] == entries[None, None, :], axis=1)
    lower = (
        jnp.arange(local_vocab, dtype=jnp.int32)[:, None]
        < jnp.arange(local_vocab, dtype=jnp.int32)[None, :]
    )
    standing = matmul(present.astype(jnp.bfloat16), lower.astype(jnp.bfloat16)).astype(jnp.int32)
    return (rounds, own_rank, own_owner, present, standing)


def sender_choice(present, standing, turn, capacity):
    slot = turn * capacity + jnp.arange(capacity, dtype=jnp.int32)
    chosen = present[:, None, :] & (standing[:, None, :] == slot[None, :, None])
    return chosen.astype(jnp.bfloat16).reshape(present.shape[0] * capacity, present.shape[1])


def taker_choice(own_rank, own_owner, turn, capacity, devices):
    inside = own_rank - turn * capacity
    valid = (inside >= 0) & (inside < capacity)
    place = jnp.where(valid, own_owner * capacity + inside, -1)
    return (place[:, None] == jnp.arange(devices * capacity, dtype=jnp.int32)[None, :]).astype(
        jnp.bfloat16
    )


def exchange(value):
    return lax.all_to_all(value, ("dp", "mp"), 0, 0, tiled=True)


def ordered_blocks(first, own_two, other_two):
    return jnp.where(
        first,
        jnp.concatenate([own_two[0], other_two[0], other_two[1], own_two[1]], axis=0),
        jnp.concatenate([other_two[0], own_two[0], own_two[1], other_two[1]], axis=0),
    )


def body(
    pieces,
    counts,
    token_index,
    hyper_input,
    hyper_output,
    hyper_expand,
    hyper_reduce,
    hyper_norms,
    embed_weight,
    attention_gain,
    dense_gain,
    frozen_query_weight,
    frozen_key_weight,
    frozen_value_weight,
    frozen_output_weight,
    gate_weight,
    up_weight,
    down_weight,
    upstream,
):
    local_vocab = pieces.shape[0]
    mp_count = lax.axis_size("mp")
    devices = lax.axis_size("dp") * mp_count
    mp_index = lax.axis_index("mp")
    me = lax.axis_index("dp") * mp_count + mp_index
    core = (me >> 1) & 1
    lead = mp_index == 0
    bits = log2_of(devices)
    spread_order = list(range(bits - 1, 1, -1)) + [0, 1]
    width = hyper_input.shape[0] * devices
    own_rows = hyper_input.shape[0]
    length = token_index.shape[0]
    block = length // BLOCK_PARTS
    capacity = max(16, 32 * length // (devices * 32))

    norm_rows = jnp.pad(hyper_norms, ((0, 0), (0, UNIT - hyper_norms.shape[1])))
    first_pack = jnp.concatenate([fold(hyper_input, 1)[0], norm_rows], axis=0)
    second_pack = jnp.concatenate(
        [
            hyper_output,
            fold(hyper_expand, 1)[0],
            hyper_reduce,
            fold(embed_weight, 1)[0],
        ],
        axis=0,
    )
    first_all = gather_blocks(first_pack, me, devices, spread_order)
    second_all = gather_blocks(second_pack, me, devices, spread_order)
    in_parts = hyper_input.shape[1] // UNIT
    in_weight = unfold(first_all[:, : in_parts * own_rows], in_parts)
    norm_table = first_all[:, in_parts * own_rows :, : hyper_norms.shape[1]].reshape(
        width, hyper_norms.shape[1]
    )
    at = own_rows
    out_weight = second_all[:, :at].reshape(width, UNIT)
    expand_parts = hyper_expand.shape[1] // UNIT
    expand_weight = unfold(second_all[:, at : at + expand_parts * own_rows], expand_parts)
    at += expand_parts * own_rows
    reduce_weight = second_all[:, at : at + hyper_reduce.shape[0]].reshape(
        hyper_reduce.shape[0] * devices, UNIT
    )
    at += hyper_reduce.shape[0]
    embed_parts = embed_weight.shape[1] // UNIT
    embed_full = unfold(second_all[:, at:], embed_parts)
    gathered = (in_weight, out_weight, expand_weight, reduce_weight, norm_table)

    query_cut = frozen_query_weight.shape[1] // 2
    key_pair = jnp.concatenate([frozen_key_weight, frozen_value_weight], axis=1)
    query_near = swap(
        lax.dynamic_slice_in_dim(frozen_query_weight, core * query_cut, query_cut, 1), 1, devices
    )
    output_near = swap(
        lax.dynamic_slice_in_dim(frozen_output_weight, core * query_cut, query_cut, 0), 1, devices
    )
    key_other = swap(key_pair, 1, devices)
    query_far = swap(query_near, 2, devices)
    output_far = swap(output_near, 2, devices)
    kv_local = frozen_key_weight.shape[1] // HEAD_WIDTH
    span = frozen_key_weight.shape[1]

    def whole_keys(own, other):
        return jnp.where(
            lead, jnp.concatenate([own, other], axis=1), jnp.concatenate([other, own], axis=1)
        )

    key_weight = whole_keys(frozen_key_weight, key_other[:, :span])
    value_weight = whole_keys(frozen_value_weight, key_other[:, span:])
    key_heads = key_weight.shape[1] // HEAD_WIDTH
    other_base = (1 - mp_index) * kv_local
    head_order = jnp.stack(
        [mp_index * kv_local, mp_index * kv_local + 1, other_base + core, other_base + 1 - core]
    )

    rounds, own_rank, own_owner, present, standing = route(
        token_index, me, devices, local_vocab, capacity, mp_count
    )

    pooled, saved = hyper_forward(pieces, counts, gathered)

    def fetch(turn, chosen):
        sent = matmul(sender_choice(present, standing, turn, capacity), pooled).astype(jnp.bfloat16)
        came = exchange(sent)
        picked = matmul(taker_choice(own_rank, own_owner, turn, capacity, devices), came)
        return chosen + picked.astype(jnp.bfloat16)

    chosen_own = fetch(0, jnp.zeros((2 * block, pooled.shape[1]), jnp.bfloat16))
    chosen_own = lax.fori_loop(1, rounds, fetch, chosen_own)
    chosen_other = swap(chosen_own, 1, devices)

    cosine, sine = rope_tables(length, HEAD_WIDTH)
    own_base = (mp_index * block, (3 - mp_index) * block)
    other_start = ((1 - mp_index) * block, (2 + mp_index) * block)

    def own_blocks(value):
        return jnp.concatenate(
            [lax.dynamic_slice_in_dim(value, start, block, 0) for start in own_base], axis=0
        )

    def first_norm(value):
        return rms_norm(value, attention_gain)

    def second_norm(value):
        return rms_norm(value, dense_gain)

    embedded = rounded(matmul(chosen_own, embed_full))
    first_normed, first_pull = jax.vjp(first_norm, embedded)
    first_low = first_normed.astype(jnp.bfloat16)
    query_weights = (frozen_query_weight, query_near, query_far)
    output_weights = (frozen_output_weight, output_near, output_far)
    query_pre = jnp.concatenate([matmul(first_low, part) for part in query_weights], axis=1)
    heads = query_pre.shape[1] // HEAD_WIDTH
    own_cosine, own_sine = own_blocks(cosine), own_blocks(sine)

    def turn_own(value):
        return rotate(value, own_cosine[:, None, :], own_sine[:, None, :])

    queries, query_pull = jax.vjp(turn_own, query_pre.reshape(2 * block, heads, HEAD_WIDTH))
    queries = queries.astype(jnp.bfloat16)
    other_low = first_norm(rounded(matmul(chosen_other, embed_full))).astype(jnp.bfloat16)

    def in_order(own, other):
        return ordered_blocks(lead, (own[:block], own[block:]), (other[:block], other[block:]))

    key_pre = in_order(matmul(first_low, key_weight), matmul(other_low, key_weight))
    values_low = in_order(
        matmul(first_low, value_weight).astype(jnp.bfloat16),
        matmul(other_low, value_weight).astype(jnp.bfloat16),
    )
    keys = rotate(
        key_pre.reshape(length, key_heads, HEAD_WIDTH), cosine[:, None, :], sine[:, None, :]
    ).astype(jnp.bfloat16)
    keys_by = jnp.take(keys.transpose(1, 0, 2), head_order, axis=0)
    values_by = jnp.take(
        values_low.reshape(length, key_heads, HEAD_WIDTH).transpose(1, 0, 2), head_order, axis=0
    )

    sums = []
    hidden_parts = []
    second_pulls = []
    second_rows = []
    for part in range(2):
        rows = slice(part * block, (part + 1) * block)
        attended_rows, part_sums = attention_forward(
            queries[rows], keys_by, values_by, own_base[part]
        )
        sums.append(part_sums)
        flat = attended_rows.reshape(block, heads * HEAD_WIDTH)
        mixed = 0.0
        at = 0
        for weight in output_weights:
            mixed = mixed + matmul(flat[:, at : at + weight.shape[0]], weight)
            at += weight.shape[0]
        hidden_state = embedded[rows] + mixed
        hidden_parts.append(hidden_state)
        second_normed, pull = jax.vjp(second_norm, hidden_state)
        second_pulls.append(pull)
        second_low = second_normed.astype(jnp.bfloat16)
        second_rows.append(jnp.concatenate([second_low, swap(second_low, 1, devices)], axis=0))

    active_rows = []
    grad_hidden = []
    for part in range(2):
        second_low = second_rows[part]
        rising = jnp.concatenate(
            [
                lax.dynamic_slice_in_dim(upstream, own_base[part], block, 0),
                lax.dynamic_slice_in_dim(upstream, other_start[part], block, 0),
            ],
            axis=0,
        )
        gate_pre = matmul(second_low, gate_weight)
        up_pre = matmul(second_low, up_weight)
        active, active_pull = jax.vjp(gated_units, gate_pre, up_pre)
        active_rows.append(active.astype(jnp.bfloat16))
        grad_gate, grad_up = active_pull(matmul_last(rising, down_weight))
        grad_second = (
            matmul_last(grad_gate.astype(jnp.bfloat16), gate_weight)
            + matmul_last(grad_up.astype(jnp.bfloat16), up_weight)
        ).astype(jnp.bfloat16)
        total = grad_second[:block].astype(jnp.float32) + swap(
            grad_second[block:], 1, devices
        ).astype(jnp.float32)
        (grad_hidden_norm,) = second_pulls[part](total)
        grad_hidden.append(rising[:block].astype(jnp.float32) + grad_hidden_norm)

    share = upstream.shape[1] // mp_count
    own_out = []
    other_out = []
    for part in range(2):
        dense = matmul(active_rows[part], down_weight)
        dense_own = dense[:block] + hidden_parts[part]
        dense_other = dense[block:]

        def columns(value, index):
            return lax.dynamic_slice_in_dim(value, index * share, share, 1)

        leaving = jnp.concatenate(
            [columns(dense_other, 1 - mp_index), columns(dense_own, 1 - mp_index)], axis=0
        ).astype(jnp.bfloat16)
        arrived = swap(leaving, 1, devices).astype(jnp.float32)
        own_out.append((columns(dense_own, mp_index) + arrived[:block]).astype(jnp.bfloat16))
        other_out.append((columns(dense_other, mp_index) + arrived[block:]).astype(jnp.bfloat16))
    model_out = ordered_blocks(lead, own_out, other_out)

    grad_queries = []
    grad_keys = 0.0
    grad_values = 0.0
    for part in range(2):
        rows = slice(part * block, (part + 1) * block)
        hidden_low = grad_hidden[part].astype(jnp.bfloat16)
        grad_attended = jnp.concatenate(
            [matmul_last(hidden_low, weight).astype(jnp.bfloat16) for weight in output_weights],
            axis=1,
        ).reshape(block, heads, HEAD_WIDTH)
        part_queries, part_keys, part_values = attention_backward(
            queries[rows], keys_by, values_by, grad_attended, sums[part], own_base[part]
        )
        grad_queries.append(part_queries)
        grad_keys = grad_keys + part_keys
        grad_values = grad_values + part_values
    back_order = jnp.argsort(head_order)
    pair_grad = jnp.stack(
        [jnp.take(grad_keys, back_order, axis=0), jnp.take(grad_values, back_order, axis=0)], axis=0
    )

    def pick_blocks(starts):
        return jnp.concatenate(
            [lax.dynamic_slice_in_dim(pair_grad, start, block, 2) for start in starts], axis=2
        )

    pair_total = pick_blocks(own_base) + swap(
        pick_blocks(other_start).astype(jnp.bfloat16), 1, devices
    ).astype(jnp.float32)
    (grad_query_pre,) = query_pull(jnp.concatenate(grad_queries, axis=0))
    grad_query_low = grad_query_pre.reshape(2 * block, heads * HEAD_WIDTH).astype(jnp.bfloat16)
    grad_key_own = pair_total[0].transpose(1, 0, 2)
    grad_key_pre = rotate(grad_key_own, own_cosine[:, None, :], -own_sine[:, None, :])
    grad_key_low = grad_key_pre.reshape(2 * block, key_heads * HEAD_WIDTH).astype(jnp.bfloat16)
    grad_value_low = (
        pair_total[1].transpose(1, 0, 2).reshape(2 * block, key_heads * HEAD_WIDTH).astype(jnp.bfloat16)
    )
    grad_first = matmul_last(grad_key_low, key_weight) + matmul_last(grad_value_low, value_weight)
    at = 0
    for weight in query_weights:
        grad_first = grad_first + matmul_last(grad_query_low[:, at : at + weight.shape[1]], weight)
        at += weight.shape[1]
    (grad_embed_norm,) = first_pull(grad_first)
    embedded_grad_low = (jnp.concatenate(grad_hidden, axis=0) + grad_embed_norm).astype(
        jnp.bfloat16
    )
    token_grad = matmul_last(embedded_grad_low, embed_full).astype(jnp.bfloat16)
    embed_grad = matmul_first(chosen_own, embedded_grad_low)

    def give_back(turn, total):
        taker = taker_choice(own_rank, own_owner, turn, capacity, devices)
        leaving = matmul_first(taker, token_grad).astype(jnp.bfloat16)
        came = exchange(leaving)
        return total + matmul_first(sender_choice(present, standing, turn, capacity), came)

    grad_pooled = give_back(0, jnp.zeros(pooled.shape, jnp.float32))
    grad_pooled = lax.fori_loop(1, rounds, give_back, grad_pooled)

    grad_rows, grads = hyper_backward(saved, grad_pooled, gathered)
    input_grad, output_grad, expand_grad, reduce_grad, norm_grad = grads
    final_order = spread_order[::-1]
    packed = jnp.concatenate(
        [
            fold(input_grad, devices),
            fold(output_grad, devices),
            fold(expand_grad, devices),
            reduce_grad.reshape(devices, hyper_reduce.shape[0], UNIT),
            fold(jnp.pad(norm_grad, ((0, 0), (0, UNIT - norm_grad.shape[1]))), devices),
        ],
        axis=1,
    )
    embed_own = scatter_blocks(fold(embed_grad, devices), me, devices, final_order)
    own = scatter_blocks(packed, me, devices, final_order)

    def spread(rows, parts):
        return unfold(rows[None], parts)

    at = in_parts * own_rows
    input_own = spread(own[:at], in_parts)
    output_own = own[at : at + own_rows]
    at += own_rows
    expand_own = spread(own[at : at + expand_parts * own_rows], expand_parts)
    at += expand_parts * own_rows
    reduce_own = own[at : at + hyper_reduce.shape[0]]
    at += hyper_reduce.shape[0]
    norm_own = own[at:, : hyper_norms.shape[1]]
    return (
        model_out,
        grad_rows.astype(jnp.bfloat16),
        input_own,
        output_own,
        expand_own,
        reduce_own,
        norm_own,
        spread(embed_own, embed_parts),
    )


def solution(mesh):
    return jax.shard_map(
        body,
        mesh=mesh,
        in_specs=(
            P(("dp", "mp"), None, None),
            P(("dp", "mp")),
            P("dp"),
            P(("dp", "mp"), None),
            P(("dp", "mp"), None),
            P(("dp", "mp"), None),
            P(("dp", "mp"), None),
            P(("dp", "mp"), None),
            P(("dp", "mp"), None),
            P(),
            P(),
            P(None, "mp"),
            P(None, "mp"),
            P(None, "mp"),
            P("mp", None),
            P(None, "mp"),
            P(None, "mp"),
            P("mp", None),
            P("dp", None),
        ),
        out_specs=(
            P("dp", "mp"),
            P(("dp", "mp"), None, None),
            P(("dp", "mp"), None),
            P(("dp", "mp"), None),
            P(("dp", "mp"), None),
            P(("dp", "mp"), None),
            P(("dp", "mp"), None),
            P(("dp", "mp"), None),
        ),
        check_vma=False,
    )
```

```python
import jax
import jax.numpy as jnp
import numpy as np
from jax import lax
from jax.experimental import pallas as pl
from jax.experimental.pallas import tpu as pltpu
from jax.sharding import PartitionSpec as P

HEAD_WIDTH = 64
HHD = 64
BLOCK_PARTS = 4
UNIT = 512
PAIR = 2 * HEAD_WIDTH
VMEM_LIMIT = 48 << 20
ENTRY_BLOCK = 64
UNIT_ROWS = 256


EPS = 1e-05
NEGATIVE = -1000000000.0


def matmul(left, right):
    return jnp.dot(left, right, preferred_element_type=jnp.float32)


def matmul_first(left, right):
    return lax.dot_general(
        left, right, (((0,), (0,)), ((), ())), preferred_element_type=jnp.float32
    )


def matmul_last(left, right):
    return lax.dot_general(
        left, right, (((1,), (1,)), ((), ())), preferred_element_type=jnp.float32
    )


def rms_norm(value, gain):
    return value * lax.rsqrt(jnp.mean(value * value, axis=-1, keepdims=True) + EPS) * gain


def gated_units(gate_pre, up_pre):
    return jax.nn.silu(gate_pre) * up_pre


def rounded(value):
    return lax.optimization_barrier(value.astype(jnp.bfloat16)).astype(jnp.float32)


def log2_of(number):
    return number.bit_length() - 1


def swap(value, mask, devices):
    return lax.ppermute(value, ("dp", "mp"), [(d, d ^ mask) for d in range(devices)])


def gather_blocks(block, me, devices, order):
    bits = log2_of(devices)
    held = block.reshape((1,) * bits + block.shape)
    begun = None
    for bit in order:
        axis = bits - 1 - bit
        arrived = swap(held, 1 << bit, devices)
        upper = ((me >> bit) & 1) == 1
        held = jnp.where(
            upper,
            jnp.concatenate([arrived, held], axis),
            jnp.concatenate([held, arrived], axis),
        )
        begun = held if begun is None else begun
    return (held.reshape((devices * block.shape[0],) + block.shape[1:]), begun)


def scatter_blocks(blocks, me, devices, order):
    bits = log2_of(devices)
    held = blocks.reshape((2,) * bits + (blocks.shape[0] // devices,) + blocks.shape[1:])
    for bit in order:
        axis = bits - 1 - bit
        mine = (me >> bit) & 1
        leaving = lax.dynamic_slice_in_dim(held, 1 - mine, 1, axis).astype(jnp.bfloat16)
        staying = lax.dynamic_slice_in_dim(held, mine, 1, axis)
        held = staying.astype(jnp.float32) + swap(leaving, 1 << bit, devices).astype(jnp.float32)
    return held.reshape(held.shape[bits:])


def lanes(shape):
    return lax.broadcasted_iota(jnp.int32, shape, len(shape) - 1)


def half_swap(value):
    quarter = HEAD_WIDTH // 2
    upper = (lanes(value.shape) & quarter) != 0
    return jnp.where(
        upper, pltpu.roll(value, quarter, 1), pltpu.roll(value, PAIR - quarter, 1)
    )


def to_low(value):
    return value.astype(jnp.bfloat16)


def causal_of(shape, block_at, rows):
    key_at = lax.broadcasted_iota(jnp.int32, shape, 0)
    query_at = lax.broadcasted_iota(jnp.int32, shape, 1) + block_at * rows
    return key_at <= query_at


def head_views(pair_ref, cos_ref, sin_ref):
    pair = pair_ref[...]
    turned = to_low(pair * cos_ref[...] + half_swap(pair) * sin_ref[...]).astype(jnp.float32)
    other = pltpu.roll(turned, HEAD_WIDTH, 1)
    left = lanes(turned.shape) < HEAD_WIDTH
    return (
        jnp.where(left, turned, 0.0),
        jnp.where(left, 0.0, other),
        jnp.where(left, other, 0.0),
        jnp.where(left, 0.0, turned),
    )


def attention_forward_kernel(
    info, near_ref, mid_ref, far_ref, pair_ref, cos_pair, sin_pair, cos_ref, sin_ref,
    out_ref, low_ref, lse_ref, even, odd, across, query_ref,
):
    group = pl.program_id(0)
    key_left, key_right, value_left, _ = head_views(pair_ref, cos_pair, sin_pair)
    even[...] = to_low(key_left)
    odd[...] = to_low(key_right)
    across[...] = to_low(value_left.T[:HEAD_WIDTH])

    @pl.when(group < 2)
    def take_near():
        query_ref[...] = near_ref[...]

    @pl.when(group == 2)
    def take_mid():
        query_ref[...] = mid_ref[...]

    @pl.when(group == 3)
    def take_far():
        query_ref[...] = far_ref[...]

    rows = query_ref.shape[0]
    length = pair_ref.shape[0]
    causal = causal_of((length, rows), info[0], rows)
    for pair in range(query_ref.shape[1] // PAIR):
        span = slice(pair * PAIR, (pair + 1) * PAIR)
        query = query_ref[:, span]
        turned = to_low(query * cos_ref[...] + half_swap(query) * sin_ref[...])
        low = to_low(turned.astype(jnp.float32) * HEAD_WIDTH ** (-0.5))
        low_ref[:, span] = low
        outs = []
        for at, keys in enumerate((even, odd)):
            scores = jnp.where(causal, matmul_last(keys[...], low), NEGATIVE)
            highest = jnp.max(scores, axis=0, keepdims=True)
            weight = jnp.exp(scores - highest)
            total = jnp.sum(weight, axis=0, keepdims=True)
            outs.append(matmul(across[...], to_low(weight)) / total)
            lse_ref[0, 2 * pair + at : 2 * pair + at + 1, :] = highest + jnp.log(total)
        out_ref[:, span] = to_low(jnp.concatenate(outs, axis=0).T)


def attention_backward_kernel(
    info, low_ref, near_ref, mid_ref, far_ref, lse_ref, pair_ref, cos_pair, sin_pair, cos_ref, sin_ref,
    query_ref, pair_grad_ref, even, odd, value_even, value_odd, across,
    key_even, key_odd, sum_even, sum_odd, grad_ref,
):
    group = pl.program_id(0)
    key_left, key_right, value_left, value_right = head_views(pair_ref, cos_pair, sin_pair)
    even[...] = to_low(key_left)
    odd[...] = to_low(key_right)
    value_even[...] = to_low(value_left)
    value_odd[...] = to_low(value_right)
    across[...] = to_low(key_left.T[:HEAD_WIDTH])
    for total in (key_even, key_odd, sum_even, sum_odd):
        total[...] = jnp.zeros_like(total)

    @pl.when(group < 2)
    def take_near():
        grad_ref[...] = near_ref[...]

    @pl.when(group == 2)
    def take_mid():
        grad_ref[...] = mid_ref[...]

    @pl.when(group == 3)
    def take_far():
        grad_ref[...] = far_ref[...]

    rows = low_ref.shape[0]
    length = pair_ref.shape[0]
    causal = causal_of((length, rows), info[0], rows)
    sides = ((even, value_even, key_even, sum_even), (odd, value_odd, key_odd, sum_odd))
    for pair in range(low_ref.shape[1] // PAIR):
        span = slice(pair * PAIR, (pair + 1) * PAIR)
        low = low_ref[:, span]
        grad = grad_ref[:, span]
        outs = []
        for at, (keys, values, key_total, value_total) in enumerate(sides):
            scores = jnp.where(causal, matmul_last(keys[...], low), NEGATIVE)
            probs = jnp.exp(scores - lse_ref[0, 2 * pair + at : 2 * pair + at + 1, :])
            value_total[...] += matmul(to_low(probs), grad)
            moved = probs * matmul_last(values[...], grad)
            mean = jnp.sum(moved, axis=0, keepdims=True)
            grad_scores = to_low(moved - probs * mean)
            key_total[...] += matmul(grad_scores, low)
            outs.append(matmul(across[...], grad_scores))
        turned = jnp.concatenate(outs, axis=0).T * HEAD_WIDTH ** (-0.5)
        query_ref[:, span] = to_low(turned * cos_ref[...] - half_swap(turned) * sin_ref[...])
    left = lanes((length, PAIR)) < HEAD_WIDTH
    pair_grad_ref[0] = jnp.where(
        left,
        key_even[...] + pltpu.roll(key_odd[...], HEAD_WIDTH, 1),
        pltpu.roll(sum_even[...], HEAD_WIDTH, 1) + sum_odd[...],
    )


def attention_specs(part, rows, length):
    span = (rows, 4 * PAIR)
    return {
        "table_pair": pl.BlockSpec((length, PAIR), lambda g, s: (0, 0)),
        "table": pl.BlockSpec((rows, PAIR), lambda g, s: (s[0], 0)),
        "pair": pl.BlockSpec((length, PAIR), lambda g, s: (0, s[1 + g])),
        "near": pl.BlockSpec(span, lambda g, s: (part, jnp.minimum(g, 1))),
        "one": pl.BlockSpec(span, lambda g, s: (part, 0)),
        "wide": pl.BlockSpec(span, lambda g, s: (0, g)),
        "sums": pl.BlockSpec((1, 8, rows), lambda g, s: (g, 0, 0)),
    }


def attention_cost(rows, length, heads, matmuls):
    work = rows * length * heads * HEAD_WIDTH * matmuls * 2
    return pl.CostEstimate(
        flops=work, bytes_accessed=16 * rows * heads * HEAD_WIDTH, transcendentals=rows * length * heads
    )


def attention_forward(info, queries, pair_pre, tables, part, length):
    cos_pair, sin_pair, cosine, sine = tables
    rows = cosine.shape[0] // BLOCK_PARTS
    heads = 4 * 4 * PAIR // HEAD_WIDTH
    spec = attention_specs(part, rows, length)
    half = pltpu.VMEM((length, PAIR), jnp.bfloat16)
    wide = (rows, heads * HEAD_WIDTH)
    return pl.pallas_call(
        attention_forward_kernel,
        grid_spec=pltpu.PrefetchScalarGridSpec(
            num_scalar_prefetch=1,
            grid=(4,),
            in_specs=[
                spec["near"], spec["one"], spec["one"], spec["pair"],
                spec["table_pair"], spec["table_pair"], spec["table"], spec["table"],
            ],
            out_specs=[spec["wide"], spec["wide"], spec["sums"]],
            scratch_shapes=[
                half, half,
                pltpu.VMEM((HEAD_WIDTH, length), jnp.bfloat16),
                pltpu.VMEM((rows, 4 * PAIR), jnp.float32),
            ],
        ),
        out_shape=[
            jax.ShapeDtypeStruct(wide, jnp.bfloat16),
            jax.ShapeDtypeStruct(wide, jnp.bfloat16),
            jax.ShapeDtypeStruct((4, 8, rows), jnp.float32),
        ],
        compiler_params=pltpu.CompilerParams(
            dimension_semantics=("arbitrary",), vmem_limit_bytes=VMEM_LIMIT
        ),
        cost_estimate=attention_cost(rows, length, heads, 2),
        name="attention_forward",
    )(info, *queries, pair_pre, cos_pair, sin_pair, cosine, sine)


def attention_backward(info, low, grads, sums, pair_pre, tables, length):
    cos_pair, sin_pair, cosine, sine = tables
    rows = cosine.shape[0] // BLOCK_PARTS
    heads = low.shape[1] // HEAD_WIDTH
    spec = attention_specs(0, rows, length)
    half = pltpu.VMEM((length, PAIR), jnp.bfloat16)
    full = pltpu.VMEM((length, PAIR), jnp.float32)
    return pl.pallas_call(
        attention_backward_kernel,
        grid_spec=pltpu.PrefetchScalarGridSpec(
            num_scalar_prefetch=1,
            grid=(4,),
            in_specs=[
                spec["wide"], spec["near"], spec["one"], spec["one"], spec["sums"], spec["pair"],
                spec["table_pair"], spec["table_pair"], spec["table"], spec["table"],
            ],
            out_specs=[spec["wide"], pl.BlockSpec((1, length, PAIR), lambda g, s: (s[1 + g], 0, 0))],
            scratch_shapes=[
                half, half, half, half,
                pltpu.VMEM((HEAD_WIDTH, length), jnp.bfloat16),
                full, full, full, full,
                pltpu.VMEM((rows, 4 * PAIR), jnp.bfloat16),
            ],
        ),
        out_shape=[
            jax.ShapeDtypeStruct(low.shape, jnp.bfloat16),
            jax.ShapeDtypeStruct((4, length, PAIR), jnp.float32),
        ],
        compiler_params=pltpu.CompilerParams(
            dimension_semantics=("arbitrary",), vmem_limit_bytes=VMEM_LIMIT
        ),
        cost_estimate=attention_cost(rows, length, heads, 5),
        name="attention_backward",
    )(info, low, *grads, sums, pair_pre, cos_pair, sin_pair, cosine, sine)


def pair_finish_kernel(info, own_ref, came_ref, cos_ref, sin_ref, out_ref):
    total = own_ref[0] + came_ref[0].astype(jnp.float32)
    out_ref[...] = to_low(total * cos_ref[...] - half_swap(total) * sin_ref[...])


def pair_finish(info, own, came, cos_pair, sin_pair):
    heads, both, _ = own.shape
    rows = both // 2
    part = pl.BlockSpec((1, rows, PAIR), lambda h, p, s: (h, p, 0))
    table = pl.BlockSpec((rows, PAIR), lambda h, p, s: (s[p], 0))
    return pl.pallas_call(
        pair_finish_kernel,
        grid_spec=pltpu.PrefetchScalarGridSpec(
            num_scalar_prefetch=1,
            grid=(heads, 2),
            in_specs=[part, part, table, table],
            out_specs=pl.BlockSpec((rows, PAIR), lambda h, p, s: (p, h)),
        ),
        out_shape=jax.ShapeDtypeStruct((both, heads * PAIR), jnp.bfloat16),
        name="pair_finish",
    )(info, own, came, cos_pair, sin_pair)


def rope_tables(length):
    positions = np.arange(length, dtype=np.float32)
    inverse = 10000.0 ** (-np.arange(0, HEAD_WIDTH, 2, dtype=np.float32) / HEAD_WIDTH)
    angles = positions[:, None] * inverse.astype(np.float32)[None, :]
    cosine, sine = np.cos(angles).astype(np.float32), np.sin(angles).astype(np.float32)
    head_cos = np.concatenate([cosine, cosine], axis=1)
    head_sin = np.concatenate([-sine, sine], axis=1)
    still = np.ones_like(head_cos)
    return tuple(
        jnp.asarray(np.concatenate(sides, axis=1))
        for sides in (
            (head_cos, still), (head_sin, 0 * still), (head_cos, head_cos), (head_sin, head_sin)
        )
    )


def head_marks(width, transposed):
    shape = (PAIR, width) if transposed else (width, PAIR)
    head_at, column_at = (0, 1) if transposed else (1, 0)
    head = lax.broadcasted_iota(jnp.int32, shape, head_at)
    column = lax.broadcasted_iota(jnp.int32, shape, column_at)
    return (column // HHD == head).astype(jnp.bfloat16)


def head_sums(value, marks):
    high = to_low(value)
    rest = to_low(value - high.astype(jnp.float32))
    return matmul(high, marks) + matmul(rest, marks)


def normalize(value):
    centered = value - jnp.mean(value, axis=-1, keepdims=True)
    inverse = lax.rsqrt(jnp.mean(centered * centered, axis=-1, keepdims=True) + EPS)
    return (centered * inverse, inverse)


def norm_back(grad, gain, hat, inverse):
    scaled = grad * gain
    mean = jnp.mean(scaled, axis=-1, keepdims=True)
    along = jnp.mean(scaled * hat, axis=-1, keepdims=True)
    return inverse * (scaled - mean - hat * along)


def slot_attention_kernel(
    pieces_ref, counts_ref, weight_ref, norm_ref, mixed_ref, probs_ref, attended_ref, lead_ref
):
    entries, slots, width = pieces_ref.shape
    rows = entries * slots
    tall = (entries, slots, width)
    pieces = pieces_ref[...].astype(jnp.float32)
    hat, _ = normalize(pieces.reshape(rows, width))
    low = to_low(hat * norm_ref[0:1, :] + norm_ref[1:2, :])
    mixed = []
    for part in range(3):
        span = slice(part * width, (part + 1) * width)
        value = to_low(matmul(low, weight_ref[:, span]))
        mixed_ref[:, span] = value
        mixed.append(value.astype(jnp.float32).reshape(tall))
    query, keys, values = mixed
    marks = head_marks(width, False)
    product = (keys * query[:, 0:1, :]).reshape(rows, width)
    scores = head_sums(product, marks).reshape(entries, slots, PAIR) * HHD ** (-0.5)
    live = lax.broadcasted_iota(jnp.int32, scores.shape, 1) < counts_ref[...]
    scores = jnp.where(live, scores, NEGATIVE)
    weight = jnp.exp(scores - jnp.max(scores, axis=1, keepdims=True))
    probs = weight / jnp.sum(weight, axis=1, keepdims=True)
    probs_ref[...] = probs
    spread = matmul(to_low(probs.reshape(rows, PAIR)), head_marks(width, True)).reshape(tall)
    attended_ref[...] = to_low(jnp.sum(spread * values, axis=1))
    lead_ref[...] = pieces[:, 0, :]


def slot_attention(pieces, counts, in_weight, norm_rows):
    entries, slots, width = pieces.shape
    part = min(ENTRY_BLOCK, entries)
    counts = jnp.broadcast_to(counts[:, None, None], (entries, 1, PAIR))
    whole = lambda shape: pl.BlockSpec(shape, lambda i: (0,) * len(shape))
    tall = pl.BlockSpec((part, slots, width), lambda i: (i, 0, 0))
    flat = pl.BlockSpec((part, width), lambda i: (i, 0))
    return pl.pallas_call(
        slot_attention_kernel,
        grid=(entries // part,),
        in_specs=[
            tall,
            pl.BlockSpec((part, 1, PAIR), lambda i: (i, 0, 0)),
            whole(in_weight.shape),
            whole(norm_rows.shape),
        ],
        out_specs=[
            pl.BlockSpec((part * slots, 3 * width), lambda i: (i, 0)),
            pl.BlockSpec((part, slots, PAIR), lambda i: (i, 0, 0)),
            flat,
            flat,
        ],
        out_shape=[
            jax.ShapeDtypeStruct((entries * slots, 3 * width), jnp.bfloat16),
            jax.ShapeDtypeStruct((entries, slots, PAIR), jnp.float32),
            jax.ShapeDtypeStruct((entries, width), jnp.bfloat16),
            jax.ShapeDtypeStruct((entries, width), jnp.float32),
        ],
        compiler_params=pltpu.CompilerParams(
            dimension_semantics=("arbitrary",), vmem_limit_bytes=VMEM_LIMIT
        ),
        cost_estimate=pl.CostEstimate(
            flops=8 * entries * slots * width * width, bytes_accessed=entries * slots * width * 8, transcendentals=0
        ),
        name="slot_attention",
    )(pieces, counts, in_weight, norm_rows)


def gelu_of(value):
    cdf = 0.5 * (1.0 + lax.erf(value * np.float32(0.5 ** 0.5)))
    return (value * cdf, cdf)


def gelu_slope(value, cdf):
    return cdf + value * (jnp.exp(-0.5 * value * value) * np.float32((2 * np.pi) ** -0.5))


def units_forward_kernel(
    attended_ref, lead_ref, wide_weight_ref, reduce_ref, norm_ref, pooled_ref, hidden_ref
):
    width = lead_ref.shape[1]
    hidden = lead_ref[...] + matmul(attended_ref[...], wide_weight_ref[:, :width])
    hidden_ref[...] = hidden
    hat, _ = normalize(hidden)
    second = to_low(hat * norm_ref[2:3, :] + norm_ref[3:4, :])
    total = hidden
    units = reduce_ref.shape[0]
    step = min(UNIT, units)
    for at in range(0, units, step):
        active, _ = gelu_of(matmul(second, wide_weight_ref[:, width + at : width + at + step]))
        total = total + matmul(to_low(active), reduce_ref[at : at + step, :])
    pooled_ref[...] = to_low(total)


def units_forward(attended, lead, wide_weight, reduce_weight, norm_rows):
    entries, width = attended.shape
    part = min(UNIT_ROWS, entries)
    whole = lambda shape: pl.BlockSpec(shape, lambda i: (0,) * len(shape))
    flat = pl.BlockSpec((part, width), lambda i: (i, 0))
    return pl.pallas_call(
        units_forward_kernel,
        grid=(entries // part,),
        in_specs=[flat, flat]
        + [whole(x.shape) for x in (wide_weight, reduce_weight, norm_rows)],
        out_specs=[flat, flat],
        out_shape=[
            jax.ShapeDtypeStruct((entries, width), jnp.bfloat16),
            jax.ShapeDtypeStruct((entries, width), jnp.float32),
        ],
        compiler_params=pltpu.CompilerParams(
            dimension_semantics=("arbitrary",), vmem_limit_bytes=VMEM_LIMIT
        ),
        cost_estimate=pl.CostEstimate(
            flops=2 * entries * width * (width + 2 * reduce_weight.shape[0]), bytes_accessed=8 << 20, transcendentals=0
        ),
        name="units_forward",
    )(attended, lead, wide_weight, reduce_weight, norm_rows)


def units_backward_kernel(
    grad_ref, hidden_ref, attended_ref, wide_weight_ref, reduce_ref, norm_ref,
    hidden_grad_ref, attended_grad_ref, wide_ref, reduce_grad_ref, norm_grad_ref,
    wide_total, reduce_total,
):
    step_at = pl.program_id(0)
    width = hidden_ref.shape[1]
    units = reduce_ref.shape[0]

    @pl.when(step_at == 0)
    def start():
        wide_total[...] = jnp.zeros_like(wide_total)
        reduce_total[...] = jnp.zeros_like(reduce_total)
        norm_grad_ref[...] = jnp.zeros_like(norm_grad_ref)

    grad = grad_ref[...]
    grad_low = to_low(grad)
    hat, inverse = normalize(hidden_ref[...])
    second = to_low(hat * norm_ref[2:3, :] + norm_ref[3:4, :])
    grad_normed = jnp.zeros_like(grad)
    step = min(UNIT, units)
    for at in range(0, units, step):
        span = slice(at, at + step)
        wide_span = slice(width + at, width + at + step)
        expanded = matmul(second, wide_weight_ref[:, wide_span])
        active, cdf = gelu_of(expanded)
        reduce_total[span, :] += matmul_first(to_low(active), grad_low)
        grad_active = matmul_last(grad_low, reduce_ref[span, :])
        grad_expanded = to_low(grad_active * gelu_slope(expanded, cdf))
        wide_total[:, wide_span] += matmul_first(second, grad_expanded)
        grad_normed = grad_normed + matmul_last(grad_expanded, wide_weight_ref[:, wide_span])
    norm_grad_ref[2:3, :] += jnp.sum(grad_normed * hat, axis=0, keepdims=True)
    norm_grad_ref[3:4, :] += jnp.sum(grad_normed, axis=0, keepdims=True)
    hidden_grad = grad + norm_back(grad_normed, norm_ref[2:3, :], hat, inverse)
    hidden_grad_ref[...] = hidden_grad
    hidden_low = to_low(hidden_grad)
    wide_total[:, :width] += matmul_first(attended_ref[...], hidden_low)
    attended_grad_ref[...] = to_low(matmul_last(hidden_low, wide_weight_ref[:, :width]))

    @pl.when(step_at == pl.num_programs(0) - 1)
    def finish():
        wide_ref[...] = to_low(wide_total[...])
        reduce_grad_ref[...] = to_low(reduce_total[...])


def units_backward(grad, hidden, attended, wide_weight, reduce_weight, norm_rows):
    entries, width = attended.shape
    part = min(UNIT_ROWS, entries)
    units = reduce_weight.shape[0]
    whole = lambda shape: pl.BlockSpec(shape, lambda i: (0,) * len(shape))
    flat = pl.BlockSpec((part, width), lambda i: (i, 0))
    wide = (width, width + units)
    return pl.pallas_call(
        units_backward_kernel,
        grid=(entries // part,),
        in_specs=[flat, flat, flat]
        + [whole(x.shape) for x in (wide_weight, reduce_weight, norm_rows)],
        out_specs=[flat, flat, whole(wide), whole((units, width)), whole((8, width))],
        out_shape=[
            jax.ShapeDtypeStruct((entries, width), jnp.float32),
            jax.ShapeDtypeStruct((entries, width), jnp.bfloat16),
            jax.ShapeDtypeStruct(wide, jnp.bfloat16),
            jax.ShapeDtypeStruct((units, width), jnp.bfloat16),
            jax.ShapeDtypeStruct((8, width), jnp.float32),
        ],
        scratch_shapes=[pltpu.VMEM(wide, jnp.float32), pltpu.VMEM((units, width), jnp.float32)],
        compiler_params=pltpu.CompilerParams(
            dimension_semantics=("arbitrary",), vmem_limit_bytes=VMEM_LIMIT
        ),
        cost_estimate=pl.CostEstimate(
            flops=2 * entries * width * (2 * width + 5 * units), bytes_accessed=16 << 20, transcendentals=0
        ),
        name="units_backward",
    )(grad, hidden, attended, wide_weight, reduce_weight, norm_rows)


def slot_backward_kernel(
    pieces_ref, mixed_ref, probs_ref, attended_grad_ref, hidden_grad_ref, weight_ref, norm_ref, later_ref,
    pieces_grad_ref, input_grad_ref, total, norm_total,
):
    step_at = pl.program_id(0)
    entries, slots, width = pieces_ref.shape
    rows = entries * slots
    tall = (entries, slots, width)

    @pl.when(step_at == 0)
    def start():
        total[...] = jnp.zeros_like(total)
        norm_total[...] = jnp.zeros_like(norm_total)
        norm_total[2:4, :] = later_ref[2:4, :]

    hat, inverse = normalize(pieces_ref[...].astype(jnp.float32).reshape(rows, width))
    low = to_low(hat * norm_ref[0:1, :] + norm_ref[1:2, :])
    scale = HHD ** (-0.5)
    query, keys, values = [
        mixed_ref[:, part * width : (part + 1) * width].astype(jnp.float32).reshape(tall) for part in range(3)
    ]
    probs = probs_ref[...]
    grad_attended = jnp.broadcast_to(attended_grad_ref[...].astype(jnp.float32)[:, None, :], tall)
    grad_probs = head_sums((grad_attended * values).reshape(rows, width), head_marks(width, False))
    moved = probs * grad_probs.reshape(probs.shape)
    grad_scores = to_low(moved - probs * jnp.sum(moved, axis=1, keepdims=True))
    marks = head_marks(width, True)
    spread = matmul(grad_scores.reshape(rows, PAIR), marks).reshape(tall) * scale
    first_slot = lax.broadcasted_iota(jnp.int32, tall, 1) == 0
    grad_query = jnp.where(first_slot, jnp.sum(spread * keys, axis=1, keepdims=True), 0.0)
    grad_keys = spread * query[:, 0:1, :]
    grad_values = matmul(to_low(probs.reshape(rows, PAIR)), marks).reshape(tall) * grad_attended
    grad_normed = jnp.zeros((rows, width), jnp.float32)
    for part, grad in enumerate((grad_query, grad_keys, grad_values)):
        span = slice(part * width, (part + 1) * width)
        grad_low = to_low(grad.reshape(rows, width))
        total[:, span] += matmul_first(low, grad_low)
        grad_normed = grad_normed + matmul_last(grad_low, weight_ref[:, span])
    norm_total[0:1, :] += jnp.sum(grad_normed * hat, axis=0, keepdims=True)
    norm_total[1:2, :] += jnp.sum(grad_normed, axis=0, keepdims=True)
    grad_pieces = norm_back(grad_normed, norm_ref[0:1, :], hat, inverse).reshape(tall)
    hidden_grad = jnp.broadcast_to(hidden_grad_ref[...][:, None, :], tall)
    pieces_grad_ref[...] = to_low(grad_pieces + jnp.where(first_slot, hidden_grad, 0.0))

    @pl.when(step_at == pl.num_programs(0) - 1)
    def finish():
        input_grad_ref[:, : 3 * width] = to_low(total[...])
        input_grad_ref[:, 3 * width :] = to_low(norm_total[...].T)


def slot_backward(
    pieces, mixed, probs, attended_grad, hidden_grad, in_weight, norm_rows, later_norms
):
    entries, slots, width = pieces.shape
    part = min(ENTRY_BLOCK, entries)
    whole = lambda shape: pl.BlockSpec(shape, lambda i: (0,) * len(shape))
    tall = pl.BlockSpec((part, slots, width), lambda i: (i, 0, 0))
    flat = pl.BlockSpec((part, width), lambda i: (i, 0))
    return pl.pallas_call(
        slot_backward_kernel,
        grid=(entries // part,),
        in_specs=[
            tall,
            pl.BlockSpec((part * slots, 3 * width), lambda i: (i, 0)),
            pl.BlockSpec((part, slots, PAIR), lambda i: (i, 0, 0)),
            flat,
            flat,
            whole(in_weight.shape),
            whole(norm_rows.shape),
            whole(later_norms.shape),
        ],
        out_specs=[tall, whole((width, 3 * width + PAIR))],
        out_shape=[
            jax.ShapeDtypeStruct(pieces.shape, jnp.bfloat16),
            jax.ShapeDtypeStruct((width, 3 * width + PAIR), jnp.bfloat16),
        ],
        scratch_shapes=[
            pltpu.VMEM((width, 3 * width), jnp.float32),
            pltpu.VMEM((PAIR, width), jnp.float32),
        ],
        compiler_params=pltpu.CompilerParams(
            dimension_semantics=("arbitrary",), vmem_limit_bytes=VMEM_LIMIT
        ),
        cost_estimate=pl.CostEstimate(
            flops=14 * entries * slots * width * width, bytes_accessed=entries * slots * width * 10, transcendentals=0
        ),
        name="slot_backward",
    )(pieces, mixed, probs, attended_grad, hidden_grad, in_weight, norm_rows, later_norms)


def route(token_index, me, devices, local_vocab, capacity, mp_count):
    step = token_index.shape[0] // BLOCK_PARTS
    cut = token_index.reshape(BLOCK_PARTS, step)
    own = jnp.where(me % mp_count == 0, cut[jnp.array([0, 3])], cut[jnp.array([1, 2])]).reshape(1, 2 * step)
    asked = exchange(jnp.broadcast_to(own, (devices, 2 * step)))
    count = 2 * step
    places = jnp.arange(count, dtype=jnp.int32)
    same = asked[:, :, None] == asked[:, None, :]
    earlier = places[:, None] > places[None, :]
    repeated = jnp.any(same & earlier[None], axis=2)
    first = jnp.logical_not(repeated)
    owner = asked // local_vocab
    before = (
        (owner[:, :, None] == owner[:, None, :])
        & (asked[:, None, :] < asked[:, :, None])
        & first[:, None, :]
    )
    rank = jnp.sum(before.astype(jnp.int32), axis=2)
    rounds = jnp.max(rank) // capacity + 1
    own_rank = lax.dynamic_index_in_dim(rank, me, 0, False)
    own_owner = lax.dynamic_index_in_dim(owner, me, 0, False)
    entries = me * local_vocab + jnp.arange(local_vocab, dtype=jnp.int32)
    present = jnp.any(asked[:, :, None] == entries[None, None, :], axis=1)
    lower = (
        jnp.arange(local_vocab, dtype=jnp.int32)[:, None]
        < jnp.arange(local_vocab, dtype=jnp.int32)[None, :]
    )
    standing = matmul(present.astype(jnp.bfloat16), lower.astype(jnp.bfloat16)).astype(jnp.int32)
    return (rounds, own_rank, own_owner, present, standing)


def sender_choice(present, standing, turn, capacity):
    slot = turn * capacity + jnp.arange(capacity, dtype=jnp.int32)
    chosen = present[:, None, :] & (standing[:, None, :] == slot[None, :, None])
    return chosen.astype(jnp.bfloat16).reshape(present.shape[0] * capacity, present.shape[1])


def taker_choice(own_rank, own_owner, turn, capacity, devices):
    inside = own_rank - turn * capacity
    valid = (inside >= 0) & (inside < capacity)
    place = jnp.where(valid, own_owner * capacity + inside, -1)
    return (place[:, None] == jnp.arange(devices * capacity, dtype=jnp.int32)[None, :]).astype(
        jnp.bfloat16
    )


def exchange(value):
    return lax.all_to_all(value, ("dp", "mp"), 0, 0, tiled=True)


def ordered_blocks(first, own_two, other_two):
    return jnp.where(
        first,
        jnp.concatenate([own_two[0], other_two[0], other_two[1], own_two[1]], axis=0),
        jnp.concatenate([other_two[0], own_two[0], own_two[1], other_two[1]], axis=0),
    )


def body(
    pieces,
    counts,
    token_index,
    hyper_input,
    hyper_output,
    hyper_expand,
    hyper_reduce,
    hyper_norms,
    embed_weight,
    attention_gain,
    dense_gain,
    frozen_query_weight,
    frozen_key_weight,
    frozen_value_weight,
    frozen_output_weight,
    gate_weight,
    up_weight,
    down_weight,
    upstream,
):
    local_vocab = pieces.shape[0]
    mp_count = lax.axis_size("mp")
    devices = lax.axis_size("dp") * mp_count
    mp_index = lax.axis_index("mp")
    me = lax.axis_index("dp") * mp_count + mp_index
    core = (me >> 1) & 1
    lead = mp_index == 0
    bits = log2_of(devices)
    far_bits = list(range(bits - 1, 1, -1))
    length = token_index.shape[0]
    block = length // BLOCK_PARTS
    capacity = max(16, length // devices)

    norm_count = hyper_norms.shape[1]
    in_width = hyper_input.shape[1]
    norm_lanes = jnp.pad(hyper_norms, ((0, 0), (0, PAIR - norm_count)))
    in_weight, begun = gather_blocks(
        jnp.concatenate([hyper_input, norm_lanes], axis=1), me, devices, [0] + far_bits + [1]
    )
    wide_weight, _ = gather_blocks(
        jnp.concatenate([hyper_output, hyper_expand], axis=1), me, devices, [0] + far_bits + [1]
    )
    reduce_weight, _ = gather_blocks(hyper_reduce, me, devices, far_bits + [0, 1])
    embed_full, _ = gather_blocks(embed_weight, me, devices, far_bits + [0, 1])
    norm_rows = in_weight[:, in_width : in_width + 8].astype(jnp.float32).T

    query_cut = frozen_query_weight.shape[1] // 2
    frozen_query_weight, frozen_output_weight, begun = lax.optimization_barrier(
        (frozen_query_weight, frozen_output_weight, begun)
    )
    kv_local = frozen_key_weight.shape[1] // HEAD_WIDTH
    key_own = jnp.concatenate(
        [
            weight[:, at * HEAD_WIDTH : (at + 1) * HEAD_WIDTH]
            for at in range(kv_local)
            for weight in (frozen_key_weight, frozen_value_weight)
        ],
        axis=1,
    )
    query_near = swap(
        lax.dynamic_slice_in_dim(frozen_query_weight, core * query_cut, query_cut, 1), 1, devices
    )
    output_near = swap(
        lax.dynamic_slice_in_dim(frozen_output_weight, core * query_cut, query_cut, 0), 1, devices
    )
    key_other = swap(key_own, 1, devices)
    query_far = swap(query_near, 2, devices)
    output_far = swap(output_near, 2, devices)
    pair_weight = jnp.where(
        lead,
        jnp.concatenate([key_own, key_other], axis=1),
        jnp.concatenate([key_other, key_own], axis=1),
    )
    other_base = (1 - mp_index) * kv_local
    head_order = [mp_index * kv_local, mp_index * kv_local + 1, other_base + core, other_base + 1 - core]

    rounds, own_rank, own_owner, present, standing = route(
        token_index, me, devices, local_vocab, capacity, mp_count
    )

    slot_mixed, slot_probs, hyper_attended, lead_rows = slot_attention(pieces, counts, in_weight, norm_rows)
    pooled, hyper_hidden = units_forward(
        hyper_attended, lead_rows, wide_weight, reduce_weight, norm_rows
    )

    def fetch(turn, chosen):
        sent = matmul(sender_choice(present, standing, turn, capacity), pooled).astype(jnp.bfloat16)
        came = exchange(sent)
        picked = matmul(taker_choice(own_rank, own_owner, turn, capacity, devices), came)
        return chosen + picked.astype(jnp.bfloat16)

    chosen_own = fetch(0, jnp.zeros((2 * block, pooled.shape[1]), jnp.bfloat16))
    chosen_own = lax.fori_loop(1, rounds, fetch, chosen_own)
    chosen_other = swap(chosen_own, 1, devices)

    tables = rope_tables(length)
    own_at = (mp_index, 3 - mp_index)
    own_base = tuple(at * block for at in own_at)
    other_start = ((1 - mp_index) * block, (2 + mp_index) * block)
    infos = [jnp.stack([at] + head_order).astype(jnp.int32) for at in own_at]

    def first_norm(value):
        return rms_norm(value, attention_gain)

    def second_norm(value):
        return rms_norm(value, dense_gain)

    embedded = rounded(matmul(chosen_own, embed_full))
    first_normed, first_pull = jax.vjp(first_norm, embedded)
    first_low = first_normed.astype(jnp.bfloat16)
    query_weights = (frozen_query_weight, query_near, query_far)
    output_weights = (frozen_output_weight, output_near, output_far)
    queries = [matmul(first_low, part) for part in query_weights]
    other_low = first_norm(rounded(matmul(chosen_other, embed_full))).astype(jnp.bfloat16)
    pair_own = matmul(first_low, pair_weight)
    pair_other = matmul(other_low, pair_weight)
    pair_pre = ordered_blocks(
        lead, (pair_own[:block], pair_own[block:]), (pair_other[:block], pair_other[block:])
    )
    spans = (2 * block, length)

    sums = []
    lows = []
    hidden_parts = []
    second_pulls = []
    second_rows = []
    for part in range(2):
        rows = slice(part * block, (part + 1) * block)
        flat, low, part_sums = attention_forward(
            infos[part], queries, pair_pre, tables, part, spans[part]
        )
        sums.append(part_sums)
        lows.append(low)
        mixed = 0.0
        at = 0
        for weight in output_weights:
            mixed = mixed + matmul(flat[:, at : at + weight.shape[0]], weight)
            at += weight.shape[0]
        hidden_state = embedded[rows] + mixed
        hidden_parts.append(hidden_state)
        second_normed, pull = jax.vjp(second_norm, hidden_state)
        second_pulls.append(pull)
        second_low = second_normed.astype(jnp.bfloat16)
        second_rows.append(jnp.concatenate([second_low, swap(second_low, 1, devices)], axis=0))

    active_rows = []
    grad_hidden = []
    for part in range(2):
        second_low = second_rows[part]
        rising = jnp.concatenate(
            [
                lax.dynamic_slice_in_dim(upstream, own_base[part], block, 0),
                lax.dynamic_slice_in_dim(upstream, other_start[part], block, 0),
            ],
            axis=0,
        )
        gate_pre = matmul(second_low, gate_weight)
        up_pre = matmul(second_low, up_weight)
        active, active_pull = jax.vjp(gated_units, gate_pre, up_pre)
        active_rows.append(active.astype(jnp.bfloat16))
        grad_gate, grad_up = active_pull(matmul_last(rising, down_weight))
        grad_second = (
            matmul_last(grad_gate.astype(jnp.bfloat16), gate_weight)
            + matmul_last(grad_up.astype(jnp.bfloat16), up_weight)
        ).astype(jnp.bfloat16)
        total = grad_second[:block].astype(jnp.float32) + swap(
            grad_second[block:], 1, devices
        ).astype(jnp.float32)
        (grad_hidden_norm,) = second_pulls[part](total)
        grad_hidden.append(rising[:block].astype(jnp.float32) + grad_hidden_norm)

    share = upstream.shape[1] // mp_count
    own_out = []
    other_out = []
    for part in range(2):
        dense = matmul(active_rows[part], down_weight)
        dense_own = dense[:block] + hidden_parts[part]
        dense_other = dense[block:]

        def columns(value, index):
            return lax.dynamic_slice_in_dim(value, index * share, share, 1)

        leaving = jnp.concatenate(
            [columns(dense_other, 1 - mp_index), columns(dense_own, 1 - mp_index)], axis=0
        ).astype(jnp.bfloat16)
        arrived = swap(leaving, 1, devices).astype(jnp.float32)
        own_out.append((columns(dense_own, mp_index) + arrived[:block]).astype(jnp.bfloat16))
        other_out.append((columns(dense_other, mp_index) + arrived[block:]).astype(jnp.bfloat16))
    model_out = ordered_blocks(lead, own_out, other_out)

    grad_queries = []
    pair_grads = []
    for part in range(2):
        hidden_low = grad_hidden[part].astype(jnp.bfloat16)
        grad_attended = [
            matmul_last(hidden_low, weight).astype(jnp.bfloat16) for weight in output_weights
        ]
        part_queries, part_pairs = attention_backward(
            infos[part], lows[part], grad_attended, sums[part], pair_pre, tables, spans[part]
        )
        grad_queries.append(part_queries)
        pair_grads.append(part_pairs)
    pair_grad = jnp.concatenate(
        [pair_grads[0] + pair_grads[1][:, : 2 * block], pair_grads[1][:, 2 * block :]], axis=1
    )

    def pick_blocks(starts):
        return jnp.concatenate(
            [lax.dynamic_slice_in_dim(pair_grad, start, block, 1) for start in starts], axis=1
        )

    pair_came = swap(pick_blocks(other_start).astype(jnp.bfloat16), 1, devices)
    pair_low = pair_finish(
        jnp.stack(own_at).astype(jnp.int32), pick_blocks(own_base), pair_came, tables[0], tables[1]
    )
    grad_first = matmul_last(pair_low, pair_weight)
    grad_query_low = jnp.concatenate(grad_queries, axis=0)
    at = 0
    for weight in query_weights:
        grad_first = grad_first + matmul_last(grad_query_low[:, at : at + weight.shape[1]], weight)
        at += weight.shape[1]
    (grad_embed_norm,) = first_pull(grad_first)
    embedded_grad_low = (jnp.concatenate(grad_hidden, axis=0) + grad_embed_norm).astype(
        jnp.bfloat16
    )
    token_grad = matmul_last(embedded_grad_low, embed_full).astype(jnp.bfloat16)
    embed_grad = to_low(matmul_first(chosen_own, embedded_grad_low))

    def give_back(turn, total):
        taker = taker_choice(own_rank, own_owner, turn, capacity, devices)
        leaving = matmul_first(taker, token_grad).astype(jnp.bfloat16)
        came = exchange(leaving)
        return total + matmul_first(sender_choice(present, standing, turn, capacity), came)

    grad_pooled = give_back(0, jnp.zeros(pooled.shape, jnp.float32))
    grad_pooled = lax.fori_loop(1, rounds, give_back, grad_pooled)

    back_order = [1, 0] + far_bits[::-1]
    embed_own = scatter_blocks(embed_grad, me, devices, back_order)
    hidden_grad, attended_grad, wide_grad, reduce_grad, later_norms = units_backward(
        grad_pooled, hyper_hidden, hyper_attended, wide_weight, reduce_weight, norm_rows
    )
    wide_own = scatter_blocks(wide_grad, me, devices, back_order)
    reduce_own = scatter_blocks(reduce_grad, me, devices, back_order)
    pieces_grad, input_grad = slot_backward(
        pieces, slot_mixed, slot_probs, attended_grad, hidden_grad, in_weight, norm_rows, later_norms
    )
    input_own = scatter_blocks(input_grad, me, devices, back_order)
    out_width = hyper_output.shape[1]
    return (
        model_out,
        pieces_grad,
        input_own[:, :in_width],
        wide_own[:, :out_width],
        wide_own[:, out_width:],
        reduce_own,
        input_own[:, in_width : in_width + norm_count],
        embed_own,
    )


def solution(mesh):
    return jax.shard_map(
        body,
        mesh=mesh,
        in_specs=(
            P(("dp", "mp"), None, None),
            P(("dp", "mp")),
            P("dp"),
            P(("dp", "mp"), None),
            P(("dp", "mp"), None),
            P(("dp", "mp"), None),
            P(("dp", "mp"), None),
            P(("dp", "mp"), None),
            P(("dp", "mp"), None),
            P(),
            P(),
            P(None, "mp"),
            P(None, "mp"),
            P(None, "mp"),
            P("mp", None),
            P(None, "mp"),
            P(None, "mp"),
            P("mp", None),
            P("dp", None),
        ),
        out_specs=(
            P("dp", "mp"),
            P(("dp", "mp"), None, None),
            P(("dp", "mp"), None),
            P(("dp", "mp"), None),
            P(("dp", "mp"), None),
            P(("dp", "mp"), None),
            P(("dp", "mp"), None),
            P(("dp", "mp"), None),
        ),
        check_vma=False,
    )
```

```python
import functools

import jax
import jax.numpy as jnp
import numpy as np
from jax import lax
from jax.experimental import pallas as pl
from jax.experimental.pallas import tpu as pltpu
from jax.sharding import PartitionSpec as P

HEAD_WIDTH = 64
HHD = 64
BLOCK_PARTS = 4
UNIT = 512
PAIR = 2 * HEAD_WIDTH
VMEM_LIMIT = 48 << 20
ENTRY_BLOCK = 64
SLOT_PARTS = 2
UNIT_STEP = 256
COLUMN_STEP = 256
UNIT_ROWS = 256


EPS = 1e-05
NEGATIVE = -1000000000.0


def matmul(left, right):
    return jnp.dot(left, right, preferred_element_type=jnp.float32)


def matmul_first(left, right):
    return lax.dot_general(
        left, right, (((0,), (0,)), ((), ())), preferred_element_type=jnp.float32
    )


def matmul_last(left, right):
    return lax.dot_general(
        left, right, (((1,), (1,)), ((), ())), preferred_element_type=jnp.float32
    )


def log2_of(number):
    return number.bit_length() - 1


def swap(value, mask, devices):
    return lax.ppermute(value, ("dp", "mp"), [(d, d ^ mask) for d in range(devices)])


def gather_start(block, devices):
    return block.reshape((1,) * log2_of(devices) + block.shape)


def masks_of(bits):
    masks = [0]
    for bit in bits:
        masks += [mask | (1 << bit) for mask in masks]
    return masks


def gather_send(held, bits, devices):
    return [swap(held, mask, devices) for mask in masks_of(bits)[1:]]


def gather_join(held, came, bits, me, devices):
    blocks = [held, *came]
    for bit in bits:
        axis = log2_of(devices) - 1 - bit
        upper = ((me >> bit) & 1) == 1
        blocks = [
            jnp.where(
                upper,
                jnp.concatenate([other, own], axis),
                jnp.concatenate([own, other], axis),
            )
            for own, other in zip(blocks[::2], blocks[1::2])
        ]
    return blocks[0]


def gather_step(held, bits, me, devices):
    return gather_join(held, gather_send(held, bits, devices), bits, me, devices)


def gather_end(held):
    return held.reshape((-1, held.shape[-1]))


def scatter_start(blocks, devices):
    bits = log2_of(devices)
    return blocks.reshape((2,) * bits + (blocks.shape[0] // devices,) + blocks.shape[1:])


def scatter_send(held, bits, me, devices):
    def part(mask, value):
        for bit in bits:
            axis = log2_of(devices) - 1 - bit
            value = lax.dynamic_slice_in_dim(value, ((me ^ mask) >> bit) & 1, 1, axis)
        return value

    came = [swap(to_low(part(mask, held)), mask, devices) for mask in masks_of(bits)[1:]]
    return (part(0, held), came)


def scatter_add(staying, came):
    total = staying.astype(jnp.float32)
    for share in came:
        total = total + share.astype(jnp.float32)
    return total


def scatter_step(held, bits, me, devices):
    return scatter_add(*scatter_send(held, bits, me, devices))


def scatter_end(held):
    return held.reshape(held.shape[-2:])


def lanes(shape):
    return lax.broadcasted_iota(jnp.int32, shape, len(shape) - 1)


def half_swap(value):
    quarter = HEAD_WIDTH // 2
    upper = (lanes(value.shape) & quarter) != 0
    return jnp.where(
        upper, pltpu.roll(value, quarter, 1), pltpu.roll(value, PAIR - quarter, 1)
    )


def to_low(value):
    return value.astype(jnp.bfloat16)


def causal_of(shape, block_at, rows):
    key_at = lax.broadcasted_iota(jnp.int32, shape, 0)
    query_at = lax.broadcasted_iota(jnp.int32, shape, 1) + block_at * rows
    return key_at <= query_at


def head_views(pair_ref, cos_ref, sin_ref):
    pair = pair_ref[...]
    turned = to_low(pair * cos_ref[...] + half_swap(pair) * sin_ref[...]).astype(jnp.float32)
    other = pltpu.roll(turned, HEAD_WIDTH, 1)
    left = lanes(turned.shape) < HEAD_WIDTH
    return (
        jnp.where(left, turned, 0.0),
        jnp.where(left, 0.0, other),
        jnp.where(left, other, 0.0),
        jnp.where(left, 0.0, turned),
    )


def attention_forward_kernel(
    info, query_ref, pair_ref, cos_pair, sin_pair, cos_ref, sin_ref,
    out_ref, low_ref, lse_ref, even, odd, across,
):
    key_left, key_right, value_left, _ = head_views(pair_ref, cos_pair, sin_pair)
    even[...] = to_low(key_left)
    odd[...] = to_low(key_right)
    across[...] = to_low(value_left.T[:HEAD_WIDTH])

    rows = query_ref.shape[0]
    length = pair_ref.shape[0]
    causal = causal_of((length, rows), info[0], rows)
    for pair in range(query_ref.shape[1] // PAIR):
        span = slice(pair * PAIR, (pair + 1) * PAIR)
        query = query_ref[:, span]
        turned = to_low(query * cos_ref[...] + half_swap(query) * sin_ref[...])
        low = to_low(turned.astype(jnp.float32) * HEAD_WIDTH ** (-0.5))
        low_ref[:, span] = low
        outs = []
        for at, keys in enumerate((even, odd)):
            scores = jnp.where(causal, matmul_last(keys[...], low), NEGATIVE)
            highest = jnp.max(scores, axis=0, keepdims=True)
            weight = jnp.exp(scores - highest)
            total = jnp.sum(weight, axis=0, keepdims=True)
            outs.append(matmul(across[...], to_low(weight)) / total)
            lse_ref[0, 2 * pair + at : 2 * pair + at + 1, :] = highest + jnp.log(total)
        out_ref[:, span] = to_low(jnp.concatenate(outs, axis=0).T)


def attention_backward_kernel(
    info, low_ref, grad_ref, lse_ref, pair_ref, cos_pair, sin_pair, cos_ref, sin_ref, *refs,
):
    query_ref, pair_grad_ref, even, odd, value_even, value_odd, across = refs[-11:-4]
    key_even, key_odd, sum_even, sum_odd = refs[-4:]
    key_left, key_right, value_left, value_right = head_views(pair_ref, cos_pair, sin_pair)
    even[...] = to_low(key_left)
    odd[...] = to_low(key_right)
    value_even[...] = to_low(value_left)
    value_odd[...] = to_low(value_right)
    across[...] = to_low(key_left.T[:HEAD_WIDTH])
    for total in (key_even, key_odd, sum_even, sum_odd):
        total[...] = jnp.zeros_like(total)

    rows = low_ref.shape[0]
    length = pair_ref.shape[0]
    causal = causal_of((length, rows), info[0], rows)
    sides = ((even, value_even, key_even, sum_even), (odd, value_odd, key_odd, sum_odd))
    for pair in range(low_ref.shape[1] // PAIR):
        span = slice(pair * PAIR, (pair + 1) * PAIR)
        low = low_ref[:, span]
        grad = grad_ref[:, span]
        outs = []
        for at, (keys, values, key_total, value_total) in enumerate(sides):
            scores = jnp.where(causal, matmul_last(keys[...], low), NEGATIVE)
            probs = jnp.exp(scores - lse_ref[0, 2 * pair + at : 2 * pair + at + 1, :])
            value_total[...] += matmul(to_low(probs), grad)
            moved = probs * matmul_last(values[...], grad)
            mean = jnp.sum(moved, axis=0, keepdims=True)
            grad_scores = to_low(moved - probs * mean)
            key_total[...] += matmul(grad_scores, low)
            outs.append(matmul(across[...], grad_scores))
        turned = jnp.concatenate(outs, axis=0).T * HEAD_WIDTH ** (-0.5)
        query_ref[:, span] = to_low(turned * cos_ref[...] - half_swap(turned) * sin_ref[...])
    left = lanes((length, PAIR)) < HEAD_WIDTH
    pair_grad_ref[0] = jnp.where(
        left,
        key_even[...] + pltpu.roll(key_odd[...], HEAD_WIDTH, 1),
        pltpu.roll(sum_even[...], HEAD_WIDTH, 1) + sum_odd[...],
    )


def attention_specs(part, rows, length):
    span = (rows, 4 * PAIR)
    return {
        "table_pair": pl.BlockSpec((length, PAIR), lambda g, s: (0, 0)),
        "table": pl.BlockSpec((rows, PAIR), lambda g, s: (s[0], 0)),
        "pair": pl.BlockSpec((length, PAIR), lambda g, s: (0, s[1 + g])),
        "part": pl.BlockSpec(span, lambda g, s: (part, g)),
        "wide": pl.BlockSpec(span, lambda g, s: (0, g)),
        "sums": pl.BlockSpec((1, 8, rows), lambda g, s: (g, 0, 0)),
    }


def attention_cost(rows, length, heads, matmuls):
    work = 20 * rows * length * heads * HEAD_WIDTH * matmuls
    return pl.CostEstimate(
        flops=work, bytes_accessed=16 * rows * heads * HEAD_WIDTH, transcendentals=rows * length * heads
    )


def attention_forward(info, queries, pair_pre, tables, part, length):
    cos_pair, sin_pair, cosine, sine = tables
    rows = cosine.shape[0] // BLOCK_PARTS
    heads = 4 * 4 * PAIR // HEAD_WIDTH
    spec = attention_specs(part, rows, length)
    half = pltpu.VMEM((length, PAIR), jnp.bfloat16)
    wide = (rows, heads * HEAD_WIDTH)
    return pl.pallas_call(
        attention_forward_kernel,
        grid_spec=pltpu.PrefetchScalarGridSpec(
            num_scalar_prefetch=1,
            grid=(4,),
            in_specs=[
                spec["part"], spec["pair"],
                spec["table_pair"], spec["table_pair"], spec["table"], spec["table"],
            ],
            out_specs=[spec["wide"], spec["wide"], spec["sums"]],
            scratch_shapes=[
                half, half,
                pltpu.VMEM((HEAD_WIDTH, length), jnp.bfloat16),
            ],
        ),
        out_shape=[
            jax.ShapeDtypeStruct(wide, jnp.bfloat16),
            jax.ShapeDtypeStruct(wide, jnp.bfloat16),
            jax.ShapeDtypeStruct((4, 8, rows), jnp.float32),
        ],
        compiler_params=pltpu.CompilerParams(
            dimension_semantics=("arbitrary",), vmem_limit_bytes=VMEM_LIMIT
        ),
        cost_estimate=attention_cost(rows, length, heads, 2),
        name="attention_forward",
    )(info, queries, pair_pre, cos_pair, sin_pair, cosine, sine)


def attention_backward(info, low, grad, sums, pair_pre, tables, part, length, before):
    cos_pair, sin_pair, cosine, sine = tables
    rows = cosine.shape[0] // BLOCK_PARTS
    heads = low.shape[1] // HEAD_WIDTH
    spec = attention_specs(part, rows, length)
    before = [] if before is None else [before]
    half = pltpu.VMEM((length, PAIR), jnp.bfloat16)
    full = pltpu.VMEM((length, PAIR), jnp.float32)
    return pl.pallas_call(
        attention_backward_kernel,
        grid_spec=pltpu.PrefetchScalarGridSpec(
            num_scalar_prefetch=1,
            grid=(4,),
            in_specs=[
                spec["wide"], spec["wide"], spec["sums"], spec["pair"],
                spec["table_pair"], spec["table_pair"], spec["table"], spec["table"],
            ]
            + [pl.BlockSpec(memory_space=pl.ANY)] * len(before),
            out_specs=[spec["part"], pl.BlockSpec((1, length, PAIR), lambda g, s: (s[1 + g], 0, 0))],
            scratch_shapes=[
                half, half, half, half,
                pltpu.VMEM((HEAD_WIDTH, length), jnp.bfloat16),
                full, full, full, full,
            ],
        ),
        out_shape=[
            jax.ShapeDtypeStruct((2 * rows, low.shape[1]), jnp.bfloat16),
            jax.ShapeDtypeStruct((4, length, PAIR), jnp.float32),
        ],
        input_output_aliases={9: 0} if before else {},
        compiler_params=pltpu.CompilerParams(
            dimension_semantics=("arbitrary",), vmem_limit_bytes=VMEM_LIMIT
        ),
        cost_estimate=attention_cost(rows, length, heads, 5),
        name="attention_backward",
    )(info, low, grad, sums, pair_pre, cos_pair, sin_pair, cosine, sine, *before)


def rope_tables(length):
    positions = np.arange(length, dtype=np.float32)
    inverse = 10000.0 ** (-np.arange(0, HEAD_WIDTH, 2, dtype=np.float32) / HEAD_WIDTH)
    angles = positions[:, None] * inverse.astype(np.float32)[None, :]
    cosine, sine = np.cos(angles).astype(np.float32), np.sin(angles).astype(np.float32)
    head_cos = np.concatenate([cosine, cosine], axis=1)
    head_sin = np.concatenate([-sine, sine], axis=1)
    still = np.ones_like(head_cos)
    return tuple(
        jnp.asarray(np.concatenate(sides, axis=1))
        for sides in (
            (head_cos, still), (head_sin, 0 * still), (head_cos, head_cos), (head_sin, head_sin)
        )
    )


def head_marks(width, transposed):
    shape = (PAIR, width) if transposed else (width, PAIR)
    head_at, column_at = (0, 1) if transposed else (1, 0)
    head = lax.broadcasted_iota(jnp.int32, shape, head_at)
    column = lax.broadcasted_iota(jnp.int32, shape, column_at)
    return (column // HHD == head).astype(jnp.bfloat16)


def head_sums(value, marks):
    high = to_low(value)
    rest = to_low(value - high.astype(jnp.float32))
    return matmul(high, marks) + matmul(rest, marks)


def normalize(value):
    centered = value - jnp.mean(value, axis=-1, keepdims=True)
    inverse = lax.rsqrt(jnp.mean(centered * centered, axis=-1, keepdims=True) + EPS)
    return (centered * inverse, inverse)


def norm_back(grad, gain, hat, inverse):
    scaled = grad * gain
    mean = jnp.mean(scaled, axis=-1, keepdims=True)
    along = jnp.mean(scaled * hat, axis=-1, keepdims=True)
    return inverse * (scaled - mean - hat * along)


def slot_attention_kernel(pieces_ref, counts_ref, weight_ref, norm_ref, *refs):
    mixed_ref, probs_ref, attended_ref, lead_ref = refs[-4:]
    entries, slots, width = pieces_ref.shape
    rows = entries * slots
    tall = (entries, slots, width)
    pieces = pieces_ref[...].astype(jnp.float32)
    hat, _ = normalize(pieces.reshape(rows, width))
    low = to_low(hat * norm_ref[0:1, :] + norm_ref[1:2, :])
    mixed = []
    for part in range(3):
        span = slice(part * width, (part + 1) * width)
        value = to_low(matmul(low, weight_ref[:, span]))
        mixed_ref[:, span] = value
        mixed.append(value.astype(jnp.float32).reshape(tall))
    query, keys, values = mixed
    marks = head_marks(width, False)
    product = (keys * query[:, 0:1, :]).reshape(rows, width)
    scores = head_sums(product, marks).reshape(entries, slots, PAIR) * HHD ** (-0.5)
    live = lax.broadcasted_iota(jnp.int32, scores.shape, 1) < counts_ref[...]
    scores = jnp.where(live, scores, NEGATIVE)
    weight = jnp.exp(scores - jnp.max(scores, axis=1, keepdims=True))
    probs = weight / jnp.sum(weight, axis=1, keepdims=True)
    probs_ref[...] = probs
    spread = matmul(to_low(probs.reshape(rows, PAIR)), head_marks(width, True)).reshape(tall)
    attended_ref[...] = to_low(jnp.sum(spread * values, axis=1))
    lead_ref[...] = pieces[:, 0, :]


def slot_attention(at, before, pieces, counts, in_weight, norm_rows):
    entries, slots, width = pieces.shape
    part = min(ENTRY_BLOCK, entries // 2)
    steps = entries // 2 // part
    counts = jnp.broadcast_to(counts[:, None, None], (entries, 1, PAIR))
    whole = lambda shape: pl.BlockSpec(shape, lambda i: (0,) * len(shape))
    tall = pl.BlockSpec((part, slots, width), lambda i: (i + at * steps, 0, 0))
    flat = pl.BlockSpec((part, width), lambda i: (i + at * steps, 0))
    before = [] if before is None else list(before)
    return list(
        pl.pallas_call(
            slot_attention_kernel,
            grid=(steps,),
            in_specs=[
                tall,
                pl.BlockSpec((part, 1, PAIR), lambda i: (i + at * steps, 0, 0)),
                whole(in_weight.shape),
                whole(norm_rows.shape),
            ]
            + [pl.BlockSpec(memory_space=pl.ANY)] * len(before),
            out_specs=[
                pl.BlockSpec((part * slots, 3 * width), lambda i: (i + at * steps, 0)),
                pl.BlockSpec((part, slots, PAIR), lambda i: (i + at * steps, 0, 0)),
                flat,
                flat,
            ],
            out_shape=[
                jax.ShapeDtypeStruct((entries * slots, 3 * width), jnp.bfloat16),
                jax.ShapeDtypeStruct((entries, slots, PAIR), jnp.float32),
                jax.ShapeDtypeStruct((entries, width), jnp.bfloat16),
                jax.ShapeDtypeStruct((entries, width), jnp.float32),
            ],
            input_output_aliases={4 + i: i for i in range(len(before))},
            compiler_params=pltpu.CompilerParams(
                dimension_semantics=("arbitrary",), vmem_limit_bytes=VMEM_LIMIT
            ),
            cost_estimate=pl.CostEstimate(
                flops=entries * slots * width, bytes_accessed=entries * slots, transcendentals=0
            ),
            name="slot_attention",
        )(pieces, counts, in_weight, norm_rows, *before)
    )


def gelu_of(value):
    cdf = 0.5 * (1.0 + lax.erf(value * np.float32(0.5 ** 0.5)))
    return (value * cdf, cdf)


def gelu_slope(value, cdf):
    return cdf + value * (jnp.exp(-0.5 * value * value) * np.float32((2 * np.pi) ** -0.5))


def units_forward_kernel(
    attended_ref, lead_ref, wide_weight_ref, reduce_ref, norm_ref, pooled_ref, hidden_ref
):
    width = lead_ref.shape[1]
    hidden = lead_ref[...] + matmul(attended_ref[...], wide_weight_ref[:, :width])
    hidden_ref[...] = hidden
    hat, _ = normalize(hidden)
    second = to_low(hat * norm_ref[2:3, :] + norm_ref[3:4, :])
    total = hidden
    units = reduce_ref.shape[0]
    step = min(UNIT, units)
    for at in range(0, units, step):
        active, _ = gelu_of(matmul(second, wide_weight_ref[:, width + at : width + at + step]))
        total = total + matmul(to_low(active), reduce_ref[at : at + step, :])
    pooled_ref[...] = to_low(total)


def units_forward(attended, lead, wide_weight, reduce_weight, norm_rows):
    entries, width = attended.shape
    part = min(UNIT_ROWS, entries)
    whole = lambda shape: pl.BlockSpec(shape, lambda i: (0,) * len(shape))
    flat = pl.BlockSpec((part, width), lambda i: (i, 0))
    return pl.pallas_call(
        units_forward_kernel,
        grid=(entries // part,),
        in_specs=[flat, flat]
        + [whole(x.shape) for x in (wide_weight, reduce_weight, norm_rows)],
        out_specs=[flat, flat],
        out_shape=[
            jax.ShapeDtypeStruct((entries, width), jnp.bfloat16),
            jax.ShapeDtypeStruct((entries, width), jnp.float32),
        ],
        compiler_params=pltpu.CompilerParams(
            dimension_semantics=("arbitrary",), vmem_limit_bytes=VMEM_LIMIT
        ),
        cost_estimate=pl.CostEstimate(
            flops=entries * width, bytes_accessed=entries * width, transcendentals=0
        ),
        name="units_forward",
    )(attended, lead, wide_weight, reduce_weight, norm_rows)


def units_backward_kernel(
    grad_ref, hidden_ref, attended_ref, wide_weight_ref, reduce_ref, norm_ref,
    hidden_grad_ref, attended_grad_ref, wide_ref, reduce_grad_ref, norm_grad_ref,
    wide_total, reduce_total,
):
    step_at = pl.program_id(0)
    width = hidden_ref.shape[1]
    units = reduce_ref.shape[0]

    @pl.when(step_at == 0)
    def start():
        wide_total[...] = jnp.zeros_like(wide_total)
        reduce_total[...] = jnp.zeros_like(reduce_total)
        norm_grad_ref[...] = jnp.zeros_like(norm_grad_ref)

    grad = grad_ref[...]
    grad_low = to_low(grad)
    hat, inverse = normalize(hidden_ref[...])
    second = to_low(hat * norm_ref[2:3, :] + norm_ref[3:4, :])
    grad_normed = jnp.zeros_like(grad)
    step = min(UNIT, units)
    for at in range(0, units, step):
        span = slice(at, at + step)
        wide_span = slice(width + at, width + at + step)
        expanded = matmul(second, wide_weight_ref[:, wide_span])
        active, cdf = gelu_of(expanded)
        reduce_total[span, :] += matmul_first(to_low(active), grad_low)
        grad_active = matmul_last(grad_low, reduce_ref[span, :])
        grad_expanded = to_low(grad_active * gelu_slope(expanded, cdf))
        wide_total[:, wide_span] += matmul_first(second, grad_expanded)
        grad_normed = grad_normed + matmul_last(grad_expanded, wide_weight_ref[:, wide_span])
    norm_grad_ref[2:3, :] += jnp.sum(grad_normed * hat, axis=0, keepdims=True)
    norm_grad_ref[3:4, :] += jnp.sum(grad_normed, axis=0, keepdims=True)
    hidden_grad = grad + norm_back(grad_normed, norm_ref[2:3, :], hat, inverse)
    hidden_grad_ref[...] = hidden_grad
    hidden_low = to_low(hidden_grad)
    wide_total[:, :width] += matmul_first(attended_ref[...], hidden_low)
    attended_grad_ref[...] = to_low(matmul_last(hidden_low, wide_weight_ref[:, :width]))

    @pl.when(step_at == pl.num_programs(0) - 1)
    def finish():
        wide_ref[...] = to_low(wide_total[...])
        reduce_grad_ref[...] = to_low(reduce_total[...])


def units_backward(grad, hidden, attended, wide_weight, reduce_weight, norm_rows):
    entries, width = attended.shape
    part = min(UNIT_ROWS, entries)
    units = reduce_weight.shape[0]
    whole = lambda shape: pl.BlockSpec(shape, lambda i: (0,) * len(shape))
    flat = pl.BlockSpec((part, width), lambda i: (i, 0))
    wide = (width, width + units)
    return pl.pallas_call(
        units_backward_kernel,
        grid=(entries // part,),
        in_specs=[flat, flat, flat]
        + [whole(x.shape) for x in (wide_weight, reduce_weight, norm_rows)],
        out_specs=[flat, flat, whole(wide), whole((units, width)), whole((8, width))],
        out_shape=[
            jax.ShapeDtypeStruct((entries, width), jnp.float32),
            jax.ShapeDtypeStruct((entries, width), jnp.bfloat16),
            jax.ShapeDtypeStruct(wide, jnp.bfloat16),
            jax.ShapeDtypeStruct((units, width), jnp.bfloat16),
            jax.ShapeDtypeStruct((8, width), jnp.float32),
        ],
        scratch_shapes=[pltpu.VMEM(wide, jnp.float32), pltpu.VMEM((units, width), jnp.float32)],
        compiler_params=pltpu.CompilerParams(
            dimension_semantics=("arbitrary",), vmem_limit_bytes=VMEM_LIMIT
        ),
        cost_estimate=pl.CostEstimate(
            flops=6 * entries * width * (2 * width + 5 * units), bytes_accessed=16 << 20, transcendentals=0
        ),
        name="units_backward",
    )(grad, hidden, attended, wide_weight, reduce_weight, norm_rows)


def slot_backward_kernel(
    first, last, pieces_ref, mixed_ref, probs_ref, attended_grad_ref, hidden_grad_ref, weight_ref, norm_ref,
    later_ref, *refs,
):
    if first:
        pieces_grad_ref, input_grad_ref, norm_grad_ref, total, norm_total = refs
    else:
        _, total_ref, pieces_grad_ref, input_grad_ref, norm_grad_ref, total, norm_total = refs
    step_at = pl.program_id(0)
    entries, slots, width = pieces_ref.shape
    rows = entries * slots
    tall = (entries, slots, width)

    @pl.when(step_at == 0)
    def start():
        norm_total[...] = jnp.zeros_like(norm_total)
        norm_total[0:8, :] = later_ref[...]
        total[...] = jnp.zeros_like(total) if first else total_ref[...]

    hat, inverse = normalize(pieces_ref[...].astype(jnp.float32).reshape(rows, width))
    low = to_low(hat * norm_ref[0:1, :] + norm_ref[1:2, :])
    scale = HHD ** (-0.5)
    query, keys, values = [
        mixed_ref[:, part * width : (part + 1) * width].astype(jnp.float32).reshape(tall) for part in range(3)
    ]
    probs = probs_ref[...]
    grad_attended = jnp.broadcast_to(attended_grad_ref[...].astype(jnp.float32)[:, None, :], tall)
    grad_probs = head_sums((grad_attended * values).reshape(rows, width), head_marks(width, False))
    moved = probs * grad_probs.reshape(probs.shape)
    grad_scores = to_low(moved - probs * jnp.sum(moved, axis=1, keepdims=True))
    marks = head_marks(width, True)
    spread = matmul(grad_scores.reshape(rows, PAIR), marks).reshape(tall) * scale
    first_slot = lax.broadcasted_iota(jnp.int32, tall, 1) == 0
    grad_query = jnp.where(first_slot, jnp.sum(spread * keys, axis=1, keepdims=True), 0.0)
    grad_keys = spread * query[:, 0:1, :]
    grad_values = matmul(to_low(probs.reshape(rows, PAIR)), marks).reshape(tall) * grad_attended
    grad_normed = jnp.zeros((rows, width), jnp.float32)
    for part, grad in enumerate((grad_query, grad_keys, grad_values)):
        span = slice(part * width, (part + 1) * width)
        grad_low = to_low(grad.reshape(rows, width))
        total[:, span] += matmul_first(low, grad_low)
        grad_normed = grad_normed + matmul_last(grad_low, weight_ref[:, span])
    norm_total[0:1, :] += jnp.sum(grad_normed * hat, axis=0, keepdims=True)
    norm_total[1:2, :] += jnp.sum(grad_normed, axis=0, keepdims=True)
    grad_pieces = norm_back(grad_normed, norm_ref[0:1, :], hat, inverse).reshape(tall)
    hidden_grad = jnp.broadcast_to(hidden_grad_ref[...][:, None, :], tall)
    pieces_grad_ref[...] = to_low(grad_pieces + jnp.where(first_slot, hidden_grad, 0.0))

    @pl.when(step_at == pl.num_programs(0) - 1)
    def finish():
        norm_grad_ref[...] = norm_total[0:8, :]
        if last:
            input_grad_ref[:, : 3 * width] = to_low(total[...])
            input_grad_ref[:, 3 * width :] = to_low(norm_total[...].T)
        else:
            input_grad_ref[...] = total[...]


def slot_backward(at, parts, held, saved, grads, in_weight, norm_rows):
    pieces, mixed, probs = saved
    pieces_grad, total, norm_grad = held
    entries, slots, width = pieces.shape
    first, last = at == 0, at == parts - 1
    part = min(ENTRY_BLOCK, entries // parts)
    steps = entries // parts // part
    whole = lambda shape: pl.BlockSpec(shape, lambda i: (0,) * len(shape))
    tall = pl.BlockSpec((part, slots, width), lambda i: (i + at * steps, 0, 0))
    flat = pl.BlockSpec((part, width), lambda i: (i + at * steps, 0))
    total_shape = (
        jax.ShapeDtypeStruct((width, 3 * width + PAIR), jnp.bfloat16)
        if last
        else jax.ShapeDtypeStruct((width, 3 * width), jnp.float32)
    )
    in_specs = [
        tall,
        pl.BlockSpec((part * slots, 3 * width), lambda i: (i + at * steps, 0)),
        pl.BlockSpec((part, slots, PAIR), lambda i: (i + at * steps, 0, 0)),
        flat,
        flat,
        whole(in_weight.shape),
        whole(norm_rows.shape),
        whole(norm_grad.shape),
    ]
    operands = [pieces, mixed, probs, *grads, in_weight, norm_rows, norm_grad]
    if not first:
        in_specs += [pl.BlockSpec(memory_space=pl.ANY), whole(total.shape)]
        operands += [pieces_grad, total]
    return pl.pallas_call(
        functools.partial(slot_backward_kernel, first, last),
        grid=(steps,),
        in_specs=in_specs,
        out_specs=[tall, whole(total_shape.shape), whole(norm_grad.shape)],
        out_shape=[
            jax.ShapeDtypeStruct(pieces.shape, jnp.bfloat16),
            total_shape,
            jax.ShapeDtypeStruct(norm_grad.shape, jnp.float32),
        ],
        input_output_aliases={} if first else {len(operands) - 2: 0},
        scratch_shapes=[
            pltpu.VMEM((width, 3 * width), jnp.float32),
            pltpu.VMEM((PAIR, width), jnp.float32),
        ],
        compiler_params=pltpu.CompilerParams(
            dimension_semantics=("arbitrary",), vmem_limit_bytes=VMEM_LIMIT
        ),
        cost_estimate=pl.CostEstimate(
            flops=entries * slots * width // parts,
            bytes_accessed=entries * slots // parts,
            transcendentals=0,
        ),
        name="slot_backward",
    )(*operands)


def feed_forward_kernel(
    rows_ref, other_ref, rise_ref, rise_other_ref, hidden_ref, gate_ref, up_ref, down_ref,
    gate_rows, up_rows, down_columns, grad_ref, dense_ref, rows, rise, active, grad_gate, grad_up,
):
    at = pl.program_id(0)
    half = rows_ref.shape[0]
    step = gate_ref.shape[1]
    tiles = active.shape[1] // step

    @pl.when(at == 0)
    def start():
        rows[:half, :] = rows_ref[...]
        rows[half:, :] = other_ref[...]
        rise[:half, :] = rise_ref[...]
        rise[half:, :] = rise_other_ref[...]

    @pl.when(at < tiles)
    def units():
        gate = matmul(rows[...], gate_ref[...])
        up = matmul(rows[...], up_ref[...])
        rising = matmul_last(rise[...], down_ref[...])
        sign = 1.0 / (1.0 + jnp.exp(-gate))
        silu = gate * sign
        span = pl.ds(pl.multiple_of(at * step, step), step)
        active[:, span] = to_low(silu * up)
        grad_up[:, span] = to_low(rising * silu)
        grad_gate[:, span] = to_low(rising * up * (sign * (1.0 + gate * (1.0 - sign))))

    @pl.when(at >= tiles)
    def columns():
        dense = matmul(active[...], down_columns[...])
        grad = matmul_last(grad_gate[...], gate_rows[...]) + matmul_last(grad_up[...], up_rows[...])
        grad_ref[...] = to_low(grad)
        dense_ref[:half, :] = to_low(dense[:half] + hidden_ref[...])
        dense_ref[half:, :] = to_low(dense[half:])


def feed_forward(rows, other, upstream, hidden, info, gate_weight, up_weight, down_weight):
    half, width = rows.shape
    units = gate_weight.shape[1]
    step = UNIT_STEP
    tiles = units // step
    column = COLUMN_STEP
    fixed_rows = pl.BlockSpec((half, width), lambda i, s: (0, 0), pipeline_mode=pl.Buffered(1))
    early = lambda i: jnp.minimum(i, tiles - 1)
    late = lambda i: jnp.maximum(i - tiles, 0)
    tall = (2 * half, width)
    out = pl.BlockSpec((2 * half, column), lambda i, s: (0, late(i)))
    return pl.pallas_call(
        lambda info, *refs: feed_forward_kernel(*refs),
        grid_spec=pltpu.PrefetchScalarGridSpec(
            num_scalar_prefetch=1,
            grid=(tiles + width // column,),
            in_specs=[
                fixed_rows,
                fixed_rows,
                pl.BlockSpec((half, width), lambda i, s: (s[0], 0), pipeline_mode=pl.Buffered(1)),
                pl.BlockSpec((half, width), lambda i, s: (s[1], 0), pipeline_mode=pl.Buffered(1)),
                pl.BlockSpec((half, column), lambda i, s: (0, late(i))),
                pl.BlockSpec((width, step), lambda i, s: (0, early(i))),
                pl.BlockSpec((width, step), lambda i, s: (0, early(i))),
                pl.BlockSpec((step, width), lambda i, s: (early(i), 0)),
                pl.BlockSpec((column, units), lambda i, s: (late(i), 0)),
                pl.BlockSpec((column, units), lambda i, s: (late(i), 0)),
                pl.BlockSpec((units, column), lambda i, s: (0, late(i))),
            ],
            out_specs=[out, out],
            scratch_shapes=[
                pltpu.VMEM(tall, jnp.bfloat16),
                pltpu.VMEM(tall, jnp.bfloat16),
                *[pltpu.VMEM((2 * half, units), jnp.bfloat16)] * 3,
            ],
        ),
        out_shape=[jax.ShapeDtypeStruct(tall, jnp.bfloat16)] * 2,
        compiler_params=pltpu.CompilerParams(
            dimension_semantics=("arbitrary",), vmem_limit_bytes=VMEM_LIMIT
        ),
        cost_estimate=pl.CostEstimate(
            flops=34 * half * width * units, bytes_accessed=12 * width * units, transcendentals=0
        ),
        name="feed_forward",
    )(
        info, rows, other, upstream, upstream, hidden, gate_weight, up_weight, down_weight,
        gate_weight, up_weight, down_weight,
    )


def fixed(shape):
    return pl.BlockSpec(shape, lambda *_: (0,) * len(shape), pipeline_mode=pl.Buffered(1))


def root_mean(value):
    return lax.rsqrt(jnp.mean(value * value, axis=-1, keepdims=True) + EPS)


def root_mean_back(grad, gain, value):
    scaled = grad * gain
    inverse = root_mean(value)
    along = jnp.mean(value * scaled, axis=-1, keepdims=True)
    return inverse * scaled - value * (inverse * inverse * inverse * along)


def project_kernel(with_queries, info, chosen_ref, embed_ref, gain_ref, pair_weight_ref, *refs):
    embedded = to_low(matmul(chosen_ref[...], embed_ref[...]))
    value = embedded.astype(jnp.float32)
    low = to_low(value * root_mean(value) * gain_ref[...])
    if not with_queries:
        refs[-1][...] = matmul(low, pair_weight_ref[...])
        return
    near_ref, mid_a, mid_b, far_a, far_b, pair_ref, embedded_ref, query_ref = refs
    pair_ref[...] = matmul(low, pair_weight_ref[...])
    embedded_ref[...] = embedded
    near = near_ref.shape[1]
    step = mid_a.shape[1]
    half = mid_a.shape[0]
    query_ref[:, :near] = matmul(low, near_ref[...])
    for start, upper, lower in ((near, mid_a, mid_b), (near + step, far_a, far_b)):
        query_ref[:, start : start + step] = matmul(low[:, :half], upper[...]) + matmul(
            low[:, half:], lower[...]
        )


def project(info, chosen, embed, gain, pair_weight, query_weights, pair_before):
    rows, width = chosen.shape
    block = rows // 2
    wide = embed.shape[1]
    row = pl.BlockSpec((block, wide), lambda i, s: (i, 0))
    pairs = pair_weight.shape[1]
    before = [] if pair_before is None else [pair_before]
    more = bool(query_weights)
    return pl.pallas_call(
        functools.partial(project_kernel, more),
        grid_spec=pltpu.PrefetchScalarGridSpec(
            num_scalar_prefetch=1,
            grid=(2,),
            in_specs=[
                pl.BlockSpec((block, width), lambda i, s: (i, 0)),
                fixed(embed.shape),
                fixed((1, wide)),
                fixed(pair_weight.shape),
                *[fixed(weight.shape) for weight in query_weights],
                *[pl.BlockSpec(memory_space=pl.ANY)] * len(before),
            ],
            out_specs=[pl.BlockSpec((block, pairs), lambda i, s: (s[i], 0))] + [row, row] * more,
        ),
        out_shape=[jax.ShapeDtypeStruct((2 * rows, pairs), jnp.float32)]
        + [
            jax.ShapeDtypeStruct((rows, wide), jnp.bfloat16),
            jax.ShapeDtypeStruct((rows, wide), jnp.float32),
        ]
        * more,
        input_output_aliases={5: 0} if before else {},
        compiler_params=pltpu.CompilerParams(
            dimension_semantics=("arbitrary",), vmem_limit_bytes=VMEM_LIMIT
        ),
        cost_estimate=pl.CostEstimate(flops=1 << 30, bytes_accessed=1 << 20, transcendentals=0),
        name="project",
    )(info, chosen, embed, gain.reshape(1, -1), pair_weight, *query_weights, *before)


def output_kernel(rows_ref, embedded_ref, gain_ref, near_ref, mid_a, mid_b, far_a, far_b, hidden_ref, low_ref):
    total = embedded_ref[...].astype(jnp.float32)
    at = 0
    for ref in (near_ref, mid_a, mid_b, far_a, far_b):
        total = total + matmul(rows_ref[:, at : at + ref.shape[0]], ref[...])
        at += ref.shape[0]
    hidden_ref[...] = total
    low_ref[...] = to_low(total * root_mean(total) * gain_ref[...])


def output_project(part, rows, embedded, gain, weights):
    block, wide = rows.shape
    spec = pl.BlockSpec((block, wide), lambda i: (0, 0))
    return pl.pallas_call(
        output_kernel,
        grid=(1,),
        in_specs=[
            spec,
            pl.BlockSpec((block, wide), lambda i: (part, 0)),
            fixed((1, wide)),
            *[fixed(weight.shape) for weight in weights],
        ],
        out_specs=[spec, spec],
        out_shape=[
            jax.ShapeDtypeStruct((block, wide), jnp.float32),
            jax.ShapeDtypeStruct((block, wide), jnp.bfloat16),
        ],
        compiler_params=pltpu.CompilerParams(
            dimension_semantics=("arbitrary",), vmem_limit_bytes=VMEM_LIMIT
        ),
        cost_estimate=pl.CostEstimate(flops=4 << 30, bytes_accessed=12 << 20, transcendentals=0),
        name="output_project",
    )(rows, embedded, gain.reshape(1, -1), *weights)


def hidden_backward_kernel(
    info, here_ref, came_ref, hidden_ref, rising_ref, gain_ref, near_ref, mid_a, mid_b, far_a, far_b,
    grad_ref, rows_ref,
):
    grad = here_ref[...].astype(jnp.float32) + came_ref[...].astype(jnp.float32)
    total = rising_ref[...].astype(jnp.float32) + root_mean_back(grad, gain_ref[...], hidden_ref[...])
    grad_ref[...] = total
    low = to_low(total)
    at = 0
    for ref in (near_ref, mid_a, mid_b, far_a, far_b):
        rows_ref[:, at : at + ref.shape[0]] = to_low(matmul_last(low, ref[...]))
        at += ref.shape[0]


def hidden_backward(info, here, came, hidden, upstream, gain, weights):
    block, wide = hidden.shape
    spec = pl.BlockSpec((block, wide), lambda i, s: (0, 0))
    return pl.pallas_call(
        hidden_backward_kernel,
        grid_spec=pltpu.PrefetchScalarGridSpec(
            num_scalar_prefetch=1,
            grid=(1,),
            in_specs=[
                spec,
                spec,
                spec,
                pl.BlockSpec((block, wide), lambda i, s: (s[0], 0)),
                fixed((1, wide)),
                *[fixed(weight.shape) for weight in weights],
            ],
            out_specs=[spec, spec],
        ),
        out_shape=[
            jax.ShapeDtypeStruct((block, wide), jnp.float32),
            jax.ShapeDtypeStruct((block, wide), jnp.bfloat16),
        ],
        compiler_params=pltpu.CompilerParams(
            dimension_semantics=("arbitrary",), vmem_limit_bytes=VMEM_LIMIT
        ),
        cost_estimate=pl.CostEstimate(flops=4 << 30, bytes_accessed=14 << 20, transcendentals=0),
        name="hidden_backward",
    )(info, here, came, hidden, upstream, gain.reshape(1, -1), *weights)


def embed_backward_kernel(
    info, query_ref, own_ref, came_ref, short_ref, cos_ref, sin_ref, first_ref, second_ref, embedded_ref, gain_ref,
    embed_ref, near_ref, mid_a, mid_b, far_a, far_b, pair_weight_ref, grad_ref, token_ref,
):
    total = None
    for head in range(own_ref.shape[0]):
        short = jnp.where(pl.program_id(0) == 0, short_ref[head].astype(jnp.float32), 0.0)
        pair = own_ref[head] + came_ref[head].astype(jnp.float32) + short
        low = to_low(pair * cos_ref[...] - half_swap(pair) * sin_ref[...])
        term = matmul_last(low, pair_weight_ref[:, head * PAIR : (head + 1) * PAIR])
        total = term if total is None else total + term
    near = near_ref.shape[1]
    step = mid_a.shape[1]
    half = mid_a.shape[0]
    total = total + matmul_last(query_ref[:, :near], near_ref[...])
    mid = query_ref[:, near : near + step]
    far = query_ref[:, near + step : near + 2 * step]
    spread = jnp.concatenate(
        [
            matmul_last(mid, mid_a[...]) + matmul_last(far, far_a[...]),
            matmul_last(mid, mid_b[...]) + matmul_last(far, far_b[...]),
        ],
        axis=1,
    )
    value = embedded_ref[...].astype(jnp.float32)
    hidden = jnp.where(pl.program_id(0) == 0, first_ref[...], second_ref[...])
    grad = to_low(hidden + root_mean_back(total + spread, gain_ref[...], value))
    grad_ref[...] = grad
    token_ref[...] = to_low(matmul_last(grad, embed_ref[...]))


def embed_backward(
    info, query_grad, own, came, short, tables, hidden_grads, embedded, gain, embed, query_weights, pair_weight
):
    rows, wide = embedded.shape
    block = rows // 2
    heads = own.shape[0]
    row = pl.BlockSpec((block, wide), lambda i, s: (i, 0))
    once = pl.BlockSpec((block, wide), lambda i, s: (0, 0))
    pair = pl.BlockSpec((heads, block, PAIR), lambda i, s: (0, i, 0))
    table = pl.BlockSpec((block, PAIR), lambda i, s: (s[i], 0))
    return pl.pallas_call(
        embed_backward_kernel,
        grid_spec=pltpu.PrefetchScalarGridSpec(
            num_scalar_prefetch=1,
            grid=(2,),
            in_specs=[
                row, pair, pair, pl.BlockSpec((heads, block, PAIR), lambda i, s: (0, 0, 0)), table, table, once, once, row, fixed((1, wide)), fixed(embed.shape),
                *[fixed(weight.shape) for weight in query_weights],
                fixed(pair_weight.shape),
            ],
            out_specs=[row, pl.BlockSpec((block, embed.shape[0]), lambda i, s: (i, 0))],
        ),
        out_shape=[
            jax.ShapeDtypeStruct((rows, wide), jnp.bfloat16),
            jax.ShapeDtypeStruct((rows, embed.shape[0]), jnp.bfloat16),
        ],
        compiler_params=pltpu.CompilerParams(
            dimension_semantics=("arbitrary",), vmem_limit_bytes=VMEM_LIMIT
        ),
        cost_estimate=pl.CostEstimate(flops=12 << 30, bytes_accessed=20 << 20, transcendentals=0),
        name="embed_backward",
    )(
        info, query_grad, own, came, short, tables[0], tables[1], *hidden_grads, embedded, gain.reshape(1, -1), embed,
        *query_weights, pair_weight,
    )


def own_route(own, local_vocab):
    places = jnp.arange(own.shape[0], dtype=jnp.int32)
    same = own[:, None] == own[None, :]
    repeated = jnp.any(same & (places[:, None] > places[None, :]), axis=1)
    owner = own // local_vocab
    before = (owner[:, None] == owner[None, :]) & (own[None, :] < own[:, None])
    rank = jnp.sum((before & jnp.logical_not(repeated)[None, :]).astype(jnp.int32), axis=1)
    return (rank, owner)


def asked_of_me(asked, me, local_vocab):
    entries = me * local_vocab + jnp.arange(local_vocab, dtype=jnp.int32)
    present = jnp.any(asked[:, :, None] == entries[None, None, :], axis=1)
    places = jnp.arange(local_vocab, dtype=jnp.int32)
    lower = places[:, None] < places[None, :]
    standing = matmul(present.astype(jnp.bfloat16), lower.astype(jnp.bfloat16)).astype(jnp.int32)
    return (present, standing)


def sender_choice(present, standing, turn, capacity):
    place = jnp.arange(capacity, dtype=jnp.int32)
    slot = jnp.where(place < capacity - 1, turn * (capacity - 1) + place, -1)
    chosen = present[:, None, :] & (standing[:, None, :] == slot[None, :, None])
    return chosen.astype(jnp.bfloat16).reshape(present.shape[0] * capacity, present.shape[1])


def taker_choice(own_rank, own_owner, turn, capacity, devices):
    inside = own_rank - turn * (capacity - 1)
    valid = (inside >= 0) & (inside < capacity - 1)
    place = jnp.where(valid, own_owner * capacity + inside, -1)
    return (place[:, None] == jnp.arange(devices * capacity, dtype=jnp.int32)[None, :]).astype(
        jnp.bfloat16
    )


def exchange(value):
    return lax.all_to_all(value, ("dp", "mp"), 0, 0, tiled=True)


def ordered_blocks(first, own_two, other_two):
    return jnp.where(
        first,
        jnp.concatenate([own_two[0], other_two[0], other_two[1], own_two[1]], axis=0),
        jnp.concatenate([other_two[0], own_two[0], own_two[1], other_two[1]], axis=0),
    )


def body(
    pieces,
    counts,
    token_index,
    hyper_input,
    hyper_output,
    hyper_expand,
    hyper_reduce,
    hyper_norms,
    embed_weight,
    attention_gain,
    dense_gain,
    frozen_query_weight,
    frozen_key_weight,
    frozen_value_weight,
    frozen_output_weight,
    gate_weight,
    up_weight,
    down_weight,
    upstream,
):
    local_vocab = pieces.shape[0]
    mp_count = lax.axis_size("mp")
    devices = lax.axis_size("dp") * mp_count
    mp_index = lax.axis_index("mp")
    me = lax.axis_index("dp") * mp_count + mp_index
    core = (me >> 1) & 1
    lead = mp_index == 0
    bits = log2_of(devices)
    far_bits = list(range(bits - 1, 1, -1))
    length = token_index.shape[0]
    block = length // BLOCK_PARTS
    capacity = max(16, length // devices)

    norm_count = hyper_norms.shape[1]
    in_width = hyper_input.shape[1]
    norm_lanes = jnp.pad(hyper_norms, ((0, 0), (0, PAIR - norm_count)))
    cut = token_index.reshape(BLOCK_PARTS, block)
    own_tokens = jnp.where(
        lead, jnp.concatenate([cut[0], cut[3]]), jnp.concatenate([cut[1], cut[2]])
    )
    digits = jnp.concatenate([own_tokens // PAIR, own_tokens % PAIR]).astype(jnp.bfloat16)
    digits = digits.reshape(hyper_input.shape[0], -1)
    digit_width = digits.shape[1]
    digit_lanes = jnp.pad(digits, ((0, 0), (0, -digit_width % PAIR)))
    spread_order = [[bit] for bit in [0] + far_bits + [1]]
    in_held = gather_start(jnp.concatenate([hyper_input, norm_lanes, digit_lanes], axis=1), devices)
    later_held = [
        gather_start(jnp.concatenate([hyper_output, hyper_expand], axis=1), devices),
        gather_start(hyper_reduce, devices),
    ]
    for at, step in enumerate(spread_order):
        in_held = gather_step(in_held, step, me, devices)
        if at == 1:
            in_held, later_held = lax.optimization_barrier((in_held, later_held))
    in_weight = gather_end(in_held)
    for step in spread_order[:-3]:
        later_held = [gather_step(x, step, me, devices) for x in later_held]
        if step == spread_order[0]:
            begun = later_held
    later_came = [gather_send(x, spread_order[-3], devices) for x in later_held]
    embed_full = lax.all_gather(embed_weight, ("dp", "mp"), axis=0, tiled=True)
    norm_rows = in_weight[:, in_width : in_width + 8].astype(jnp.float32).T
    digit_at = in_width + PAIR
    all_digits = in_weight[:, digit_at : digit_at + digit_width].reshape(devices, 2, 2 * block)
    all_digits = all_digits.astype(jnp.int32)
    asked = all_digits[:, 0] * PAIR + all_digits[:, 1]

    query_cut = frozen_query_weight.shape[1] // 2
    kv_local = frozen_key_weight.shape[1] // HEAD_WIDTH
    key_own = jnp.concatenate(
        [
            weight[:, at * HEAD_WIDTH : (at + 1) * HEAD_WIDTH]
            for at in range(kv_local)
            for weight in (frozen_key_weight, frozen_value_weight)
        ],
        axis=1,
    )
    frozen_query_weight, key_own, *_ = lax.optimization_barrier((frozen_query_weight, key_own, *begun))
    query_near = lax.dynamic_slice_in_dim(frozen_query_weight, core * query_cut, query_cut, 1)
    half_in = query_near.shape[0] // 2
    query_near = [swap(query_near[:half_in], 1, devices), swap(query_near[half_in:], 1, devices)]
    key_other = swap(key_own, 1, devices)
    other_base = (1 - mp_index) * kv_local
    head_order = [mp_index * kv_local, mp_index * kv_local + 1, other_base + core, other_base + 1 - core]

    slots_done = slot_attention(0, None, pieces, counts, in_weight, norm_rows)
    slots_done[2], later_came, asked, key_other = lax.optimization_barrier(
        (slots_done[2], later_came, asked, key_other)
    )
    later_held = [
        gather_join(held, came, spread_order[-3], me, devices)
        for held, came in zip(later_held, later_came)
    ]
    later_came = [gather_send(x, spread_order[-2], devices) for x in later_held]
    slots_done = slot_attention(1, slots_done, pieces, counts, in_weight, norm_rows)
    slots_done[2], later_came, embed_full, query_near[0] = lax.optimization_barrier(
        (slots_done[2], later_came, embed_full, query_near[0])
    )
    later_held = [
        gather_join(held, came, spread_order[-2], me, devices)
        for held, came in zip(later_held, later_came)
    ]
    slot_mixed, slot_probs, hyper_attended, lead_rows = slots_done
    wide_weight, reduce_weight = [
        gather_end(gather_step(held, spread_order[-1], me, devices)) for held in later_held
    ]
    hyper_attended, query_near[1] = lax.optimization_barrier((hyper_attended, query_near[1]))
    query_far = [swap(x, 2, devices) for x in query_near]
    output_near, *_ = lax.optimization_barrier((frozen_output_weight, *query_near))
    output_near = lax.dynamic_slice_in_dim(output_near, core * query_cut, query_cut, 0)
    half_out = output_near.shape[0] // 2
    output_near = [swap(output_near[:half_out], 1, devices), swap(output_near[half_out:], 1, devices)]
    pooled, hyper_hidden = units_forward(
        hyper_attended, lead_rows, wide_weight, reduce_weight, norm_rows
    )
    pooled, output_near[0] = lax.optimization_barrier((pooled, output_near[0]))
    pair_weight = jnp.where(
        lead,
        jnp.concatenate([key_own, key_other], axis=1),
        jnp.concatenate([key_other, key_own], axis=1),
    )
    present, standing = asked_of_me(asked, me, local_vocab)
    own_rank, own_owner = own_route(lax.dynamic_index_in_dim(asked, me, 0, False), local_vocab)
    most = jnp.max(jnp.sum(present.astype(jnp.int32), axis=1))
    needed = ((most + capacity - 2) // (capacity - 1)).astype(jnp.float32)

    def fetch(turn):
        sent = matmul(sender_choice(present, standing, turn, capacity), pooled)
        sent = sent.reshape(devices, capacity, pooled.shape[1])
        free = lax.broadcasted_iota(jnp.int32, sent.shape, 1) == capacity - 1
        sent = to_low(jnp.where(free, needed, sent)).reshape(devices * capacity, pooled.shape[1])
        came = exchange(sent)
        picked = matmul(taker_choice(own_rank, own_owner, turn, capacity, devices), came)
        return (to_low(picked), came)

    chosen_own, came = fetch(0)
    chosen_own, came, pair_weight, output_near[1], query_far = lax.optimization_barrier(
        (chosen_own, came, pair_weight, output_near[1], query_far)
    )
    needs = came.reshape(devices, capacity, pooled.shape[1])[:, capacity - 1, 0]
    rounds = jnp.max(needs.astype(jnp.float32)).astype(jnp.int32)
    chosen_own = lax.fori_loop(1, rounds, lambda turn, chosen: chosen + fetch(turn)[0], chosen_own)
    chosen_other = swap(chosen_own, 1, devices)

    tables = rope_tables(length)
    own_at = (mp_index, 3 - mp_index)
    own_base = tuple(at * block for at in own_at)
    other_start = ((1 - mp_index) * block, (2 + mp_index) * block)
    infos = [jnp.stack([at] + head_order).astype(jnp.int32) for at in own_at]

    other_at = (1 - mp_index, 2 + mp_index)
    query_weights = (frozen_query_weight, *query_near, *query_far)
    own_info = jnp.stack(own_at).astype(jnp.int32)
    other_info = jnp.stack(other_at).astype(jnp.int32)
    pair_pre, embedded, queries = project(
        own_info, chosen_own, embed_full, attention_gain, pair_weight, query_weights, None
    )
    (pair_pre,) = project(
        other_info, chosen_other, embed_full, attention_gain, pair_weight, (), pair_pre
    )
    output_far = [swap(x, 2, devices) for x in output_near]
    output_weights = (frozen_output_weight, *output_near, *output_far)
    spans = (2 * block, length)

    sums = [None, None]
    lows = [None, None]
    hidden_parts = [None, None]
    second_low = [None, None]
    second_other = [None, None]
    for part in (1, 0):
        flat, lows[part], sums[part] = attention_forward(
            infos[part], queries, pair_pre, tables, part, spans[part]
        )
        if part == 0:
            flat, second_other[1] = lax.optimization_barrier((flat, second_other[1]))
        hidden_parts[part], second_low[part] = output_project(
            part, flat, embedded, dense_gain, output_weights
        )
        second_other[part] = swap(second_low[part], 1, devices)
        pair_pre, second_low[part] = lax.optimization_barrier((pair_pre, second_low[part]))

    second_low = list(lax.optimization_barrier(tuple(second_low)))
    dense_rows = [None, None]
    second_came = [None, None]
    for part in (1, 0):
        info = jnp.stack([own_at[part], other_at[part]]).astype(jnp.int32)
        grad_second, dense_rows[part] = feed_forward(
            second_low[part], second_other[part], upstream, hidden_parts[part], info,
            gate_weight, up_weight, down_weight,
        )
        second_came[part] = (grad_second[:block], swap(grad_second[block:], 1, devices))

    query_grad = None
    grad_hidden = [None, None]
    pair_grads = [None, None]
    for part in (1, 0):
        here, came = second_came[part]
        if part == 1:
            here, came, dense_rows[0] = lax.optimization_barrier((here, came, dense_rows[0]))
        else:
            here, came, query_grad = lax.optimization_barrier((here, came, query_grad))
        grad_hidden[part], grad_attended = hidden_backward(
            infos[part], here, came, hidden_parts[part], upstream, dense_gain, output_weights
        )
        query_grad, pair_grads[part] = attention_backward(
            infos[part], lows[part], grad_attended, sums[part], pair_pre, tables, part, spans[part], query_grad
        )

    def pick_block(value, at):
        return lax.dynamic_slice_in_dim(value, at * block, block, 1)

    came_long = swap(
        to_low(jnp.concatenate([pick_block(pair_grads[1], at) for at in other_at], axis=1)), 1, devices
    )
    pair_grads[0], came_long = lax.optimization_barrier((pair_grads[0], came_long))
    came_short = swap(to_low(pick_block(pair_grads[0], other_at[0])), 1, devices)
    pair_own = jnp.concatenate(
        [
            pick_block(pair_grads[1], own_at[0]) + pick_block(pair_grads[0], own_at[0]),
            pick_block(pair_grads[1], own_at[1]),
        ],
        axis=1,
    )

    share = upstream.shape[1] // mp_count

    def columns(value, index):
        return lax.dynamic_slice_in_dim(value, index * share, share, 1)

    dense_came = [swap(columns(dense_rows[part], 1 - mp_index), 1, devices) for part in range(2)]
    pair_grads[0], *dense_came = lax.optimization_barrier((pair_grads[0], *dense_came))

    embedded_grad_low, token_grad = embed_backward(
        own_info, query_grad, pair_own, came_long, came_short, tables, grad_hidden, embedded,
        attention_gain, embed_full, query_weights, pair_weight,
    )
    own_out = []
    other_out = []
    for part in range(2):
        kept = columns(dense_rows[part], mp_index).astype(jnp.float32)
        arrived = dense_came[part].astype(jnp.float32)
        own_out.append(to_low(kept[:block] + arrived[block:]))
        other_out.append(to_low(kept[block:] + arrived[:block]))
    model_out = ordered_blocks(lead, own_out, other_out)
    embed_grad = to_low(matmul_first(chosen_own, embedded_grad_low))

    def give_back(turn, total):
        taker = taker_choice(own_rank, own_owner, turn, capacity, devices)
        leaving = matmul_first(taker, token_grad).astype(jnp.bfloat16)
        came = exchange(leaving)
        return total + matmul_first(sender_choice(present, standing, turn, capacity), came)

    embed_start = scatter_start(embed_grad, devices)
    grad_pooled = give_back(0, jnp.zeros(pooled.shape, jnp.float32))
    grad_pooled = lax.fori_loop(1, rounds, give_back, grad_pooled)

    back_order = [[bit] for bit in [1, 0] + far_bits[::-1]]
    embed_held = scatter_step(embed_start, back_order[0], me, devices)
    embed_held, grad_pooled = lax.optimization_barrier((embed_held, grad_pooled))
    embed_held = scatter_step(embed_held, back_order[1], me, devices)
    hidden_grad, attended_grad, wide_grad, reduce_grad, later_norms = units_backward(
        grad_pooled, hyper_hidden, hyper_attended, wide_weight, reduce_weight, norm_rows
    )
    hidden_grad, embed_held = lax.optimization_barrier((hidden_grad, embed_held))
    held = [embed_held, scatter_start(wide_grad, devices), scatter_start(reduce_grad, devices)]
    turned_order = [back_order[0], back_order[2], back_order[1]] + back_order[3:]
    orders = [back_order[2:], back_order, turned_order]

    def depart(at):
        return [
            scatter_send(x, order[at], me, devices) if at < len(order) else (x, [])
            for x, order in zip(held, orders)
        ]

    def arrive(moving):
        return [scatter_add(*x) for x in moving]

    slots_saved = (pieces, slot_mixed, slot_probs)
    slots_held = (None, None, later_norms)
    for part in range(SLOT_PARTS):
        moving = depart(part)
        slots_held = slot_backward(
            part, SLOT_PARTS, slots_held, slots_saved, (attended_grad, hidden_grad), in_weight, norm_rows
        )
        slots_held, moving = lax.optimization_barrier((tuple(slots_held), moving))
        held = arrive(moving)
    pieces_grad, input_grad, _ = slots_held
    input_held = scatter_start(input_grad, devices)
    for at, step in enumerate(back_order):
        moving = depart(SLOT_PARTS + at)
        input_held = scatter_step(input_held, step, me, devices)
        _, moving = lax.optimization_barrier((input_held, moving))
        held = arrive(moving)
    embed_own, wide_own, reduce_own, input_own = [scatter_end(x) for x in (*held, input_held)]
    out_width = hyper_output.shape[1]
    return (
        model_out,
        pieces_grad,
        input_own[:, :in_width],
        wide_own[:, :out_width],
        wide_own[:, out_width:],
        reduce_own,
        input_own[:, in_width : in_width + norm_count],
        embed_own,
    )


def solution(mesh):
    return jax.shard_map(
        body,
        mesh=mesh,
        in_specs=(
            P(("dp", "mp"), None, None),
            P(("dp", "mp")),
            P("dp"),
            P(("dp", "mp"), None),
            P(("dp", "mp"), None),
            P(("dp", "mp"), None),
            P(("dp", "mp"), None),
            P(("dp", "mp"), None),
            P(("dp", "mp"), None),
            P(),
            P(),
            P(None, "mp"),
            P(None, "mp"),
            P(None, "mp"),
            P("mp", None),
            P(None, "mp"),
            P(None, "mp"),
            P("mp", None),
            P("dp", None),
        ),
        out_specs=(
            P("dp", "mp"),
            P(("dp", "mp"), None, None),
            P(("dp", "mp"), None),
            P(("dp", "mp"), None),
            P(("dp", "mp"), None),
            P(("dp", "mp"), None),
            P(("dp", "mp"), None),
            P(("dp", "mp"), None),
        ),
        check_vma=False,
    )
```

```python
import functools

import jax
import jax.numpy as jnp
import numpy as np
from jax import lax
from jax.experimental import pallas as pl
from jax.experimental.pallas import tpu as pltpu
from jax.sharding import PartitionSpec as P

HEAD_WIDTH = 64
HHD = 64
BLOCK_PARTS = 4
UNIT = 512
PAIR = 2 * HEAD_WIDTH
VMEM_LIMIT = 48 << 20
ENTRY_BLOCK = 64
SLOT_PARTS = 2
UNIT_STEP = 256
COLUMN_STEP = 256
UNIT_ROWS = 256


EPS = 1e-05
NEGATIVE = -1000000000.0


def matmul(left, right):
    return jnp.dot(left, right, preferred_element_type=jnp.float32)


def matmul_first(left, right):
    return lax.dot_general(
        left, right, (((0,), (0,)), ((), ())), preferred_element_type=jnp.float32
    )


def matmul_last(left, right):
    return lax.dot_general(
        left, right, (((1,), (1,)), ((), ())), preferred_element_type=jnp.float32
    )


def log2_of(number):
    return number.bit_length() - 1


def swap(value, mask, devices):
    return lax.ppermute(value, ("dp", "mp"), [(d, d ^ mask) for d in range(devices)])


def gather_join(held, arrived, bit, done, me):
    rows, width = held.shape
    outer = 1 << sum(other > bit for other in done)
    held, arrived = [x.reshape(outer, rows // outer, width) for x in (held, arrived)]
    joined = jnp.where(
        ((me >> bit) & 1) == 1,
        jnp.concatenate([arrived, held], axis=1),
        jnp.concatenate([held, arrived], axis=1),
    )
    return joined.reshape(2 * rows, width)


def scatter_send(held, bit, left, me, devices):
    rows, width = held.shape
    outer = 1 << sum(other > bit for other in left)
    parts = held.reshape(outer, 2, rows // outer // 2, width)
    mine = (me >> bit) & 1

    def part(at):
        return lax.dynamic_slice_in_dim(parts, at, 1, 1).reshape(rows // 2, width)

    return (part(mine), swap(to_low(part(1 - mine)), 1 << bit, devices))


def scatter_add(staying, came):
    return staying.astype(jnp.float32) + came.astype(jnp.float32)


def lanes(shape):
    return lax.broadcasted_iota(jnp.int32, shape, len(shape) - 1)


def half_swap(value):
    quarter = HEAD_WIDTH // 2
    upper = (lanes(value.shape) & quarter) != 0
    return jnp.where(
        upper, pltpu.roll(value, quarter, 1), pltpu.roll(value, PAIR - quarter, 1)
    )


def to_low(value):
    return value.astype(jnp.bfloat16)


def causal_of(rows):
    return lax.broadcasted_iota(jnp.int32, (rows, rows), 0) <= lax.broadcasted_iota(
        jnp.int32, (rows, rows), 1
    )


def masked_scores(keys, low, causal):
    rows = causal.shape[0]
    length = keys.shape[0]
    last = jnp.where(causal, matmul_last(keys[length - rows :, :], low), NEGATIVE)
    return [matmul_last(keys[: length - rows, :], low), last] if length > rows else [last]


def for_lengths(block_at, rows, length, work):
    for count in (length - rows, length):
        pl.when(block_at == count // rows - 1)(functools.partial(work, count))


def turn_left(value, cosine, sine):
    left = lanes(value.shape) < HEAD_WIDTH
    return jnp.where(left, value * cosine + half_swap(value) * sine, value)


def head_views(pair_ref, cos_ref, sin_ref, rows):
    span = slice(0, rows)
    turned = to_low(turn_left(pair_ref[span, :], cos_ref[span, :], sin_ref[span, :])).astype(jnp.float32)
    other = pltpu.roll(turned, HEAD_WIDTH, 1)
    left = lanes(turned.shape) < HEAD_WIDTH
    return (
        jnp.where(left, turned, 0.0),
        jnp.where(left, 0.0, other),
        jnp.where(left, other, 0.0),
        jnp.where(left, 0.0, turned),
    )


def attention_forward_kernel(
    info, query_ref, pair_ref, cos_pair, sin_pair, cos_ref, sin_ref,
    out_ref, low_ref, lse_ref, even, odd, across,
):
    rows = query_ref.shape[0]
    causal = causal_of(rows)

    def work(length):
        span = slice(0, length)
        key_left, key_right, value_left, _ = head_views(pair_ref, cos_pair, sin_pair, length)
        even[span, :] = to_low(key_left)
        odd[span, :] = to_low(key_right)
        across[:, span] = to_low(value_left.T[:HEAD_WIDTH])
        for pair in range(query_ref.shape[1] // PAIR):
            columns = slice(pair * PAIR, (pair + 1) * PAIR)
            query = query_ref[:, columns]
            turned = to_low(query * cos_ref[...] + half_swap(query) * sin_ref[...])
            low = to_low(turned.astype(jnp.float32) * HEAD_WIDTH ** (-0.5))
            low_ref[:, columns] = low
            outs = []
            for at, keys in enumerate((even, odd)):
                scores = masked_scores(keys[span, :], low, causal)
                highest = functools.reduce(
                    jnp.maximum, [jnp.max(x, axis=0, keepdims=True) for x in scores]
                )
                weights = [jnp.exp(x - highest) for x in scores]
                total = sum(jnp.sum(x, axis=0, keepdims=True) for x in weights)
                out = 0.0
                start = 0
                for x in weights:
                    out = out + matmul(across[:, start : start + x.shape[0]], to_low(x))
                    start += x.shape[0]
                outs.append(out / total)
                lse_ref[0, 2 * pair + at : 2 * pair + at + 1, :] = highest + jnp.log(total)
            out_ref[:, columns] = to_low(jnp.concatenate(outs, axis=0).T)

    for_lengths(info[0], rows, pair_ref.shape[0], work)


def attention_backward_kernel(
    info, low_ref, grad_ref, lse_ref, pair_ref, cos_pair, sin_pair, cos_ref, sin_ref, *refs,
):
    query_ref, pair_grad_ref, even, odd, value_even, value_odd, across = refs[-11:-4]
    key_even, key_odd, sum_even, sum_odd = refs[-4:]
    rows = low_ref.shape[0]
    causal = causal_of(rows)

    def work(length):
        span = slice(0, length)
        key_left, key_right, value_left, value_right = head_views(pair_ref, cos_pair, sin_pair, length)
        even[span, :] = to_low(key_left)
        odd[span, :] = to_low(key_right)
        value_even[span, :] = to_low(value_left)
        value_odd[span, :] = to_low(value_right)
        across[:, span] = to_low(key_left.T[:HEAD_WIDTH])
        sides = ((even, value_even, key_even, sum_even), (odd, value_odd, key_odd, sum_odd))
        for total in (key_even, key_odd, sum_even, sum_odd):
            total[span, :] = jnp.zeros((length, PAIR), jnp.float32)
        for pair in range(low_ref.shape[1] // PAIR):
            columns = slice(pair * PAIR, (pair + 1) * PAIR)
            low = low_ref[:, columns]
            grad = grad_ref[:, columns]
            outs = []
            for at, (keys, values, key_total, value_total) in enumerate(sides):
                lse = lse_ref[0, 2 * pair + at : 2 * pair + at + 1, :]
                probs = [jnp.exp(x - lse) for x in masked_scores(keys[span, :], low, causal)]
                moved = []
                start = 0
                for x in probs:
                    part = slice(start, start + x.shape[0])
                    value_total[part, :] += matmul(to_low(x), grad)
                    moved.append(x * matmul_last(values[part, :], grad))
                    start += x.shape[0]
                mean = sum(jnp.sum(x, axis=0, keepdims=True) for x in moved)
                out = 0.0
                start = 0
                for x, y in zip(probs, moved):
                    part = slice(start, start + x.shape[0])
                    grad_scores = to_low(y - x * mean)
                    key_total[part, :] += matmul(grad_scores, low)
                    out = out + matmul(across[:, part], grad_scores)
                    start += x.shape[0]
                outs.append(out)
            turned = jnp.concatenate(outs, axis=0).T * HEAD_WIDTH ** (-0.5)
            query_ref[:, columns] = to_low(turned * cos_ref[...] - half_swap(turned) * sin_ref[...])
        left = lanes((length, PAIR)) < HEAD_WIDTH
        pair_grad_ref[0, span, :] = jnp.where(
            left,
            key_even[span, :] + pltpu.roll(key_odd[span, :], HEAD_WIDTH, 1),
            pltpu.roll(sum_even[span, :], HEAD_WIDTH, 1) + sum_odd[span, :],
        )
        if length < pair_ref.shape[0]:
            rest = (pair_ref.shape[0] - length, PAIR)
            pair_grad_ref[0, length:, :] = jnp.zeros(rest, jnp.float32)

    for_lengths(info[0], rows, pair_ref.shape[0], work)


def attention_specs(part, rows, length):
    span = (rows, 4 * PAIR)
    return {
        "table_pair": pl.BlockSpec((length, PAIR), lambda g, s: (0, 0)),
        "table": pl.BlockSpec((rows, PAIR), lambda g, s: (s[0], 0)),
        "pair": pl.BlockSpec((length, PAIR), lambda g, s: (0, g)),
        "part": pl.BlockSpec(span, lambda g, s: (part, g)),
        "wide": pl.BlockSpec(span, lambda g, s: (0, g)),
        "sums": pl.BlockSpec((1, 8, rows), lambda g, s: (g, 0, 0)),
    }


def attention_cost(rows, length, heads, matmuls):
    work = 20 * rows * length * heads * HEAD_WIDTH * matmuls
    return pl.CostEstimate(
        flops=work, bytes_accessed=16 * rows * heads * HEAD_WIDTH, transcendentals=rows * length * heads
    )


def attention_forward(info, queries, pair_pre, tables, part, length):
    cosine, sine = tables
    rows = cosine.shape[0] // BLOCK_PARTS
    heads = 4 * 4 * PAIR // HEAD_WIDTH
    spec = attention_specs(part, rows, length)
    half = pltpu.VMEM((length, PAIR), jnp.bfloat16)
    wide = (rows, heads * HEAD_WIDTH)
    return pl.pallas_call(
        attention_forward_kernel,
        grid_spec=pltpu.PrefetchScalarGridSpec(
            num_scalar_prefetch=1,
            grid=(4,),
            in_specs=[
                spec["part"], spec["pair"],
                spec["table_pair"], spec["table_pair"], spec["table"], spec["table"],
            ],
            out_specs=[spec["wide"], spec["wide"], spec["sums"]],
            scratch_shapes=[
                half, half,
                pltpu.VMEM((HEAD_WIDTH, length), jnp.bfloat16),
            ],
        ),
        out_shape=[
            jax.ShapeDtypeStruct(wide, jnp.bfloat16),
            jax.ShapeDtypeStruct(wide, jnp.bfloat16),
            jax.ShapeDtypeStruct((4, 8, rows), jnp.float32),
        ],
        compiler_params=pltpu.CompilerParams(
            dimension_semantics=("arbitrary",), vmem_limit_bytes=VMEM_LIMIT
        ),
        cost_estimate=attention_cost(rows, length, heads, 2),
        name="attention_forward",
    )(info, queries, pair_pre, cosine, sine, cosine, sine)


def attention_backward(info, low, grad, sums, pair_pre, tables, part, length, before):
    cosine, sine = tables
    rows = cosine.shape[0] // BLOCK_PARTS
    heads = low.shape[1] // HEAD_WIDTH
    spec = attention_specs(part, rows, length)
    before = [] if before is None else [before]
    half = pltpu.VMEM((length, PAIR), jnp.bfloat16)
    full = pltpu.VMEM((length, PAIR), jnp.float32)
    return pl.pallas_call(
        attention_backward_kernel,
        grid_spec=pltpu.PrefetchScalarGridSpec(
            num_scalar_prefetch=1,
            grid=(4,),
            in_specs=[
                spec["wide"], spec["wide"], spec["sums"], spec["pair"],
                spec["table_pair"], spec["table_pair"], spec["table"], spec["table"],
            ]
            + [pl.BlockSpec(memory_space=pl.ANY)] * len(before),
            out_specs=[spec["part"], pl.BlockSpec((1, length, PAIR), lambda g, s: (s[1 + g], 0, 0))],
            scratch_shapes=[
                half, half, half, half,
                pltpu.VMEM((HEAD_WIDTH, length), jnp.bfloat16),
                full, full, full, full,
            ],
        ),
        out_shape=[
            jax.ShapeDtypeStruct((2 * rows, low.shape[1]), jnp.bfloat16),
            jax.ShapeDtypeStruct((4, length, PAIR), jnp.float32),
        ],
        input_output_aliases={9: 0} if before else {},
        compiler_params=pltpu.CompilerParams(
            dimension_semantics=("arbitrary",), vmem_limit_bytes=VMEM_LIMIT
        ),
        cost_estimate=attention_cost(rows, length, heads, 5),
        name="attention_backward",
    )(info, low, grad, sums, pair_pre, cosine, sine, cosine, sine, *before)


def rope_tables(length):
    positions = np.arange(length, dtype=np.float32)
    inverse = 10000.0 ** (-np.arange(0, HEAD_WIDTH, 2, dtype=np.float32) / HEAD_WIDTH)
    angles = positions[:, None] * inverse.astype(np.float32)[None, :]
    cosine, sine = np.cos(angles).astype(np.float32), np.sin(angles).astype(np.float32)
    return (
        jnp.asarray(np.concatenate([cosine] * 4, axis=1)),
        jnp.asarray(np.concatenate([-sine, sine, -sine, sine], axis=1)),
    )


def head_marks(width, transposed):
    shape = (PAIR, width) if transposed else (width, PAIR)
    head_at, column_at = (0, 1) if transposed else (1, 0)
    head = lax.broadcasted_iota(jnp.int32, shape, head_at)
    column = lax.broadcasted_iota(jnp.int32, shape, column_at)
    return (column // HHD == head).astype(jnp.bfloat16)


def head_sums(value, marks):
    high = to_low(value)
    rest = to_low(value - high.astype(jnp.float32))
    return matmul(high, marks) + matmul(rest, marks)


def normalize(value):
    centered = value - jnp.mean(value, axis=-1, keepdims=True)
    inverse = lax.rsqrt(jnp.mean(centered * centered, axis=-1, keepdims=True) + EPS)
    return (centered * inverse, inverse)


def norm_back(grad, gain, hat, inverse):
    scaled = grad * gain
    mean = jnp.mean(scaled, axis=-1, keepdims=True)
    along = jnp.mean(scaled * hat, axis=-1, keepdims=True)
    return inverse * (scaled - mean - hat * along)


def slot_attention_kernel(
    pieces_ref, counts_ref, weight_ref, norm_ref, mixed_ref, probs_ref, attended_ref, lead_ref
):
    entries, slots, width = pieces_ref.shape
    rows = entries * slots
    tall = (entries, slots, width)
    pieces = pieces_ref[...].astype(jnp.float32)
    hat, _ = normalize(pieces.reshape(rows, width))
    low = to_low(hat * norm_ref[0:1, :] + norm_ref[1:2, :])
    mixed = []
    for part in range(3):
        span = slice(part * width, (part + 1) * width)
        value = to_low(matmul(low, weight_ref[:, span]))
        mixed_ref[:, span] = value
        mixed.append(value.astype(jnp.float32).reshape(tall))
    query, keys, values = mixed
    marks = head_marks(width, False)
    product = (keys * query[:, 0:1, :]).reshape(rows, width)
    scores = head_sums(product, marks).reshape(entries, slots, PAIR) * HHD ** (-0.5)
    live = lax.broadcasted_iota(jnp.int32, scores.shape, 1) < counts_ref[...]
    scores = jnp.where(live, scores, NEGATIVE)
    weight = jnp.exp(scores - jnp.max(scores, axis=1, keepdims=True))
    probs = weight / jnp.sum(weight, axis=1, keepdims=True)
    probs_ref[...] = probs
    spread = matmul(to_low(probs.reshape(rows, PAIR)), head_marks(width, True)).reshape(tall)
    attended_ref[...] = to_low(jnp.sum(spread * values, axis=1))
    lead_ref[...] = pieces[:, 0, :]


def slot_attention(pieces, counts, in_weight, norm_rows):
    entries, slots, width = pieces.shape
    part = min(ENTRY_BLOCK, entries)
    whole = lambda shape: pl.BlockSpec(shape, lambda i: (0,) * len(shape))
    tall = pl.BlockSpec((part, slots, width), lambda i: (i, 0, 0))
    flat = pl.BlockSpec((part, width), lambda i: (i, 0))
    return pl.pallas_call(
        slot_attention_kernel,
        grid=(entries // part,),
        in_specs=[
            tall,
            pl.BlockSpec((part, 1, PAIR), lambda i: (i, 0, 0)),
            whole(in_weight.shape),
            whole(norm_rows.shape),
        ],
        out_specs=[
            pl.BlockSpec((part * slots, 3 * width), lambda i: (i, 0)),
            pl.BlockSpec((part, slots, PAIR), lambda i: (i, 0, 0)),
            flat,
            flat,
        ],
        out_shape=[
            jax.ShapeDtypeStruct((entries * slots, 3 * width), jnp.bfloat16),
            jax.ShapeDtypeStruct((entries, slots, PAIR), jnp.float32),
            jax.ShapeDtypeStruct((entries, width), jnp.bfloat16),
            jax.ShapeDtypeStruct((entries, width), jnp.float32),
        ],
        compiler_params=pltpu.CompilerParams(
            dimension_semantics=("arbitrary",), vmem_limit_bytes=VMEM_LIMIT
        ),
        cost_estimate=pl.CostEstimate(
            flops=entries * slots * width, bytes_accessed=entries * slots, transcendentals=0
        ),
        name="slot_attention",
    )(pieces, counts, in_weight, norm_rows)


def gelu_of(value):
    cdf = 0.5 * (1.0 + lax.erf(value * np.float32(0.5 ** 0.5)))
    return (value * cdf, cdf)


def gelu_slope(value, cdf):
    return cdf + value * (jnp.exp(-0.5 * value * value) * np.float32((2 * np.pi) ** -0.5))


def units_forward_kernel(
    split, places, attended_ref, lead_ref, *refs
):
    *weights, norm_ref, pooled_ref, hidden_ref = refs[: 11 if split else 5]
    if not split:
        wide_weight_ref, reduce_ref = weights
    else:
        wide_weight_ref, reduce_ref = refs[11:]

        @pl.when(pl.program_id(0) == 0)
        def join():
            core = places[0]
            for whole, parts in ((wide_weight_ref, weights[:4]), (reduce_ref, weights[4:])):
                rows = parts[0].shape[0] // split
                for at, part in enumerate(parts):
                    side = places[1] if at % 2 == 0 else 1 - places[1]
                    place = 2 * side + (core if at < 2 else 1 - core)
                    for group in range(split):
                        start = pl.multiple_of((4 * group + place) * rows, rows)
                        whole[pl.ds(start, rows), :] = part[group * rows : (group + 1) * rows, :]

    width = lead_ref.shape[1]
    hidden = lead_ref[...] + matmul(attended_ref[...], wide_weight_ref[:, :width])
    hidden_ref[...] = hidden
    hat, _ = normalize(hidden)
    second = to_low(hat * norm_ref[2:3, :] + norm_ref[3:4, :])
    total = hidden
    units = reduce_ref.shape[0]
    step = min(UNIT, units)
    for at in range(0, units, step):
        active, _ = gelu_of(matmul(second, wide_weight_ref[:, width + at : width + at + step]))
        total = total + matmul(to_low(active), reduce_ref[at : at + step, :])
    pooled_ref[...] = to_low(total)


def units_forward(groups, places, attended, lead, wide_weight, reduce_weight, norm_rows):
    entries, width = attended.shape
    part = min(UNIT_ROWS, entries)
    split = groups if len(wide_weight) == 4 else 0
    whole = lambda shape: pl.BlockSpec(shape, lambda i, s: (0,) * len(shape))
    flat = pl.BlockSpec((part, width), lambda i, s: (i, 0))
    weights = [*wide_weight, *reduce_weight]
    joined = [
        pltpu.VMEM((4 * parts[0].shape[0], parts[0].shape[1]), jnp.bfloat16)
        for parts in (wide_weight, reduce_weight)
    ]
    return pl.pallas_call(
        functools.partial(units_forward_kernel, split),
        grid_spec=pltpu.PrefetchScalarGridSpec(
            num_scalar_prefetch=1,
            grid=(entries // part,),
            in_specs=[flat, flat] + [whole(x.shape) for x in (*weights, norm_rows)],
            out_specs=[flat, flat],
            scratch_shapes=joined if split else [],
        ),
        out_shape=[
            jax.ShapeDtypeStruct((entries, width), jnp.bfloat16),
            jax.ShapeDtypeStruct((entries, width), jnp.float32),
        ],
        compiler_params=pltpu.CompilerParams(
            dimension_semantics=("arbitrary",), vmem_limit_bytes=VMEM_LIMIT
        ),
        cost_estimate=pl.CostEstimate(
            flops=entries * width, bytes_accessed=entries * width, transcendentals=0
        ),
        name="units_forward",
    )(places.astype(jnp.int32), attended, lead, *weights, norm_rows)


def units_backward_kernel(
    grad_ref, hidden_ref, attended_ref, wide_weight_ref, reduce_ref, norm_ref,
    hidden_grad_ref, attended_grad_ref, wide_ref, reduce_grad_ref, norm_grad_ref,
    wide_total, reduce_total,
):
    step_at = pl.program_id(0)
    width = hidden_ref.shape[1]
    units = reduce_ref.shape[0]

    @pl.when(step_at == 0)
    def start():
        wide_total[...] = jnp.zeros_like(wide_total)
        reduce_total[...] = jnp.zeros_like(reduce_total)
        norm_grad_ref[...] = jnp.zeros_like(norm_grad_ref)

    grad = grad_ref[...]
    grad_low = to_low(grad)
    hat, inverse = normalize(hidden_ref[...])
    second = to_low(hat * norm_ref[2:3, :] + norm_ref[3:4, :])
    grad_normed = jnp.zeros_like(grad)
    step = min(UNIT, units)
    for at in range(0, units, step):
        span = slice(at, at + step)
        wide_span = slice(width + at, width + at + step)
        expanded = matmul(second, wide_weight_ref[:, wide_span])
        active, cdf = gelu_of(expanded)
        reduce_total[span, :] += matmul_first(to_low(active), grad_low)
        grad_active = matmul_last(grad_low, reduce_ref[span, :])
        grad_expanded = to_low(grad_active * gelu_slope(expanded, cdf))
        wide_total[:, wide_span] += matmul_first(second, grad_expanded)
        grad_normed = grad_normed + matmul_last(grad_expanded, wide_weight_ref[:, wide_span])
    norm_grad_ref[2:3, :] += jnp.sum(grad_normed * hat, axis=0, keepdims=True)
    norm_grad_ref[3:4, :] += jnp.sum(grad_normed, axis=0, keepdims=True)
    hidden_grad = grad + norm_back(grad_normed, norm_ref[2:3, :], hat, inverse)
    hidden_grad_ref[...] = hidden_grad
    hidden_low = to_low(hidden_grad)
    wide_total[:, :width] += matmul_first(attended_ref[...], hidden_low)
    attended_grad_ref[...] = to_low(matmul_last(hidden_low, wide_weight_ref[:, :width]))

    @pl.when(step_at == pl.num_programs(0) - 1)
    def finish():
        wide_ref[...] = to_low(wide_total[...])
        reduce_grad_ref[...] = to_low(reduce_total[...])


def units_backward(grad, hidden, attended, wide_weight, reduce_weight, norm_rows):
    entries, width = attended.shape
    part = min(UNIT_ROWS, entries)
    units = reduce_weight.shape[0]
    whole = lambda shape: pl.BlockSpec(shape, lambda i: (0,) * len(shape))
    flat = pl.BlockSpec((part, width), lambda i: (i, 0))
    wide = (width, width + units)
    return pl.pallas_call(
        units_backward_kernel,
        grid=(entries // part,),
        in_specs=[flat, flat, flat]
        + [whole(x.shape) for x in (wide_weight, reduce_weight, norm_rows)],
        out_specs=[flat, flat, whole(wide), whole((units, width)), whole((8, width))],
        out_shape=[
            jax.ShapeDtypeStruct((entries, width), jnp.float32),
            jax.ShapeDtypeStruct((entries, width), jnp.bfloat16),
            jax.ShapeDtypeStruct(wide, jnp.bfloat16),
            jax.ShapeDtypeStruct((units, width), jnp.bfloat16),
            jax.ShapeDtypeStruct((8, width), jnp.float32),
        ],
        scratch_shapes=[pltpu.VMEM(wide, jnp.float32), pltpu.VMEM((units, width), jnp.float32)],
        compiler_params=pltpu.CompilerParams(
            dimension_semantics=("arbitrary",), vmem_limit_bytes=VMEM_LIMIT
        ),
        cost_estimate=pl.CostEstimate(
            flops=6 * entries * width * (2 * width + 5 * units), bytes_accessed=16 << 20, transcendentals=0
        ),
        name="units_backward",
    )(grad, hidden, attended, wide_weight, reduce_weight, norm_rows)


def slot_backward_kernel(
    first, last, pieces_ref, mixed_ref, probs_ref, attended_grad_ref, hidden_grad_ref, weight_ref, norm_ref,
    later_ref, *refs,
):
    if first:
        pieces_grad_ref, input_grad_ref, norm_grad_ref, total, norm_total = refs
    else:
        _, total_ref, pieces_grad_ref, input_grad_ref, norm_grad_ref, total, norm_total = refs
    step_at = pl.program_id(0)
    entries, slots, width = pieces_ref.shape
    rows = entries * slots
    tall = (entries, slots, width)

    @pl.when(step_at == 0)
    def start():
        norm_total[...] = jnp.zeros_like(norm_total)
        norm_total[0:8, :] = later_ref[...]
        total[...] = jnp.zeros_like(total) if first else total_ref[...]

    hat, inverse = normalize(pieces_ref[...].astype(jnp.float32).reshape(rows, width))
    low = to_low(hat * norm_ref[0:1, :] + norm_ref[1:2, :])
    scale = HHD ** (-0.5)
    query, keys, values = [
        mixed_ref[:, part * width : (part + 1) * width].astype(jnp.float32).reshape(tall) for part in range(3)
    ]
    probs = probs_ref[...]
    grad_attended = jnp.broadcast_to(attended_grad_ref[...].astype(jnp.float32)[:, None, :], tall)
    grad_probs = head_sums((grad_attended * values).reshape(rows, width), head_marks(width, False))
    moved = probs * grad_probs.reshape(probs.shape)
    grad_scores = to_low(moved - probs * jnp.sum(moved, axis=1, keepdims=True))
    marks = head_marks(width, True)
    spread = matmul(grad_scores.reshape(rows, PAIR), marks).reshape(tall) * scale
    first_slot = lax.broadcasted_iota(jnp.int32, tall, 1) == 0
    grad_query = jnp.where(first_slot, jnp.sum(spread * keys, axis=1, keepdims=True), 0.0)
    grad_keys = spread * query[:, 0:1, :]
    grad_values = matmul(to_low(probs.reshape(rows, PAIR)), marks).reshape(tall) * grad_attended
    grad_normed = jnp.zeros((rows, width), jnp.float32)
    for part, grad in enumerate((grad_query, grad_keys, grad_values)):
        span = slice(part * width, (part + 1) * width)
        grad_low = to_low(grad.reshape(rows, width))
        total[:, span] += matmul_first(low, grad_low)
        grad_normed = grad_normed + matmul_last(grad_low, weight_ref[:, span])
    norm_total[0:1, :] += jnp.sum(grad_normed * hat, axis=0, keepdims=True)
    norm_total[1:2, :] += jnp.sum(grad_normed, axis=0, keepdims=True)
    grad_pieces = norm_back(grad_normed, norm_ref[0:1, :], hat, inverse).reshape(tall)
    hidden_grad = jnp.broadcast_to(hidden_grad_ref[...][:, None, :], tall)
    pieces_grad_ref[...] = to_low(grad_pieces + jnp.where(first_slot, hidden_grad, 0.0))

    @pl.when(step_at == pl.num_programs(0) - 1)
    def finish():
        norm_grad_ref[...] = norm_total[0:8, :]
        if last:
            input_grad_ref[:, : 3 * width] = to_low(total[...])
            input_grad_ref[:, 3 * width :] = to_low(norm_total[...].T)
        else:
            input_grad_ref[...] = total[...]


def slot_backward(at, parts, held, saved, grads, in_weight, norm_rows):
    pieces, mixed, probs = saved
    pieces_grad, total, norm_grad = held
    entries, slots, width = pieces.shape
    first, last = at == 0, at == parts - 1
    part = min(ENTRY_BLOCK, entries // parts)
    steps = entries // parts // part
    whole = lambda shape: pl.BlockSpec(shape, lambda i: (0,) * len(shape))
    tall = pl.BlockSpec((part, slots, width), lambda i: (i + at * steps, 0, 0))
    flat = pl.BlockSpec((part, width), lambda i: (i + at * steps, 0))
    total_shape = (
        jax.ShapeDtypeStruct((width, 3 * width + PAIR), jnp.bfloat16)
        if last
        else jax.ShapeDtypeStruct((width, 3 * width), jnp.float32)
    )
    in_specs = [
        tall,
        pl.BlockSpec((part * slots, 3 * width), lambda i: (i + at * steps, 0)),
        pl.BlockSpec((part, slots, PAIR), lambda i: (i + at * steps, 0, 0)),
        flat,
        flat,
        whole(in_weight.shape),
        whole(norm_rows.shape),
        whole(norm_grad.shape),
    ]
    operands = [pieces, mixed, probs, *grads, in_weight, norm_rows, norm_grad]
    if not first:
        in_specs += [pl.BlockSpec(memory_space=pl.ANY), whole(total.shape)]
        operands += [pieces_grad, total]
    return pl.pallas_call(
        functools.partial(slot_backward_kernel, first, last),
        grid=(steps,),
        in_specs=in_specs,
        out_specs=[tall, whole(total_shape.shape), whole(norm_grad.shape)],
        out_shape=[
            jax.ShapeDtypeStruct(pieces.shape, jnp.bfloat16),
            total_shape,
            jax.ShapeDtypeStruct(norm_grad.shape, jnp.float32),
        ],
        input_output_aliases={} if first else {len(operands) - 2: 0},
        scratch_shapes=[
            pltpu.VMEM((width, 3 * width), jnp.float32),
            pltpu.VMEM((PAIR, width), jnp.float32),
        ],
        compiler_params=pltpu.CompilerParams(
            dimension_semantics=("arbitrary",), vmem_limit_bytes=VMEM_LIMIT
        ),
        cost_estimate=pl.CostEstimate(
            flops=entries * slots * width // parts,
            bytes_accessed=entries * slots // parts,
            transcendentals=0,
        ),
        name="slot_backward",
    )(*operands)


def feed_forward_kernel(
    rows_ref, other_ref, rise_ref, rise_other_ref, hidden_ref, gate_ref, up_ref, down_ref,
    gate_rows, up_rows, down_columns, grad_ref, dense_ref, rows, rise, active, grad_gate, grad_up,
):
    at = pl.program_id(0)
    half = rows_ref.shape[0]
    step = gate_ref.shape[1]
    tiles = active.shape[1] // step

    @pl.when(at == 0)
    def start():
        rows[:half, :] = rows_ref[...]
        rows[half:, :] = other_ref[...]
        rise[:half, :] = rise_ref[...]
        rise[half:, :] = rise_other_ref[...]

    @pl.when(at < tiles)
    def units():
        gate = matmul(rows[...], gate_ref[...])
        up = matmul(rows[...], up_ref[...])
        rising = matmul_last(rise[...], down_ref[...])
        sign = 1.0 / (1.0 + jnp.exp(-gate))
        silu = gate * sign
        span = pl.ds(pl.multiple_of(at * step, step), step)
        active[:, span] = to_low(silu * up)
        grad_up[:, span] = to_low(rising * silu)
        grad_gate[:, span] = to_low(rising * up * (sign * (1.0 + gate * (1.0 - sign))))

    @pl.when(at >= tiles)
    def columns():
        dense = matmul(active[...], down_columns[...])
        grad = matmul_last(grad_gate[...], gate_rows[...]) + matmul_last(grad_up[...], up_rows[...])
        grad_ref[...] = to_low(grad)
        dense_ref[:half, :] = to_low(dense[:half] + hidden_ref[...])
        dense_ref[half:, :] = to_low(dense[half:])


def feed_forward(rows, other, upstream, hidden, info, gate_weight, up_weight, down_weight):
    half, width = rows.shape
    units = gate_weight.shape[1]
    step = UNIT_STEP
    tiles = units // step
    column = COLUMN_STEP
    fixed_rows = pl.BlockSpec((half, width), lambda i, s: (0, 0), pipeline_mode=pl.Buffered(1))
    early = lambda i: jnp.minimum(i, tiles - 1)
    late = lambda i: jnp.maximum(i - tiles, 0)
    tall = (2 * half, width)
    out = pl.BlockSpec((2 * half, column), lambda i, s: (0, late(i)))
    return pl.pallas_call(
        lambda info, *refs: feed_forward_kernel(*refs),
        grid_spec=pltpu.PrefetchScalarGridSpec(
            num_scalar_prefetch=1,
            grid=(tiles + width // column,),
            in_specs=[
                fixed_rows,
                fixed_rows,
                pl.BlockSpec((half, width), lambda i, s: (s[0], 0), pipeline_mode=pl.Buffered(1)),
                pl.BlockSpec((half, width), lambda i, s: (s[1], 0), pipeline_mode=pl.Buffered(1)),
                pl.BlockSpec((half, column), lambda i, s: (0, late(i))),
                pl.BlockSpec((width, step), lambda i, s: (0, early(i))),
                pl.BlockSpec((width, step), lambda i, s: (0, early(i))),
                pl.BlockSpec((step, width), lambda i, s: (early(i), 0)),
                pl.BlockSpec((column, units), lambda i, s: (late(i), 0)),
                pl.BlockSpec((column, units), lambda i, s: (late(i), 0)),
                pl.BlockSpec((units, column), lambda i, s: (0, late(i))),
            ],
            out_specs=[out, out],
            scratch_shapes=[
                pltpu.VMEM(tall, jnp.bfloat16),
                pltpu.VMEM(tall, jnp.bfloat16),
                *[pltpu.VMEM((2 * half, units), jnp.bfloat16)] * 3,
            ],
        ),
        out_shape=[jax.ShapeDtypeStruct(tall, jnp.bfloat16)] * 2,
        compiler_params=pltpu.CompilerParams(
            dimension_semantics=("arbitrary",), vmem_limit_bytes=VMEM_LIMIT
        ),
        cost_estimate=pl.CostEstimate(
            flops=34 * half * width * units, bytes_accessed=12 * width * units, transcendentals=0
        ),
        name="feed_forward",
    )(
        info, rows, other, upstream, upstream, hidden, gate_weight, up_weight, down_weight,
        gate_weight, up_weight, down_weight,
    )


def fixed(shape):
    return pl.BlockSpec(shape, lambda *_: (0,) * len(shape), pipeline_mode=pl.Buffered(1))


def root_mean(value):
    return lax.rsqrt(jnp.mean(value * value, axis=-1, keepdims=True) + EPS)


def root_mean_back(grad, gain, value):
    scaled = grad * gain
    inverse = root_mean(value)
    along = jnp.mean(value * scaled, axis=-1, keepdims=True)
    return inverse * scaled - value * (inverse * inverse * inverse * along)


def project_kernel(with_queries, info, chosen_ref, embed_ref, gain_ref, pair_own, pair_near, pair_far, *refs):
    embedded = to_low(matmul(chosen_ref[...], embed_ref[...]))
    value = embedded.astype(jnp.float32)
    low = to_low(value * root_mean(value) * gain_ref[...])
    pair_ref = refs[-3] if with_queries else refs[-1]
    at = 0
    for ref in (pair_own, pair_near, pair_far):
        pair_ref[:, at : at + ref.shape[1]] = matmul(low, ref[...])
        at += ref.shape[1]
    if not with_queries:
        return
    near_ref, mid_a, mid_b, far_a, far_b, _, embedded_ref, query_ref = refs
    embedded_ref[...] = embedded
    near = near_ref.shape[1]
    step = mid_a.shape[1]
    half = mid_a.shape[0]
    query_ref[:, :near] = matmul(low, near_ref[...])
    for start, upper, lower in ((near, mid_a, mid_b), (near + step, far_a, far_b)):
        query_ref[:, start : start + step] = matmul(low[:, :half], upper[...]) + matmul(
            low[:, half:], lower[...]
        )


def project(info, chosen, embed, gain, pair_weights, query_weights, pair_before):
    rows, width = chosen.shape
    block = rows // 2
    wide = embed.shape[1]
    row = pl.BlockSpec((block, wide), lambda i, s: (i, 0))
    pairs = sum(weight.shape[1] for weight in pair_weights)
    before = [] if pair_before is None else [pair_before]
    more = bool(query_weights)
    return pl.pallas_call(
        functools.partial(project_kernel, more),
        grid_spec=pltpu.PrefetchScalarGridSpec(
            num_scalar_prefetch=1,
            grid=(2,),
            in_specs=[
                pl.BlockSpec((block, width), lambda i, s: (i, 0)),
                fixed(embed.shape),
                fixed((1, wide)),
                *[fixed(weight.shape) for weight in pair_weights],
                *[fixed(weight.shape) for weight in query_weights],
                *[pl.BlockSpec(memory_space=pl.ANY)] * len(before),
            ],
            out_specs=[pl.BlockSpec((block, pairs), lambda i, s: (s[i], 0))] + [row, row] * more,
        ),
        out_shape=[jax.ShapeDtypeStruct((2 * rows, pairs), jnp.float32)]
        + [
            jax.ShapeDtypeStruct((rows, wide), jnp.bfloat16),
            jax.ShapeDtypeStruct((rows, wide), jnp.float32),
        ]
        * more,
        input_output_aliases={7: 0} if before else {},
        compiler_params=pltpu.CompilerParams(
            dimension_semantics=("arbitrary",), vmem_limit_bytes=VMEM_LIMIT
        ),
        cost_estimate=pl.CostEstimate(flops=1 << 30, bytes_accessed=1 << 20, transcendentals=0),
        name="project",
    )(info, chosen, embed, gain.reshape(1, -1), *pair_weights, *query_weights, *before)


def output_kernel(rows_ref, embedded_ref, gain_ref, near_ref, mid_a, mid_b, far_a, far_b, hidden_ref, low_ref):
    total = embedded_ref[...].astype(jnp.float32)
    at = 0
    for ref in (near_ref, mid_a, mid_b, far_a, far_b):
        total = total + matmul(rows_ref[:, at : at + ref.shape[0]], ref[...])
        at += ref.shape[0]
    hidden_ref[...] = total
    low_ref[...] = to_low(total * root_mean(total) * gain_ref[...])


def output_project(part, rows, embedded, gain, weights):
    block, wide = rows.shape
    spec = pl.BlockSpec((block, wide), lambda i: (0, 0))
    return pl.pallas_call(
        output_kernel,
        grid=(1,),
        in_specs=[
            spec,
            pl.BlockSpec((block, wide), lambda i: (part, 0)),
            fixed((1, wide)),
            *[fixed(weight.shape) for weight in weights],
        ],
        out_specs=[spec, spec],
        out_shape=[
            jax.ShapeDtypeStruct((block, wide), jnp.float32),
            jax.ShapeDtypeStruct((block, wide), jnp.bfloat16),
        ],
        compiler_params=pltpu.CompilerParams(
            dimension_semantics=("arbitrary",), vmem_limit_bytes=VMEM_LIMIT
        ),
        cost_estimate=pl.CostEstimate(flops=4 << 30, bytes_accessed=12 << 20, transcendentals=0),
        name="output_project",
    )(rows, embedded, gain.reshape(1, -1), *weights)


def hidden_backward_kernel(
    info, here_ref, came_ref, hidden_ref, rising_ref, gain_ref, near_ref, mid_a, mid_b, far_a, far_b,
    grad_ref, rows_ref,
):
    grad = here_ref[...].astype(jnp.float32) + came_ref[...].astype(jnp.float32)
    total = rising_ref[...].astype(jnp.float32) + root_mean_back(grad, gain_ref[...], hidden_ref[...])
    grad_ref[...] = total
    low = to_low(total)
    at = 0
    for ref in (near_ref, mid_a, mid_b, far_a, far_b):
        rows_ref[:, at : at + ref.shape[0]] = to_low(matmul_last(low, ref[...]))
        at += ref.shape[0]


def hidden_backward(info, here, came, hidden, upstream, gain, weights):
    block, wide = hidden.shape
    spec = pl.BlockSpec((block, wide), lambda i, s: (0, 0))
    return pl.pallas_call(
        hidden_backward_kernel,
        grid_spec=pltpu.PrefetchScalarGridSpec(
            num_scalar_prefetch=1,
            grid=(1,),
            in_specs=[
                spec,
                spec,
                spec,
                pl.BlockSpec((block, wide), lambda i, s: (s[0], 0)),
                fixed((1, wide)),
                *[fixed(weight.shape) for weight in weights],
            ],
            out_specs=[spec, spec],
        ),
        out_shape=[
            jax.ShapeDtypeStruct((block, wide), jnp.float32),
            jax.ShapeDtypeStruct((block, wide), jnp.bfloat16),
        ],
        compiler_params=pltpu.CompilerParams(
            dimension_semantics=("arbitrary",), vmem_limit_bytes=VMEM_LIMIT
        ),
        cost_estimate=pl.CostEstimate(flops=4 << 30, bytes_accessed=14 << 20, transcendentals=0),
        name="hidden_backward",
    )(info, here, came, hidden, upstream, gain.reshape(1, -1), *weights)


def embed_backward_kernel(
    info, query_ref, own_ref, came_ref, short_ref, cos_ref, sin_ref, first_ref, second_ref, embedded_ref, gain_ref,
    embed_ref, near_ref, mid_a, mid_b, far_a, far_b, pair_own, pair_near, pair_far, grad_ref, token_ref,
):
    total = None
    weights = [pair_own[:, :PAIR], pair_own[:, PAIR:], pair_near[...], pair_far[...]]
    for group, weight in enumerate(weights):
        head = info[2 + group]
        short = jnp.where(pl.program_id(0) == 0, short_ref[head].astype(jnp.float32), 0.0)
        pair = own_ref[head] + came_ref[head].astype(jnp.float32) + short
        low = to_low(turn_left(pair, cos_ref[...], -sin_ref[...]))
        term = matmul_last(low, weight)
        total = term if total is None else total + term
    near = near_ref.shape[1]
    step = mid_a.shape[1]
    half = mid_a.shape[0]
    total = total + matmul_last(query_ref[:, :near], near_ref[...])
    mid = query_ref[:, near : near + step]
    far = query_ref[:, near + step : near + 2 * step]
    spread = jnp.concatenate(
        [
            matmul_last(mid, mid_a[...]) + matmul_last(far, far_a[...]),
            matmul_last(mid, mid_b[...]) + matmul_last(far, far_b[...]),
        ],
        axis=1,
    )
    value = embedded_ref[...].astype(jnp.float32)
    hidden = jnp.where(pl.program_id(0) == 0, first_ref[...], second_ref[...])
    grad = to_low(hidden + root_mean_back(total + spread, gain_ref[...], value))
    grad_ref[...] = grad
    token_ref[...] = to_low(matmul_last(grad, embed_ref[...]))


def embed_backward(
    info, query_grad, own, came, short, tables, hidden_grads, embedded, gain, embed, query_weights, pair_weights
):
    rows, wide = embedded.shape
    block = rows // 2
    heads = own.shape[0]
    row = pl.BlockSpec((block, wide), lambda i, s: (i, 0))
    once = pl.BlockSpec((block, wide), lambda i, s: (0, 0))
    pair = pl.BlockSpec((heads, block, PAIR), lambda i, s: (0, i, 0))
    table = pl.BlockSpec((block, PAIR), lambda i, s: (s[i], 0))
    return pl.pallas_call(
        embed_backward_kernel,
        grid_spec=pltpu.PrefetchScalarGridSpec(
            num_scalar_prefetch=1,
            grid=(2,),
            in_specs=[
                row, pair, pair, pl.BlockSpec((heads, block, PAIR), lambda i, s: (0, 0, 0)), table, table, once, once, row, fixed((1, wide)), fixed(embed.shape),
                *[fixed(weight.shape) for weight in (*query_weights, *pair_weights)],
            ],
            out_specs=[row, pl.BlockSpec((block, embed.shape[0]), lambda i, s: (i, 0))],
        ),
        out_shape=[
            jax.ShapeDtypeStruct((rows, wide), jnp.bfloat16),
            jax.ShapeDtypeStruct((rows, embed.shape[0]), jnp.bfloat16),
        ],
        compiler_params=pltpu.CompilerParams(
            dimension_semantics=("arbitrary",), vmem_limit_bytes=VMEM_LIMIT
        ),
        cost_estimate=pl.CostEstimate(flops=12 << 30, bytes_accessed=20 << 20, transcendentals=0),
        name="embed_backward",
    )(
        info, query_grad, own, came, short, tables[0], tables[1], *hidden_grads, embedded, gain.reshape(1, -1), embed,
        *query_weights, *pair_weights,
    )


def own_route(own, local_vocab):
    places = jnp.arange(own.shape[0], dtype=jnp.int32)
    same = own[:, None] == own[None, :]
    repeated = jnp.any(same & (places[:, None] > places[None, :]), axis=1)
    owner = own // local_vocab
    before = (owner[:, None] == owner[None, :]) & (own[None, :] < own[:, None])
    rank = jnp.sum((before & jnp.logical_not(repeated)[None, :]).astype(jnp.int32), axis=1)
    return (rank, owner)


def asked_of_me(asked, me, local_vocab):
    entries = me * local_vocab + jnp.arange(local_vocab, dtype=jnp.int32)
    present = jnp.any(asked[:, :, None] == entries[None, None, :], axis=1)
    places = jnp.arange(local_vocab, dtype=jnp.int32)
    lower = places[:, None] < places[None, :]
    standing = matmul(present.astype(jnp.bfloat16), lower.astype(jnp.bfloat16)).astype(jnp.int32)
    return (present, standing)


def sender_choice(present, standing, turn, capacity):
    place = jnp.arange(capacity, dtype=jnp.int32)
    slot = jnp.where(place < capacity - 1, turn * (capacity - 1) + place, -1)
    chosen = present[:, None, :] & (standing[:, None, :] == slot[None, :, None])
    return chosen.astype(jnp.bfloat16).reshape(present.shape[0] * capacity, present.shape[1])


def taker_choice(own_rank, own_owner, turn, capacity, devices):
    inside = own_rank - turn * (capacity - 1)
    valid = (inside >= 0) & (inside < capacity - 1)
    place = jnp.where(valid, own_owner * capacity + inside, -1)
    return (place[:, None] == jnp.arange(devices * capacity, dtype=jnp.int32)[None, :]).astype(
        jnp.bfloat16
    )


def exchange(value):
    return lax.all_to_all(value, ("dp", "mp"), 0, 0, tiled=True)


def ordered_blocks(first, own_two, other_two):
    return jnp.where(
        first,
        jnp.concatenate([own_two[0], other_two[0], other_two[1], own_two[1]], axis=0),
        jnp.concatenate([other_two[0], own_two[0], own_two[1], other_two[1]], axis=0),
    )


def body(
    pieces,
    counts,
    token_index,
    hyper_input,
    hyper_output,
    hyper_expand,
    hyper_reduce,
    hyper_norms,
    embed_weight,
    attention_gain,
    dense_gain,
    frozen_query_weight,
    frozen_key_weight,
    frozen_value_weight,
    frozen_output_weight,
    gate_weight,
    up_weight,
    down_weight,
    upstream,
):
    local_vocab = pieces.shape[0]
    mp_count = lax.axis_size("mp")
    devices = lax.axis_size("dp") * mp_count
    mp_index = lax.axis_index("mp")
    me = lax.axis_index("dp") * mp_count + mp_index
    core = (me >> 1) & 1
    lead = mp_index == 0
    bits = log2_of(devices)
    far_bits = list(range(bits - 1, 1, -1))
    length = token_index.shape[0]
    block = length // BLOCK_PARTS
    capacity = max(16, length // devices)

    norm_count = hyper_norms.shape[1]
    in_width = hyper_input.shape[1]
    norm_lanes = jnp.pad(hyper_norms, ((0, 0), (0, PAIR - norm_count)))
    cut = token_index.reshape(BLOCK_PARTS, block)
    own_tokens = jnp.where(
        lead, jnp.concatenate([cut[0], cut[3]]), jnp.concatenate([cut[1], cut[2]])
    )
    digits = jnp.concatenate([own_tokens // PAIR, own_tokens % PAIR]).astype(jnp.bfloat16)
    digits = digits.reshape(hyper_input.shape[0], -1)
    digit_width = digits.shape[1]
    digit_lanes = jnp.pad(digits, ((0, 0), (0, -digit_width % PAIR)))
    kv_local = frozen_key_weight.shape[1] // HEAD_WIDTH
    key_own = jnp.concatenate(
        [
            weight[:, at * HEAD_WIDTH : (at + 1) * HEAD_WIDTH]
            for at in range(kv_local)
            for weight in (frozen_key_weight, frozen_value_weight)
        ],
        axis=1,
    )
    key_near = swap(lax.dynamic_slice_in_dim(key_own, core * PAIR, PAIR, 1), 1, devices)
    query_cut = frozen_query_weight.shape[1] // 2
    side = (me >> 2) & 1
    half_in = frozen_query_weight.shape[0] // 2
    query_slice = lax.dynamic_slice(
        frozen_query_weight, (side * half_in, core * query_cut), (half_in, query_cut)
    )
    half_out = query_cut // 2
    output_slice = lax.dynamic_slice_in_dim(
        frozen_output_weight, core * query_cut + side * half_out, half_out, 0
    )
    count_rows = jnp.broadcast_to(counts[:, None, None], (counts.shape[0], 1, PAIR))
    early_x = far_bits[:1] + [0] + far_bits[1:] + [1]
    late_y = far_bits[:-1] + [0] + far_bits[-1:] + [1]
    gathers = [
        (jnp.concatenate([hyper_input, norm_lanes, digit_lanes], axis=1), late_y),
        (jnp.concatenate([hyper_output, hyper_expand], axis=1), late_y),
        (hyper_reduce, early_x),
    ]
    gather_held = [x for x, _ in gathers]

    def send(which, at):
        return swap(gather_held[which], 1 << gathers[which][1][at], devices)

    def join(which, came, at):
        order = gathers[which][1]
        return gather_join(gather_held[which], came, order[at], order[:at], me)

    for at in range(bits - 3):
        gather_held = [join(which, send(which, at), at) for which in range(3)]
        if at == bits - 4:
            gather_held, key_near, query_slice, output_slice, count_rows = lax.optimization_barrier(
                (gather_held, key_near, query_slice, output_slice, count_rows)
            )
            key_far = swap(key_near, 2, devices)
    later_came = [send(which, bits - 3) for which in (1, 2)]
    gather_held[0] = join(0, send(0, bits - 3), bits - 3)
    begun = gather_held[:1]
    in_held = join(0, send(0, bits - 2), bits - 2)
    in_held, later_came = lax.optimization_barrier((in_held, later_came))
    gather_held = [in_held] + [join(which, came, bits - 3) for which, came in zip((1, 2), later_came)]
    later_came = [send(which, bits - 2) for which in (1, 2)]
    in_came = send(0, bits - 1)
    in_weight = join(0, in_came, bits - 1)
    small = gather_join(
        in_held[:, in_width:], in_came[:, in_width:], late_y[-1], late_y[:-1], me
    )
    embed_full = lax.all_gather(embed_weight, ("dp", "mp"), axis=0, tiled=True)
    norm_rows = small[:, :8].astype(jnp.float32).T
    digit_at = PAIR
    all_digits = small[:, digit_at : digit_at + digit_width].reshape(devices, 2, 2 * block)
    all_digits = all_digits.astype(jnp.int32)
    asked = all_digits[:, 0] * PAIR + all_digits[:, 1]

    query_slice, *_ = lax.optimization_barrier((query_slice, *begun))
    query_near = swap(query_slice, 1, devices)

    def by_side(own, other):
        return [jnp.where(side == 0, own, other), jnp.where(side == 0, other, own)]

    other_base = (1 - mp_index) * kv_local
    head_order = [mp_index * kv_local, mp_index * kv_local + 1, other_base + core, other_base + 1 - core]

    slot_mixed, slot_probs, hyper_attended, lead_rows = slot_attention(
        pieces, count_rows, in_weight, norm_rows
    )
    asked, _ = lax.optimization_barrier((asked, hyper_attended))
    hyper_attended, embed_full, later_came, query_near = lax.optimization_barrier(
        (hyper_attended, embed_full, later_came, query_near)
    )
    last = late_y[-1]

    def joined(which, parts):
        order = gathers[which][1]
        halves = [gather_join(*parts[at : at + 2], order[-2], order[:-2], me) for at in (0, 2)]
        return gather_join(*halves, last, order[:-1], me)

    later_parts = [(gather_held[which], came) for which, came in zip((1, 2), later_came)]
    later_parts = [(*own, *[swap(x, 1 << last, devices) for x in own]) for own in later_parts]
    together = hyper_input.shape[0] * 2 % 16 == 0
    if together:
        forward_weights = later_parts
    else:
        forward_weights = [[joined(which, later_parts[which - 1])] for which in (1, 2)]
    query_far_row = swap(query_near, 4, devices)
    output_slice, _ = lax.optimization_barrier((output_slice, query_near))
    output_near = swap(output_slice, 1, devices)
    pooled, hyper_hidden = units_forward(
        devices // 8, jnp.stack([core, side]), hyper_attended, lead_rows, *forward_weights, norm_rows
    )
    _, query_far_row = lax.optimization_barrier((pooled, query_far_row))
    present, standing = asked_of_me(asked, me, local_vocab)
    own_rank, own_owner = own_route(lax.dynamic_index_in_dim(asked, me, 0, False), local_vocab)
    most = jnp.max(jnp.sum(present.astype(jnp.int32), axis=1))
    needed = ((most + capacity - 2) // (capacity - 1)).astype(jnp.float32)

    def fetch(turn):
        sent = matmul(sender_choice(present, standing, turn, capacity), pooled)
        sent = sent.reshape(devices, capacity, pooled.shape[1])
        free = lax.broadcasted_iota(jnp.int32, sent.shape, 1) == capacity - 1
        sent = to_low(jnp.where(free, needed, sent)).reshape(devices * capacity, pooled.shape[1])
        came = exchange(sent)
        picked = matmul(taker_choice(own_rank, own_owner, turn, capacity, devices), came)
        return (to_low(picked), came)

    chosen_own, came = fetch(0)
    query_near = by_side(query_near, query_far_row)
    query_far = [swap(x, 2, devices) for x in query_near]
    chosen_own, came, query_far, output_near = lax.optimization_barrier(
        (chosen_own, came, query_far, output_near)
    )
    output_far_row = swap(output_near, 4, devices)
    needs = came.reshape(devices, capacity, pooled.shape[1])[:, capacity - 1, 0]
    rounds = jnp.max(needs.astype(jnp.float32)).astype(jnp.int32)
    chosen_own = lax.fori_loop(1, rounds, lambda turn, chosen: chosen + fetch(turn)[0], chosen_own)
    chosen_other = swap(chosen_own, 1, devices)

    tables = rope_tables(length)
    own_at = (mp_index, 3 - mp_index)
    own_base = tuple(at * block for at in own_at)
    other_start = ((1 - mp_index) * block, (2 + mp_index) * block)
    infos = [jnp.stack([at] + head_order).astype(jnp.int32) for at in own_at]

    other_at = (1 - mp_index, 2 + mp_index)
    query_weights = (frozen_query_weight, *query_near, *query_far)
    pair_weights = (key_own, key_near, key_far)
    own_info = jnp.stack(own_at).astype(jnp.int32)
    other_info = jnp.stack(other_at).astype(jnp.int32)
    pair_pre, embedded, queries = project(
        own_info, chosen_own, embed_full, attention_gain, pair_weights, query_weights, None
    )
    (pair_pre,) = project(
        other_info, chosen_other, embed_full, attention_gain, pair_weights, (), pair_pre
    )
    pair_pre, output_far_row = lax.optimization_barrier((pair_pre, output_far_row))
    output_near = by_side(output_near, output_far_row)
    output_far = [swap(x, 2, devices) for x in output_near]
    output_weights = (frozen_output_weight, *output_near, *output_far)
    spans = (2 * block, length)

    sums = [None, None]
    lows = [None, None]
    hidden_parts = [None, None]
    second_low = [None, None]
    second_other = [None, None]
    for part in (1, 0):
        flat, lows[part], sums[part] = attention_forward(
            infos[part], queries, pair_pre, tables, part, spans[part]
        )
        hidden_parts[part], second_low[part] = output_project(
            part, flat, embedded, dense_gain, output_weights
        )
        second_other[part] = swap(second_low[part], 1, devices)
        pair_pre, second_low[part] = lax.optimization_barrier((pair_pre, second_low[part]))

    second_low, second_other[1] = lax.optimization_barrier((second_low, second_other[1]))
    dense_rows = [None, None]
    second_came = [None, None]
    for part in (1, 0):
        info = jnp.stack([own_at[part], other_at[part]]).astype(jnp.int32)
        grad_second, dense_rows[part] = feed_forward(
            second_low[part], second_other[part], upstream, hidden_parts[part], info,
            gate_weight, up_weight, down_weight,
        )
        second_came[part] = (grad_second[:block], swap(grad_second[block:], 1, devices))

    query_grad = None
    grad_hidden = [None, None]
    pair_grads = [None, None]
    for part in (1, 0):
        here, came = second_came[part]
        if part == 1:
            here, came, dense_rows[0] = lax.optimization_barrier((here, came, dense_rows[0]))
        else:
            here, came, query_grad = lax.optimization_barrier((here, came, query_grad))
        grad_hidden[part], grad_attended = hidden_backward(
            infos[part], here, came, hidden_parts[part], upstream, dense_gain, output_weights
        )
        query_grad, pair_grads[part] = attention_backward(
            infos[part], lows[part], grad_attended, sums[part], pair_pre, tables, part, spans[part], query_grad
        )

    def pick_block(value, at):
        return lax.dynamic_slice_in_dim(value, at * block, block, 1)

    came_long = swap(
        to_low(jnp.concatenate([pick_block(pair_grads[1], at) for at in other_at], axis=1)), 1, devices
    )
    pair_grads[0], came_long = lax.optimization_barrier((pair_grads[0], came_long))
    came_short = swap(to_low(pick_block(pair_grads[0], other_at[0])), 1, devices)
    pair_own = jnp.concatenate(
        [
            pick_block(pair_grads[1], own_at[0]) + pick_block(pair_grads[0], own_at[0]),
            pick_block(pair_grads[1], own_at[1]),
        ],
        axis=1,
    )

    share = upstream.shape[1] // mp_count

    def columns(value, index):
        return lax.dynamic_slice_in_dim(value, index * share, share, 1)

    dense_came = [swap(columns(dense_rows[part], 1 - mp_index), 1, devices) for part in range(2)]
    pair_grads[0], *dense_came = lax.optimization_barrier((pair_grads[0], *dense_came))

    embedded_grad_low, token_grad = embed_backward(
        jnp.stack([*own_at, *head_order]).astype(jnp.int32), query_grad, pair_own, came_long, came_short, tables, grad_hidden, embedded,
        attention_gain, embed_full, query_weights, pair_weights,
    )
    own_out = []
    other_out = []
    for part in range(2):
        kept = columns(dense_rows[part], mp_index).astype(jnp.float32)
        arrived = dense_came[part].astype(jnp.float32)
        own_out.append(to_low(kept[:block] + arrived[block:]))
        other_out.append(to_low(kept[block:] + arrived[:block]))
    model_out = ordered_blocks(lead, own_out, other_out)
    embed_grad = to_low(matmul_first(chosen_own, embedded_grad_low))
    _, later_parts = lax.optimization_barrier((token_grad, later_parts))
    wide_weight, reduce_weight = [joined(which, later_parts[which - 1]) for which in (1, 2)]

    def give_back(turn, total):
        taker = taker_choice(own_rank, own_owner, turn, capacity, devices)
        leaving = matmul_first(taker, token_grad).astype(jnp.bfloat16)
        came = exchange(leaving)
        return total + matmul_first(sender_choice(present, standing, turn, capacity), came)

    grad_pooled = give_back(0, jnp.zeros(pooled.shape, jnp.float32))
    grad_pooled = lax.fori_loop(1, rounds, give_back, grad_pooled)

    back_order = [1, 0] + far_bits[::-1]

    def scatter(held, order, at):
        return scatter_send(held, order[at], order[at + 1 :], me, devices)

    embed_held = scatter_add(*scatter(embed_grad, back_order, 0))
    embed_held, grad_pooled = lax.optimization_barrier((embed_held, grad_pooled))
    embed_held = scatter_add(*scatter(embed_held, back_order, 1))
    hidden_grad, attended_grad, wide_grad, reduce_grad, later_norms = units_backward(
        grad_pooled, hyper_hidden, hyper_attended, wide_weight, reduce_weight, norm_rows
    )
    hidden_grad, embed_held = lax.optimization_barrier((hidden_grad, embed_held))
    held = [embed_held, wide_grad, reduce_grad]
    turned_order = [back_order[0], back_order[2], back_order[3], back_order[1]] + back_order[4:]
    orders = [back_order, back_order, turned_order]
    ahead = [2, 0, 0]

    def depart(at):
        return [
            scatter(x, order, at + skip) if at + skip < bits else (x, None)
            for x, order, skip in zip(held, orders, ahead)
        ]

    def arrive(moving):
        return [x if came is None else scatter_add(x, came) for x, came in moving]

    slots_saved = (pieces, slot_mixed, slot_probs)
    slots_held = (None, None, later_norms)
    for part in range(SLOT_PARTS):
        moving = depart(part)
        slots_held = slot_backward(
            part, SLOT_PARTS, slots_held, slots_saved, (attended_grad, hidden_grad), in_weight, norm_rows
        )
        slots_held, moving = lax.optimization_barrier((tuple(slots_held), moving))
        held = arrive(moving)
    pieces_grad, input_grad, _ = slots_held
    input_held = input_grad
    moving = depart(SLOT_PARTS)
    for at in range(bits):
        input_held = scatter_add(*scatter(input_held, back_order, at))
        if at > 0:
            _, moving = lax.optimization_barrier((input_held, moving))
            held = arrive(moving)
            moving = depart(SLOT_PARTS + at)
    held = arrive(moving)
    embed_own, wide_own, reduce_own, input_own = (*held, input_held)
    out_width = hyper_output.shape[1]
    return (
        model_out,
        pieces_grad,
        input_own[:, :in_width],
        wide_own[:, :out_width],
        wide_own[:, out_width:],
        reduce_own,
        input_own[:, in_width : in_width + norm_count],
        embed_own,
    )


def solution(mesh):
    return jax.shard_map(
        body,
        mesh=mesh,
        in_specs=(
            P(("dp", "mp"), None, None),
            P(("dp", "mp")),
            P("dp"),
            P(("dp", "mp"), None),
            P(("dp", "mp"), None),
            P(("dp", "mp"), None),
            P(("dp", "mp"), None),
            P(("dp", "mp"), None),
            P(("dp", "mp"), None),
            P(),
            P(),
            P(None, "mp"),
            P(None, "mp"),
            P(None, "mp"),
            P("mp", None),
            P(None, "mp"),
            P(None, "mp"),
            P("mp", None),
            P("dp", None),
        ),
        out_specs=(
            P("dp", "mp"),
            P(("dp", "mp"), None, None),
            P(("dp", "mp"), None),
            P(("dp", "mp"), None),
            P(("dp", "mp"), None),
            P(("dp", "mp"), None),
            P(("dp", "mp"), None),
            P(("dp", "mp"), None),
        ),
        check_vma=False,
    )
```

```python
import functools

import jax
import jax.numpy as jnp
import numpy as np
from jax import lax
from jax.experimental import pallas as pl
from jax.experimental.pallas import tpu as pltpu
from jax.sharding import PartitionSpec as P

HEAD_WIDTH = 64
HHD = 64
BLOCK_PARTS = 4
UNIT = 512
PAIR = 2 * HEAD_WIDTH
VMEM_LIMIT = 48 << 20
ENTRY_BLOCK = 64
SLOT_PARTS = 2
UNIT_STEP = 256
COLUMN_STEP = 256
UNIT_ROWS = 256


EPS = 1e-05
NEGATIVE = -1000000000.0


def matmul(left, right):
    return jnp.dot(left, right, preferred_element_type=jnp.float32)


def matmul_first(left, right):
    return lax.dot_general(
        left, right, (((0,), (0,)), ((), ())), preferred_element_type=jnp.float32
    )


def matmul_last(left, right):
    return lax.dot_general(
        left, right, (((1,), (1,)), ((), ())), preferred_element_type=jnp.float32
    )


def log2_of(number):
    return number.bit_length() - 1


def swap(value, mask, devices):
    return lax.ppermute(value, ("dp", "mp"), [(d, d ^ mask) for d in range(devices)])


def gather_join(held, arrived, bit, done, me):
    rows, width = held.shape
    outer = 1 << sum(other > bit for other in done)
    held, arrived = [x.reshape(outer, rows // outer, width) for x in (held, arrived)]
    joined = jnp.where(
        ((me >> bit) & 1) == 1,
        jnp.concatenate([arrived, held], axis=1),
        jnp.concatenate([held, arrived], axis=1),
    )
    return joined.reshape(2 * rows, width)


def scatter_send(held, bit, left, me, devices):
    rows, width = held.shape
    outer = 1 << sum(other > bit for other in left)
    parts = held.reshape(outer, 2, rows // outer // 2, width)
    mine = (me >> bit) & 1

    def part(at):
        return lax.dynamic_slice_in_dim(parts, at, 1, 1).reshape(rows // 2, width)

    return (part(mine), swap(to_low(part(1 - mine)), 1 << bit, devices))


def scatter_add(staying, came):
    return staying.astype(jnp.float32) + came.astype(jnp.float32)


def lanes(shape):
    return lax.broadcasted_iota(jnp.int32, shape, len(shape) - 1)


def half_swap(value):
    quarter = HEAD_WIDTH // 2
    upper = (lanes(value.shape) & quarter) != 0
    return jnp.where(
        upper, pltpu.roll(value, quarter, 1), pltpu.roll(value, PAIR - quarter, 1)
    )


def to_low(value):
    return value.astype(jnp.bfloat16)


def causal_of(rows):
    return lax.broadcasted_iota(jnp.int32, (rows, rows), 0) <= lax.broadcasted_iota(
        jnp.int32, (rows, rows), 1
    )


def masked_scores(keys, low, causal):
    rows = causal.shape[0]
    length = keys.shape[0]
    last = jnp.where(causal, matmul_last(keys[length - rows :, :], low), NEGATIVE)
    return [matmul_last(keys[: length - rows, :], low), last] if length > rows else [last]


def for_lengths(block_at, rows, length, work):
    for count in (length - rows, length):
        pl.when(block_at == count // rows - 1)(functools.partial(work, count))


def turn_left(value, cosine, sine):
    left = lanes(value.shape) < HEAD_WIDTH
    return jnp.where(left, value * cosine + half_swap(value) * sine, value)


def head_views(pair_ref, cos_ref, sin_ref, rows):
    span = slice(0, rows)
    turned = to_low(turn_left(pair_ref[span, :], cos_ref[span, :], sin_ref[span, :])).astype(jnp.float32)
    other = pltpu.roll(turned, HEAD_WIDTH, 1)
    left = lanes(turned.shape) < HEAD_WIDTH
    return (
        jnp.where(left, turned, 0.0),
        jnp.where(left, 0.0, other),
        jnp.where(left, other, 0.0),
        jnp.where(left, 0.0, turned),
    )


def attention_forward_kernel(
    info, query_ref, pair_ref, cos_pair, sin_pair, cos_ref, sin_ref,
    out_ref, low_ref, lse_ref, even, odd, across,
):
    rows = query_ref.shape[0]
    causal = causal_of(rows)

    def work(length):
        span = slice(0, length)
        key_left, key_right, value_left, _ = head_views(pair_ref, cos_pair, sin_pair, length)
        even[span, :] = to_low(key_left)
        odd[span, :] = to_low(key_right)
        across[:, span] = to_low(value_left.T[:HEAD_WIDTH])
        for pair in range(query_ref.shape[1] // PAIR):
            columns = slice(pair * PAIR, (pair + 1) * PAIR)
            query = query_ref[:, columns]
            turned = to_low(query * cos_ref[...] + half_swap(query) * sin_ref[...])
            low = to_low(turned.astype(jnp.float32) * HEAD_WIDTH ** (-0.5))
            low_ref[:, columns] = low
            outs = []
            for at, keys in enumerate((even, odd)):
                scores = masked_scores(keys[span, :], low, causal)
                highest = functools.reduce(
                    jnp.maximum, [jnp.max(x, axis=0, keepdims=True) for x in scores]
                )
                weights = [jnp.exp(x - highest) for x in scores]
                total = sum(jnp.sum(x, axis=0, keepdims=True) for x in weights)
                out = 0.0
                start = 0
                for x in weights:
                    out = out + matmul(across[:, start : start + x.shape[0]], to_low(x))
                    start += x.shape[0]
                outs.append(out / total)
                lse_ref[0, 2 * pair + at : 2 * pair + at + 1, :] = highest + jnp.log(total)
            out_ref[:, columns] = to_low(jnp.concatenate(outs, axis=0).T)

    for_lengths(info[0], rows, pair_ref.shape[0], work)


def attention_backward_kernel(
    info, low_ref, grad_ref, lse_ref, pair_ref, cos_pair, sin_pair, cos_ref, sin_ref, *refs,
):
    query_ref, pair_grad_ref, even, odd, value_even, value_odd, across = refs[-11:-4]
    key_even, key_odd, sum_even, sum_odd = refs[-4:]
    rows = low_ref.shape[0]
    causal = causal_of(rows)

    def work(length):
        span = slice(0, length)
        key_left, key_right, value_left, value_right = head_views(pair_ref, cos_pair, sin_pair, length)
        even[span, :] = to_low(key_left)
        odd[span, :] = to_low(key_right)
        value_even[span, :] = to_low(value_left)
        value_odd[span, :] = to_low(value_right)
        across[:, span] = to_low(key_left.T[:HEAD_WIDTH])
        sides = ((even, value_even, key_even, sum_even), (odd, value_odd, key_odd, sum_odd))
        for total in (key_even, key_odd, sum_even, sum_odd):
            total[span, :] = jnp.zeros((length, PAIR), jnp.float32)
        for pair in range(low_ref.shape[1] // PAIR):
            columns = slice(pair * PAIR, (pair + 1) * PAIR)
            low = low_ref[:, columns]
            grad = grad_ref[:, columns]
            outs = []
            for at, (keys, values, key_total, value_total) in enumerate(sides):
                lse = lse_ref[0, 2 * pair + at : 2 * pair + at + 1, :]
                probs = [jnp.exp(x - lse) for x in masked_scores(keys[span, :], low, causal)]
                moved = []
                start = 0
                for x in probs:
                    part = slice(start, start + x.shape[0])
                    value_total[part, :] += matmul(to_low(x), grad)
                    moved.append(x * matmul_last(values[part, :], grad))
                    start += x.shape[0]
                mean = sum(jnp.sum(x, axis=0, keepdims=True) for x in moved)
                out = 0.0
                start = 0
                for x, y in zip(probs, moved):
                    part = slice(start, start + x.shape[0])
                    grad_scores = to_low(y - x * mean)
                    key_total[part, :] += matmul(grad_scores, low)
                    out = out + matmul(across[:, part], grad_scores)
                    start += x.shape[0]
                outs.append(out)
            turned = jnp.concatenate(outs, axis=0).T * HEAD_WIDTH ** (-0.5)
            query_ref[:, columns] = to_low(turned * cos_ref[...] - half_swap(turned) * sin_ref[...])
        left = lanes((length, PAIR)) < HEAD_WIDTH
        pair_grad_ref[0, span, :] = jnp.where(
            left,
            key_even[span, :] + pltpu.roll(key_odd[span, :], HEAD_WIDTH, 1),
            pltpu.roll(sum_even[span, :], HEAD_WIDTH, 1) + sum_odd[span, :],
        )
        if length < pair_ref.shape[0]:
            rest = (pair_ref.shape[0] - length, PAIR)
            pair_grad_ref[0, length:, :] = jnp.zeros(rest, jnp.float32)

    for_lengths(info[0], rows, pair_ref.shape[0], work)


def attention_specs(part, rows, length):
    span = (rows, 4 * PAIR)
    return {
        "table_pair": pl.BlockSpec((length, PAIR), lambda g, s: (0, 0)),
        "table": pl.BlockSpec((rows, PAIR), lambda g, s: (s[0], 0)),
        "pair": pl.BlockSpec((length, PAIR), lambda g, s: (0, g)),
        "part": pl.BlockSpec(span, lambda g, s: (part, g)),
        "wide": pl.BlockSpec(span, lambda g, s: (0, g)),
        "sums": pl.BlockSpec((1, 8, rows), lambda g, s: (g, 0, 0)),
    }


def attention_cost(rows, length, heads, matmuls):
    work = 20 * rows * length * heads * HEAD_WIDTH * matmuls
    return pl.CostEstimate(
        flops=work, bytes_accessed=16 * rows * heads * HEAD_WIDTH, transcendentals=rows * length * heads
    )


def attention_forward(info, queries, pair_pre, tables, part, length):
    cosine, sine = tables
    rows = cosine.shape[0] // BLOCK_PARTS
    heads = 4 * 4 * PAIR // HEAD_WIDTH
    spec = attention_specs(part, rows, length)
    half = pltpu.VMEM((length, PAIR), jnp.bfloat16)
    wide = (rows, heads * HEAD_WIDTH)
    return pl.pallas_call(
        attention_forward_kernel,
        grid_spec=pltpu.PrefetchScalarGridSpec(
            num_scalar_prefetch=1,
            grid=(4,),
            in_specs=[
                spec["part"], spec["pair"],
                spec["table_pair"], spec["table_pair"], spec["table"], spec["table"],
            ],
            out_specs=[spec["wide"], spec["wide"], spec["sums"]],
            scratch_shapes=[
                half, half,
                pltpu.VMEM((HEAD_WIDTH, length), jnp.bfloat16),
            ],
        ),
        out_shape=[
            jax.ShapeDtypeStruct(wide, jnp.bfloat16),
            jax.ShapeDtypeStruct(wide, jnp.bfloat16),
            jax.ShapeDtypeStruct((4, 8, rows), jnp.float32),
        ],
        compiler_params=pltpu.CompilerParams(
            dimension_semantics=("arbitrary",), vmem_limit_bytes=VMEM_LIMIT
        ),
        cost_estimate=attention_cost(rows, length, heads, 2),
        name="attention_forward",
    )(info, queries, pair_pre, cosine, sine, cosine, sine)


def attention_backward(info, low, grad, sums, pair_pre, tables, part, length, before):
    cosine, sine = tables
    rows = cosine.shape[0] // BLOCK_PARTS
    heads = low.shape[1] // HEAD_WIDTH
    spec = attention_specs(part, rows, length)
    before = [] if before is None else [before]
    half = pltpu.VMEM((length, PAIR), jnp.bfloat16)
    full = pltpu.VMEM((length, PAIR), jnp.float32)
    return pl.pallas_call(
        attention_backward_kernel,
        grid_spec=pltpu.PrefetchScalarGridSpec(
            num_scalar_prefetch=1,
            grid=(4,),
            in_specs=[
                spec["wide"], spec["wide"], spec["sums"], spec["pair"],
                spec["table_pair"], spec["table_pair"], spec["table"], spec["table"],
            ]
            + [pl.BlockSpec(memory_space=pl.ANY)] * len(before),
            out_specs=[spec["part"], pl.BlockSpec((1, length, PAIR), lambda g, s: (s[1 + g], 0, 0))],
            scratch_shapes=[
                half, half, half, half,
                pltpu.VMEM((HEAD_WIDTH, length), jnp.bfloat16),
                full, full, full, full,
            ],
        ),
        out_shape=[
            jax.ShapeDtypeStruct((2 * rows, low.shape[1]), jnp.bfloat16),
            jax.ShapeDtypeStruct((4, length, PAIR), jnp.float32),
        ],
        input_output_aliases={9: 0} if before else {},
        compiler_params=pltpu.CompilerParams(
            dimension_semantics=("arbitrary",), vmem_limit_bytes=VMEM_LIMIT
        ),
        cost_estimate=attention_cost(rows, length, heads, 5),
        name="attention_backward",
    )(info, low, grad, sums, pair_pre, cosine, sine, cosine, sine, *before)


def rope_tables(length):
    positions = np.arange(length, dtype=np.float32)
    inverse = 10000.0 ** (-np.arange(0, HEAD_WIDTH, 2, dtype=np.float32) / HEAD_WIDTH)
    angles = positions[:, None] * inverse.astype(np.float32)[None, :]
    cosine, sine = np.cos(angles).astype(np.float32), np.sin(angles).astype(np.float32)
    return (
        jnp.asarray(np.concatenate([cosine] * 4, axis=1)),
        jnp.asarray(np.concatenate([-sine, sine, -sine, sine], axis=1)),
    )


def head_marks(width, transposed):
    shape = (PAIR, width) if transposed else (width, PAIR)
    head_at, column_at = (0, 1) if transposed else (1, 0)
    head = lax.broadcasted_iota(jnp.int32, shape, head_at)
    column = lax.broadcasted_iota(jnp.int32, shape, column_at)
    return (column // HHD == head).astype(jnp.bfloat16)


def head_sums(value, marks):
    high = to_low(value)
    rest = to_low(value - high.astype(jnp.float32))
    return matmul(high, marks) + matmul(rest, marks)


def normalize(value):
    centered = value - jnp.mean(value, axis=-1, keepdims=True)
    inverse = lax.rsqrt(jnp.mean(centered * centered, axis=-1, keepdims=True) + EPS)
    return (centered * inverse, inverse)


def norm_back(grad, gain, hat, inverse):
    scaled = grad * gain
    mean = jnp.mean(scaled, axis=-1, keepdims=True)
    along = jnp.mean(scaled * hat, axis=-1, keepdims=True)
    return inverse * (scaled - mean - hat * along)


def slot_attention_kernel(
    pieces_ref, counts_ref, weight_ref, mixed_ref, probs_ref, attended_ref, lead_ref, norm_ref
):
    entries, slots, width = pieces_ref.shape

    @pl.when(pl.program_id(0) == 0)
    def norms():
        norm_ref[...] = weight_ref[:, 3 * width : 3 * width + PAIR].astype(jnp.float32).T[:8]

    rows = entries * slots
    tall = (entries, slots, width)
    pieces = pieces_ref[...].astype(jnp.float32)
    hat, _ = normalize(pieces.reshape(rows, width))
    low = to_low(hat * norm_ref[0:1, :] + norm_ref[1:2, :])
    mixed = []
    for part in range(3):
        span = slice(part * width, (part + 1) * width)
        value = to_low(matmul(low, weight_ref[:, span]))
        mixed_ref[:, span] = value
        mixed.append(value.astype(jnp.float32).reshape(tall))
    query, keys, values = mixed
    marks = head_marks(width, False)
    product = (keys * query[:, 0:1, :]).reshape(rows, width)
    scores = head_sums(product, marks).reshape(entries, slots, PAIR) * HHD ** (-0.5)
    live = lax.broadcasted_iota(jnp.int32, scores.shape, 1) < counts_ref[...]
    scores = jnp.where(live, scores, NEGATIVE)
    weight = jnp.exp(scores - jnp.max(scores, axis=1, keepdims=True))
    probs = weight / jnp.sum(weight, axis=1, keepdims=True)
    probs_ref[...] = probs
    spread = matmul(to_low(probs.reshape(rows, PAIR)), head_marks(width, True)).reshape(tall)
    attended_ref[...] = to_low(jnp.sum(spread * values, axis=1))
    lead_ref[...] = pieces[:, 0, :]


def slot_attention(pieces, counts, in_weight):
    entries, slots, width = pieces.shape
    part = min(ENTRY_BLOCK, entries)
    whole = lambda shape: pl.BlockSpec(shape, lambda i: (0,) * len(shape))
    tall = pl.BlockSpec((part, slots, width), lambda i: (i, 0, 0))
    flat = pl.BlockSpec((part, width), lambda i: (i, 0))
    return pl.pallas_call(
        slot_attention_kernel,
        grid=(entries // part,),
        in_specs=[
            tall,
            pl.BlockSpec((part, 1, PAIR), lambda i: (i, 0, 0)),
            whole(in_weight.shape),
        ],
        out_specs=[
            pl.BlockSpec((part * slots, 3 * width), lambda i: (i, 0)),
            pl.BlockSpec((part, slots, PAIR), lambda i: (i, 0, 0)),
            flat,
            flat,
            whole((8, width)),
        ],
        out_shape=[
            jax.ShapeDtypeStruct((entries * slots, 3 * width), jnp.bfloat16),
            jax.ShapeDtypeStruct((entries, slots, PAIR), jnp.float32),
            jax.ShapeDtypeStruct((entries, width), jnp.bfloat16),
            jax.ShapeDtypeStruct((entries, width), jnp.float32),
            jax.ShapeDtypeStruct((8, width), jnp.float32),
        ],
        compiler_params=pltpu.CompilerParams(
            dimension_semantics=("arbitrary",), vmem_limit_bytes=VMEM_LIMIT
        ),
        cost_estimate=pl.CostEstimate(
            flops=entries * slots * width, bytes_accessed=entries * slots, transcendentals=0
        ),
        name="slot_attention",
    )(pieces, counts, in_weight)


def gelu_of(value):
    cdf = 0.5 * (1.0 + lax.erf(value * np.float32(0.5 ** 0.5)))
    return (value * cdf, cdf)


def gelu_slope(value, cdf):
    return cdf + value * (jnp.exp(-0.5 * value * value) * np.float32((2 * np.pi) ** -0.5))


def place_parts(split, places, wholes, parts):
    @pl.when(pl.program_id(0) == 0)
    def join():
        core, side = places[0], places[1]
        for index, whole in enumerate(wholes):
            for at, part in enumerate(parts[4 * index : 4 * index + 4]):
                rows = part.shape[0] // split
                place = 2 * (side if at % 2 == 0 else 1 - side) + (core if at < 2 else 1 - core)
                for group in range(split):
                    start = pl.multiple_of((4 * group + place) * rows, rows)
                    whole[pl.ds(start, rows), :] = part[group * rows : (group + 1) * rows, :]


def units_forward_kernel(
    split, places, attended_ref, lead_ref, *refs
):
    *weights, norm_ref, pooled_ref, hidden_ref = refs[: 11 if split else 5]
    if not split:
        wide_weight_ref, reduce_ref = weights
    else:
        wide_weight_ref, reduce_ref = refs[11:]

        place_parts(split, places, (wide_weight_ref, reduce_ref), weights)

    width = lead_ref.shape[1]
    hidden = lead_ref[...] + matmul(attended_ref[...], wide_weight_ref[:, :width])
    hidden_ref[...] = hidden
    hat, _ = normalize(hidden)
    second = to_low(hat * norm_ref[2:3, :] + norm_ref[3:4, :])
    total = hidden
    units = reduce_ref.shape[0]
    step = min(UNIT, units)
    for at in range(0, units, step):
        active, _ = gelu_of(matmul(second, wide_weight_ref[:, width + at : width + at + step]))
        total = total + matmul(to_low(active), reduce_ref[at : at + step, :])
    pooled_ref[...] = to_low(total)


def units_forward(groups, places, attended, lead, wide_weight, reduce_weight, norm_rows):
    entries, width = attended.shape
    part = min(UNIT_ROWS, entries)
    split = groups if len(wide_weight) == 4 else 0
    whole = lambda shape: pl.BlockSpec(shape, lambda i, s: (0,) * len(shape))
    flat = pl.BlockSpec((part, width), lambda i, s: (i, 0))
    weights = [*wide_weight, *reduce_weight]
    joined = [
        pltpu.VMEM((4 * parts[0].shape[0], parts[0].shape[1]), jnp.bfloat16)
        for parts in (wide_weight, reduce_weight)
    ]
    return pl.pallas_call(
        functools.partial(units_forward_kernel, split),
        grid_spec=pltpu.PrefetchScalarGridSpec(
            num_scalar_prefetch=1,
            grid=(entries // part,),
            in_specs=[flat, flat] + [whole(x.shape) for x in (*weights, norm_rows)],
            out_specs=[flat, flat],
            scratch_shapes=joined if split else [],
        ),
        out_shape=[
            jax.ShapeDtypeStruct((entries, width), jnp.bfloat16),
            jax.ShapeDtypeStruct((entries, width), jnp.float32),
        ],
        compiler_params=pltpu.CompilerParams(
            dimension_semantics=("arbitrary",), vmem_limit_bytes=VMEM_LIMIT
        ),
        cost_estimate=pl.CostEstimate(
            flops=entries * width, bytes_accessed=entries * width, transcendentals=0
        ),
        name="units_forward",
    )(places.astype(jnp.int32), attended, lead, *weights, norm_rows)


def units_backward_kernel(split, places, grad_ref, hidden_ref, attended_ref, *refs):
    *weights, norm_ref, hidden_grad_ref, attended_grad_ref, norm_grad_ref = refs[: 12 if split else 6]
    if split:
        *sums, wide_total, reduce_total, wide_weight_ref, reduce_ref = refs[12:]
        place_parts(split, places, (wide_weight_ref, reduce_ref), weights)
    else:
        wide_weight_ref, reduce_ref = weights
        *sums, wide_total, reduce_total = refs[6:]
    step_at = pl.program_id(0)
    width = hidden_ref.shape[1]
    units = reduce_ref.shape[0]

    @pl.when(step_at == 0)
    def start():
        wide_total[...] = jnp.zeros_like(wide_total)
        reduce_total[...] = jnp.zeros_like(reduce_total)
        norm_grad_ref[...] = jnp.zeros_like(norm_grad_ref)

    grad = grad_ref[...]
    grad_low = to_low(grad)
    hat, inverse = normalize(hidden_ref[...])
    second = to_low(hat * norm_ref[2:3, :] + norm_ref[3:4, :])
    grad_normed = jnp.zeros_like(grad)
    step = min(UNIT, units)
    for at in range(0, units, step):
        span = slice(at, at + step)
        wide_span = slice(width + at, width + at + step)
        expanded = matmul(second, wide_weight_ref[:, wide_span])
        active, cdf = gelu_of(expanded)
        reduce_total[span, :] += matmul_first(to_low(active), grad_low)
        grad_active = matmul_last(grad_low, reduce_ref[span, :])
        grad_expanded = to_low(grad_active * gelu_slope(expanded, cdf))
        wide_total[:, wide_span] += matmul_first(second, grad_expanded)
        grad_normed = grad_normed + matmul_last(grad_expanded, wide_weight_ref[:, wide_span])
    norm_grad_ref[2:3, :] += jnp.sum(grad_normed * hat, axis=0, keepdims=True)
    norm_grad_ref[3:4, :] += jnp.sum(grad_normed, axis=0, keepdims=True)
    hidden_grad = grad + norm_back(grad_normed, norm_ref[2:3, :], hat, inverse)
    hidden_grad_ref[...] = hidden_grad
    hidden_low = to_low(hidden_grad)
    wide_total[:, :width] += matmul_first(attended_ref[...], hidden_low)
    attended_grad_ref[...] = to_low(matmul_last(hidden_low, wide_weight_ref[:, :width]))

    @pl.when(step_at == pl.num_programs(0) - 1)
    def finish():
        if not split:
            sums[0][...] = to_low(wide_total[...])
            sums[1][...] = to_low(reduce_total[...])
            return
        core = places[0]
        for total, halves in ((wide_total, sums[:2]), (reduce_total, sums[2:])):
            rows = halves[0].shape[0] // (2 * split)
            for half, place in zip(halves, (core, 1 - core)):
                for group in range(2 * split):
                    start = pl.multiple_of((2 * group + place) * rows, rows)
                    half[group * rows : (group + 1) * rows, :] = to_low(total[pl.ds(start, rows), :])


def units_backward(groups, places, grad, hidden, attended, wide_weight, reduce_weight, norm_rows):
    entries, width = attended.shape
    part = min(UNIT_ROWS, entries)
    split = groups if len(wide_weight) == 4 else 0
    weights = [*wide_weight, *reduce_weight]
    units = reduce_weight[0].shape[0] * len(reduce_weight)
    whole = lambda shape: pl.BlockSpec(shape, lambda i, s: (0,) * len(shape))
    flat = pl.BlockSpec((part, width), lambda i, s: (i, 0))
    wide = (width, width + units)
    tall = (units, width)
    half = lambda shape: (shape[0] // 2, shape[1])
    sums = [half(wide)] * 2 + [half(tall)] * 2 if split else [wide, tall]
    return pl.pallas_call(
        functools.partial(units_backward_kernel, split),
        grid_spec=pltpu.PrefetchScalarGridSpec(
            num_scalar_prefetch=1,
            grid=(entries // part,),
            in_specs=[flat, flat, flat] + [fixed(x.shape) for x in (*weights, norm_rows)],
            out_specs=[flat, flat, whole((8, width))] + [whole(x) for x in sums],
            scratch_shapes=[pltpu.VMEM(wide, jnp.float32), pltpu.VMEM(tall, jnp.float32)]
            + [pltpu.VMEM(x, jnp.bfloat16) for x in (wide, tall)] * bool(split),
        ),
        out_shape=[
            jax.ShapeDtypeStruct((entries, width), jnp.float32),
            jax.ShapeDtypeStruct((entries, width), jnp.bfloat16),
            jax.ShapeDtypeStruct((8, width), jnp.float32),
        ]
        + [jax.ShapeDtypeStruct(x, jnp.bfloat16) for x in sums],
        compiler_params=pltpu.CompilerParams(
            dimension_semantics=("arbitrary",), vmem_limit_bytes=VMEM_LIMIT
        ),
        cost_estimate=pl.CostEstimate(
            flops=6 * entries * width * (2 * width + 5 * units), bytes_accessed=16 << 20, transcendentals=0
        ),
        name="units_backward",
    )(places.astype(jnp.int32), grad, hidden, attended, *weights, norm_rows)


def slot_backward_kernel(
    first, last, pieces_ref, mixed_ref, probs_ref, attended_grad_ref, hidden_grad_ref, weight_ref, norm_ref,
    later_ref, *refs,
):
    if first:
        pieces_grad_ref, input_grad_ref, norm_grad_ref, total, norm_total = refs
    else:
        _, total_ref, pieces_grad_ref, input_grad_ref, norm_grad_ref, total, norm_total = refs
    step_at = pl.program_id(0)
    entries, slots, width = pieces_ref.shape
    rows = entries * slots
    tall = (entries, slots, width)

    @pl.when(step_at == 0)
    def start():
        norm_total[...] = jnp.zeros_like(norm_total)
        norm_total[0:8, :] = later_ref[...]
        total[...] = jnp.zeros_like(total) if first else total_ref[...]

    hat, inverse = normalize(pieces_ref[...].astype(jnp.float32).reshape(rows, width))
    low = to_low(hat * norm_ref[0:1, :] + norm_ref[1:2, :])
    scale = HHD ** (-0.5)
    query, keys, values = [
        mixed_ref[:, part * width : (part + 1) * width].astype(jnp.float32).reshape(tall) for part in range(3)
    ]
    probs = probs_ref[...]
    grad_attended = jnp.broadcast_to(attended_grad_ref[...].astype(jnp.float32)[:, None, :], tall)
    grad_probs = head_sums((grad_attended * values).reshape(rows, width), head_marks(width, False))
    moved = probs * grad_probs.reshape(probs.shape)
    grad_scores = to_low(moved - probs * jnp.sum(moved, axis=1, keepdims=True))
    marks = head_marks(width, True)
    spread = matmul(grad_scores.reshape(rows, PAIR), marks).reshape(tall) * scale
    first_slot = lax.broadcasted_iota(jnp.int32, tall, 1) == 0
    grad_query = jnp.where(first_slot, jnp.sum(spread * keys, axis=1, keepdims=True), 0.0)
    grad_keys = spread * query[:, 0:1, :]
    grad_values = matmul(to_low(probs.reshape(rows, PAIR)), marks).reshape(tall) * grad_attended
    grad_normed = jnp.zeros((rows, width), jnp.float32)
    for part, grad in enumerate((grad_query, grad_keys, grad_values)):
        span = slice(part * width, (part + 1) * width)
        grad_low = to_low(grad.reshape(rows, width))
        total[:, span] += matmul_first(low, grad_low)
        grad_normed = grad_normed + matmul_last(grad_low, weight_ref[:, span])
    norm_total[0:1, :] += jnp.sum(grad_normed * hat, axis=0, keepdims=True)
    norm_total[1:2, :] += jnp.sum(grad_normed, axis=0, keepdims=True)
    grad_pieces = norm_back(grad_normed, norm_ref[0:1, :], hat, inverse).reshape(tall)
    hidden_grad = jnp.broadcast_to(hidden_grad_ref[...][:, None, :], tall)
    pieces_grad_ref[...] = to_low(grad_pieces + jnp.where(first_slot, hidden_grad, 0.0))

    @pl.when(step_at == pl.num_programs(0) - 1)
    def finish():
        norm_grad_ref[...] = norm_total[0:8, :]
        if last:
            input_grad_ref[:, : 3 * width] = to_low(total[...])
            input_grad_ref[:, 3 * width :] = to_low(norm_total[...].T)
        else:
            input_grad_ref[...] = total[...]


def slot_backward(at, parts, held, saved, grads, in_weight, norm_rows):
    pieces, mixed, probs = saved
    pieces_grad, total, norm_grad = held
    entries, slots, width = pieces.shape
    first, last = at == 0, at == parts - 1
    part = min(ENTRY_BLOCK, entries // parts)
    steps = entries // parts // part
    whole = lambda shape: pl.BlockSpec(shape, lambda i: (0,) * len(shape))
    tall = pl.BlockSpec((part, slots, width), lambda i: (i + at * steps, 0, 0))
    flat = pl.BlockSpec((part, width), lambda i: (i + at * steps, 0))
    total_shape = (
        jax.ShapeDtypeStruct((width, 3 * width + PAIR), jnp.bfloat16)
        if last
        else jax.ShapeDtypeStruct((width, 3 * width), jnp.float32)
    )
    in_specs = [
        tall,
        pl.BlockSpec((part * slots, 3 * width), lambda i: (i + at * steps, 0)),
        pl.BlockSpec((part, slots, PAIR), lambda i: (i + at * steps, 0, 0)),
        flat,
        flat,
        whole(in_weight.shape),
        whole(norm_rows.shape),
        whole(norm_grad.shape),
    ]
    operands = [pieces, mixed, probs, *grads, in_weight, norm_rows, norm_grad]
    if not first:
        in_specs += [pl.BlockSpec(memory_space=pl.ANY), whole(total.shape)]
        operands += [pieces_grad, total]
    return pl.pallas_call(
        functools.partial(slot_backward_kernel, first, last),
        grid=(steps,),
        in_specs=in_specs,
        out_specs=[tall, whole(total_shape.shape), whole(norm_grad.shape)],
        out_shape=[
            jax.ShapeDtypeStruct(pieces.shape, jnp.bfloat16),
            total_shape,
            jax.ShapeDtypeStruct(norm_grad.shape, jnp.float32),
        ],
        input_output_aliases={} if first else {len(operands) - 2: 0},
        scratch_shapes=[
            pltpu.VMEM((width, 3 * width), jnp.float32),
            pltpu.VMEM((PAIR, width), jnp.float32),
        ],
        compiler_params=pltpu.CompilerParams(
            dimension_semantics=("arbitrary",), vmem_limit_bytes=VMEM_LIMIT
        ),
        cost_estimate=pl.CostEstimate(
            flops=entries * slots * width // parts,
            bytes_accessed=entries * slots // parts,
            transcendentals=0,
        ),
        name="slot_backward",
    )(*operands)


def feed_forward_kernel(
    rows_ref, other_ref, rise_ref, rise_other_ref, hidden_ref, gate_ref, up_ref, down_ref,
    gate_rows, up_rows, down_columns, grad_ref, dense_ref, rows, rise, active, grad_gate, grad_up,
):
    at = pl.program_id(0)
    half = rows_ref.shape[0]
    step = gate_ref.shape[1]
    tiles = active.shape[1] // step

    @pl.when(at == 0)
    def start():
        rows[:half, :] = rows_ref[...]
        rows[half:, :] = other_ref[...]
        rise[:half, :] = rise_ref[...]
        rise[half:, :] = rise_other_ref[...]

    @pl.when(at < tiles)
    def units():
        gate = matmul(rows[...], gate_ref[...])
        up = matmul(rows[...], up_ref[...])
        rising = matmul_last(rise[...], down_ref[...])
        sign = 1.0 / (1.0 + jnp.exp(-gate))
        silu = gate * sign
        span = pl.ds(pl.multiple_of(at * step, step), step)
        active[:, span] = to_low(silu * up)
        grad_up[:, span] = to_low(rising * silu)
        grad_gate[:, span] = to_low(rising * up * (sign * (1.0 + gate * (1.0 - sign))))

    @pl.when(at >= tiles)
    def columns():
        dense = matmul(active[...], down_columns[...])
        grad = matmul_last(grad_gate[...], gate_rows[...]) + matmul_last(grad_up[...], up_rows[...])
        grad_ref[...] = to_low(grad)
        dense_ref[:half, :] = to_low(dense[:half] + hidden_ref[...])
        dense_ref[half:, :] = to_low(dense[half:])


def feed_forward(rows, other, upstream, hidden, info, gate_weight, up_weight, down_weight):
    half, width = rows.shape
    units = gate_weight.shape[1]
    step = UNIT_STEP
    tiles = units // step
    column = COLUMN_STEP
    fixed_rows = pl.BlockSpec((half, width), lambda i, s: (0, 0), pipeline_mode=pl.Buffered(1))
    early = lambda i: jnp.minimum(i, tiles - 1)
    late = lambda i: jnp.maximum(i - tiles, 0)
    tall = (2 * half, width)
    out = pl.BlockSpec((2 * half, column), lambda i, s: (0, late(i)))
    return pl.pallas_call(
        lambda info, *refs: feed_forward_kernel(*refs),
        grid_spec=pltpu.PrefetchScalarGridSpec(
            num_scalar_prefetch=1,
            grid=(tiles + width // column,),
            in_specs=[
                fixed_rows,
                fixed_rows,
                pl.BlockSpec((half, width), lambda i, s: (s[0], 0), pipeline_mode=pl.Buffered(1)),
                pl.BlockSpec((half, width), lambda i, s: (s[1], 0), pipeline_mode=pl.Buffered(1)),
                pl.BlockSpec((half, column), lambda i, s: (0, late(i))),
                pl.BlockSpec((width, step), lambda i, s: (0, early(i))),
                pl.BlockSpec((width, step), lambda i, s: (0, early(i))),
                pl.BlockSpec((step, width), lambda i, s: (early(i), 0)),
                pl.BlockSpec((column, units), lambda i, s: (late(i), 0)),
                pl.BlockSpec((column, units), lambda i, s: (late(i), 0)),
                pl.BlockSpec((units, column), lambda i, s: (0, late(i))),
            ],
            out_specs=[out, out],
            scratch_shapes=[
                pltpu.VMEM(tall, jnp.bfloat16),
                pltpu.VMEM(tall, jnp.bfloat16),
                *[pltpu.VMEM((2 * half, units), jnp.bfloat16)] * 3,
            ],
        ),
        out_shape=[jax.ShapeDtypeStruct(tall, jnp.bfloat16)] * 2,
        compiler_params=pltpu.CompilerParams(
            dimension_semantics=("arbitrary",), vmem_limit_bytes=VMEM_LIMIT
        ),
        cost_estimate=pl.CostEstimate(
            flops=34 * half * width * units, bytes_accessed=12 * width * units, transcendentals=0
        ),
        name="feed_forward",
    )(
        info, rows, other, upstream, upstream, hidden, gate_weight, up_weight, down_weight,
        gate_weight, up_weight, down_weight,
    )


def fixed(shape):
    return pl.BlockSpec(shape, lambda *_: (0,) * len(shape), pipeline_mode=pl.Buffered(1))


def root_mean(value):
    return lax.rsqrt(jnp.mean(value * value, axis=-1, keepdims=True) + EPS)


def root_mean_back(grad, gain, value):
    scaled = grad * gain
    inverse = root_mean(value)
    along = jnp.mean(value * scaled, axis=-1, keepdims=True)
    return inverse * scaled - value * (inverse * inverse * inverse * along)


def project_kernel(with_queries, info, chosen_ref, embed_ref, gain_ref, pair_own, pair_near, pair_far, *refs):
    embedded = to_low(matmul(chosen_ref[...], embed_ref[...]))
    value = embedded.astype(jnp.float32)
    low = to_low(value * root_mean(value) * gain_ref[...])
    pair_ref = refs[-3] if with_queries else refs[-1]
    at = 0
    for ref in (pair_own, pair_near, pair_far):
        pair_ref[:, at : at + ref.shape[1]] = matmul(low, ref[...])
        at += ref.shape[1]
    if not with_queries:
        return
    near_ref, mid_a, mid_b, far_a, far_b, _, embedded_ref, query_ref = refs
    embedded_ref[...] = embedded
    near = near_ref.shape[1]
    step = mid_a.shape[1]
    half = mid_a.shape[0]
    query_ref[:, :near] = matmul(low, near_ref[...])
    for start, upper, lower in ((near, mid_a, mid_b), (near + step, far_a, far_b)):
        query_ref[:, start : start + step] = matmul(low[:, :half], upper[...]) + matmul(
            low[:, half:], lower[...]
        )


def project(info, chosen, embed, gain, pair_weights, query_weights, pair_before):
    rows, width = chosen.shape
    block = rows // 2
    wide = embed.shape[1]
    row = pl.BlockSpec((block, wide), lambda i, s: (i, 0))
    pairs = sum(weight.shape[1] for weight in pair_weights)
    before = [] if pair_before is None else [pair_before]
    more = bool(query_weights)
    return pl.pallas_call(
        functools.partial(project_kernel, more),
        grid_spec=pltpu.PrefetchScalarGridSpec(
            num_scalar_prefetch=1,
            grid=(2,),
            in_specs=[
                pl.BlockSpec((block, width), lambda i, s: (i, 0)),
                fixed(embed.shape),
                fixed((1, wide)),
                *[fixed(weight.shape) for weight in pair_weights],
                *[fixed(weight.shape) for weight in query_weights],
                *[pl.BlockSpec(memory_space=pl.ANY)] * len(before),
            ],
            out_specs=[pl.BlockSpec((block, pairs), lambda i, s: (s[i], 0))] + [row, row] * more,
        ),
        out_shape=[jax.ShapeDtypeStruct((2 * rows, pairs), jnp.float32)]
        + [
            jax.ShapeDtypeStruct((rows, wide), jnp.bfloat16),
            jax.ShapeDtypeStruct((rows, wide), jnp.float32),
        ]
        * more,
        input_output_aliases={7: 0} if before else {},
        compiler_params=pltpu.CompilerParams(
            dimension_semantics=("arbitrary",), vmem_limit_bytes=VMEM_LIMIT
        ),
        cost_estimate=pl.CostEstimate(flops=1 << 30, bytes_accessed=1 << 20, transcendentals=0),
        name="project",
    )(info, chosen, embed, gain.reshape(1, -1), *pair_weights, *query_weights, *before)


def output_kernel(rows_ref, embedded_ref, gain_ref, near_ref, mid_a, mid_b, far_a, far_b, hidden_ref, low_ref):
    total = embedded_ref[...].astype(jnp.float32)
    at = 0
    for ref in (near_ref, mid_a, mid_b, far_a, far_b):
        total = total + matmul(rows_ref[:, at : at + ref.shape[0]], ref[...])
        at += ref.shape[0]
    hidden_ref[...] = total
    low_ref[...] = to_low(total * root_mean(total) * gain_ref[...])


def output_project(part, rows, embedded, gain, weights):
    block, wide = rows.shape
    spec = pl.BlockSpec((block, wide), lambda i: (0, 0))
    return pl.pallas_call(
        output_kernel,
        grid=(1,),
        in_specs=[
            spec,
            pl.BlockSpec((block, wide), lambda i: (part, 0)),
            fixed((1, wide)),
            *[fixed(weight.shape) for weight in weights],
        ],
        out_specs=[spec, spec],
        out_shape=[
            jax.ShapeDtypeStruct((block, wide), jnp.float32),
            jax.ShapeDtypeStruct((block, wide), jnp.bfloat16),
        ],
        compiler_params=pltpu.CompilerParams(
            dimension_semantics=("arbitrary",), vmem_limit_bytes=VMEM_LIMIT
        ),
        cost_estimate=pl.CostEstimate(flops=4 << 30, bytes_accessed=12 << 20, transcendentals=0),
        name="output_project",
    )(rows, embedded, gain.reshape(1, -1), *weights)


def hidden_backward_kernel(
    info, here_ref, came_ref, hidden_ref, rising_ref, gain_ref, near_ref, mid_a, mid_b, far_a, far_b,
    grad_ref, rows_ref,
):
    grad = here_ref[...].astype(jnp.float32) + came_ref[...].astype(jnp.float32)
    total = rising_ref[...].astype(jnp.float32) + root_mean_back(grad, gain_ref[...], hidden_ref[...])
    grad_ref[...] = total
    low = to_low(total)
    at = 0
    for ref in (near_ref, mid_a, mid_b, far_a, far_b):
        rows_ref[:, at : at + ref.shape[0]] = to_low(matmul_last(low, ref[...]))
        at += ref.shape[0]


def hidden_backward(info, here, came, hidden, upstream, gain, weights):
    block, wide = hidden.shape
    spec = pl.BlockSpec((block, wide), lambda i, s: (0, 0))
    return pl.pallas_call(
        hidden_backward_kernel,
        grid_spec=pltpu.PrefetchScalarGridSpec(
            num_scalar_prefetch=1,
            grid=(1,),
            in_specs=[
                spec,
                spec,
                spec,
                pl.BlockSpec((block, wide), lambda i, s: (s[0], 0)),
                fixed((1, wide)),
                *[fixed(weight.shape) for weight in weights],
            ],
            out_specs=[spec, spec],
        ),
        out_shape=[
            jax.ShapeDtypeStruct((block, wide), jnp.float32),
            jax.ShapeDtypeStruct((block, wide), jnp.bfloat16),
        ],
        compiler_params=pltpu.CompilerParams(
            dimension_semantics=("arbitrary",), vmem_limit_bytes=VMEM_LIMIT
        ),
        cost_estimate=pl.CostEstimate(flops=4 << 30, bytes_accessed=14 << 20, transcendentals=0),
        name="hidden_backward",
    )(info, here, came, hidden, upstream, gain.reshape(1, -1), *weights)


def embed_backward_kernel(
    info, query_ref, own_ref, came_ref, short_ref, cos_ref, sin_ref, first_ref, second_ref, embedded_ref, gain_ref,
    embed_ref, near_ref, mid_a, mid_b, far_a, far_b, pair_own, pair_near, pair_far, grad_ref, token_ref,
):
    total = None
    weights = [pair_own[:, :PAIR], pair_own[:, PAIR:], pair_near[...], pair_far[...]]
    for group, weight in enumerate(weights):
        head = info[2 + group]
        short = jnp.where(pl.program_id(0) == 0, short_ref[head].astype(jnp.float32), 0.0)
        pair = own_ref[head] + came_ref[head].astype(jnp.float32) + short
        low = to_low(turn_left(pair, cos_ref[...], -sin_ref[...]))
        term = matmul_last(low, weight)
        total = term if total is None else total + term
    near = near_ref.shape[1]
    step = mid_a.shape[1]
    half = mid_a.shape[0]
    total = total + matmul_last(query_ref[:, :near], near_ref[...])
    mid = query_ref[:, near : near + step]
    far = query_ref[:, near + step : near + 2 * step]
    spread = jnp.concatenate(
        [
            matmul_last(mid, mid_a[...]) + matmul_last(far, far_a[...]),
            matmul_last(mid, mid_b[...]) + matmul_last(far, far_b[...]),
        ],
        axis=1,
    )
    value = embedded_ref[...].astype(jnp.float32)
    hidden = jnp.where(pl.program_id(0) == 0, first_ref[...], second_ref[...])
    grad = to_low(hidden + root_mean_back(total + spread, gain_ref[...], value))
    grad_ref[...] = grad
    token_ref[...] = to_low(matmul_last(grad, embed_ref[...]))


def embed_backward(
    info, query_grad, own, came, short, tables, hidden_grads, embedded, gain, embed, query_weights, pair_weights
):
    rows, wide = embedded.shape
    block = rows // 2
    heads = own.shape[0]
    row = pl.BlockSpec((block, wide), lambda i, s: (i, 0))
    once = pl.BlockSpec((block, wide), lambda i, s: (0, 0))
    pair = pl.BlockSpec((heads, block, PAIR), lambda i, s: (0, i, 0))
    table = pl.BlockSpec((block, PAIR), lambda i, s: (s[i], 0))
    return pl.pallas_call(
        embed_backward_kernel,
        grid_spec=pltpu.PrefetchScalarGridSpec(
            num_scalar_prefetch=1,
            grid=(2,),
            in_specs=[
                row, pair, pair, pl.BlockSpec((heads, block, PAIR), lambda i, s: (0, 0, 0)), table, table, once, once, row, fixed((1, wide)), fixed(embed.shape),
                *[fixed(weight.shape) for weight in (*query_weights, *pair_weights)],
            ],
            out_specs=[row, pl.BlockSpec((block, embed.shape[0]), lambda i, s: (i, 0))],
        ),
        out_shape=[
            jax.ShapeDtypeStruct((rows, wide), jnp.bfloat16),
            jax.ShapeDtypeStruct((rows, embed.shape[0]), jnp.bfloat16),
        ],
        compiler_params=pltpu.CompilerParams(
            dimension_semantics=("arbitrary",), vmem_limit_bytes=VMEM_LIMIT
        ),
        cost_estimate=pl.CostEstimate(flops=12 << 30, bytes_accessed=20 << 20, transcendentals=0),
        name="embed_backward",
    )(
        info, query_grad, own, came, short, tables[0], tables[1], *hidden_grads, embedded, gain.reshape(1, -1), embed,
        *query_weights, *pair_weights,
    )


def own_route(own, local_vocab):
    places = jnp.arange(own.shape[0], dtype=jnp.int32)
    same = own[:, None] == own[None, :]
    repeated = jnp.any(same & (places[:, None] > places[None, :]), axis=1)
    owner = own // local_vocab
    before = (owner[:, None] == owner[None, :]) & (own[None, :] < own[:, None])
    rank = jnp.sum((before & jnp.logical_not(repeated)[None, :]).astype(jnp.int32), axis=1)
    return (rank, owner)


def asked_of_me(asked, me, local_vocab):
    entries = me * local_vocab + jnp.arange(local_vocab, dtype=jnp.int32)
    present = jnp.any(asked[:, :, None] == entries[None, None, :], axis=1)
    places = jnp.arange(local_vocab, dtype=jnp.int32)
    lower = places[:, None] < places[None, :]
    standing = matmul(present.astype(jnp.bfloat16), lower.astype(jnp.bfloat16)).astype(jnp.int32)
    return (present, standing)


def sender_choice(present, standing, turn, capacity):
    place = jnp.arange(capacity, dtype=jnp.int32)
    slot = jnp.where(place < capacity - 1, turn * (capacity - 1) + place, -1)
    chosen = present[:, None, :] & (standing[:, None, :] == slot[None, :, None])
    return chosen.astype(jnp.bfloat16).reshape(present.shape[0] * capacity, present.shape[1])


def taker_choice(own_rank, own_owner, turn, capacity, devices):
    inside = own_rank - turn * (capacity - 1)
    valid = (inside >= 0) & (inside < capacity - 1)
    place = jnp.where(valid, own_owner * capacity + inside, -1)
    return (place[:, None] == jnp.arange(devices * capacity, dtype=jnp.int32)[None, :]).astype(
        jnp.bfloat16
    )


def exchange(value):
    return lax.all_to_all(value, ("dp", "mp"), 0, 0, tiled=True)


def ordered_blocks(first, own_two, other_two):
    return jnp.where(
        first,
        jnp.concatenate([own_two[0], other_two[0], other_two[1], own_two[1]], axis=0),
        jnp.concatenate([other_two[0], own_two[0], own_two[1], other_two[1]], axis=0),
    )


def body(
    pieces,
    counts,
    token_index,
    hyper_input,
    hyper_output,
    hyper_expand,
    hyper_reduce,
    hyper_norms,
    embed_weight,
    attention_gain,
    dense_gain,
    frozen_query_weight,
    frozen_key_weight,
    frozen_value_weight,
    frozen_output_weight,
    gate_weight,
    up_weight,
    down_weight,
    upstream,
):
    local_vocab = pieces.shape[0]
    mp_count = lax.axis_size("mp")
    devices = lax.axis_size("dp") * mp_count
    mp_index = lax.axis_index("mp")
    me = lax.axis_index("dp") * mp_count + mp_index
    core = (me >> 1) & 1
    lead = mp_index == 0
    bits = log2_of(devices)
    far_bits = list(range(bits - 1, 1, -1))
    length = token_index.shape[0]
    block = length // BLOCK_PARTS
    capacity = max(16, length // devices)

    norm_count = hyper_norms.shape[1]
    in_width = hyper_input.shape[1]
    norm_lanes = jnp.pad(hyper_norms, ((0, 0), (0, PAIR - norm_count)))
    cut = token_index.reshape(BLOCK_PARTS, block)
    own_tokens = jnp.where(
        lead, jnp.concatenate([cut[0], cut[3]]), jnp.concatenate([cut[1], cut[2]])
    )
    digits = jnp.concatenate([own_tokens // PAIR, own_tokens % PAIR]).astype(jnp.bfloat16)
    digits = digits.reshape(hyper_input.shape[0], -1)
    digit_width = digits.shape[1]
    digit_lanes = jnp.pad(digits, ((0, 0), (0, -digit_width % PAIR)))
    kv_local = frozen_key_weight.shape[1] // HEAD_WIDTH
    key_own = jnp.concatenate(
        [
            weight[:, at * HEAD_WIDTH : (at + 1) * HEAD_WIDTH]
            for at in range(kv_local)
            for weight in (frozen_key_weight, frozen_value_weight)
        ],
        axis=1,
    )
    key_near = swap(lax.dynamic_slice_in_dim(key_own, core * PAIR, PAIR, 1), 1, devices)
    query_cut = frozen_query_weight.shape[1] // 2
    side = (me >> 2) & 1
    half_in = frozen_query_weight.shape[0] // 2
    query_slice = lax.dynamic_slice(
        frozen_query_weight, (side * half_in, core * query_cut), (half_in, query_cut)
    )
    half_out = query_cut // 2
    output_slice = lax.dynamic_slice_in_dim(
        frozen_output_weight, core * query_cut + side * half_out, half_out, 0
    )
    count_rows = jnp.broadcast_to(counts[:, None, None], (counts.shape[0], 1, PAIR))
    early_x = far_bits[:1] + [0] + far_bits[1:] + [1]
    late_y = far_bits[:-1] + [0] + far_bits[-1:] + [1]
    gathers = [
        (jnp.concatenate([hyper_input, norm_lanes, digit_lanes], axis=1), late_y),
        (jnp.concatenate([hyper_output, hyper_expand], axis=1), late_y),
        (hyper_reduce, early_x),
    ]
    gather_held = [x for x, _ in gathers]

    def send(which, at):
        return swap(gather_held[which], 1 << gathers[which][1][at], devices)

    def join(which, came, at):
        order = gathers[which][1]
        return gather_join(gather_held[which], came, order[at], order[:at], me)

    for at in range(bits - 3):
        gather_held = [join(which, send(which, at), at) for which in range(3)]
        if at == bits - 4:
            gather_held, key_near, query_slice, output_slice, count_rows = lax.optimization_barrier(
                (gather_held, key_near, query_slice, output_slice, count_rows)
            )
            key_far = swap(key_near, 2, devices)
    later_came = [send(which, bits - 3) for which in (1, 2)]
    gather_held[0] = join(0, send(0, bits - 3), bits - 3)
    begun = gather_held[:1]
    in_held = join(0, send(0, bits - 2), bits - 2)
    in_held, later_came = lax.optimization_barrier((in_held, later_came))
    gather_held = [in_held] + [join(which, came, bits - 3) for which, came in zip((1, 2), later_came)]
    later_came = [send(which, bits - 2) for which in (1, 2)]
    in_came = send(0, bits - 1)
    in_weight = join(0, in_came, bits - 1)
    small = gather_join(
        in_held[:, in_width + PAIR :], in_came[:, in_width + PAIR :], late_y[-1], late_y[:-1], me
    )
    embed_full = lax.all_gather(embed_weight, ("dp", "mp"), axis=0, tiled=True)
    all_digits = small[:, :digit_width].reshape(devices, 2, 2 * block)
    all_digits = all_digits.astype(jnp.int32)
    asked = all_digits[:, 0] * PAIR + all_digits[:, 1]

    query_slice, *_ = lax.optimization_barrier((query_slice, *begun))
    query_near = swap(query_slice, 1, devices)

    def by_side(own, other):
        return [jnp.where(side == 0, own, other), jnp.where(side == 0, other, own)]

    other_base = (1 - mp_index) * kv_local
    head_order = [mp_index * kv_local, mp_index * kv_local + 1, other_base + core, other_base + 1 - core]

    slot_mixed, slot_probs, hyper_attended, lead_rows, norm_rows = slot_attention(
        pieces, count_rows, in_weight
    )
    asked, _ = lax.optimization_barrier((asked, hyper_attended))
    hyper_attended, embed_full, later_came, query_near = lax.optimization_barrier(
        (hyper_attended, embed_full, later_came, query_near)
    )
    last = late_y[-1]

    def joined(which, parts):
        order = gathers[which][1]
        halves = [gather_join(*parts[at : at + 2], order[-2], order[:-2], me) for at in (0, 2)]
        return gather_join(*halves, last, order[:-1], me)

    later_parts = [(gather_held[which], came) for which, came in zip((1, 2), later_came)]
    later_parts = [(*own, *[swap(x, 1 << last, devices) for x in own]) for own in later_parts]
    together = hyper_input.shape[0] * 2 % 16 == 0
    if together:
        forward_weights = later_parts
    else:
        forward_weights = [[joined(which, later_parts[which - 1])] for which in (1, 2)]
    query_far_row = swap(query_near, 4, devices)
    output_slice, _ = lax.optimization_barrier((output_slice, query_near))
    output_near = swap(output_slice, 1, devices)
    places = jnp.stack([core, side])
    pooled, hyper_hidden = units_forward(
        devices // 8, places, hyper_attended, lead_rows, *forward_weights, norm_rows
    )
    _, query_far_row = lax.optimization_barrier((pooled, query_far_row))
    present, standing = asked_of_me(asked, me, local_vocab)
    own_rank, own_owner = own_route(lax.dynamic_index_in_dim(asked, me, 0, False), local_vocab)
    most = jnp.max(jnp.sum(present.astype(jnp.int32), axis=1))
    needed = ((most + capacity - 2) // (capacity - 1)).astype(jnp.float32)

    def fetch(turn):
        sent = matmul(sender_choice(present, standing, turn, capacity), pooled)
        sent = sent.reshape(devices, capacity, pooled.shape[1])
        free = lax.broadcasted_iota(jnp.int32, sent.shape, 1) == capacity - 1
        sent = to_low(jnp.where(free, needed, sent)).reshape(devices * capacity, pooled.shape[1])
        came = exchange(sent)
        picked = matmul(taker_choice(own_rank, own_owner, turn, capacity, devices), came)
        return (to_low(picked), came)

    chosen_own, came = fetch(0)
    query_near = by_side(query_near, query_far_row)
    query_far = [swap(x, 2, devices) for x in query_near]
    chosen_own, came, query_far, output_near = lax.optimization_barrier(
        (chosen_own, came, query_far, output_near)
    )
    output_far_row = swap(output_near, 4, devices)
    needs = came.reshape(devices, capacity, pooled.shape[1])[:, capacity - 1, 0]
    rounds = jnp.max(needs.astype(jnp.float32)).astype(jnp.int32)
    chosen_own = lax.fori_loop(1, rounds, lambda turn, chosen: chosen + fetch(turn)[0], chosen_own)
    chosen_other = swap(chosen_own, 1, devices)

    tables = rope_tables(length)
    own_at = (mp_index, 3 - mp_index)
    own_base = tuple(at * block for at in own_at)
    other_start = ((1 - mp_index) * block, (2 + mp_index) * block)
    infos = [jnp.stack([at] + head_order).astype(jnp.int32) for at in own_at]

    other_at = (1 - mp_index, 2 + mp_index)
    query_weights = (frozen_query_weight, *query_near, *query_far)
    pair_weights = (key_own, key_near, key_far)
    own_info = jnp.stack(own_at).astype(jnp.int32)
    other_info = jnp.stack(other_at).astype(jnp.int32)
    pair_pre, embedded, queries = project(
        own_info, chosen_own, embed_full, attention_gain, pair_weights, query_weights, None
    )
    (pair_pre,) = project(
        other_info, chosen_other, embed_full, attention_gain, pair_weights, (), pair_pre
    )
    pair_pre, output_far_row = lax.optimization_barrier((pair_pre, output_far_row))
    output_near = by_side(output_near, output_far_row)
    output_far = [swap(x, 2, devices) for x in output_near]
    output_weights = (frozen_output_weight, *output_near, *output_far)
    spans = (2 * block, length)

    sums = [None, None]
    lows = [None, None]
    hidden_parts = [None, None]
    second_low = [None, None]
    second_other = [None, None]
    for part in (1, 0):
        flat, lows[part], sums[part] = attention_forward(
            infos[part], queries, pair_pre, tables, part, spans[part]
        )
        hidden_parts[part], second_low[part] = output_project(
            part, flat, embedded, dense_gain, output_weights
        )
        second_other[part] = swap(second_low[part], 1, devices)
        pair_pre, second_low[part] = lax.optimization_barrier((pair_pre, second_low[part]))

    second_low, second_other[1] = lax.optimization_barrier((second_low, second_other[1]))
    dense_rows = [None, None]
    second_came = [None, None]
    for part in (1, 0):
        info = jnp.stack([own_at[part], other_at[part]]).astype(jnp.int32)
        grad_second, dense_rows[part] = feed_forward(
            second_low[part], second_other[part], upstream, hidden_parts[part], info,
            gate_weight, up_weight, down_weight,
        )
        second_came[part] = (grad_second[:block], swap(grad_second[block:], 1, devices))

    query_grad = None
    grad_hidden = [None, None]
    pair_grads = [None, None]
    for part in (1, 0):
        here, came = second_came[part]
        if part == 1:
            here, came, dense_rows[0] = lax.optimization_barrier((here, came, dense_rows[0]))
        else:
            here, came, query_grad = lax.optimization_barrier((here, came, query_grad))
        grad_hidden[part], grad_attended = hidden_backward(
            infos[part], here, came, hidden_parts[part], upstream, dense_gain, output_weights
        )
        query_grad, pair_grads[part] = attention_backward(
            infos[part], lows[part], grad_attended, sums[part], pair_pre, tables, part, spans[part], query_grad
        )

    def pick_block(value, at):
        return lax.dynamic_slice_in_dim(value, at * block, block, 1)

    came_long = swap(
        to_low(jnp.concatenate([pick_block(pair_grads[1], at) for at in other_at], axis=1)), 1, devices
    )
    pair_grads[0], came_long = lax.optimization_barrier((pair_grads[0], came_long))
    came_short = swap(to_low(pick_block(pair_grads[0], other_at[0])), 1, devices)
    pair_own = jnp.concatenate(
        [
            pick_block(pair_grads[1], own_at[0]) + pick_block(pair_grads[0], own_at[0]),
            pick_block(pair_grads[1], own_at[1]),
        ],
        axis=1,
    )

    share = upstream.shape[1] // mp_count

    def columns(value, index):
        return lax.dynamic_slice_in_dim(value, index * share, share, 1)

    leaving = [columns(dense_rows[part], 1 - mp_index) for part in range(2)]
    _, leaving[0] = lax.optimization_barrier((came_short, leaving[0]))
    dense_came = [swap(x, 1, devices) for x in leaving]

    embedded_grad_low, token_grad = embed_backward(
        jnp.stack([*own_at, *head_order]).astype(jnp.int32), query_grad, pair_own, came_long, came_short, tables, grad_hidden, embedded,
        attention_gain, embed_full, query_weights, pair_weights,
    )
    own_out = []
    other_out = []
    for part in range(2):
        kept = columns(dense_rows[part], mp_index).astype(jnp.float32)
        arrived = dense_came[part].astype(jnp.float32)
        own_out.append(to_low(kept[:block] + arrived[block:]))
        other_out.append(to_low(kept[block:] + arrived[:block]))
    model_out = ordered_blocks(lead, own_out, other_out)
    embed_grad = to_low(matmul_first(chosen_own, embedded_grad_low))

    def give_back(turn, total):
        taker = taker_choice(own_rank, own_owner, turn, capacity, devices)
        leaving = matmul_first(taker, token_grad).astype(jnp.bfloat16)
        came = exchange(leaving)
        return total + matmul_first(sender_choice(present, standing, turn, capacity), came)

    grad_pooled = give_back(0, jnp.zeros(pooled.shape, jnp.float32))
    grad_pooled = lax.fori_loop(1, rounds, give_back, grad_pooled)

    back_order = [1, 0] + far_bits[::-1]

    def scatter(held, order, at):
        return scatter_send(held, order[at], order[at + 1 :], me, devices)

    embed_held = scatter_add(*scatter(embed_grad, back_order, 0))
    embed_held, grad_pooled = lax.optimization_barrier((embed_held, grad_pooled))
    embed_held = scatter_add(*scatter(embed_held, back_order, 1))
    hidden_grad, attended_grad, later_norms, *unit_sums = units_backward(
        devices // 8, places, grad_pooled, hyper_hidden, hyper_attended, *forward_weights, norm_rows
    )
    hidden_grad, embed_held = lax.optimization_barrier((hidden_grad, embed_held))
    held = [embed_held, *([unit_sums[:2], unit_sums[2:]] if together else unit_sums)]
    turned_order = [back_order[0], back_order[2], back_order[3], back_order[1]] + back_order[4:]
    orders = [back_order, back_order, turned_order]
    ahead = [2, 0, 0]

    def depart(at):
        moving = []
        for x, order, skip in zip(held, orders, ahead):
            if at + skip >= bits:
                moving.append((x, None))
            elif isinstance(x, list):
                moving.append((x[0], swap(x[1], 1 << order[0], devices)))
            else:
                moving.append(scatter(x, order, at + skip))
        return moving

    def arrive(moving):
        return [x if came is None else scatter_add(x, came) for x, came in moving]

    slots_saved = (pieces, slot_mixed, slot_probs)
    slots_held = (None, None, later_norms)
    for part in range(SLOT_PARTS):
        moving = depart(part)
        slots_held = slot_backward(
            part, SLOT_PARTS, slots_held, slots_saved, (attended_grad, hidden_grad), in_weight, norm_rows
        )
        slots_held, moving = lax.optimization_barrier((tuple(slots_held), moving))
        held = arrive(moving)
    pieces_grad, input_grad, _ = slots_held
    input_held = input_grad
    moving = depart(SLOT_PARTS)
    for at in range(bits):
        input_held = scatter_add(*scatter(input_held, back_order, at))
        if at > 0:
            _, moving = lax.optimization_barrier((input_held, moving))
            held = arrive(moving)
            moving = depart(SLOT_PARTS + at)
    held = arrive(moving)
    embed_own, wide_own, reduce_own, input_own = (*held, input_held)
    out_width = hyper_output.shape[1]
    return (
        model_out,
        pieces_grad,
        input_own[:, :in_width],
        wide_own[:, :out_width],
        wide_own[:, out_width:],
        reduce_own,
        input_own[:, in_width : in_width + norm_count],
        embed_own,
    )


def solution(mesh):
    return jax.shard_map(
        body,
        mesh=mesh,
        in_specs=(
            P(("dp", "mp"), None, None),
            P(("dp", "mp")),
            P("dp"),
            P(("dp", "mp"), None),
            P(("dp", "mp"), None),
            P(("dp", "mp"), None),
            P(("dp", "mp"), None),
            P(("dp", "mp"), None),
            P(("dp", "mp"), None),
            P(),
            P(),
            P(None, "mp"),
            P(None, "mp"),
            P(None, "mp"),
            P("mp", None),
            P(None, "mp"),
            P(None, "mp"),
            P("mp", None),
            P("dp", None),
        ),
        out_specs=(
            P("dp", "mp"),
            P(("dp", "mp"), None, None),
            P(("dp", "mp"), None),
            P(("dp", "mp"), None),
            P(("dp", "mp"), None),
            P(("dp", "mp"), None),
            P(("dp", "mp"), None),
            P(("dp", "mp"), None),
        ),
        check_vma=False,
    )
```

```python
import functools

import jax
import jax.numpy as jnp
import numpy as np
from jax import lax
from jax.experimental import pallas as pl
from jax.experimental.pallas import tpu as pltpu
from jax.sharding import PartitionSpec as P

HEAD_WIDTH = 64
HHD = 64
BLOCK_PARTS = 4
UNIT = 512
PAIR = 2 * HEAD_WIDTH
VMEM_LIMIT = 48 << 20
ENTRY_BLOCK = 64
SLOT_PARTS = 2
UNIT_STEP = 256
COLUMN_STEP = 256
UNIT_ROWS = 512


EPS = 1e-05
NEGATIVE = -1000000000.0


def matmul(left, right):
    return jnp.dot(left, right, preferred_element_type=jnp.float32)


def matmul_first(left, right):
    return lax.dot_general(
        left, right, (((0,), (0,)), ((), ())), preferred_element_type=jnp.float32
    )


def matmul_last(left, right):
    return lax.dot_general(
        left, right, (((1,), (1,)), ((), ())), preferred_element_type=jnp.float32
    )


def log2_of(number):
    return number.bit_length() - 1


def swap(value, mask, devices):
    return lax.ppermute(value, ("dp", "mp"), [(d, d ^ mask) for d in range(devices)])


def gather_join(held, arrived, bit, done, me):
    rows, width = held.shape
    outer = 1 << sum(other > bit for other in done)
    held, arrived = [x.reshape(outer, rows // outer, width) for x in (held, arrived)]
    joined = jnp.where(
        ((me >> bit) & 1) == 1,
        jnp.concatenate([arrived, held], axis=1),
        jnp.concatenate([held, arrived], axis=1),
    )
    return joined.reshape(2 * rows, width)


def scatter_send(held, bit, left, me, devices):
    rows, width = held.shape
    outer = 1 << sum(other > bit for other in left)
    parts = held.reshape(outer, 2, rows // outer // 2, width)
    mine = (me >> bit) & 1

    def part(at):
        return lax.dynamic_slice_in_dim(parts, at, 1, 1).reshape(rows // 2, width)

    return (part(mine), swap(to_low(part(1 - mine)), 1 << bit, devices))


def scatter_add(staying, came):
    return staying.astype(jnp.float32) + came.astype(jnp.float32)


def lanes(shape):
    return lax.broadcasted_iota(jnp.int32, shape, len(shape) - 1)


def half_swap(value):
    quarter = HEAD_WIDTH // 2
    upper = (lanes(value.shape) & quarter) != 0
    return jnp.where(
        upper, pltpu.roll(value, quarter, 1), pltpu.roll(value, PAIR - quarter, 1)
    )


def to_low(value):
    return value.astype(jnp.bfloat16)


def causal_of(rows):
    return lax.broadcasted_iota(jnp.int32, (rows, rows), 0) <= lax.broadcasted_iota(
        jnp.int32, (rows, rows), 1
    )


def masked_scores(keys, low, causal):
    rows = causal.shape[0]
    length = keys.shape[0]
    last = jnp.where(causal, matmul_last(keys[length - rows :, :], low), NEGATIVE)
    return [matmul_last(keys[: length - rows, :], low), last] if length > rows else [last]


def for_lengths(block_at, rows, length, work):
    for count in (length - rows, length):
        pl.when(block_at == count // rows - 1)(functools.partial(work, count))


def turn_left(value, cosine, sine):
    left = lanes(value.shape) < HEAD_WIDTH
    return jnp.where(left, value * cosine + half_swap(value) * sine, value)


def head_views(pair_ref, cos_ref, sin_ref, rows):
    span = slice(0, rows)
    turned = to_low(turn_left(pair_ref[span, :], cos_ref[span, :], sin_ref[span, :])).astype(jnp.float32)
    other = pltpu.roll(turned, HEAD_WIDTH, 1)
    left = lanes(turned.shape) < HEAD_WIDTH
    return (
        jnp.where(left, turned, 0.0),
        jnp.where(left, 0.0, other),
        jnp.where(left, other, 0.0),
        jnp.where(left, 0.0, turned),
    )


def attention_forward_kernel(
    info, query_ref, pair_ref, cos_pair, sin_pair, cos_ref, sin_ref,
    out_ref, low_ref, lse_ref, even, odd, across,
):
    rows = query_ref.shape[0]
    causal = causal_of(rows)

    def work(length):
        span = slice(0, length)
        key_left, key_right, value_left, _ = head_views(pair_ref, cos_pair, sin_pair, length)
        even[span, :] = to_low(key_left)
        odd[span, :] = to_low(key_right)
        across[:, span] = to_low(value_left.T[:HEAD_WIDTH])
        for pair in range(query_ref.shape[1] // PAIR):
            columns = slice(pair * PAIR, (pair + 1) * PAIR)
            query = query_ref[:, columns]
            turned = to_low(query * cos_ref[...] + half_swap(query) * sin_ref[...])
            low = to_low(turned.astype(jnp.float32) * HEAD_WIDTH ** (-0.5))
            low_ref[:, columns] = low
            outs = []
            for at, keys in enumerate((even, odd)):
                scores = masked_scores(keys[span, :], low, causal)
                highest = functools.reduce(
                    jnp.maximum, [jnp.max(x, axis=0, keepdims=True) for x in scores]
                )
                weights = [jnp.exp(x - highest) for x in scores]
                total = sum(jnp.sum(x, axis=0, keepdims=True) for x in weights)
                out = 0.0
                start = 0
                for x in weights:
                    out = out + matmul(across[:, start : start + x.shape[0]], to_low(x))
                    start += x.shape[0]
                outs.append(out / total)
                lse_ref[0, 2 * pair + at : 2 * pair + at + 1, :] = highest + jnp.log(total)
            out_ref[:, columns] = to_low(jnp.concatenate(outs, axis=0).T)

    for_lengths(info[0], rows, pair_ref.shape[0], work)


def attention_backward_kernel(
    info, low_ref, grad_ref, lse_ref, pair_ref, cos_pair, sin_pair, cos_ref, sin_ref, *refs,
):
    query_ref, pair_grad_ref, even, odd, value_even, value_odd, across = refs[-11:-4]
    key_even, key_odd, sum_even, sum_odd = refs[-4:]
    rows = low_ref.shape[0]
    causal = causal_of(rows)

    def work(length):
        span = slice(0, length)
        key_left, key_right, value_left, value_right = head_views(pair_ref, cos_pair, sin_pair, length)
        even[span, :] = to_low(key_left)
        odd[span, :] = to_low(key_right)
        value_even[span, :] = to_low(value_left)
        value_odd[span, :] = to_low(value_right)
        across[:, span] = to_low(key_left.T[:HEAD_WIDTH])
        sides = ((even, value_even, key_even, sum_even), (odd, value_odd, key_odd, sum_odd))
        for total in (key_even, key_odd, sum_even, sum_odd):
            total[span, :] = jnp.zeros((length, PAIR), jnp.float32)
        for pair in range(low_ref.shape[1] // PAIR):
            columns = slice(pair * PAIR, (pair + 1) * PAIR)
            low = low_ref[:, columns]
            grad = grad_ref[:, columns]
            outs = []
            for at, (keys, values, key_total, value_total) in enumerate(sides):
                lse = lse_ref[0, 2 * pair + at : 2 * pair + at + 1, :]
                probs = [jnp.exp(x - lse) for x in masked_scores(keys[span, :], low, causal)]
                moved = []
                start = 0
                for x in probs:
                    part = slice(start, start + x.shape[0])
                    value_total[part, :] += matmul(to_low(x), grad)
                    moved.append(x * matmul_last(values[part, :], grad))
                    start += x.shape[0]
                mean = sum(jnp.sum(x, axis=0, keepdims=True) for x in moved)
                out = 0.0
                start = 0
                for x, y in zip(probs, moved):
                    part = slice(start, start + x.shape[0])
                    grad_scores = to_low(y - x * mean)
                    key_total[part, :] += matmul(grad_scores, low)
                    out = out + matmul(across[:, part], grad_scores)
                    start += x.shape[0]
                outs.append(out)
            turned = jnp.concatenate(outs, axis=0).T * HEAD_WIDTH ** (-0.5)
            query_ref[:, columns] = to_low(turned * cos_ref[...] - half_swap(turned) * sin_ref[...])
        left = lanes((length, PAIR)) < HEAD_WIDTH
        pair_grad_ref[0, span, :] = jnp.where(
            left,
            key_even[span, :] + pltpu.roll(key_odd[span, :], HEAD_WIDTH, 1),
            pltpu.roll(sum_even[span, :], HEAD_WIDTH, 1) + sum_odd[span, :],
        )
        if length < pair_ref.shape[0]:
            rest = (pair_ref.shape[0] - length, PAIR)
            pair_grad_ref[0, length:, :] = jnp.zeros(rest, jnp.float32)

    for_lengths(info[0], rows, pair_ref.shape[0], work)


def attention_specs(part, rows, length, first=0):
    span = (rows, 4 * PAIR)
    return {
        "table_pair": pl.BlockSpec((length, PAIR), lambda g, s: (0, 0)),
        "table": pl.BlockSpec((rows, PAIR), lambda g, s: (s[0], 0)),
        "pair": pl.BlockSpec((length, PAIR), lambda g, s: (0, g + first)),
        "part": pl.BlockSpec(span, lambda g, s: (part, g + first)),
        "wide": pl.BlockSpec(span, lambda g, s: (0, g + first)),
        "sums": pl.BlockSpec((1, 8, rows), lambda g, s: (g + first, 0, 0)),
    }


def attention_cost(rows, length, heads, matmuls):
    work = 20 * rows * length * heads * HEAD_WIDTH * matmuls
    return pl.CostEstimate(
        flops=work, bytes_accessed=16 * rows * heads * HEAD_WIDTH, transcendentals=rows * length * heads
    )


def attention_forward(info, queries, pair_pre, tables, part, length):
    cosine, sine = tables
    rows = cosine.shape[0] // BLOCK_PARTS
    heads = 4 * 4 * PAIR // HEAD_WIDTH
    spec = attention_specs(part, rows, length)
    half = pltpu.VMEM((length, PAIR), jnp.bfloat16)
    wide = (rows, heads * HEAD_WIDTH)
    return pl.pallas_call(
        attention_forward_kernel,
        grid_spec=pltpu.PrefetchScalarGridSpec(
            num_scalar_prefetch=1,
            grid=(4,),
            in_specs=[
                spec["part"], spec["pair"],
                spec["table_pair"], spec["table_pair"], spec["table"], spec["table"],
            ],
            out_specs=[spec["wide"], spec["wide"], spec["sums"]],
            scratch_shapes=[
                half, half,
                pltpu.VMEM((HEAD_WIDTH, length), jnp.bfloat16),
            ],
        ),
        out_shape=[
            jax.ShapeDtypeStruct(wide, jnp.bfloat16),
            jax.ShapeDtypeStruct(wide, jnp.bfloat16),
            jax.ShapeDtypeStruct((4, 8, rows), jnp.float32),
        ],
        compiler_params=pltpu.CompilerParams(
            dimension_semantics=("arbitrary",), vmem_limit_bytes=VMEM_LIMIT
        ),
        cost_estimate=attention_cost(rows, length, heads, 2),
        name="attention_forward",
    )(info, queries, pair_pre, cosine, sine, cosine, sine)


def attention_backward(info, low, grad, sums, pair_pre, tables, part, length, groups, before):
    first, count = groups
    cosine, sine = tables
    rows = cosine.shape[0] // BLOCK_PARTS
    heads = low.shape[1] // HEAD_WIDTH
    spec = attention_specs(part, rows, length, first)
    half = pltpu.VMEM((length, PAIR), jnp.bfloat16)
    full = pltpu.VMEM((length, PAIR), jnp.float32)
    return pl.pallas_call(
        attention_backward_kernel,
        grid_spec=pltpu.PrefetchScalarGridSpec(
            num_scalar_prefetch=1,
            grid=(count,),
            in_specs=[
                spec["wide"], spec["wide"], spec["sums"], spec["pair"],
                spec["table_pair"], spec["table_pair"], spec["table"], spec["table"],
            ]
            + [pl.BlockSpec(memory_space=pl.ANY)] * len(before),
            out_specs=[spec["part"], pl.BlockSpec((1, length, PAIR), lambda g, s: (s[1 + g + first], 0, 0))],
            scratch_shapes=[
                half, half, half, half,
                pltpu.VMEM((HEAD_WIDTH, length), jnp.bfloat16),
                full, full, full, full,
            ],
        ),
        out_shape=[
            jax.ShapeDtypeStruct((2 * rows, low.shape[1]), jnp.bfloat16),
            jax.ShapeDtypeStruct((4, length, PAIR), jnp.float32),
        ],
        input_output_aliases={9 + at: at for at in range(len(before))},
        compiler_params=pltpu.CompilerParams(
            dimension_semantics=("arbitrary",), vmem_limit_bytes=VMEM_LIMIT
        ),
        cost_estimate=attention_cost(rows, length, heads, 5 if count == 4 else 0),
        name="attention_backward",
    )(info, low, grad, sums, pair_pre, cosine, sine, cosine, sine, *before)


def rope_tables(length):
    positions = np.arange(length, dtype=np.float32)
    inverse = 10000.0 ** (-np.arange(0, HEAD_WIDTH, 2, dtype=np.float32) / HEAD_WIDTH)
    angles = positions[:, None] * inverse.astype(np.float32)[None, :]
    cosine, sine = np.cos(angles).astype(np.float32), np.sin(angles).astype(np.float32)
    return (
        jnp.asarray(np.concatenate([cosine] * 4, axis=1)),
        jnp.asarray(np.concatenate([-sine, sine, -sine, sine], axis=1)),
    )


def head_marks(width, transposed):
    shape = (PAIR, width) if transposed else (width, PAIR)
    head_at, column_at = (0, 1) if transposed else (1, 0)
    head = lax.broadcasted_iota(jnp.int32, shape, head_at)
    column = lax.broadcasted_iota(jnp.int32, shape, column_at)
    return (column // HHD == head).astype(jnp.bfloat16)


def head_sums(value, marks):
    high = to_low(value)
    rest = to_low(value - high.astype(jnp.float32))
    return matmul(high, marks) + matmul(rest, marks)


def normalize(value):
    centered = value - jnp.mean(value, axis=-1, keepdims=True)
    inverse = lax.rsqrt(jnp.mean(centered * centered, axis=-1, keepdims=True) + EPS)
    return (centered * inverse, inverse)


def norm_back(grad, gain, hat, inverse):
    scaled = grad * gain
    mean = jnp.mean(scaled, axis=-1, keepdims=True)
    along = jnp.mean(scaled * hat, axis=-1, keepdims=True)
    return inverse * (scaled - mean - hat * along)


def slot_attention_kernel(
    pieces_ref, counts_ref, weight_ref, mixed_ref, probs_ref, attended_ref, lead_ref, norm_ref
):
    entries, slots, width = pieces_ref.shape

    @pl.when(pl.program_id(0) == 0)
    def norms():
        norm_ref[...] = weight_ref[:, 3 * width : 3 * width + PAIR].astype(jnp.float32).T[:8]

    rows = entries * slots
    tall = (entries, slots, width)
    pieces = pieces_ref[...].astype(jnp.float32)
    hat, _ = normalize(pieces.reshape(rows, width))
    low = to_low(hat * norm_ref[0:1, :] + norm_ref[1:2, :])
    mixed = []
    for part in range(3):
        span = slice(part * width, (part + 1) * width)
        value = to_low(matmul(low, weight_ref[:, span]))
        mixed_ref[:, span] = value
        mixed.append(value.astype(jnp.float32).reshape(tall))
    query, keys, values = mixed
    marks = head_marks(width, False)
    product = (keys * query[:, 0:1, :]).reshape(rows, width)
    scores = head_sums(product, marks).reshape(entries, slots, PAIR) * HHD ** (-0.5)
    live = lax.broadcasted_iota(jnp.int32, scores.shape, 1) < counts_ref[...]
    scores = jnp.where(live, scores, NEGATIVE)
    weight = jnp.exp(scores - jnp.max(scores, axis=1, keepdims=True))
    probs = weight / jnp.sum(weight, axis=1, keepdims=True)
    probs_ref[...] = probs
    spread = matmul(to_low(probs.reshape(rows, PAIR)), head_marks(width, True)).reshape(tall)
    attended_ref[...] = to_low(jnp.sum(spread * values, axis=1))
    lead_ref[...] = pieces[:, 0, :]


def slot_attention(pieces, counts, in_weight):
    entries, slots, width = pieces.shape
    part = min(ENTRY_BLOCK, entries)
    whole = lambda shape: pl.BlockSpec(shape, lambda i: (0,) * len(shape))
    tall = pl.BlockSpec((part, slots, width), lambda i: (i, 0, 0))
    flat = pl.BlockSpec((part, width), lambda i: (i, 0))
    return pl.pallas_call(
        slot_attention_kernel,
        grid=(entries // part,),
        in_specs=[
            tall,
            pl.BlockSpec((part, 1, PAIR), lambda i: (i, 0, 0)),
            whole(in_weight.shape),
        ],
        out_specs=[
            pl.BlockSpec((part * slots, 3 * width), lambda i: (i, 0)),
            pl.BlockSpec((part, slots, PAIR), lambda i: (i, 0, 0)),
            flat,
            flat,
            whole((8, width)),
        ],
        out_shape=[
            jax.ShapeDtypeStruct((entries * slots, 3 * width), jnp.bfloat16),
            jax.ShapeDtypeStruct((entries, slots, PAIR), jnp.float32),
            jax.ShapeDtypeStruct((entries, width), jnp.bfloat16),
            jax.ShapeDtypeStruct((entries, width), jnp.float32),
            jax.ShapeDtypeStruct((8, width), jnp.float32),
        ],
        compiler_params=pltpu.CompilerParams(
            dimension_semantics=("arbitrary",), vmem_limit_bytes=VMEM_LIMIT
        ),
        cost_estimate=pl.CostEstimate(
            flops=entries * slots * width, bytes_accessed=entries * slots, transcendentals=0
        ),
        name="slot_attention",
    )(pieces, counts, in_weight)


def gelu_of(value):
    cdf = 0.5 * (1.0 + lax.erf(value * np.float32(0.5 ** 0.5)))
    return (value * cdf, cdf)


def gelu_slope(value, cdf):
    return cdf + value * (jnp.exp(-0.5 * value * value) * np.float32((2 * np.pi) ** -0.5))


def place_parts(split, places, wholes, parts):
    @pl.when(pl.program_id(0) == 0)
    def join():
        core, side = places[0], places[1]
        for index, whole in enumerate(wholes):
            for at, part in enumerate(parts[4 * index : 4 * index + 4]):
                rows = part.shape[0] // split
                place = 2 * (side if at % 2 == 0 else 1 - side) + (core if at < 2 else 1 - core)
                for group in range(split):
                    start = pl.multiple_of((4 * group + place) * rows, rows)
                    whole[pl.ds(start, rows), :] = part[group * rows : (group + 1) * rows, :]


def units_forward_kernel(
    split, places, attended_ref, lead_ref, *refs
):
    *weights, norm_ref, pooled_ref, hidden_ref = refs[: 11 if split else 5]
    if not split:
        wide_weight_ref, reduce_ref = weights
    else:
        wide_weight_ref, reduce_ref = refs[11:]

        place_parts(split, places, (wide_weight_ref, reduce_ref), weights)

    width = lead_ref.shape[1]
    hidden = lead_ref[...] + matmul(attended_ref[...], wide_weight_ref[:, :width])
    hidden_ref[...] = hidden
    hat, _ = normalize(hidden)
    second = to_low(hat * norm_ref[2:3, :] + norm_ref[3:4, :])
    total = hidden
    units = reduce_ref.shape[0]
    step = min(UNIT, units)
    for at in range(0, units, step):
        active, _ = gelu_of(matmul(second, wide_weight_ref[:, width + at : width + at + step]))
        total = total + matmul(to_low(active), reduce_ref[at : at + step, :])
    pooled_ref[...] = to_low(total)


def units_forward(groups, places, attended, lead, wide_weight, reduce_weight, norm_rows):
    entries, width = attended.shape
    part = min(UNIT_ROWS, entries)
    split = groups if len(wide_weight) == 4 else 0
    whole = lambda shape: pl.BlockSpec(shape, lambda i, s: (0,) * len(shape))
    flat = pl.BlockSpec((part, width), lambda i, s: (i, 0))
    weights = [*wide_weight, *reduce_weight]
    joined = [
        pltpu.VMEM((4 * parts[0].shape[0], parts[0].shape[1]), jnp.bfloat16)
        for parts in (wide_weight, reduce_weight)
    ]
    return pl.pallas_call(
        functools.partial(units_forward_kernel, split),
        grid_spec=pltpu.PrefetchScalarGridSpec(
            num_scalar_prefetch=1,
            grid=(entries // part,),
            in_specs=[flat, flat] + [whole(x.shape) for x in (*weights, norm_rows)],
            out_specs=[flat, flat],
            scratch_shapes=joined if split else [],
        ),
        out_shape=[
            jax.ShapeDtypeStruct((entries, width), jnp.bfloat16),
            jax.ShapeDtypeStruct((entries, width), jnp.float32),
        ],
        compiler_params=pltpu.CompilerParams(
            dimension_semantics=("arbitrary",), vmem_limit_bytes=VMEM_LIMIT
        ),
        cost_estimate=pl.CostEstimate(
            flops=entries * width, bytes_accessed=entries * width, transcendentals=0
        ),
        name="units_forward",
    )(places.astype(jnp.int32), attended, lead, *weights, norm_rows)


def units_backward_kernel(split, places, grad_ref, hidden_ref, attended_ref, *refs):
    *weights, norm_ref, hidden_grad_ref, attended_grad_ref, norm_grad_ref = refs[: 12 if split else 6]
    if split:
        *sums, wide_total, reduce_total, wide_weight_ref, reduce_ref = refs[12:]
        place_parts(split, places, (wide_weight_ref, reduce_ref), weights)
    else:
        wide_weight_ref, reduce_ref = weights
        *sums, wide_total, reduce_total = refs[6:]
    step_at = pl.program_id(0)
    width = hidden_ref.shape[1]
    units = reduce_ref.shape[0]

    @pl.when(step_at == 0)
    def start():
        wide_total[...] = jnp.zeros_like(wide_total)
        reduce_total[...] = jnp.zeros_like(reduce_total)
        norm_grad_ref[...] = jnp.zeros_like(norm_grad_ref)

    grad = grad_ref[...]
    grad_low = to_low(grad)
    hat, inverse = normalize(hidden_ref[...])
    second = to_low(hat * norm_ref[2:3, :] + norm_ref[3:4, :])
    grad_normed = jnp.zeros_like(grad)
    step = min(UNIT, units)
    for at in range(0, units, step):
        span = slice(at, at + step)
        wide_span = slice(width + at, width + at + step)
        expanded = matmul(second, wide_weight_ref[:, wide_span])
        active, cdf = gelu_of(expanded)
        reduce_total[span, :] += matmul_first(to_low(active), grad_low)
        grad_active = matmul_last(grad_low, reduce_ref[span, :])
        grad_expanded = to_low(grad_active * gelu_slope(expanded, cdf))
        wide_total[:, wide_span] += matmul_first(second, grad_expanded)
        grad_normed = grad_normed + matmul_last(grad_expanded, wide_weight_ref[:, wide_span])
    norm_grad_ref[2:3, :] += jnp.sum(grad_normed * hat, axis=0, keepdims=True)
    norm_grad_ref[3:4, :] += jnp.sum(grad_normed, axis=0, keepdims=True)
    hidden_grad = grad + norm_back(grad_normed, norm_ref[2:3, :], hat, inverse)
    hidden_grad_ref[...] = hidden_grad
    hidden_low = to_low(hidden_grad)
    wide_total[:, :width] += matmul_first(attended_ref[...], hidden_low)
    attended_grad_ref[...] = to_low(matmul_last(hidden_low, wide_weight_ref[:, :width]))

    @pl.when(step_at == pl.num_programs(0) - 1)
    def finish():
        if not split:
            sums[0][...] = to_low(wide_total[...])
            sums[1][...] = to_low(reduce_total[...])
            return
        core = places[0]
        for total, halves in ((wide_total, sums[:2]), (reduce_total, sums[2:])):
            rows = halves[0].shape[0] // (2 * split)
            for half, place in zip(halves, (core, 1 - core)):
                for group in range(2 * split):
                    start = pl.multiple_of((2 * group + place) * rows, rows)
                    half[group * rows : (group + 1) * rows, :] = to_low(total[pl.ds(start, rows), :])


def units_backward(groups, places, grad, hidden, attended, wide_weight, reduce_weight, norm_rows):
    entries, width = attended.shape
    part = min(UNIT_ROWS, entries)
    split = groups if len(wide_weight) == 4 else 0
    weights = [*wide_weight, *reduce_weight]
    units = reduce_weight[0].shape[0] * len(reduce_weight)
    whole = lambda shape: pl.BlockSpec(shape, lambda i, s: (0,) * len(shape))
    flat = pl.BlockSpec((part, width), lambda i, s: (i, 0))
    wide = (width, width + units)
    tall = (units, width)
    half = lambda shape: (shape[0] // 2, shape[1])
    sums = [half(wide)] * 2 + [half(tall)] * 2 if split else [wide, tall]
    return pl.pallas_call(
        functools.partial(units_backward_kernel, split),
        grid_spec=pltpu.PrefetchScalarGridSpec(
            num_scalar_prefetch=1,
            grid=(entries // part,),
            in_specs=[flat, flat, flat] + [fixed(x.shape) for x in (*weights, norm_rows)],
            out_specs=[flat, flat, whole((8, width))] + [whole(x) for x in sums],
            scratch_shapes=[pltpu.VMEM(wide, jnp.float32), pltpu.VMEM(tall, jnp.float32)]
            + [pltpu.VMEM(x, jnp.bfloat16) for x in (wide, tall)] * bool(split),
        ),
        out_shape=[
            jax.ShapeDtypeStruct((entries, width), jnp.float32),
            jax.ShapeDtypeStruct((entries, width), jnp.bfloat16),
            jax.ShapeDtypeStruct((8, width), jnp.float32),
        ]
        + [jax.ShapeDtypeStruct(x, jnp.bfloat16) for x in sums],
        compiler_params=pltpu.CompilerParams(
            dimension_semantics=("arbitrary",), vmem_limit_bytes=VMEM_LIMIT
        ),
        cost_estimate=pl.CostEstimate(
            flops=6 * entries * width * (2 * width + 5 * units), bytes_accessed=16 << 20, transcendentals=0
        ),
        name="units_backward",
    )(places.astype(jnp.int32), grad, hidden, attended, *weights, norm_rows)


def slot_backward_kernel(
    first, last, pieces_ref, mixed_ref, probs_ref, attended_grad_ref, hidden_grad_ref, weight_ref, norm_ref,
    later_ref, *refs,
):
    if first:
        pieces_grad_ref, input_grad_ref, norm_grad_ref, total, norm_total = refs
    else:
        _, total_ref, pieces_grad_ref, input_grad_ref, norm_grad_ref, total, norm_total = refs
    step_at = pl.program_id(0)
    entries, slots, width = pieces_ref.shape
    rows = entries * slots
    tall = (entries, slots, width)

    @pl.when(step_at == 0)
    def start():
        norm_total[...] = jnp.zeros_like(norm_total)
        norm_total[0:8, :] = later_ref[...]
        total[...] = jnp.zeros_like(total) if first else total_ref[...]

    hat, inverse = normalize(pieces_ref[...].astype(jnp.float32).reshape(rows, width))
    low = to_low(hat * norm_ref[0:1, :] + norm_ref[1:2, :])
    scale = HHD ** (-0.5)
    query, keys, values = [
        mixed_ref[:, part * width : (part + 1) * width].astype(jnp.float32).reshape(tall) for part in range(3)
    ]
    probs = probs_ref[...]
    grad_attended = jnp.broadcast_to(attended_grad_ref[...].astype(jnp.float32)[:, None, :], tall)
    grad_probs = head_sums((grad_attended * values).reshape(rows, width), head_marks(width, False))
    moved = probs * grad_probs.reshape(probs.shape)
    grad_scores = to_low(moved - probs * jnp.sum(moved, axis=1, keepdims=True))
    marks = head_marks(width, True)
    spread = matmul(grad_scores.reshape(rows, PAIR), marks).reshape(tall) * scale
    first_slot = lax.broadcasted_iota(jnp.int32, tall, 1) == 0
    grad_query = jnp.where(first_slot, jnp.sum(spread * keys, axis=1, keepdims=True), 0.0)
    grad_keys = spread * query[:, 0:1, :]
    grad_values = matmul(to_low(probs.reshape(rows, PAIR)), marks).reshape(tall) * grad_attended
    grad_normed = jnp.zeros((rows, width), jnp.float32)
    for part, grad in enumerate((grad_query, grad_keys, grad_values)):
        span = slice(part * width, (part + 1) * width)
        grad_low = to_low(grad.reshape(rows, width))
        total[:, span] += matmul_first(low, grad_low)
        grad_normed = grad_normed + matmul_last(grad_low, weight_ref[:, span])
    norm_total[0:1, :] += jnp.sum(grad_normed * hat, axis=0, keepdims=True)
    norm_total[1:2, :] += jnp.sum(grad_normed, axis=0, keepdims=True)
    grad_pieces = norm_back(grad_normed, norm_ref[0:1, :], hat, inverse).reshape(tall)
    hidden_grad = jnp.broadcast_to(hidden_grad_ref[...][:, None, :], tall)
    pieces_grad_ref[...] = to_low(grad_pieces + jnp.where(first_slot, hidden_grad, 0.0))

    @pl.when(step_at == pl.num_programs(0) - 1)
    def finish():
        norm_grad_ref[...] = norm_total[0:8, :]
        if last:
            input_grad_ref[:, : 3 * width] = to_low(total[...])
            input_grad_ref[:, 3 * width :] = to_low(norm_total[...].T)
        else:
            input_grad_ref[...] = total[...]


def slot_backward(at, parts, held, saved, grads, in_weight, norm_rows):
    pieces, mixed, probs = saved
    pieces_grad, total, norm_grad = held
    entries, slots, width = pieces.shape
    first, last = at == 0, at == parts - 1
    part = min(ENTRY_BLOCK, entries // parts)
    steps = entries // parts // part
    whole = lambda shape: pl.BlockSpec(shape, lambda i: (0,) * len(shape))
    tall = pl.BlockSpec((part, slots, width), lambda i: (i + at * steps, 0, 0))
    flat = pl.BlockSpec((part, width), lambda i: (i + at * steps, 0))
    total_shape = (
        jax.ShapeDtypeStruct((width, 3 * width + PAIR), jnp.bfloat16)
        if last
        else jax.ShapeDtypeStruct((width, 3 * width), jnp.float32)
    )
    in_specs = [
        tall,
        pl.BlockSpec((part * slots, 3 * width), lambda i: (i + at * steps, 0)),
        pl.BlockSpec((part, slots, PAIR), lambda i: (i + at * steps, 0, 0)),
        flat,
        flat,
        whole(in_weight.shape),
        whole(norm_rows.shape),
        whole(norm_grad.shape),
    ]
    operands = [pieces, mixed, probs, *grads, in_weight, norm_rows, norm_grad]
    if not first:
        in_specs += [pl.BlockSpec(memory_space=pl.ANY), whole(total.shape)]
        operands += [pieces_grad, total]
    return pl.pallas_call(
        functools.partial(slot_backward_kernel, first, last),
        grid=(steps,),
        in_specs=in_specs,
        out_specs=[tall, whole(total_shape.shape), whole(norm_grad.shape)],
        out_shape=[
            jax.ShapeDtypeStruct(pieces.shape, jnp.bfloat16),
            total_shape,
            jax.ShapeDtypeStruct(norm_grad.shape, jnp.float32),
        ],
        input_output_aliases={} if first else {len(operands) - 2: 0},
        scratch_shapes=[
            pltpu.VMEM((width, 3 * width), jnp.float32),
            pltpu.VMEM((PAIR, width), jnp.float32),
        ],
        compiler_params=pltpu.CompilerParams(
            dimension_semantics=("arbitrary",), vmem_limit_bytes=VMEM_LIMIT
        ),
        cost_estimate=pl.CostEstimate(
            flops=entries * slots * width // parts,
            bytes_accessed=entries * slots // parts,
            transcendentals=0,
        ),
        name="slot_backward",
    )(*operands)


def feed_forward_kernel(
    rows_ref, other_ref, rise_ref, rise_other_ref, hidden_ref, gate_ref, up_ref, down_ref,
    gate_rows, up_rows, down_columns, grad_ref, dense_ref, rows, rise, active, grad_gate, grad_up,
):
    at = pl.program_id(0)
    half = rows_ref.shape[0]
    step = gate_ref.shape[1]
    tiles = active.shape[1] // step

    @pl.when(at == 0)
    def start():
        rows[:half, :] = rows_ref[...]
        rows[half:, :] = other_ref[...]
        rise[:half, :] = rise_ref[...]
        rise[half:, :] = rise_other_ref[...]

    @pl.when(at < tiles)
    def units():
        gate = matmul(rows[...], gate_ref[...])
        up = matmul(rows[...], up_ref[...])
        rising = matmul_last(rise[...], down_ref[...])
        sign = 1.0 / (1.0 + jnp.exp(-gate))
        silu = gate * sign
        span = pl.ds(pl.multiple_of(at * step, step), step)
        active[:, span] = to_low(silu * up)
        grad_up[:, span] = to_low(rising * silu)
        grad_gate[:, span] = to_low(rising * up * (sign * (1.0 + gate * (1.0 - sign))))

    @pl.when(at >= tiles)
    def columns():
        dense = matmul(active[...], down_columns[...])
        grad = matmul_last(grad_gate[...], gate_rows[...]) + matmul_last(grad_up[...], up_rows[...])
        grad_ref[...] = to_low(grad)
        dense_ref[:half, :] = to_low(dense[:half] + hidden_ref[...])
        dense_ref[half:, :] = to_low(dense[half:])


def feed_forward(rows, other, upstream, hidden, info, gate_weight, up_weight, down_weight):
    half, width = rows.shape
    units = gate_weight.shape[1]
    step = UNIT_STEP
    tiles = units // step
    column = COLUMN_STEP
    fixed_rows = pl.BlockSpec((half, width), lambda i, s: (0, 0), pipeline_mode=pl.Buffered(1))
    early = lambda i: jnp.minimum(i, tiles - 1)
    late = lambda i: jnp.maximum(i - tiles, 0)
    tall = (2 * half, width)
    out = pl.BlockSpec((2 * half, column), lambda i, s: (0, late(i)))
    return pl.pallas_call(
        lambda info, *refs: feed_forward_kernel(*refs),
        grid_spec=pltpu.PrefetchScalarGridSpec(
            num_scalar_prefetch=1,
            grid=(tiles + width // column,),
            in_specs=[
                fixed_rows,
                fixed_rows,
                pl.BlockSpec((half, width), lambda i, s: (s[0], 0), pipeline_mode=pl.Buffered(1)),
                pl.BlockSpec((half, width), lambda i, s: (s[1], 0), pipeline_mode=pl.Buffered(1)),
                pl.BlockSpec((half, column), lambda i, s: (0, late(i))),
                pl.BlockSpec((width, step), lambda i, s: (0, early(i))),
                pl.BlockSpec((width, step), lambda i, s: (0, early(i))),
                pl.BlockSpec((step, width), lambda i, s: (early(i), 0)),
                pl.BlockSpec((column, units), lambda i, s: (late(i), 0)),
                pl.BlockSpec((column, units), lambda i, s: (late(i), 0)),
                pl.BlockSpec((units, column), lambda i, s: (0, late(i))),
            ],
            out_specs=[out, out],
            scratch_shapes=[
                pltpu.VMEM(tall, jnp.bfloat16),
                pltpu.VMEM(tall, jnp.bfloat16),
                *[pltpu.VMEM((2 * half, units), jnp.bfloat16)] * 3,
            ],
        ),
        out_shape=[jax.ShapeDtypeStruct(tall, jnp.bfloat16)] * 2,
        compiler_params=pltpu.CompilerParams(
            dimension_semantics=("arbitrary",), vmem_limit_bytes=VMEM_LIMIT
        ),
        cost_estimate=pl.CostEstimate(
            flops=34 * half * width * units, bytes_accessed=12 * width * units, transcendentals=0
        ),
        name="feed_forward",
    )(
        info, rows, other, upstream, upstream, hidden, gate_weight, up_weight, down_weight,
        gate_weight, up_weight, down_weight,
    )


def fixed(shape):
    return pl.BlockSpec(shape, lambda *_: (0,) * len(shape), pipeline_mode=pl.Buffered(1))


def root_mean(value):
    return lax.rsqrt(jnp.mean(value * value, axis=-1, keepdims=True) + EPS)


def root_mean_back(grad, gain, value):
    scaled = grad * gain
    inverse = root_mean(value)
    along = jnp.mean(value * scaled, axis=-1, keepdims=True)
    return inverse * scaled - value * (inverse * inverse * inverse * along)


def project_kernel(with_queries, info, chosen_ref, embed_ref, gain_ref, pair_own, pair_near, pair_far, *refs):
    embedded = to_low(matmul(chosen_ref[...], embed_ref[...]))
    value = embedded.astype(jnp.float32)
    low = to_low(value * root_mean(value) * gain_ref[...])
    pair_ref = refs[-3] if with_queries else refs[-1]
    at = 0
    for ref in (pair_own, pair_near, pair_far):
        pair_ref[:, at : at + ref.shape[1]] = matmul(low, ref[...])
        at += ref.shape[1]
    if not with_queries:
        return
    near_ref, mid_a, mid_b, far_a, far_b, _, embedded_ref, query_ref = refs
    embedded_ref[...] = embedded
    near = near_ref.shape[1]
    step = mid_a.shape[1]
    half = mid_a.shape[0]
    query_ref[:, :near] = matmul(low, near_ref[...])
    for start, upper, lower in ((near, mid_a, mid_b), (near + step, far_a, far_b)):
        query_ref[:, start : start + step] = matmul(low[:, :half], upper[...]) + matmul(
            low[:, half:], lower[...]
        )


def project(info, chosen, embed, gain, pair_weights, query_weights, pair_before):
    rows, width = chosen.shape
    block = rows // 2
    wide = embed.shape[1]
    row = pl.BlockSpec((block, wide), lambda i, s: (i, 0))
    pairs = sum(weight.shape[1] for weight in pair_weights)
    before = [] if pair_before is None else [pair_before]
    more = bool(query_weights)
    return pl.pallas_call(
        functools.partial(project_kernel, more),
        grid_spec=pltpu.PrefetchScalarGridSpec(
            num_scalar_prefetch=1,
            grid=(2,),
            in_specs=[
                pl.BlockSpec((block, width), lambda i, s: (i, 0)),
                fixed(embed.shape),
                fixed((1, wide)),
                *[fixed(weight.shape) for weight in pair_weights],
                *[fixed(weight.shape) for weight in query_weights],
                *[pl.BlockSpec(memory_space=pl.ANY)] * len(before),
            ],
            out_specs=[pl.BlockSpec((block, pairs), lambda i, s: (s[i], 0))] + [row, row] * more,
        ),
        out_shape=[jax.ShapeDtypeStruct((2 * rows, pairs), jnp.float32)]
        + [
            jax.ShapeDtypeStruct((rows, wide), jnp.bfloat16),
            jax.ShapeDtypeStruct((rows, wide), jnp.float32),
        ]
        * more,
        input_output_aliases={7: 0} if before else {},
        compiler_params=pltpu.CompilerParams(
            dimension_semantics=("arbitrary",), vmem_limit_bytes=VMEM_LIMIT
        ),
        cost_estimate=pl.CostEstimate(flops=1 << 30, bytes_accessed=1 << 20, transcendentals=0),
        name="project",
    )(info, chosen, embed, gain.reshape(1, -1), *pair_weights, *query_weights, *before)


def output_kernel(rows_ref, embedded_ref, gain_ref, near_ref, mid_a, mid_b, far_a, far_b, hidden_ref, low_ref):
    total = embedded_ref[...].astype(jnp.float32)
    at = 0
    for ref in (near_ref, mid_a, mid_b, far_a, far_b):
        total = total + matmul(rows_ref[:, at : at + ref.shape[0]], ref[...])
        at += ref.shape[0]
    hidden_ref[...] = total
    low_ref[...] = to_low(total * root_mean(total) * gain_ref[...])


def output_project(part, rows, embedded, gain, weights):
    block, wide = rows.shape
    spec = pl.BlockSpec((block, wide), lambda i: (0, 0))
    return pl.pallas_call(
        output_kernel,
        grid=(1,),
        in_specs=[
            spec,
            pl.BlockSpec((block, wide), lambda i: (part, 0)),
            fixed((1, wide)),
            *[fixed(weight.shape) for weight in weights],
        ],
        out_specs=[spec, spec],
        out_shape=[
            jax.ShapeDtypeStruct((block, wide), jnp.float32),
            jax.ShapeDtypeStruct((block, wide), jnp.bfloat16),
        ],
        compiler_params=pltpu.CompilerParams(
            dimension_semantics=("arbitrary",), vmem_limit_bytes=VMEM_LIMIT
        ),
        cost_estimate=pl.CostEstimate(flops=4 << 30, bytes_accessed=12 << 20, transcendentals=0),
        name="output_project",
    )(rows, embedded, gain.reshape(1, -1), *weights)


def hidden_backward_kernel(
    info, here_ref, came_ref, hidden_ref, rising_ref, gain_ref, near_ref, mid_a, mid_b, far_a, far_b,
    grad_ref, rows_ref,
):
    grad = here_ref[...].astype(jnp.float32) + came_ref[...].astype(jnp.float32)
    total = rising_ref[...].astype(jnp.float32) + root_mean_back(grad, gain_ref[...], hidden_ref[...])
    grad_ref[...] = total
    low = to_low(total)
    at = 0
    for ref in (near_ref, mid_a, mid_b, far_a, far_b):
        rows_ref[:, at : at + ref.shape[0]] = to_low(matmul_last(low, ref[...]))
        at += ref.shape[0]


def hidden_backward(info, here, came, hidden, upstream, gain, weights):
    block, wide = hidden.shape
    spec = pl.BlockSpec((block, wide), lambda i, s: (0, 0))
    return pl.pallas_call(
        hidden_backward_kernel,
        grid_spec=pltpu.PrefetchScalarGridSpec(
            num_scalar_prefetch=1,
            grid=(1,),
            in_specs=[
                spec,
                spec,
                spec,
                pl.BlockSpec((block, wide), lambda i, s: (s[0], 0)),
                fixed((1, wide)),
                *[fixed(weight.shape) for weight in weights],
            ],
            out_specs=[spec, spec],
        ),
        out_shape=[
            jax.ShapeDtypeStruct((block, wide), jnp.float32),
            jax.ShapeDtypeStruct((block, wide), jnp.bfloat16),
        ],
        compiler_params=pltpu.CompilerParams(
            dimension_semantics=("arbitrary",), vmem_limit_bytes=VMEM_LIMIT
        ),
        cost_estimate=pl.CostEstimate(flops=4 << 30, bytes_accessed=14 << 20, transcendentals=0),
        name="hidden_backward",
    )(info, here, came, hidden, upstream, gain.reshape(1, -1), *weights)


def embed_backward_kernel(
    info, query_ref, own_ref, came_ref, short_ref, cos_ref, sin_ref, first_ref, second_ref, embedded_ref, gain_ref,
    embed_ref, near_ref, mid_a, mid_b, far_a, far_b, pair_own, pair_near, pair_far, grad_ref, token_ref,
):
    total = None
    weights = [pair_own[:, :PAIR], pair_own[:, PAIR:], pair_near[...], pair_far[...]]
    for group, weight in enumerate(weights):
        head = info[2 + group]
        short = jnp.where(pl.program_id(0) == 0, short_ref[head].astype(jnp.float32), 0.0)
        pair = own_ref[head] + came_ref[head].astype(jnp.float32) + short
        low = to_low(turn_left(pair, cos_ref[...], -sin_ref[...]))
        term = matmul_last(low, weight)
        total = term if total is None else total + term
    near = near_ref.shape[1]
    step = mid_a.shape[1]
    half = mid_a.shape[0]
    total = total + matmul_last(query_ref[:, :near], near_ref[...])
    mid = query_ref[:, near : near + step]
    far = query_ref[:, near + step : near + 2 * step]
    spread = jnp.concatenate(
        [
            matmul_last(mid, mid_a[...]) + matmul_last(far, far_a[...]),
            matmul_last(mid, mid_b[...]) + matmul_last(far, far_b[...]),
        ],
        axis=1,
    )
    value = embedded_ref[...].astype(jnp.float32)
    hidden = jnp.where(pl.program_id(0) == 0, first_ref[...], second_ref[...])
    grad = to_low(hidden + root_mean_back(total + spread, gain_ref[...], value))
    grad_ref[...] = grad
    token_ref[...] = to_low(matmul_last(grad, embed_ref[...]))


def embed_backward(
    info, query_grad, own, came, short, tables, hidden_grads, embedded, gain, embed, query_weights, pair_weights
):
    rows, wide = embedded.shape
    block = rows // 2
    heads = own.shape[0]
    row = pl.BlockSpec((block, wide), lambda i, s: (i, 0))
    once = pl.BlockSpec((block, wide), lambda i, s: (0, 0))
    pair = pl.BlockSpec((heads, block, PAIR), lambda i, s: (0, i, 0))
    table = pl.BlockSpec((block, PAIR), lambda i, s: (s[i], 0))
    return pl.pallas_call(
        embed_backward_kernel,
        grid_spec=pltpu.PrefetchScalarGridSpec(
            num_scalar_prefetch=1,
            grid=(2,),
            in_specs=[
                row, pair, pair, pl.BlockSpec((heads, block, PAIR), lambda i, s: (0, 0, 0)), table, table, once, once, row, fixed((1, wide)), fixed(embed.shape),
                *[fixed(weight.shape) for weight in (*query_weights, *pair_weights)],
            ],
            out_specs=[row, pl.BlockSpec((block, embed.shape[0]), lambda i, s: (i, 0))],
        ),
        out_shape=[
            jax.ShapeDtypeStruct((rows, wide), jnp.bfloat16),
            jax.ShapeDtypeStruct((rows, embed.shape[0]), jnp.bfloat16),
        ],
        compiler_params=pltpu.CompilerParams(
            dimension_semantics=("arbitrary",), vmem_limit_bytes=VMEM_LIMIT
        ),
        cost_estimate=pl.CostEstimate(flops=12 << 30, bytes_accessed=20 << 20, transcendentals=0),
        name="embed_backward",
    )(
        info, query_grad, own, came, short, tables[0], tables[1], *hidden_grads, embedded, gain.reshape(1, -1), embed,
        *query_weights, *pair_weights,
    )


def own_route(own, local_vocab):
    places = jnp.arange(own.shape[0], dtype=jnp.int32)
    same = own[:, None] == own[None, :]
    repeated = jnp.any(same & (places[:, None] > places[None, :]), axis=1)
    owner = own // local_vocab
    before = (owner[:, None] == owner[None, :]) & (own[None, :] < own[:, None])
    rank = jnp.sum((before & jnp.logical_not(repeated)[None, :]).astype(jnp.int32), axis=1)
    return (rank, owner)


def asked_of_me(asked, me, local_vocab):
    entries = me * local_vocab + jnp.arange(local_vocab, dtype=jnp.int32)
    present = jnp.any(asked[:, :, None] == entries[None, None, :], axis=1)
    places = jnp.arange(local_vocab, dtype=jnp.int32)
    lower = places[:, None] < places[None, :]
    standing = matmul(present.astype(jnp.bfloat16), lower.astype(jnp.bfloat16)).astype(jnp.int32)
    return (present, standing)


def sender_choice(present, standing, turn, capacity):
    place = jnp.arange(capacity, dtype=jnp.int32)
    slot = jnp.where(place < capacity - 1, turn * (capacity - 1) + place, -1)
    chosen = present[:, None, :] & (standing[:, None, :] == slot[None, :, None])
    return chosen.astype(jnp.bfloat16).reshape(present.shape[0] * capacity, present.shape[1])


def taker_choice(own_rank, own_owner, turn, capacity, devices):
    inside = own_rank - turn * (capacity - 1)
    valid = (inside >= 0) & (inside < capacity - 1)
    place = jnp.where(valid, own_owner * capacity + inside, -1)
    return (place[:, None] == jnp.arange(devices * capacity, dtype=jnp.int32)[None, :]).astype(
        jnp.bfloat16
    )


def exchange(value):
    return lax.all_to_all(value, ("dp", "mp"), 0, 0, tiled=True)


def ordered_blocks(first, own_two, other_two):
    return jnp.where(
        first,
        jnp.concatenate([own_two[0], other_two[0], other_two[1], own_two[1]], axis=0),
        jnp.concatenate([other_two[0], own_two[0], own_two[1], other_two[1]], axis=0),
    )


def body(
    pieces,
    counts,
    token_index,
    hyper_input,
    hyper_output,
    hyper_expand,
    hyper_reduce,
    hyper_norms,
    embed_weight,
    attention_gain,
    dense_gain,
    frozen_query_weight,
    frozen_key_weight,
    frozen_value_weight,
    frozen_output_weight,
    gate_weight,
    up_weight,
    down_weight,
    upstream,
):
    local_vocab = pieces.shape[0]
    mp_count = lax.axis_size("mp")
    devices = lax.axis_size("dp") * mp_count
    mp_index = lax.axis_index("mp")
    me = lax.axis_index("dp") * mp_count + mp_index
    core = (me >> 1) & 1
    lead = mp_index == 0
    bits = log2_of(devices)
    far_bits = list(range(bits - 1, 1, -1))
    length = token_index.shape[0]
    block = length // BLOCK_PARTS
    capacity = max(16, length // devices)

    norm_count = hyper_norms.shape[1]
    in_width = hyper_input.shape[1]
    norm_lanes = jnp.pad(hyper_norms, ((0, 0), (0, PAIR - norm_count)))
    cut = token_index.reshape(BLOCK_PARTS, block)
    own_tokens = jnp.where(
        lead, jnp.concatenate([cut[0], cut[3]]), jnp.concatenate([cut[1], cut[2]])
    )
    digits = jnp.concatenate([own_tokens // PAIR, own_tokens % PAIR]).astype(jnp.bfloat16)
    digits = digits.reshape(hyper_input.shape[0], -1)
    digit_width = digits.shape[1]
    digit_lanes = jnp.pad(digits, ((0, 0), (0, -digit_width % PAIR)))
    kv_local = frozen_key_weight.shape[1] // HEAD_WIDTH
    key_own = jnp.concatenate(
        [
            weight[:, at * HEAD_WIDTH : (at + 1) * HEAD_WIDTH]
            for at in range(kv_local)
            for weight in (frozen_key_weight, frozen_value_weight)
        ],
        axis=1,
    )
    key_near = swap(lax.dynamic_slice_in_dim(key_own, core * PAIR, PAIR, 1), 1, devices)
    query_cut = frozen_query_weight.shape[1] // 2
    side = (me >> 2) & 1
    half_in = frozen_query_weight.shape[0] // 2
    query_slice = lax.dynamic_slice(
        frozen_query_weight, (side * half_in, core * query_cut), (half_in, query_cut)
    )
    half_out = query_cut // 2
    output_slice = lax.dynamic_slice_in_dim(
        frozen_output_weight, core * query_cut + side * half_out, half_out, 0
    )
    count_rows = jnp.broadcast_to(counts[:, None, None], (counts.shape[0], 1, PAIR))
    early_x = far_bits[:1] + [0] + far_bits[1:] + [1]
    late_y = far_bits[:-1] + [0] + far_bits[-1:] + [1]
    gathers = [
        (jnp.concatenate([hyper_input, norm_lanes, digit_lanes], axis=1), late_y),
        (jnp.concatenate([hyper_output, hyper_expand], axis=1), late_y),
        (hyper_reduce, early_x),
    ]
    gather_held = [x for x, _ in gathers]

    def send(which, at):
        return swap(gather_held[which], 1 << gathers[which][1][at], devices)

    def join(which, came, at):
        order = gathers[which][1]
        return gather_join(gather_held[which], came, order[at], order[:at], me)

    for at in range(bits - 3):
        gather_held = [join(which, send(which, at), at) for which in range(3)]
        if at == bits - 4:
            gather_held, key_near, query_slice, output_slice, count_rows = lax.optimization_barrier(
                (gather_held, key_near, query_slice, output_slice, count_rows)
            )
            key_far = swap(key_near, 2, devices)
    later_came = [send(which, bits - 3) for which in (1, 2)]
    gather_held[0] = join(0, send(0, bits - 3), bits - 3)
    begun = gather_held[:1]
    in_held = join(0, send(0, bits - 2), bits - 2)
    in_held, later_came = lax.optimization_barrier((in_held, later_came))
    gather_held = [in_held] + [join(which, came, bits - 3) for which, came in zip((1, 2), later_came)]
    later_came = [send(which, bits - 2) for which in (1, 2)]
    in_came = send(0, bits - 1)
    in_weight = join(0, in_came, bits - 1)
    small = gather_join(
        in_held[:, in_width + PAIR :], in_came[:, in_width + PAIR :], late_y[-1], late_y[:-1], me
    )
    embed_full = lax.all_gather(embed_weight, ("dp", "mp"), axis=0, tiled=True)
    all_digits = small[:, :digit_width].reshape(devices, 2, 2 * block)
    all_digits = all_digits.astype(jnp.int32)
    asked = all_digits[:, 0] * PAIR + all_digits[:, 1]

    query_slice, *_ = lax.optimization_barrier((query_slice, *begun))
    query_near = swap(query_slice, 1, devices)

    def by_side(own, other):
        return [jnp.where(side == 0, own, other), jnp.where(side == 0, other, own)]

    other_base = (1 - mp_index) * kv_local
    head_order = [mp_index * kv_local, mp_index * kv_local + 1, other_base + core, other_base + 1 - core]

    slot_mixed, slot_probs, hyper_attended, lead_rows, norm_rows = slot_attention(
        pieces, count_rows, in_weight
    )
    asked, _ = lax.optimization_barrier((asked, hyper_attended))
    hyper_attended, embed_full, later_came, query_near = lax.optimization_barrier(
        (hyper_attended, embed_full, later_came, query_near)
    )
    last = late_y[-1]

    def joined(which, parts):
        order = gathers[which][1]
        halves = [gather_join(*parts[at : at + 2], order[-2], order[:-2], me) for at in (0, 2)]
        return gather_join(*halves, last, order[:-1], me)

    later_parts = [(gather_held[which], came) for which, came in zip((1, 2), later_came)]
    later_parts = [(*own, *[swap(x, 1 << last, devices) for x in own]) for own in later_parts]
    together = hyper_input.shape[0] * 2 % 16 == 0
    if together:
        forward_weights = later_parts
    else:
        forward_weights = [[joined(which, later_parts[which - 1])] for which in (1, 2)]
    query_far_row = swap(query_near, 4, devices)
    output_slice, _ = lax.optimization_barrier((output_slice, query_near))
    output_near = swap(output_slice, 1, devices)
    places = jnp.stack([core, side])
    pooled, hyper_hidden = units_forward(
        devices // 8, places, hyper_attended, lead_rows, *forward_weights, norm_rows
    )
    _, query_far_row = lax.optimization_barrier((pooled, query_far_row))
    present, standing = asked_of_me(asked, me, local_vocab)
    own_rank, own_owner = own_route(lax.dynamic_index_in_dim(asked, me, 0, False), local_vocab)
    most = jnp.max(jnp.sum(present.astype(jnp.int32), axis=1))
    needed = ((most + capacity - 2) // (capacity - 1)).astype(jnp.float32)

    def fetch(turn):
        sent = matmul(sender_choice(present, standing, turn, capacity), pooled)
        sent = sent.reshape(devices, capacity, pooled.shape[1])
        free = lax.broadcasted_iota(jnp.int32, sent.shape, 1) == capacity - 1
        sent = to_low(jnp.where(free, needed, sent)).reshape(devices * capacity, pooled.shape[1])
        came = exchange(sent)
        picked = matmul(taker_choice(own_rank, own_owner, turn, capacity, devices), came)
        return (to_low(picked), came)

    chosen_own, came = fetch(0)
    query_near = by_side(query_near, query_far_row)
    query_far = [swap(x, 2, devices) for x in query_near]
    chosen_own, came, query_far, output_near = lax.optimization_barrier(
        (chosen_own, came, query_far, output_near)
    )
    output_far_row = swap(output_near, 4, devices)
    needs = came.reshape(devices, capacity, pooled.shape[1])[:, capacity - 1, 0]
    rounds = jnp.max(needs.astype(jnp.float32)).astype(jnp.int32)
    chosen_own = lax.fori_loop(1, rounds, lambda turn, chosen: chosen + fetch(turn)[0], chosen_own)
    chosen_other = swap(chosen_own, 1, devices)

    tables = rope_tables(length)
    own_at = (mp_index, 3 - mp_index)
    own_base = tuple(at * block for at in own_at)
    other_start = ((1 - mp_index) * block, (2 + mp_index) * block)
    infos = [jnp.stack([at] + head_order).astype(jnp.int32) for at in own_at]

    other_at = (1 - mp_index, 2 + mp_index)
    query_weights = (frozen_query_weight, *query_near, *query_far)
    pair_weights = (key_own, key_near, key_far)
    own_info = jnp.stack(own_at).astype(jnp.int32)
    other_info = jnp.stack(other_at).astype(jnp.int32)
    pair_pre, embedded, queries = project(
        own_info, chosen_own, embed_full, attention_gain, pair_weights, query_weights, None
    )
    (pair_pre,) = project(
        other_info, chosen_other, embed_full, attention_gain, pair_weights, (), pair_pre
    )
    pair_pre, output_far_row = lax.optimization_barrier((pair_pre, output_far_row))
    output_near = by_side(output_near, output_far_row)
    output_far = [swap(x, 2, devices) for x in output_near]
    output_weights = (frozen_output_weight, *output_near, *output_far)
    spans = (2 * block, length)

    sums = [None, None]
    lows = [None, None]
    hidden_parts = [None, None]
    second_low = [None, None]
    second_other = [None, None]
    for part in (1, 0):
        flat, lows[part], sums[part] = attention_forward(
            infos[part], queries, pair_pre, tables, part, spans[part]
        )
        hidden_parts[part], second_low[part] = output_project(
            part, flat, embedded, dense_gain, output_weights
        )
        second_other[part] = swap(second_low[part], 1, devices)
        pair_pre, second_low[part] = lax.optimization_barrier((pair_pre, second_low[part]))

    second_low, second_other[1] = lax.optimization_barrier((second_low, second_other[1]))
    dense_rows = [None, None]
    second_came = [None, None]
    for part in (1, 0):
        info = jnp.stack([own_at[part], other_at[part]]).astype(jnp.int32)
        grad_second, dense_rows[part] = feed_forward(
            second_low[part], second_other[part], upstream, hidden_parts[part], info,
            gate_weight, up_weight, down_weight,
        )
        second_came[part] = (grad_second[:block], swap(grad_second[block:], 1, devices))

    share = upstream.shape[1] // mp_count

    def columns(value, index):
        return lax.dynamic_slice_in_dim(value, index * share, share, 1)

    leaving_columns = [columns(dense_rows[part], 1 - mp_index) for part in range(2)]
    dense_came = [None, swap(leaving_columns[1], 1, devices)]

    def pick_block(value, at):
        return lax.dynamic_slice_in_dim(value, at * block, block, 1)

    query_grad = None
    grad_hidden = [None, None]
    pair_grads = [None, None]
    for part in (1, 0):
        here, came = second_came[part]
        if part == 1:
            here, came, dense_rows[0] = lax.optimization_barrier((here, came, dense_rows[0]))
        else:
            here, came, query_grad, dense_came[1] = lax.optimization_barrier(
                (here, came, query_grad, dense_came[1])
            )
        grad_hidden[part], grad_attended = hidden_backward(
            infos[part], here, came, hidden_parts[part], upstream, dense_gain, output_weights
        )
        taken = (lows[part], grad_attended, sums[part], pair_pre, tables, part, spans[part])
        if part == 1:
            query_grad, pair_grads[part] = attention_backward(infos[part], *taken, (0, 4), [])
            continue
        query_grad, pair_grads[part] = attention_backward(infos[part], *taken, (0, 2), [query_grad])
        leaving = to_low(jnp.concatenate([pick_block(pair_grads[1], at) for at in other_at], axis=1))
        leaving, pair_grads[part] = lax.optimization_barrier((leaving, pair_grads[part]))
        came_long = swap(leaving, 1, devices)
        query_grad, pair_grads[part] = attention_backward(
            infos[part], *taken, (2, 2), [query_grad, pair_grads[part]]
        )

    pair_grads[0], came_long = lax.optimization_barrier((pair_grads[0], came_long))
    came_short = swap(to_low(pick_block(pair_grads[0], other_at[0])), 1, devices)
    pair_own = jnp.concatenate(
        [
            pick_block(pair_grads[1], own_at[0]) + pick_block(pair_grads[0], own_at[0]),
            pick_block(pair_grads[1], own_at[1]),
        ],
        axis=1,
    )

    _, leaving_columns[0] = lax.optimization_barrier((came_short, leaving_columns[0]))
    dense_came[0] = swap(leaving_columns[0], 1, devices)

    embedded_grad_low, token_grad = embed_backward(
        jnp.stack([*own_at, *head_order]).astype(jnp.int32), query_grad, pair_own, came_long, came_short, tables, grad_hidden, embedded,
        attention_gain, embed_full, query_weights, pair_weights,
    )
    own_out = []
    other_out = []
    for part in range(2):
        kept = columns(dense_rows[part], mp_index).astype(jnp.float32)
        arrived = dense_came[part].astype(jnp.float32)
        own_out.append(to_low(kept[:block] + arrived[block:]))
        other_out.append(to_low(kept[block:] + arrived[:block]))
    model_out = ordered_blocks(lead, own_out, other_out)
    embed_grad = to_low(matmul_first(chosen_own, embedded_grad_low))

    def give_back(turn, total):
        taker = taker_choice(own_rank, own_owner, turn, capacity, devices)
        leaving = matmul_first(taker, token_grad).astype(jnp.bfloat16)
        came = exchange(leaving)
        return total + matmul_first(sender_choice(present, standing, turn, capacity), came)

    grad_pooled = give_back(0, jnp.zeros(pooled.shape, jnp.float32))
    grad_pooled = lax.fori_loop(1, rounds, give_back, grad_pooled)

    back_order = [1, 0] + far_bits[::-1]

    def scatter(held, order, at):
        return scatter_send(held, order[at], order[at + 1 :], me, devices)

    embed_held = scatter_add(*scatter(embed_grad, back_order, 0))
    embed_held, grad_pooled = lax.optimization_barrier((embed_held, grad_pooled))
    embed_held = scatter_add(*scatter(embed_held, back_order, 1))
    hidden_grad, attended_grad, later_norms, *unit_sums = units_backward(
        devices // 8, places, grad_pooled, hyper_hidden, hyper_attended, *forward_weights, norm_rows
    )
    hidden_grad, embed_held = lax.optimization_barrier((hidden_grad, embed_held))
    held = [embed_held, *([unit_sums[:2], unit_sums[2:]] if together else unit_sums)]
    turned_order = [back_order[0], back_order[2], back_order[3], back_order[1]] + back_order[4:]
    orders = [back_order, back_order, turned_order]
    ahead = [2, 0, 0]

    def depart(at):
        moving = []
        for x, order, skip in zip(held, orders, ahead):
            if at + skip >= bits:
                moving.append((x, None))
            elif isinstance(x, list):
                moving.append((x[0], swap(x[1], 1 << order[0], devices)))
            else:
                moving.append(scatter(x, order, at + skip))
        return moving

    def arrive(moving):
        return [x if came is None else scatter_add(x, came) for x, came in moving]

    slots_saved = (pieces, slot_mixed, slot_probs)
    slots_held = (None, None, later_norms)
    for part in range(SLOT_PARTS):
        moving = depart(part)
        slots_held = slot_backward(
            part, SLOT_PARTS, slots_held, slots_saved, (attended_grad, hidden_grad), in_weight, norm_rows
        )
        slots_held, moving = lax.optimization_barrier((tuple(slots_held), moving))
        held = arrive(moving)
    pieces_grad, input_grad, _ = slots_held
    input_held = input_grad
    moving = depart(SLOT_PARTS)
    for at in range(bits):
        input_held = scatter_add(*scatter(input_held, back_order, at))
        if at > 0:
            _, moving = lax.optimization_barrier((input_held, moving))
            held = arrive(moving)
            moving = depart(SLOT_PARTS + at)
    held = arrive(moving)
    embed_own, wide_own, reduce_own, input_own = (*held, input_held)
    out_width = hyper_output.shape[1]
    return (
        model_out,
        pieces_grad,
        input_own[:, :in_width],
        wide_own[:, :out_width],
        wide_own[:, out_width:],
        reduce_own,
        input_own[:, in_width : in_width + norm_count],
        embed_own,
    )


def solution(mesh):
    return jax.shard_map(
        body,
        mesh=mesh,
        in_specs=(
            P(("dp", "mp"), None, None),
            P(("dp", "mp")),
            P("dp"),
            P(("dp", "mp"), None),
            P(("dp", "mp"), None),
            P(("dp", "mp"), None),
            P(("dp", "mp"), None),
            P(("dp", "mp"), None),
            P(("dp", "mp"), None),
            P(),
            P(),
            P(None, "mp"),
            P(None, "mp"),
            P(None, "mp"),
            P("mp", None),
            P(None, "mp"),
            P(None, "mp"),
            P("mp", None),
            P("dp", None),
        ),
        out_specs=(
            P("dp", "mp"),
            P(("dp", "mp"), None, None),
            P(("dp", "mp"), None),
            P(("dp", "mp"), None),
            P(("dp", "mp"), None),
            P(("dp", "mp"), None),
            P(("dp", "mp"), None),
            P(("dp", "mp"), None),
        ),
        check_vma=False,
    )
```

```python
import functools

import jax
import jax.numpy as jnp
import numpy as np
from jax import lax
from jax.experimental import pallas as pl
from jax.experimental.pallas import tpu as pltpu
from jax.sharding import PartitionSpec as P

HEAD_WIDTH = 64
HHD = 64
BLOCK_PARTS = 4
UNIT = 512
PAIR = 2 * HEAD_WIDTH
VMEM_LIMIT = 48 << 20
ENTRY_BLOCK = 64
SLOT_PARTS = 2
UNIT_STEP = 256
COLUMN_STEP = 256
UNIT_ROWS = 512


EPS = 1e-05
NEGATIVE = -1000000000.0


def matmul(left, right):
    return jnp.dot(left, right, preferred_element_type=jnp.float32)


def matmul_first(left, right):
    return lax.dot_general(
        left, right, (((0,), (0,)), ((), ())), preferred_element_type=jnp.float32
    )


def matmul_last(left, right):
    return lax.dot_general(
        left, right, (((1,), (1,)), ((), ())), preferred_element_type=jnp.float32
    )


def log2_of(number):
    return number.bit_length() - 1


def swap(value, mask, devices):
    return lax.ppermute(value, ("dp", "mp"), [(d, d ^ mask) for d in range(devices)])


def gather_join(held, arrived, bit, done, me):
    rows, width = held.shape
    outer = 1 << sum(other > bit for other in done)
    held, arrived = [x.reshape(outer, rows // outer, width) for x in (held, arrived)]
    joined = jnp.where(
        ((me >> bit) & 1) == 1,
        jnp.concatenate([arrived, held], axis=1),
        jnp.concatenate([held, arrived], axis=1),
    )
    return joined.reshape(2 * rows, width)


def scatter_send(held, bit, left, me, devices):
    rows, width = held.shape
    outer = 1 << sum(other > bit for other in left)
    parts = held.reshape(outer, 2, rows // outer // 2, width)
    mine = (me >> bit) & 1

    def part(at):
        return lax.dynamic_slice_in_dim(parts, at, 1, 1).reshape(rows // 2, width)

    return (part(mine), swap(to_low(part(1 - mine)), 1 << bit, devices))


def scatter_add(staying, came):
    return staying.astype(jnp.float32) + came.astype(jnp.float32)


def lanes(shape):
    return lax.broadcasted_iota(jnp.int32, shape, len(shape) - 1)


def half_swap(value):
    quarter = HEAD_WIDTH // 2
    upper = (lanes(value.shape) & quarter) != 0
    return jnp.where(
        upper, pltpu.roll(value, quarter, 1), pltpu.roll(value, PAIR - quarter, 1)
    )


def to_low(value):
    return value.astype(jnp.bfloat16)


def causal_of(rows):
    return lax.broadcasted_iota(jnp.int32, (rows, rows), 0) <= lax.broadcasted_iota(
        jnp.int32, (rows, rows), 1
    )


def masked_scores(keys, low, causal):
    rows = causal.shape[0]
    length = keys.shape[0]
    last = jnp.where(causal, matmul_last(keys[length - rows :, :], low), NEGATIVE)
    return [matmul_last(keys[: length - rows, :], low), last] if length > rows else [last]


def for_lengths(block_at, rows, length, work):
    for count in (length - rows, length):
        pl.when(block_at == count // rows - 1)(functools.partial(work, count))


def turn_left(value, cosine, sine):
    left = lanes(value.shape) < HEAD_WIDTH
    return jnp.where(left, value * cosine + half_swap(value) * sine, value)


def head_views(pair_ref, cos_ref, sin_ref, rows):
    span = slice(0, rows)
    turned = to_low(turn_left(pair_ref[span, :], cos_ref[span, :], sin_ref[span, :])).astype(jnp.float32)
    other = pltpu.roll(turned, HEAD_WIDTH, 1)
    left = lanes(turned.shape) < HEAD_WIDTH
    return (
        jnp.where(left, turned, 0.0),
        jnp.where(left, 0.0, other),
        jnp.where(left, other, 0.0),
        jnp.where(left, 0.0, turned),
    )


def attention_forward_kernel(
    info, query_ref, pair_ref, cos_pair, sin_pair, cos_ref, sin_ref,
    out_ref, low_ref, lse_ref, even, odd, across,
):
    rows = query_ref.shape[0]
    causal = causal_of(rows)

    def work(length):
        span = slice(0, length)
        key_left, key_right, value_left, _ = head_views(pair_ref, cos_pair, sin_pair, length)
        even[span, :] = to_low(key_left)
        odd[span, :] = to_low(key_right)
        across[:, span] = to_low(value_left.T[:HEAD_WIDTH])
        for pair in range(query_ref.shape[1] // PAIR):
            columns = slice(pair * PAIR, (pair + 1) * PAIR)
            query = query_ref[:, columns]
            turned = to_low(query * cos_ref[...] + half_swap(query) * sin_ref[...])
            low = to_low(turned.astype(jnp.float32) * HEAD_WIDTH ** (-0.5))
            low_ref[:, columns] = low
            outs = []
            for at, keys in enumerate((even, odd)):
                scores = masked_scores(keys[span, :], low, causal)
                highest = functools.reduce(
                    jnp.maximum, [jnp.max(x, axis=0, keepdims=True) for x in scores]
                )
                weights = [jnp.exp(x - highest) for x in scores]
                total = sum(jnp.sum(x, axis=0, keepdims=True) for x in weights)
                out = 0.0
                start = 0
                for x in weights:
                    out = out + matmul(across[:, start : start + x.shape[0]], to_low(x))
                    start += x.shape[0]
                outs.append(out / total)
                lse_ref[0, 2 * pair + at : 2 * pair + at + 1, :] = highest + jnp.log(total)
            out_ref[:, columns] = to_low(jnp.concatenate(outs, axis=0).T)

    for_lengths(info[0], rows, pair_ref.shape[0], work)


def attention_backward_kernel(
    info, low_ref, grad_ref, lse_ref, pair_ref, cos_pair, sin_pair, cos_ref, sin_ref, *refs,
):
    query_ref, pair_grad_ref, even, odd, value_even, value_odd, across = refs[-11:-4]
    key_even, key_odd, sum_even, sum_odd = refs[-4:]
    rows = low_ref.shape[0]
    causal = causal_of(rows)

    def work(length):
        span = slice(0, length)
        key_left, key_right, value_left, value_right = head_views(pair_ref, cos_pair, sin_pair, length)
        even[span, :] = to_low(key_left)
        odd[span, :] = to_low(key_right)
        value_even[span, :] = to_low(value_left)
        value_odd[span, :] = to_low(value_right)
        across[:, span] = to_low(key_left.T[:HEAD_WIDTH])
        sides = ((even, value_even, key_even, sum_even), (odd, value_odd, key_odd, sum_odd))
        for total in (key_even, key_odd, sum_even, sum_odd):
            total[span, :] = jnp.zeros((length, PAIR), jnp.float32)
        for pair in range(low_ref.shape[1] // PAIR):
            columns = slice(pair * PAIR, (pair + 1) * PAIR)
            low = low_ref[:, columns]
            grad = grad_ref[:, columns]
            outs = []
            for at, (keys, values, key_total, value_total) in enumerate(sides):
                lse = lse_ref[0, 2 * pair + at : 2 * pair + at + 1, :]
                probs = [jnp.exp(x - lse) for x in masked_scores(keys[span, :], low, causal)]
                moved = []
                start = 0
                for x in probs:
                    part = slice(start, start + x.shape[0])
                    value_total[part, :] += matmul(to_low(x), grad)
                    moved.append(x * matmul_last(values[part, :], grad))
                    start += x.shape[0]
                mean = sum(jnp.sum(x, axis=0, keepdims=True) for x in moved)
                out = 0.0
                start = 0
                for x, y in zip(probs, moved):
                    part = slice(start, start + x.shape[0])
                    grad_scores = to_low(y - x * mean)
                    key_total[part, :] += matmul(grad_scores, low)
                    out = out + matmul(across[:, part], grad_scores)
                    start += x.shape[0]
                outs.append(out)
            turned = jnp.concatenate(outs, axis=0).T * HEAD_WIDTH ** (-0.5)
            query_ref[:, columns] = to_low(turned * cos_ref[...] - half_swap(turned) * sin_ref[...])
        left = lanes((length, PAIR)) < HEAD_WIDTH
        pair_grad_ref[0, span, :] = jnp.where(
            left,
            key_even[span, :] + pltpu.roll(key_odd[span, :], HEAD_WIDTH, 1),
            pltpu.roll(sum_even[span, :], HEAD_WIDTH, 1) + sum_odd[span, :],
        )
        if length < pair_ref.shape[0]:
            rest = (pair_ref.shape[0] - length, PAIR)
            pair_grad_ref[0, length:, :] = jnp.zeros(rest, jnp.float32)

    for_lengths(info[0], rows, pair_ref.shape[0], work)


def attention_specs(part, rows, length, first=0):
    span = (rows, 4 * PAIR)
    return {
        "table_pair": pl.BlockSpec((length, PAIR), lambda g, s: (0, 0)),
        "table": pl.BlockSpec((rows, PAIR), lambda g, s: (s[0], 0)),
        "pair": pl.BlockSpec((length, PAIR), lambda g, s: (0, g + first)),
        "part": pl.BlockSpec(span, lambda g, s: (part, g + first)),
        "wide": pl.BlockSpec(span, lambda g, s: (0, g + first)),
        "sums": pl.BlockSpec((1, 8, rows), lambda g, s: (g + first, 0, 0)),
    }


def attention_cost(rows, length, heads, matmuls):
    work = 20 * rows * length * heads * HEAD_WIDTH * matmuls
    return pl.CostEstimate(
        flops=work, bytes_accessed=16 * rows * heads * HEAD_WIDTH, transcendentals=rows * length * heads
    )


def attention_forward(info, queries, pair_pre, tables, part, length):
    cosine, sine = tables
    rows = cosine.shape[0] // BLOCK_PARTS
    heads = 4 * 4 * PAIR // HEAD_WIDTH
    spec = attention_specs(part, rows, length)
    half = pltpu.VMEM((length, PAIR), jnp.bfloat16)
    wide = (rows, heads * HEAD_WIDTH)
    return pl.pallas_call(
        attention_forward_kernel,
        grid_spec=pltpu.PrefetchScalarGridSpec(
            num_scalar_prefetch=1,
            grid=(4,),
            in_specs=[
                spec["part"], spec["pair"],
                spec["table_pair"], spec["table_pair"], spec["table"], spec["table"],
            ],
            out_specs=[spec["wide"], spec["wide"], spec["sums"]],
            scratch_shapes=[
                half, half,
                pltpu.VMEM((HEAD_WIDTH, length), jnp.bfloat16),
            ],
        ),
        out_shape=[
            jax.ShapeDtypeStruct(wide, jnp.bfloat16),
            jax.ShapeDtypeStruct(wide, jnp.bfloat16),
            jax.ShapeDtypeStruct((4, 8, rows), jnp.float32),
        ],
        compiler_params=pltpu.CompilerParams(
            dimension_semantics=("arbitrary",), vmem_limit_bytes=VMEM_LIMIT
        ),
        cost_estimate=attention_cost(rows, length, heads, 2),
        name="attention_forward",
    )(info, queries, pair_pre, cosine, sine, cosine, sine)


def attention_backward(info, low, grad, sums, pair_pre, tables, part, length, groups, before):
    first, count = groups
    cosine, sine = tables
    rows = cosine.shape[0] // BLOCK_PARTS
    heads = low.shape[1] // HEAD_WIDTH
    spec = attention_specs(part, rows, length, first)
    half = pltpu.VMEM((length, PAIR), jnp.bfloat16)
    full = pltpu.VMEM((length, PAIR), jnp.float32)
    return pl.pallas_call(
        attention_backward_kernel,
        grid_spec=pltpu.PrefetchScalarGridSpec(
            num_scalar_prefetch=1,
            grid=(count,),
            in_specs=[
                spec["wide"], spec["wide"], spec["sums"], spec["pair"],
                spec["table_pair"], spec["table_pair"], spec["table"], spec["table"],
            ]
            + [pl.BlockSpec(memory_space=pl.ANY)] * len(before),
            out_specs=[spec["part"], pl.BlockSpec((1, length, PAIR), lambda g, s: (s[1 + g + first], 0, 0))],
            scratch_shapes=[
                half, half, half, half,
                pltpu.VMEM((HEAD_WIDTH, length), jnp.bfloat16),
                full, full, full, full,
            ],
        ),
        out_shape=[
            jax.ShapeDtypeStruct((2 * rows, low.shape[1]), jnp.bfloat16),
            jax.ShapeDtypeStruct((4, length, PAIR), jnp.float32),
        ],
        input_output_aliases={9 + at: at for at in range(len(before))},
        compiler_params=pltpu.CompilerParams(
            dimension_semantics=("arbitrary",), vmem_limit_bytes=VMEM_LIMIT
        ),
        cost_estimate=attention_cost(rows, length, heads, 5 if count == 4 else 0),
        name="attention_backward",
    )(info, low, grad, sums, pair_pre, cosine, sine, cosine, sine, *before)


def rope_tables(length):
    positions = np.arange(length, dtype=np.float32)
    inverse = 10000.0 ** (-np.arange(0, HEAD_WIDTH, 2, dtype=np.float32) / HEAD_WIDTH)
    angles = positions[:, None] * inverse.astype(np.float32)[None, :]
    cosine, sine = np.cos(angles).astype(np.float32), np.sin(angles).astype(np.float32)
    return (
        jnp.asarray(np.concatenate([cosine] * 4, axis=1)),
        jnp.asarray(np.concatenate([-sine, sine, -sine, sine], axis=1)),
    )


def head_marks(width, transposed):
    shape = (PAIR, width) if transposed else (width, PAIR)
    head_at, column_at = (0, 1) if transposed else (1, 0)
    head = lax.broadcasted_iota(jnp.int32, shape, head_at)
    column = lax.broadcasted_iota(jnp.int32, shape, column_at)
    return (column // HHD == head).astype(jnp.bfloat16)


def head_sums(value, marks):
    high = to_low(value)
    rest = to_low(value - high.astype(jnp.float32))
    return matmul(high, marks) + matmul(rest, marks)


def normalize(value):
    centered = value - jnp.mean(value, axis=-1, keepdims=True)
    inverse = lax.rsqrt(jnp.mean(centered * centered, axis=-1, keepdims=True) + EPS)
    return (centered * inverse, inverse)


def norm_back(grad, gain, hat, inverse):
    scaled = grad * gain
    mean = jnp.mean(scaled, axis=-1, keepdims=True)
    along = jnp.mean(scaled * hat, axis=-1, keepdims=True)
    return inverse * (scaled - mean - hat * along)


def slot_attention_kernel(
    pieces_ref, counts_ref, weight_ref, mixed_ref, probs_ref, attended_ref, lead_ref, norm_ref
):
    entries, slots, width = pieces_ref.shape

    @pl.when(pl.program_id(0) == 0)
    def norms():
        norm_ref[...] = weight_ref[:, 3 * width : 3 * width + PAIR].astype(jnp.float32).T[:8]

    rows = entries * slots
    tall = (entries, slots, width)
    pieces = pieces_ref[...].astype(jnp.float32)
    hat, _ = normalize(pieces.reshape(rows, width))
    low = to_low(hat * norm_ref[0:1, :] + norm_ref[1:2, :])
    mixed = []
    for part in range(3):
        span = slice(part * width, (part + 1) * width)
        value = to_low(matmul(low, weight_ref[:, span]))
        mixed_ref[:, span] = value
        mixed.append(value.astype(jnp.float32).reshape(tall))
    query, keys, values = mixed
    marks = head_marks(width, False)
    product = (keys * query[:, 0:1, :]).reshape(rows, width)
    scores = head_sums(product, marks).reshape(entries, slots, PAIR) * HHD ** (-0.5)
    live = lax.broadcasted_iota(jnp.int32, scores.shape, 1) < counts_ref[...]
    scores = jnp.where(live, scores, NEGATIVE)
    weight = jnp.exp(scores - jnp.max(scores, axis=1, keepdims=True))
    probs = weight / jnp.sum(weight, axis=1, keepdims=True)
    probs_ref[...] = probs
    spread = matmul(to_low(probs.reshape(rows, PAIR)), head_marks(width, True)).reshape(tall)
    attended_ref[...] = to_low(jnp.sum(spread * values, axis=1))
    lead_ref[...] = pieces[:, 0, :]


def slot_attention(pieces, counts, in_weight):
    entries, slots, width = pieces.shape
    part = min(ENTRY_BLOCK, entries)
    whole = lambda shape: pl.BlockSpec(shape, lambda i: (0,) * len(shape))
    tall = pl.BlockSpec((part, slots, width), lambda i: (i, 0, 0))
    flat = pl.BlockSpec((part, width), lambda i: (i, 0))
    return pl.pallas_call(
        slot_attention_kernel,
        grid=(entries // part,),
        in_specs=[
            tall,
            pl.BlockSpec((part, 1, PAIR), lambda i: (i, 0, 0)),
            whole(in_weight.shape),
        ],
        out_specs=[
            pl.BlockSpec((part * slots, 3 * width), lambda i: (i, 0)),
            pl.BlockSpec((part, slots, PAIR), lambda i: (i, 0, 0)),
            flat,
            flat,
            whole((8, width)),
        ],
        out_shape=[
            jax.ShapeDtypeStruct((entries * slots, 3 * width), jnp.bfloat16),
            jax.ShapeDtypeStruct((entries, slots, PAIR), jnp.float32),
            jax.ShapeDtypeStruct((entries, width), jnp.bfloat16),
            jax.ShapeDtypeStruct((entries, width), jnp.float32),
            jax.ShapeDtypeStruct((8, width), jnp.float32),
        ],
        compiler_params=pltpu.CompilerParams(
            dimension_semantics=("arbitrary",), vmem_limit_bytes=VMEM_LIMIT
        ),
        cost_estimate=pl.CostEstimate(
            flops=entries * slots * width, bytes_accessed=entries * slots, transcendentals=0
        ),
        name="slot_attention",
    )(pieces, counts, in_weight)


def gelu_of(value):
    cdf = 0.5 * (1.0 + lax.erf(value * np.float32(0.5 ** 0.5)))
    return (value * cdf, cdf)


def gelu_slope(value, cdf):
    return cdf + value * (jnp.exp(-0.5 * value * value) * np.float32((2 * np.pi) ** -0.5))


def place_parts(split, places, wholes, parts):
    @pl.when(pl.program_id(0) == 0)
    def join():
        core, side = places[0], places[1]
        for index, whole in enumerate(wholes):
            for at, part in enumerate(parts[4 * index : 4 * index + 4]):
                rows = part.shape[0] // split
                place = 2 * (side if at % 2 == 0 else 1 - side) + (core if at < 2 else 1 - core)
                for group in range(split):
                    start = pl.multiple_of((4 * group + place) * rows, rows)
                    whole[pl.ds(start, rows), :] = part[group * rows : (group + 1) * rows, :]


def units_forward_kernel(
    split, places, attended_ref, lead_ref, *refs
):
    *weights, norm_ref, pooled_ref, hidden_ref = refs[: 11 if split else 5]
    if not split:
        wide_weight_ref, reduce_ref = weights
    else:
        wide_weight_ref, reduce_ref = refs[11:]

        place_parts(split, places, (wide_weight_ref, reduce_ref), weights)

    width = lead_ref.shape[1]
    hidden = lead_ref[...] + matmul(attended_ref[...], wide_weight_ref[:, :width])
    hidden_ref[...] = hidden
    hat, _ = normalize(hidden)
    second = to_low(hat * norm_ref[2:3, :] + norm_ref[3:4, :])
    total = hidden
    units = reduce_ref.shape[0]
    step = min(UNIT, units)
    for at in range(0, units, step):
        active, _ = gelu_of(matmul(second, wide_weight_ref[:, width + at : width + at + step]))
        total = total + matmul(to_low(active), reduce_ref[at : at + step, :])
    pooled_ref[...] = to_low(total)


def units_forward(groups, places, attended, lead, wide_weight, reduce_weight, norm_rows):
    entries, width = attended.shape
    part = min(UNIT_ROWS, entries)
    split = groups if len(wide_weight) == 4 else 0
    whole = lambda shape: pl.BlockSpec(shape, lambda i, s: (0,) * len(shape))
    flat = pl.BlockSpec((part, width), lambda i, s: (i, 0))
    weights = [*wide_weight, *reduce_weight]
    joined = [
        pltpu.VMEM((4 * parts[0].shape[0], parts[0].shape[1]), jnp.bfloat16)
        for parts in (wide_weight, reduce_weight)
    ]
    return pl.pallas_call(
        functools.partial(units_forward_kernel, split),
        grid_spec=pltpu.PrefetchScalarGridSpec(
            num_scalar_prefetch=1,
            grid=(entries // part,),
            in_specs=[flat, flat] + [whole(x.shape) for x in (*weights, norm_rows)],
            out_specs=[flat, flat],
            scratch_shapes=joined if split else [],
        ),
        out_shape=[
            jax.ShapeDtypeStruct((entries, width), jnp.bfloat16),
            jax.ShapeDtypeStruct((entries, width), jnp.float32),
        ],
        compiler_params=pltpu.CompilerParams(
            dimension_semantics=("arbitrary",), vmem_limit_bytes=VMEM_LIMIT
        ),
        cost_estimate=pl.CostEstimate(
            flops=entries * width, bytes_accessed=entries * width, transcendentals=0
        ),
        name="units_forward",
    )(places.astype(jnp.int32), attended, lead, *weights, norm_rows)


def units_backward_kernel(split, places, grad_ref, hidden_ref, attended_ref, *refs):
    *weights, norm_ref, hidden_grad_ref, attended_grad_ref, norm_grad_ref = refs[: 12 if split else 6]
    if split:
        *sums, wide_total, reduce_total, wide_weight_ref, reduce_ref = refs[12:]
        place_parts(split, places, (wide_weight_ref, reduce_ref), weights)
    else:
        wide_weight_ref, reduce_ref = weights
        *sums, wide_total, reduce_total = refs[6:]
    step_at = pl.program_id(0)
    width = hidden_ref.shape[1]
    units = reduce_ref.shape[0]

    @pl.when(step_at == 0)
    def start():
        wide_total[...] = jnp.zeros_like(wide_total)
        reduce_total[...] = jnp.zeros_like(reduce_total)
        norm_grad_ref[...] = jnp.zeros_like(norm_grad_ref)

    grad = grad_ref[...]
    grad_low = to_low(grad)
    hat, inverse = normalize(hidden_ref[...])
    second = to_low(hat * norm_ref[2:3, :] + norm_ref[3:4, :])
    grad_normed = jnp.zeros_like(grad)
    step = min(UNIT, units)
    for at in range(0, units, step):
        span = slice(at, at + step)
        wide_span = slice(width + at, width + at + step)
        expanded = matmul(second, wide_weight_ref[:, wide_span])
        active, cdf = gelu_of(expanded)
        reduce_total[span, :] += matmul_first(to_low(active), grad_low)
        grad_active = matmul_last(grad_low, reduce_ref[span, :])
        grad_expanded = to_low(grad_active * gelu_slope(expanded, cdf))
        wide_total[:, wide_span] += matmul_first(second, grad_expanded)
        grad_normed = grad_normed + matmul_last(grad_expanded, wide_weight_ref[:, wide_span])
    norm_grad_ref[2:3, :] += jnp.sum(grad_normed * hat, axis=0, keepdims=True)
    norm_grad_ref[3:4, :] += jnp.sum(grad_normed, axis=0, keepdims=True)
    hidden_grad = grad + norm_back(grad_normed, norm_ref[2:3, :], hat, inverse)
    hidden_grad_ref[...] = hidden_grad
    hidden_low = to_low(hidden_grad)
    wide_total[:, :width] += matmul_first(attended_ref[...], hidden_low)
    attended_grad_ref[...] = to_low(matmul_last(hidden_low, wide_weight_ref[:, :width]))

    @pl.when(step_at == pl.num_programs(0) - 1)
    def finish():
        if not split:
            sums[0][...] = to_low(wide_total[...])
            sums[1][...] = to_low(reduce_total[...])
            return
        core = places[0]
        for total, halves in ((wide_total, sums[:2]), (reduce_total, sums[2:])):
            rows = halves[0].shape[0] // (2 * split)
            for half, place in zip(halves, (core, 1 - core)):
                for group in range(2 * split):
                    start = pl.multiple_of((2 * group + place) * rows, rows)
                    half[group * rows : (group + 1) * rows, :] = to_low(total[pl.ds(start, rows), :])


def units_backward(groups, places, grad, hidden, attended, wide_weight, reduce_weight, norm_rows):
    entries, width = attended.shape
    part = min(UNIT_ROWS, entries)
    split = groups if len(wide_weight) == 4 else 0
    weights = [*wide_weight, *reduce_weight]
    units = reduce_weight[0].shape[0] * len(reduce_weight)
    whole = lambda shape: pl.BlockSpec(shape, lambda i, s: (0,) * len(shape))
    flat = pl.BlockSpec((part, width), lambda i, s: (i, 0))
    wide = (width, width + units)
    tall = (units, width)
    half = lambda shape: (shape[0] // 2, shape[1])
    sums = [half(wide)] * 2 + [half(tall)] * 2 if split else [wide, tall]
    return pl.pallas_call(
        functools.partial(units_backward_kernel, split),
        grid_spec=pltpu.PrefetchScalarGridSpec(
            num_scalar_prefetch=1,
            grid=(entries // part,),
            in_specs=[flat, flat, flat] + [fixed(x.shape) for x in (*weights, norm_rows)],
            out_specs=[flat, flat, whole((8, width))] + [whole(x) for x in sums],
            scratch_shapes=[pltpu.VMEM(wide, jnp.float32), pltpu.VMEM(tall, jnp.float32)]
            + [pltpu.VMEM(x, jnp.bfloat16) for x in (wide, tall)] * bool(split),
        ),
        out_shape=[
            jax.ShapeDtypeStruct((entries, width), jnp.float32),
            jax.ShapeDtypeStruct((entries, width), jnp.bfloat16),
            jax.ShapeDtypeStruct((8, width), jnp.float32),
        ]
        + [jax.ShapeDtypeStruct(x, jnp.bfloat16) for x in sums],
        compiler_params=pltpu.CompilerParams(
            dimension_semantics=("arbitrary",), vmem_limit_bytes=VMEM_LIMIT
        ),
        cost_estimate=pl.CostEstimate(
            flops=6 * entries * width * (2 * width + 5 * units), bytes_accessed=16 << 20, transcendentals=0
        ),
        name="units_backward",
    )(places.astype(jnp.int32), grad, hidden, attended, *weights, norm_rows)


def slot_backward_kernel(
    first, last, pieces_ref, mixed_ref, probs_ref, attended_grad_ref, hidden_grad_ref, weight_ref, norm_ref,
    later_ref, *refs,
):
    if first:
        pieces_grad_ref, input_grad_ref, norm_grad_ref, total, norm_total = refs
    else:
        _, total_ref, pieces_grad_ref, input_grad_ref, norm_grad_ref, total, norm_total = refs
    step_at = pl.program_id(0)
    entries, slots, width = pieces_ref.shape
    rows = entries * slots
    tall = (entries, slots, width)

    @pl.when(step_at == 0)
    def start():
        norm_total[...] = jnp.zeros_like(norm_total)
        norm_total[0:8, :] = later_ref[...]
        total[...] = jnp.zeros_like(total) if first else total_ref[...]

    hat, inverse = normalize(pieces_ref[...].astype(jnp.float32).reshape(rows, width))
    low = to_low(hat * norm_ref[0:1, :] + norm_ref[1:2, :])
    scale = HHD ** (-0.5)
    query, keys, values = [
        mixed_ref[:, part * width : (part + 1) * width].astype(jnp.float32).reshape(tall) for part in range(3)
    ]
    probs = probs_ref[...]
    grad_attended = jnp.broadcast_to(attended_grad_ref[...].astype(jnp.float32)[:, None, :], tall)
    grad_probs = head_sums((grad_attended * values).reshape(rows, width), head_marks(width, False))
    moved = probs * grad_probs.reshape(probs.shape)
    grad_scores = to_low(moved - probs * jnp.sum(moved, axis=1, keepdims=True))
    marks = head_marks(width, True)
    spread = matmul(grad_scores.reshape(rows, PAIR), marks).reshape(tall) * scale
    first_slot = lax.broadcasted_iota(jnp.int32, tall, 1) == 0
    grad_query = jnp.where(first_slot, jnp.sum(spread * keys, axis=1, keepdims=True), 0.0)
    grad_keys = spread * query[:, 0:1, :]
    grad_values = matmul(to_low(probs.reshape(rows, PAIR)), marks).reshape(tall) * grad_attended
    grad_normed = jnp.zeros((rows, width), jnp.float32)
    for part, grad in enumerate((grad_query, grad_keys, grad_values)):
        span = slice(part * width, (part + 1) * width)
        grad_low = to_low(grad.reshape(rows, width))
        total[:, span] += matmul_first(low, grad_low)
        grad_normed = grad_normed + matmul_last(grad_low, weight_ref[:, span])
    norm_total[0:1, :] += jnp.sum(grad_normed * hat, axis=0, keepdims=True)
    norm_total[1:2, :] += jnp.sum(grad_normed, axis=0, keepdims=True)
    grad_pieces = norm_back(grad_normed, norm_ref[0:1, :], hat, inverse).reshape(tall)
    hidden_grad = jnp.broadcast_to(hidden_grad_ref[...][:, None, :], tall)
    pieces_grad_ref[...] = to_low(grad_pieces + jnp.where(first_slot, hidden_grad, 0.0))

    @pl.when(step_at == pl.num_programs(0) - 1)
    def finish():
        norm_grad_ref[...] = norm_total[0:8, :]
        if last:
            input_grad_ref[:, : 3 * width] = to_low(total[...])
            input_grad_ref[:, 3 * width :] = to_low(norm_total[...].T)
        else:
            input_grad_ref[...] = total[...]


def slot_backward(at, parts, held, saved, grads, in_weight, norm_rows):
    pieces, mixed, probs = saved
    pieces_grad, total, norm_grad = held
    entries, slots, width = pieces.shape
    first, last = at == 0, at == parts - 1
    part = min(ENTRY_BLOCK, entries // parts)
    steps = entries // parts // part
    whole = lambda shape: pl.BlockSpec(shape, lambda i: (0,) * len(shape))
    tall = pl.BlockSpec((part, slots, width), lambda i: (i + at * steps, 0, 0))
    flat = pl.BlockSpec((part, width), lambda i: (i + at * steps, 0))
    total_shape = (
        jax.ShapeDtypeStruct((width, 3 * width + PAIR), jnp.bfloat16)
        if last
        else jax.ShapeDtypeStruct((width, 3 * width), jnp.float32)
    )
    in_specs = [
        tall,
        pl.BlockSpec((part * slots, 3 * width), lambda i: (i + at * steps, 0)),
        pl.BlockSpec((part, slots, PAIR), lambda i: (i + at * steps, 0, 0)),
        flat,
        flat,
        whole(in_weight.shape),
        whole(norm_rows.shape),
        whole(norm_grad.shape),
    ]
    operands = [pieces, mixed, probs, *grads, in_weight, norm_rows, norm_grad]
    if not first:
        in_specs += [pl.BlockSpec(memory_space=pl.ANY), whole(total.shape)]
        operands += [pieces_grad, total]
    return pl.pallas_call(
        functools.partial(slot_backward_kernel, first, last),
        grid=(steps,),
        in_specs=in_specs,
        out_specs=[tall, whole(total_shape.shape), whole(norm_grad.shape)],
        out_shape=[
            jax.ShapeDtypeStruct(pieces.shape, jnp.bfloat16),
            total_shape,
            jax.ShapeDtypeStruct(norm_grad.shape, jnp.float32),
        ],
        input_output_aliases={} if first else {len(operands) - 2: 0},
        scratch_shapes=[
            pltpu.VMEM((width, 3 * width), jnp.float32),
            pltpu.VMEM((PAIR, width), jnp.float32),
        ],
        compiler_params=pltpu.CompilerParams(
            dimension_semantics=("arbitrary",), vmem_limit_bytes=VMEM_LIMIT
        ),
        cost_estimate=pl.CostEstimate(
            flops=entries * slots * width // parts,
            bytes_accessed=entries * slots // parts,
            transcendentals=0,
        ),
        name="slot_backward",
    )(*operands)


def feed_forward_kernel(
    rows_ref, other_ref, rise_ref, rise_other_ref, hidden_ref, gate_ref, up_ref, down_ref,
    gate_rows, up_rows, down_columns, grad_ref, dense_ref, rows, rise, active, grad_gate, grad_up,
):
    at = pl.program_id(0)
    half = rows_ref.shape[0]
    step = gate_ref.shape[1]
    tiles = active.shape[1] // step

    @pl.when(at == 0)
    def start():
        rows[:half, :] = rows_ref[...]
        rows[half:, :] = other_ref[...]
        rise[:half, :] = rise_ref[...]
        rise[half:, :] = rise_other_ref[...]

    @pl.when(at < tiles)
    def units():
        gate = matmul(rows[...], gate_ref[...])
        up = matmul(rows[...], up_ref[...])
        rising = matmul_last(rise[...], down_ref[...])
        sign = 1.0 / (1.0 + jnp.exp(-gate))
        silu = gate * sign
        span = pl.ds(pl.multiple_of(at * step, step), step)
        active[:, span] = to_low(silu * up)
        grad_up[:, span] = to_low(rising * silu)
        grad_gate[:, span] = to_low(rising * up * (sign * (1.0 + gate * (1.0 - sign))))

    @pl.when(at >= tiles)
    def columns():
        dense = matmul(active[...], down_columns[...])
        grad = matmul_last(grad_gate[...], gate_rows[...]) + matmul_last(grad_up[...], up_rows[...])
        grad_ref[...] = to_low(grad)
        dense_ref[:half, :] = to_low(dense[:half] + hidden_ref[...])
        dense_ref[half:, :] = to_low(dense[half:])


def feed_forward(rows, other, upstream, hidden, info, gate_weight, up_weight, down_weight):
    half, width = rows.shape
    units = gate_weight.shape[1]
    step = UNIT_STEP
    tiles = units // step
    column = COLUMN_STEP
    fixed_rows = pl.BlockSpec((half, width), lambda i, s: (0, 0), pipeline_mode=pl.Buffered(1))
    early = lambda i: jnp.minimum(i, tiles - 1)
    late = lambda i: jnp.maximum(i - tiles, 0)
    tall = (2 * half, width)
    out = pl.BlockSpec((2 * half, column), lambda i, s: (0, late(i)))
    return pl.pallas_call(
        lambda info, *refs: feed_forward_kernel(*refs),
        grid_spec=pltpu.PrefetchScalarGridSpec(
            num_scalar_prefetch=1,
            grid=(tiles + width // column,),
            in_specs=[
                fixed_rows,
                fixed_rows,
                pl.BlockSpec((half, width), lambda i, s: (s[0], 0), pipeline_mode=pl.Buffered(1)),
                pl.BlockSpec((half, width), lambda i, s: (s[1], 0), pipeline_mode=pl.Buffered(1)),
                pl.BlockSpec((half, column), lambda i, s: (0, late(i))),
                pl.BlockSpec((width, step), lambda i, s: (0, early(i))),
                pl.BlockSpec((width, step), lambda i, s: (0, early(i))),
                pl.BlockSpec((step, width), lambda i, s: (early(i), 0)),
                pl.BlockSpec((column, units), lambda i, s: (late(i), 0)),
                pl.BlockSpec((column, units), lambda i, s: (late(i), 0)),
                pl.BlockSpec((units, column), lambda i, s: (0, late(i))),
            ],
            out_specs=[out, out],
            scratch_shapes=[
                pltpu.VMEM(tall, jnp.bfloat16),
                pltpu.VMEM(tall, jnp.bfloat16),
                *[pltpu.VMEM((2 * half, units), jnp.bfloat16)] * 3,
            ],
        ),
        out_shape=[jax.ShapeDtypeStruct(tall, jnp.bfloat16)] * 2,
        compiler_params=pltpu.CompilerParams(
            dimension_semantics=("arbitrary",), vmem_limit_bytes=VMEM_LIMIT
        ),
        cost_estimate=pl.CostEstimate(
            flops=34 * half * width * units, bytes_accessed=12 * width * units, transcendentals=0
        ),
        name="feed_forward",
    )(
        info, rows, other, upstream, upstream, hidden, gate_weight, up_weight, down_weight,
        gate_weight, up_weight, down_weight,
    )


def fixed(shape):
    return pl.BlockSpec(shape, lambda *_: (0,) * len(shape), pipeline_mode=pl.Buffered(1))


def root_mean(value):
    return lax.rsqrt(jnp.mean(value * value, axis=-1, keepdims=True) + EPS)


def root_mean_back(grad, gain, value):
    scaled = grad * gain
    inverse = root_mean(value)
    along = jnp.mean(value * scaled, axis=-1, keepdims=True)
    return inverse * scaled - value * (inverse * inverse * inverse * along)


def project_kernel(with_queries, info, chosen_ref, embed_ref, gain_ref, pair_own, pair_near, pair_far, *refs):
    embedded = to_low(matmul(chosen_ref[...], embed_ref[...]))
    value = embedded.astype(jnp.float32)
    low = to_low(value * root_mean(value) * gain_ref[...])
    pair_ref = refs[-3] if with_queries else refs[-1]
    at = 0
    for ref in (pair_own, pair_near, pair_far):
        pair_ref[:, at : at + ref.shape[1]] = matmul(low, ref[...])
        at += ref.shape[1]
    if not with_queries:
        return
    near_ref, mid_a, mid_b, far_a, far_b, _, embedded_ref, query_ref = refs
    embedded_ref[...] = embedded
    near = near_ref.shape[1]
    step = mid_a.shape[1]
    half = mid_a.shape[0]
    query_ref[:, :near] = matmul(low, near_ref[...])
    for start, upper, lower in ((near, mid_a, mid_b), (near + step, far_a, far_b)):
        query_ref[:, start : start + step] = matmul(low[:, :half], upper[...]) + matmul(
            low[:, half:], lower[...]
        )


def project(info, chosen, embed, gain, pair_weights, query_weights, pair_before):
    rows, width = chosen.shape
    block = rows // 2
    wide = embed.shape[1]
    row = pl.BlockSpec((block, wide), lambda i, s: (i, 0))
    pairs = sum(weight.shape[1] for weight in pair_weights)
    before = [] if pair_before is None else [pair_before]
    more = bool(query_weights)
    return pl.pallas_call(
        functools.partial(project_kernel, more),
        grid_spec=pltpu.PrefetchScalarGridSpec(
            num_scalar_prefetch=1,
            grid=(2,),
            in_specs=[
                pl.BlockSpec((block, width), lambda i, s: (i, 0)),
                fixed(embed.shape),
                fixed((1, wide)),
                *[fixed(weight.shape) for weight in pair_weights],
                *[fixed(weight.shape) for weight in query_weights],
                *[pl.BlockSpec(memory_space=pl.ANY)] * len(before),
            ],
            out_specs=[pl.BlockSpec((block, pairs), lambda i, s: (s[i], 0))] + [row, row] * more,
        ),
        out_shape=[jax.ShapeDtypeStruct((2 * rows, pairs), jnp.float32)]
        + [
            jax.ShapeDtypeStruct((rows, wide), jnp.bfloat16),
            jax.ShapeDtypeStruct((rows, wide), jnp.float32),
        ]
        * more,
        input_output_aliases={7: 0} if before else {},
        compiler_params=pltpu.CompilerParams(
            dimension_semantics=("arbitrary",), vmem_limit_bytes=VMEM_LIMIT
        ),
        cost_estimate=pl.CostEstimate(flops=1 << 30, bytes_accessed=1 << 20, transcendentals=0),
        name="project",
    )(info, chosen, embed, gain.reshape(1, -1), *pair_weights, *query_weights, *before)


def output_kernel(rows_ref, embedded_ref, gain_ref, near_ref, mid_a, mid_b, far_a, far_b, hidden_ref, low_ref):
    total = embedded_ref[...].astype(jnp.float32)
    at = 0
    for ref in (near_ref, mid_a, mid_b, far_a, far_b):
        total = total + matmul(rows_ref[:, at : at + ref.shape[0]], ref[...])
        at += ref.shape[0]
    hidden_ref[...] = total
    low_ref[...] = to_low(total * root_mean(total) * gain_ref[...])


def output_project(part, rows, embedded, gain, weights):
    block, wide = rows.shape
    spec = pl.BlockSpec((block, wide), lambda i: (0, 0))
    return pl.pallas_call(
        output_kernel,
        grid=(1,),
        in_specs=[
            spec,
            pl.BlockSpec((block, wide), lambda i: (part, 0)),
            fixed((1, wide)),
            *[fixed(weight.shape) for weight in weights],
        ],
        out_specs=[spec, spec],
        out_shape=[
            jax.ShapeDtypeStruct((block, wide), jnp.float32),
            jax.ShapeDtypeStruct((block, wide), jnp.bfloat16),
        ],
        compiler_params=pltpu.CompilerParams(
            dimension_semantics=("arbitrary",), vmem_limit_bytes=VMEM_LIMIT
        ),
        cost_estimate=pl.CostEstimate(flops=4 << 30, bytes_accessed=12 << 20, transcendentals=0),
        name="output_project",
    )(rows, embedded, gain.reshape(1, -1), *weights)


def hidden_backward_kernel(
    info, here_ref, came_ref, hidden_ref, rising_ref, gain_ref, near_ref, mid_a, mid_b, far_a, far_b,
    grad_ref, rows_ref,
):
    grad = here_ref[...].astype(jnp.float32) + came_ref[...].astype(jnp.float32)
    total = rising_ref[...].astype(jnp.float32) + root_mean_back(grad, gain_ref[...], hidden_ref[...])
    grad_ref[...] = total
    low = to_low(total)
    at = 0
    for ref in (near_ref, mid_a, mid_b, far_a, far_b):
        rows_ref[:, at : at + ref.shape[0]] = to_low(matmul_last(low, ref[...]))
        at += ref.shape[0]


def hidden_backward(info, here, came, hidden, upstream, gain, weights):
    block, wide = hidden.shape
    spec = pl.BlockSpec((block, wide), lambda i, s: (0, 0))
    return pl.pallas_call(
        hidden_backward_kernel,
        grid_spec=pltpu.PrefetchScalarGridSpec(
            num_scalar_prefetch=1,
            grid=(1,),
            in_specs=[
                spec,
                spec,
                spec,
                pl.BlockSpec((block, wide), lambda i, s: (s[0], 0)),
                fixed((1, wide)),
                *[fixed(weight.shape) for weight in weights],
            ],
            out_specs=[spec, spec],
        ),
        out_shape=[
            jax.ShapeDtypeStruct((block, wide), jnp.float32),
            jax.ShapeDtypeStruct((block, wide), jnp.bfloat16),
        ],
        compiler_params=pltpu.CompilerParams(
            dimension_semantics=("arbitrary",), vmem_limit_bytes=VMEM_LIMIT
        ),
        cost_estimate=pl.CostEstimate(flops=4 << 30, bytes_accessed=14 << 20, transcendentals=0),
        name="hidden_backward",
    )(info, here, came, hidden, upstream, gain.reshape(1, -1), *weights)


def embed_backward_kernel(
    info, query_ref, own_ref, came_ref, short_ref, cos_ref, sin_ref, first_ref, second_ref, embedded_ref, gain_ref,
    embed_ref, near_ref, mid_a, mid_b, far_a, far_b, pair_own, pair_near, pair_far, grad_ref, token_ref,
):
    total = None
    weights = [pair_own[:, :PAIR], pair_own[:, PAIR:], pair_near[...], pair_far[...]]
    for group, weight in enumerate(weights):
        head = info[2 + group]
        short = jnp.where(pl.program_id(0) == 0, short_ref[head].astype(jnp.float32), 0.0)
        pair = own_ref[head] + came_ref[head].astype(jnp.float32) + short
        low = to_low(turn_left(pair, cos_ref[...], -sin_ref[...]))
        term = matmul_last(low, weight)
        total = term if total is None else total + term
    near = near_ref.shape[1]
    step = mid_a.shape[1]
    half = mid_a.shape[0]
    total = total + matmul_last(query_ref[:, :near], near_ref[...])
    mid = query_ref[:, near : near + step]
    far = query_ref[:, near + step : near + 2 * step]
    spread = jnp.concatenate(
        [
            matmul_last(mid, mid_a[...]) + matmul_last(far, far_a[...]),
            matmul_last(mid, mid_b[...]) + matmul_last(far, far_b[...]),
        ],
        axis=1,
    )
    value = embedded_ref[...].astype(jnp.float32)
    hidden = jnp.where(pl.program_id(0) == 0, first_ref[...], second_ref[...])
    grad = to_low(hidden + root_mean_back(total + spread, gain_ref[...], value))
    grad_ref[...] = grad
    token_ref[...] = to_low(matmul_last(grad, embed_ref[...]))


def embed_backward(
    info, query_grad, own, came, short, tables, hidden_grads, embedded, gain, embed, query_weights, pair_weights
):
    rows, wide = embedded.shape
    block = rows // 2
    heads = own.shape[0]
    row = pl.BlockSpec((block, wide), lambda i, s: (i, 0))
    once = pl.BlockSpec((block, wide), lambda i, s: (0, 0))
    pair = pl.BlockSpec((heads, block, PAIR), lambda i, s: (0, i, 0))
    table = pl.BlockSpec((block, PAIR), lambda i, s: (s[i], 0))
    return pl.pallas_call(
        embed_backward_kernel,
        grid_spec=pltpu.PrefetchScalarGridSpec(
            num_scalar_prefetch=1,
            grid=(2,),
            in_specs=[
                row, pair, pair, pl.BlockSpec((heads, block, PAIR), lambda i, s: (0, 0, 0)), table, table, once, once, row, fixed((1, wide)), fixed(embed.shape),
                *[fixed(weight.shape) for weight in (*query_weights, *pair_weights)],
            ],
            out_specs=[row, pl.BlockSpec((block, embed.shape[0]), lambda i, s: (i, 0))],
        ),
        out_shape=[
            jax.ShapeDtypeStruct((rows, wide), jnp.bfloat16),
            jax.ShapeDtypeStruct((rows, embed.shape[0]), jnp.bfloat16),
        ],
        compiler_params=pltpu.CompilerParams(
            dimension_semantics=("arbitrary",), vmem_limit_bytes=VMEM_LIMIT
        ),
        cost_estimate=pl.CostEstimate(flops=12 << 30, bytes_accessed=20 << 20, transcendentals=0),
        name="embed_backward",
    )(
        info, query_grad, own, came, short, tables[0], tables[1], *hidden_grads, embedded, gain.reshape(1, -1), embed,
        *query_weights, *pair_weights,
    )


def own_route(own, local_vocab):
    places = jnp.arange(own.shape[0], dtype=jnp.int32)
    same = own[:, None] == own[None, :]
    repeated = jnp.any(same & (places[:, None] > places[None, :]), axis=1)
    owner = own // local_vocab
    before = (owner[:, None] == owner[None, :]) & (own[None, :] < own[:, None])
    rank = jnp.sum((before & jnp.logical_not(repeated)[None, :]).astype(jnp.int32), axis=1)
    return (rank, owner)


def asked_of_me(asked, me, local_vocab):
    entries = me * local_vocab + jnp.arange(local_vocab, dtype=jnp.int32)
    present = jnp.any(asked[:, :, None] == entries[None, None, :], axis=1)
    places = jnp.arange(local_vocab, dtype=jnp.int32)
    lower = places[:, None] < places[None, :]
    standing = matmul(present.astype(jnp.bfloat16), lower.astype(jnp.bfloat16)).astype(jnp.int32)
    return (present, standing)


def sender_choice(present, standing, turn, capacity):
    place = jnp.arange(capacity, dtype=jnp.int32)
    slot = jnp.where(place < capacity - 1, turn * (capacity - 1) + place, -1)
    chosen = present[:, None, :] & (standing[:, None, :] == slot[None, :, None])
    return chosen.astype(jnp.bfloat16).reshape(present.shape[0] * capacity, present.shape[1])


def taker_choice(own_rank, own_owner, turn, capacity, devices):
    inside = own_rank - turn * (capacity - 1)
    valid = (inside >= 0) & (inside < capacity - 1)
    place = jnp.where(valid, own_owner * capacity + inside, -1)
    return (place[:, None] == jnp.arange(devices * capacity, dtype=jnp.int32)[None, :]).astype(
        jnp.bfloat16
    )


def exchange(value):
    return lax.all_to_all(value, ("dp", "mp"), 0, 0, tiled=True)


def ordered_blocks(first, own_two, other_two):
    return jnp.where(
        first,
        jnp.concatenate([own_two[0], other_two[0], other_two[1], own_two[1]], axis=0),
        jnp.concatenate([other_two[0], own_two[0], own_two[1], other_two[1]], axis=0),
    )


def body(
    pieces,
    counts,
    token_index,
    hyper_input,
    hyper_output,
    hyper_expand,
    hyper_reduce,
    hyper_norms,
    embed_weight,
    attention_gain,
    dense_gain,
    frozen_query_weight,
    frozen_key_weight,
    frozen_value_weight,
    frozen_output_weight,
    gate_weight,
    up_weight,
    down_weight,
    upstream,
):
    local_vocab = pieces.shape[0]
    mp_count = lax.axis_size("mp")
    devices = lax.axis_size("dp") * mp_count
    mp_index = lax.axis_index("mp")
    me = lax.axis_index("dp") * mp_count + mp_index
    core = (me >> 1) & 1
    lead = mp_index == 0
    bits = log2_of(devices)
    far_bits = list(range(bits - 1, 1, -1))
    length = token_index.shape[0]
    block = length // BLOCK_PARTS
    capacity = max(16, length // devices)

    norm_count = hyper_norms.shape[1]
    in_width = hyper_input.shape[1]
    norm_lanes = jnp.pad(hyper_norms, ((0, 0), (0, PAIR - norm_count)))
    cut = token_index.reshape(BLOCK_PARTS, block)
    own_tokens = jnp.where(
        lead, jnp.concatenate([cut[0], cut[3]]), jnp.concatenate([cut[1], cut[2]])
    )
    digits = jnp.concatenate([own_tokens // PAIR, own_tokens % PAIR]).astype(jnp.bfloat16)
    digits = digits.reshape(hyper_input.shape[0], -1)
    digit_width = digits.shape[1]
    digit_lanes = jnp.pad(digits, ((0, 0), (0, -digit_width % PAIR)))
    kv_local = frozen_key_weight.shape[1] // HEAD_WIDTH
    key_own = jnp.concatenate(
        [
            weight[:, at * HEAD_WIDTH : (at + 1) * HEAD_WIDTH]
            for at in range(kv_local)
            for weight in (frozen_key_weight, frozen_value_weight)
        ],
        axis=1,
    )
    key_near = swap(lax.dynamic_slice_in_dim(key_own, core * PAIR, PAIR, 1), 1, devices)
    query_cut = frozen_query_weight.shape[1] // 2
    side = (me >> 2) & 1
    half_in = frozen_query_weight.shape[0] // 2
    query_slice = lax.dynamic_slice(
        frozen_query_weight, (side * half_in, core * query_cut), (half_in, query_cut)
    )
    half_out = query_cut // 2
    output_slice = lax.dynamic_slice_in_dim(
        frozen_output_weight, core * query_cut + side * half_out, half_out, 0
    )
    count_rows = jnp.broadcast_to(counts[:, None, None], (counts.shape[0], 1, PAIR))
    early_x = far_bits[:1] + [0] + far_bits[1:] + [1]
    late_y = far_bits[:-1] + [0] + far_bits[-1:] + [1]
    gathers = [
        (jnp.concatenate([hyper_input, norm_lanes, digit_lanes], axis=1), late_y),
        (jnp.concatenate([hyper_output, hyper_expand], axis=1), late_y),
        (hyper_reduce, early_x),
    ]
    gather_held = [x for x, _ in gathers]

    def send(which, at):
        return swap(gather_held[which], 1 << gathers[which][1][at], devices)

    def join(which, came, at):
        order = gathers[which][1]
        return gather_join(gather_held[which], came, order[at], order[:at], me)

    for at in range(bits - 3):
        gather_held = [join(which, send(which, at), at) for which in range(3)]
        if at == bits - 4:
            gather_held, key_near, query_slice, output_slice, count_rows = lax.optimization_barrier(
                (gather_held, key_near, query_slice, output_slice, count_rows)
            )
            key_far = swap(key_near, 2, devices)
    later_came = [send(which, bits - 3) for which in (1, 2)]
    gather_held[0] = join(0, send(0, bits - 3), bits - 3)
    begun = gather_held[:1]
    in_held = join(0, send(0, bits - 2), bits - 2)
    in_held, later_came = lax.optimization_barrier((in_held, later_came))
    gather_held = [in_held] + [join(which, came, bits - 3) for which, came in zip((1, 2), later_came)]
    later_came = [send(which, bits - 2) for which in (1, 2)]
    in_came = send(0, bits - 1)
    in_weight = join(0, in_came, bits - 1)
    small = gather_join(
        in_held[:, in_width + PAIR :], in_came[:, in_width + PAIR :], late_y[-1], late_y[:-1], me
    )
    embed_full = lax.all_gather(embed_weight, ("dp", "mp"), axis=0, tiled=True)
    all_digits = small[:, :digit_width].reshape(devices, 2, 2 * block)
    all_digits = all_digits.astype(jnp.int32)
    asked = all_digits[:, 0] * PAIR + all_digits[:, 1]

    query_slice, *_ = lax.optimization_barrier((query_slice, *begun))
    query_near = swap(query_slice, 1, devices)

    def by_side(own, other):
        return [jnp.where(side == 0, own, other), jnp.where(side == 0, other, own)]

    other_base = (1 - mp_index) * kv_local
    head_order = [mp_index * kv_local, mp_index * kv_local + 1, other_base + core, other_base + 1 - core]

    slot_mixed, slot_probs, hyper_attended, lead_rows, norm_rows = slot_attention(
        pieces, count_rows, in_weight
    )
    asked, _ = lax.optimization_barrier((asked, hyper_attended))
    hyper_attended, embed_full, later_came, query_near = lax.optimization_barrier(
        (hyper_attended, embed_full, later_came, query_near)
    )
    last = late_y[-1]

    def joined(which, parts):
        order = gathers[which][1]
        halves = [gather_join(*parts[at : at + 2], order[-2], order[:-2], me) for at in (0, 2)]
        return gather_join(*halves, last, order[:-1], me)

    later_parts = [(gather_held[which], came) for which, came in zip((1, 2), later_came)]
    later_parts = [(*own, *[swap(x, 1 << last, devices) for x in own]) for own in later_parts]
    together = hyper_input.shape[0] * 2 % 16 == 0
    if together:
        forward_weights = later_parts
    else:
        forward_weights = [[joined(which, later_parts[which - 1])] for which in (1, 2)]
    query_far_row = swap(query_near, 4, devices)
    output_slice, _ = lax.optimization_barrier((output_slice, query_near))
    output_near = swap(output_slice, 1, devices)
    places = jnp.stack([core, side])
    pooled, hyper_hidden = units_forward(
        devices // 8, places, hyper_attended, lead_rows, *forward_weights, norm_rows
    )
    _, query_far_row = lax.optimization_barrier((pooled, query_far_row))
    present, standing = asked_of_me(asked, me, local_vocab)
    own_rank, own_owner = own_route(lax.dynamic_index_in_dim(asked, me, 0, False), local_vocab)
    most = jnp.max(jnp.sum(present.astype(jnp.int32), axis=1))
    needed = ((most + capacity - 2) // (capacity - 1)).astype(jnp.float32)

    def fetch(turn):
        sent = matmul(sender_choice(present, standing, turn, capacity), pooled)
        sent = sent.reshape(devices, capacity, pooled.shape[1])
        free = lax.broadcasted_iota(jnp.int32, sent.shape, 1) == capacity - 1
        sent = to_low(jnp.where(free, needed, sent)).reshape(devices * capacity, pooled.shape[1])
        came = exchange(sent)
        picked = matmul(taker_choice(own_rank, own_owner, turn, capacity, devices), came)
        return (to_low(picked), came)

    chosen_own, came = fetch(0)
    query_near = by_side(query_near, query_far_row)
    query_far = [swap(x, 2, devices) for x in query_near]
    chosen_own, came, query_far, output_near = lax.optimization_barrier(
        (chosen_own, came, query_far, output_near)
    )
    output_far_row = swap(output_near, 4, devices)
    needs = came.reshape(devices, capacity, pooled.shape[1])[:, capacity - 1, 0]
    rounds = jnp.max(needs.astype(jnp.float32)).astype(jnp.int32)
    chosen_own = lax.fori_loop(1, rounds, lambda turn, chosen: chosen + fetch(turn)[0], chosen_own)
    chosen_other = swap(chosen_own, 1, devices)

    tables = rope_tables(length)
    own_at = (mp_index, 3 - mp_index)
    own_base = tuple(at * block for at in own_at)
    other_start = ((1 - mp_index) * block, (2 + mp_index) * block)
    infos = [jnp.stack([at] + head_order).astype(jnp.int32) for at in own_at]

    other_at = (1 - mp_index, 2 + mp_index)
    query_weights = (frozen_query_weight, *query_near, *query_far)
    pair_weights = (key_own, key_near, key_far)
    own_info = jnp.stack(own_at).astype(jnp.int32)
    other_info = jnp.stack(other_at).astype(jnp.int32)
    pair_pre, embedded, queries = project(
        own_info, chosen_own, embed_full, attention_gain, pair_weights, query_weights, None
    )
    (pair_pre,) = project(
        other_info, chosen_other, embed_full, attention_gain, pair_weights, (), pair_pre
    )
    pair_pre, output_far_row = lax.optimization_barrier((pair_pre, output_far_row))
    output_near = by_side(output_near, output_far_row)
    output_far = [swap(x, 2, devices) for x in output_near]
    output_weights = (frozen_output_weight, *output_near, *output_far)
    spans = (2 * block, length)

    sums = [None, None]
    lows = [None, None]
    hidden_parts = [None, None]
    second_low = [None, None]
    second_other = [None, None]
    for part in (1, 0):
        flat, lows[part], sums[part] = attention_forward(
            infos[part], queries, pair_pre, tables, part, spans[part]
        )
        hidden_parts[part], second_low[part] = output_project(
            part, flat, embedded, dense_gain, output_weights
        )
        second_other[part] = swap(second_low[part], 1, devices)
        pair_pre, second_low[part] = lax.optimization_barrier((pair_pre, second_low[part]))

    second_low, second_other[1] = lax.optimization_barrier((second_low, second_other[1]))
    dense_rows = [None, None]
    second_came = [None, None]
    for part in (1, 0):
        info = jnp.stack([own_at[part], other_at[part]]).astype(jnp.int32)
        grad_second, dense_rows[part] = feed_forward(
            second_low[part], second_other[part], upstream, hidden_parts[part], info,
            gate_weight, up_weight, down_weight,
        )
        second_came[part] = (grad_second[:block], swap(grad_second[block:], 1, devices))

    share = upstream.shape[1] // mp_count

    def columns(value, index):
        return lax.dynamic_slice_in_dim(value, index * share, share, 1)

    leaving_columns = [columns(dense_rows[part], 1 - mp_index) for part in range(2)]
    dense_came = [None, swap(leaving_columns[1], 1, devices)]

    def pick_block(value, at):
        return lax.dynamic_slice_in_dim(value, at * block, block, 1)

    query_grad = None
    grad_hidden = [None, None]
    pair_grads = [None, None]
    for part in (1, 0):
        here, came = second_came[part]
        if part == 1:
            here, came, dense_rows[0] = lax.optimization_barrier((here, came, dense_rows[0]))
        else:
            here, came, query_grad, dense_came[1] = lax.optimization_barrier(
                (here, came, query_grad, dense_came[1])
            )
        grad_hidden[part], grad_attended = hidden_backward(
            infos[part], here, came, hidden_parts[part], upstream, dense_gain, output_weights
        )
        taken = (lows[part], grad_attended, sums[part], pair_pre, tables, part, spans[part])
        if part == 1:
            query_grad, pair_grads[part] = attention_backward(infos[part], *taken, (0, 4), [])
            continue
        query_grad, pair_grads[part] = attention_backward(infos[part], *taken, (0, 2), [query_grad])
        leaving = to_low(jnp.concatenate([pick_block(pair_grads[1], at) for at in other_at], axis=1))
        leaving, pair_grads[part] = lax.optimization_barrier((leaving, pair_grads[part]))
        came_long = swap(leaving, 1, devices)
        query_grad, pair_grads[part] = attention_backward(
            infos[part], *taken, (2, 2), [query_grad, pair_grads[part]]
        )

    pair_grads[0], came_long = lax.optimization_barrier((pair_grads[0], came_long))
    came_short = swap(to_low(pick_block(pair_grads[0], other_at[0])), 1, devices)
    pair_own = jnp.concatenate(
        [
            pick_block(pair_grads[1], own_at[0]) + pick_block(pair_grads[0], own_at[0]),
            pick_block(pair_grads[1], own_at[1]),
        ],
        axis=1,
    )

    _, leaving_columns[0] = lax.optimization_barrier((came_short, leaving_columns[0]))
    dense_came[0] = swap(leaving_columns[0], 1, devices)

    embedded_grad_low, token_grad = embed_backward(
        jnp.stack([*own_at, *head_order]).astype(jnp.int32), query_grad, pair_own, came_long, came_short, tables, grad_hidden, embedded,
        attention_gain, embed_full, query_weights, pair_weights,
    )
    own_out = []
    other_out = []
    for part in range(2):
        kept = columns(dense_rows[part], mp_index).astype(jnp.float32)
        arrived = dense_came[part].astype(jnp.float32)
        own_out.append(to_low(kept[:block] + arrived[block:]))
        other_out.append(to_low(kept[block:] + arrived[:block]))
    model_out = ordered_blocks(lead, own_out, other_out)
    embed_grad = to_low(matmul_first(chosen_own, embedded_grad_low))

    def give_back(turn, total):
        taker = taker_choice(own_rank, own_owner, turn, capacity, devices)
        leaving = matmul_first(taker, token_grad).astype(jnp.bfloat16)
        came = exchange(leaving)
        return total + matmul_first(sender_choice(present, standing, turn, capacity), came)

    grad_pooled = give_back(0, jnp.zeros(pooled.shape, jnp.float32))
    grad_pooled = lax.fori_loop(1, rounds, give_back, grad_pooled)

    back_order = [1, 0] + far_bits[::-1]

    def scatter(held, order, at):
        return scatter_send(held, order[at], order[at + 1 :], me, devices)

    embed_held = scatter_add(*scatter(embed_grad, back_order, 0))
    embed_held, grad_pooled = lax.optimization_barrier((embed_held, grad_pooled))
    embed_held = scatter_add(*scatter(embed_held, back_order, 1))
    hidden_grad, attended_grad, later_norms, *unit_sums = units_backward(
        devices // 8, places, grad_pooled, hyper_hidden, hyper_attended, *forward_weights, norm_rows
    )
    hidden_grad, embed_held = lax.optimization_barrier((hidden_grad, embed_held))
    held = [embed_held, *([unit_sums[:2], unit_sums[2:]] if together else unit_sums)]
    turned_order = [back_order[0], back_order[2], back_order[3], back_order[1]] + back_order[4:]
    orders = [back_order, back_order, turned_order]
    ahead = [2, 0, 0]

    def depart(at):
        moving = []
        for x, order, skip in zip(held, orders, ahead):
            if at + skip >= bits:
                moving.append((x, None))
            elif isinstance(x, list):
                moving.append((x[0], swap(x[1], 1 << order[0], devices)))
            else:
                moving.append(scatter(x, order, at + skip))
        return moving

    def arrive(moving):
        return [x if came is None else scatter_add(x, came) for x, came in moving]

    slots_saved = (pieces, slot_mixed, slot_probs)
    slots_held = (None, None, later_norms)
    for part in range(SLOT_PARTS):
        moving = depart(part)
        slots_held = slot_backward(
            part, SLOT_PARTS, slots_held, slots_saved, (attended_grad, hidden_grad), in_weight, norm_rows
        )
        slots_held, moving = lax.optimization_barrier((tuple(slots_held), moving))
        held = arrive(moving)
    pieces_grad, input_grad, _ = slots_held
    input_held = input_grad
    moving = depart(SLOT_PARTS)
    cut = in_width // (2 * PAIR) * PAIR + PAIR
    for at in range(bits):
        if at == 1:
            input_held = [input_held[:, :cut], input_held[:, cut:]]
        if at in (1, 2):
            crossing = [back_order, [back_order[0], back_order[2], back_order[1]] + back_order[3:]]
            input_held = [scatter_add(*scatter(x, order, at)) for x, order in zip(input_held, crossing)]
            if at == 2:
                input_held = jnp.concatenate(input_held, axis=1)
        else:
            input_held = scatter_add(*scatter(input_held, back_order, at))
        if at > 0:
            _, moving = lax.optimization_barrier((input_held, moving))
            held = arrive(moving)
            moving = depart(SLOT_PARTS + at)
    held = arrive(moving)
    embed_own, wide_own, reduce_own, input_own = (*held, input_held)
    out_width = hyper_output.shape[1]
    return (
        model_out,
        pieces_grad,
        input_own[:, :in_width],
        wide_own[:, :out_width],
        wide_own[:, out_width:],
        reduce_own,
        input_own[:, in_width : in_width + norm_count],
        embed_own,
    )


def solution(mesh):
    return jax.shard_map(
        body,
        mesh=mesh,
        in_specs=(
            P(("dp", "mp"), None, None),
            P(("dp", "mp")),
            P("dp"),
            P(("dp", "mp"), None),
            P(("dp", "mp"), None),
            P(("dp", "mp"), None),
            P(("dp", "mp"), None),
            P(("dp", "mp"), None),
            P(("dp", "mp"), None),
            P(),
            P(),
            P(None, "mp"),
            P(None, "mp"),
            P(None, "mp"),
            P("mp", None),
            P(None, "mp"),
            P(None, "mp"),
            P("mp", None),
            P("dp", None),
        ),
        out_specs=(
            P("dp", "mp"),
            P(("dp", "mp"), None, None),
            P(("dp", "mp"), None),
            P(("dp", "mp"), None),
            P(("dp", "mp"), None),
            P(("dp", "mp"), None),
            P(("dp", "mp"), None),
            P(("dp", "mp"), None),
        ),
        check_vma=False,
    )
```
